128 devices in a mesh: dp: 16 (over x, y), expert: 8 (over z, core).
Axes of the slice: x: 4, y: 4, z: 4, core: 2. Of those that a mesh axis runs over, the one named last changes fastest.
Arguments:
- tokens: bfloat16 [16, 2048, 768], P('dp', 'expert'), may hold values from -6 to 6
- group_kind: int32 [16], P('dp'), may hold values from 0 to 1, as said below
- routes: int32 [16, 2048, 2], P('dp', 'expert'), may hold values from 0 to 15, all different within a row
- norm1_gain: float32 [768], replicated, may hold values from 0.1 to 1.9
- qkv_weight: bfloat16 [768, 2304], replicated, may hold values from -0.21875 to 0.21875
- proj_weight: bfloat16 [768, 768], replicated, may hold values from -2.5 to 2.5
- norm2_gain: float32 [768], replicated, may hold values from 0.1 to 1.9
- router_weight: bfloat16 [768, 16], replicated, may hold values from -0.15625 to 0.15625
- frozen_in: bfloat16 [8, 768, 3072], P('expert'), may hold values from -0.21875 to 0.21875
- frozen_out: bfloat16 [8, 3072, 768], P('expert'), may hold values from -0.15625 to 0.15625
- new_in: bfloat16 [8, 768, 3072], P('expert'), may hold values from -0.21875 to 0.21875
- new_out: bfloat16 [8, 3072, 768], P('expert'), may hold values from -0.15625 to 0.15625
- out_grad: bfloat16 [16, 2048, 768], P('dp', 'expert'), may hold values from -6 to 6
Outputs:
- mixed: bfloat16 [16, 2048, 768], P('dp', 'expert')
- tokens_grad: float32 [16, 2048, 768], P('dp', 'expert')
- norm1_gain_grad: float32 [768], P(('dp', 'expert'))
- qkv_grad: float32 [768, 2304], P(('dp', 'expert'))
- proj_grad: float32 [768, 768], P(('dp', 'expert'))
- norm2_gain_grad: float32 [768], P(('dp', 'expert'))
- router_grad: float32 [768, 16], P(('dp', 'expert'))
- new_in_grad: float32 [8, 768, 3072], P('expert', 'dp')
- new_out_grad: float32 [8, 3072, 768], P('expert', 'dp')
The draws below stay inside these ranges and needn't reach their ends.
Inputs may be any that keep to these rules, and one draw needn't show every extreme that they name: `group_kind`: exactly half of the 16 groups are of kind 1. `routes`: the two experts of a token differ.
All inputs are finite; a program needn't handle non-finite values.
Results may differ from the reference program's by a relative error of at most 0.017.
Values may be sent and summed in bfloat16 or wider, within the bound.
A program may use at most 256 MiB of HBM per device.

```python
import jax
import jax.numpy as jnp
from jax import lax

D = 768
HEADS = 12
HD = 64
FF = 3072
TOP = 2
LONG = 2048
SEQ_GROUPS = 16
GROUP_TOK = 256
FROZEN = 8
NEW = 8
EXPERTS = 16
CAP = 48
N_EXPERT = 8


def draw_group_kind(key, part):
    key = jax.random.fold_in(key, 3)
    order = jax.random.permutation(key, SEQ_GROUPS)
    return (order < SEQ_GROUPS // 2).astype(jnp.int32)


def levels(rng, extent, pieces, smallest, high):
    factor_of, own = 1.0, jax.random.fold_in(rng, 6)
    for position, shards_of in pieces:
        heights = jnp.exp(jax.random.uniform(jax.random.fold_in(own, position), (shards_of,), jnp.float32, smallest / len(pieces), high / len(pieces)))
        factor_of = factor_of * jnp.repeat(heights, extent[position] // shards_of).reshape([-1 if axis == position else 1 for axis in range(len(extent))])
    return factor_of


def choose_distinct(stream_key, rows, number_of, top, lift):
    order = jax.random.permutation(jax.random.fold_in(stream_key, 1), number_of)
    favour = order
    for power in range(3):
        favour = favour * favour // number_of
    favour = favour * lift // number_of
    lots = jax.random.randint(jax.random.fold_in(stream_key, 2), (rows, number_of), 0, 4096) + favour
    holders = jax.random.permutation(jax.random.fold_in(stream_key, 3), rows)[jnp.arange(number_of) % rows]
    lots = jnp.where(jnp.arange(rows)[:, None] == holders[None, :], 1 << 14, lots)
    score = lots * number_of + jnp.arange(number_of)
    return lax.top_k(score.astype(jnp.int32), top)[1].astype(jnp.int32)


def noise(own_key, shape, deviation, reach, split=(), kind=jnp.bfloat16):
    values = jax.random.normal(own_key, shape, jnp.float32) * deviation
    if len(split) > 0:
        values = levels(own_key, shape, split, -0.22, 0.18) * values
    return jnp.clip(values, min=-reach, max=reach).astype(kind)


def setup_inputs(seed: int = 0) -> dict:
    keys = jax.random.split(jax.random.key(seed), 14)
    return {
        "tokens": noise(keys[0], (SEQ_GROUPS, LONG, D), 1.0, 6.0, ((0, 16), (1, 8))),
        "group_kind": draw_group_kind(jax.random.fold_in(keys[13], 71), 0),
        "routes": choose_distinct(keys[2], SEQ_GROUPS * LONG, EXPERTS, TOP, 1024).reshape((SEQ_GROUPS, LONG, TOP)),
        "norm1_gain": jnp.clip(1.0 + 0.18 * jax.random.normal(keys[3], (D,), jnp.float32), 0.1, 1.9),
        "qkv_weight": noise(keys[4], (D, 3 * D), D ** -0.5, 0.21875),
        "proj_weight": noise(keys[5], (D, D), (D // 128) ** -0.5, 2.5),
        "norm2_gain": jnp.clip(1.0 + 0.18 * jax.random.normal(keys[6], (D,), jnp.float32), 0.1, 1.9),
        "router_weight": noise(keys[7], (D, EXPERTS), (2 * D) ** -0.5, 0.15625),
        "frozen_in": noise(keys[8], (FROZEN, D, FF), D ** -0.5, 0.21875, ((0, 8),)),
        "frozen_out": noise(keys[9], (FROZEN, FF, D), (FF // 2) ** -0.5, 0.15625, ((0, 8),)),
        "new_in": noise(keys[10], (NEW, D, FF), D ** -0.5, 0.21875, ((0, 8),)),
        "new_out": noise(keys[11], (NEW, FF, D), (FF // 2) ** -0.5, 0.15625, ((0, 8),)),
        "out_grad": noise(keys[12], (SEQ_GROUPS, LONG, D), 1.0, 6.0, ((0, 16), (1, 8))),
    }


@jax.custom_vjp
def low(v):
    return lax.optimization_barrier(v.astype(jnp.bfloat16)).astype(jnp.float32)

@jax.custom_vjp
def low_back(v):
    return v

def low_keep(v):
    return (low(v), None)

def low_pass(kept, grad):
    return (grad,)

def back_keep(v):
    return (v, None)

def back_low(kept, grad):
    return (low(grad),)
low.defvjp(low_keep, low_pass)
low_back.defvjp(back_keep, back_low)
highest = lax.Precision.HIGHEST
epsilon = 1e-05

def norm_gain(values, gain):
    average = lax.optimization_barrier(jnp.mean(values, axis=-1, keepdims=True))
    centred = values - average
    variance = lax.optimization_barrier(jnp.mean(centred * centred, axis=-1, keepdims=True))
    return centred * lax.rsqrt(variance + epsilon) * gain

def group_forward(group_items, gain_one, qkv_w, proj_w, gain_two, router_w, w_in, w_out):
    group_tokens, group_routes, group_kind_id = group_items
    hidden_one = low(norm_gain(group_tokens, gain_one))
    projected = low_back(low(jnp.dot(hidden_one, qkv_w, precision=highest)))
    queries = projected[:, :D].reshape(LONG, HEADS, HD)
    keys_all = projected[:, D:2 * D].reshape(LONG, HEADS, HD)
    values_all = projected[:, 2 * D:].reshape(LONG, HEADS, HD)
    scores = low_back(jnp.einsum('qhd,khd->hqk', queries, keys_all, precision=highest) * HD ** (-0.5))
    positions = jnp.arange(LONG, dtype=jnp.int32)
    seq_index = group_kind_id * (positions // (LONG // 2))
    allowed = (positions[None, :] <= positions[:, None]) & (seq_index[None, :] == seq_index[:, None])
    masked = jnp.where(allowed[None], scores, -1e+30)
    row_max = lax.optimization_barrier(jnp.max(masked, axis=-1, keepdims=True))
    exponent = jnp.exp(masked - row_max)
    probs = low(exponent / lax.optimization_barrier(jnp.sum(exponent, axis=-1, keepdims=True)))
    attended = jnp.einsum('hqk,khd->qhd', probs, values_all, precision=highest).reshape(LONG, D)
    attended = low_back(low(attended))
    branch = low_back(jnp.dot(attended, proj_w, precision=highest))
    residual = group_tokens + branch
    hidden_two = low(norm_gain(residual, gain_two))
    logits = low_back(jnp.dot(hidden_two, router_w, precision=highest))
    expert_ids = jnp.arange(EXPERTS, dtype=jnp.int32)
    pick_zero = (group_routes[:, 0:1] == expert_ids[None, :]).astype(jnp.int32)
    pick_one = (group_routes[:, 1:2] == expert_ids[None, :]).astype(jnp.int32)
    logit_zero = lax.optimization_barrier(jnp.sum(logits * pick_zero.astype(jnp.float32), axis=-1))
    logit_one = lax.optimization_barrier(jnp.sum(logits * pick_one.astype(jnp.float32), axis=-1))
    gate_zero = jax.nn.sigmoid(logit_zero - logit_one)
    gate_one = jax.nn.sigmoid(logit_one - logit_zero)
    named_count = (pick_zero + pick_one).reshape(N_EXPERT, GROUP_TOK, EXPERTS)
    earlier = (jnp.cumsum(named_count, axis=1) - named_count).reshape(LONG, EXPERTS)
    slot_zero = lax.optimization_barrier(jnp.sum(earlier * pick_zero, axis=-1))
    slot_one = lax.optimization_barrier(jnp.sum(earlier * pick_one, axis=-1))
    columns = jnp.arange(EXPERTS * CAP, dtype=jnp.int32)
    target_zero = group_routes[:, 0] * CAP + slot_zero
    target_one = group_routes[:, 1] * CAP + slot_one
    send_zero = ((target_zero[:, None] == columns[None, :]) & (slot_zero < CAP)[:, None]).astype(jnp.float32)
    send_one = ((target_one[:, None] == columns[None, :]) & (slot_one < CAP)[:, None]).astype(jnp.float32)
    dispatch = (send_zero + send_one).reshape(N_EXPERT, GROUP_TOK, EXPERTS * CAP)
    hidden_blocks = hidden_two.reshape(N_EXPERT, GROUP_TOK, D)
    buffers = low_back(jnp.einsum('nts,ntd->nsd', dispatch, hidden_blocks, precision=highest))
    buffers = buffers.reshape(N_EXPERT, EXPERTS, CAP, D).transpose(1, 0, 2, 3).reshape(EXPERTS, N_EXPERT * CAP, D)
    pre_act = low_back(jnp.einsum('esd,edf->esf', buffers, w_in, precision=highest))
    activated = low(jax.nn.gelu(pre_act, approximate=False))
    expert_out = low_back(low(jnp.einsum('esf,efd->esd', activated, w_out, precision=highest)))
    returned = expert_out.reshape(EXPERTS, N_EXPERT, CAP, D).transpose(1, 0, 2, 3).reshape(N_EXPERT, EXPERTS * CAP, D)
    mixing = low(gate_zero[:, None] * send_zero + gate_one[:, None] * send_one).reshape(N_EXPERT, GROUP_TOK, EXPERTS * CAP)
    combined = jnp.einsum('nts,nsd->ntd', mixing, returned, precision=highest).reshape(LONG, D)
    return residual + combined

def reference(tokens, group_kind, routes, norm1_gain, qkv_weight, proj_weight, norm2_gain, router_weight, frozen_in, frozen_out, new_in, new_out, out_grad):
    frozen_first = frozen_in.astype(jnp.float32)
    frozen_second = frozen_out.astype(jnp.float32)
    trainable = (norm1_gain, qkv_weight.astype(jnp.float32), proj_weight.astype(jnp.float32), norm2_gain, router_weight.astype(jnp.float32), new_in.astype(jnp.float32), new_out.astype(jnp.float32))

    def forward(token_values, params):
        gain_one, qkv_w, proj_w, gain_two, router_w, in_new, out_new = params
        w_in = jnp.concatenate([frozen_first, in_new], axis=0)
        w_out = jnp.concatenate([frozen_second, out_new], axis=0)

        def group_step(carried, group_items):
            return (carried, group_forward(group_items, gain_one, qkv_w, proj_w, gain_two, router_w, w_in, w_out))
        _, outputs = lax.scan(jax.checkpoint(group_step), jnp.zeros((), jnp.float32), (token_values, routes, group_kind))
        return outputs
    outputs, pullback = jax.vjp(forward, tokens.astype(jnp.float32), trainable)
    token_grad, weight_grads = pullback(out_grad.astype(jnp.float32))
    return (outputs.astype(jnp.bfloat16), token_grad, weight_grads[0], weight_grads[1], weight_grads[2], weight_grads[3], weight_grads[4], weight_grads[5], weight_grads[6])
```

```python
import jax
import jax.numpy as jnp
from jax import lax
from jax.sharding import PartitionSpec as P

HEADS = 12
HD = 64
TOP = 2
LONG = 2048


epsilon = 1e-05


def norm_parts(values):
    average = jnp.mean(values, axis=-1, keepdims=True)
    centred = values - average
    variance = jnp.mean(centred * centred, axis=-1, keepdims=True)
    inverse = lax.rsqrt(variance + epsilon)
    return (centred * inverse, inverse)


def norm_back(grad_normed, normed, inverse):
    first_mean = jnp.mean(grad_normed, axis=-1, keepdims=True)
    second_mean = jnp.mean(grad_normed * normed, axis=-1, keepdims=True)
    return inverse * (grad_normed - first_mean - normed * second_mean)


def gelu_slope(pre_act):
    cumulative = 0.5 * (1.0 + lax.erf(pre_act * 0.7071067811865476))
    density = jnp.exp(-0.5 * pre_act * pre_act) * 0.3989422804014327
    return cumulative + pre_act * density


def mask_between(seq_kind, query_pos, key_pos):
    half_length = LONG // 2
    query_seq = seq_kind * (query_pos // half_length)
    key_seq = seq_kind * (key_pos // half_length)
    return (key_pos[None, :] <= query_pos[:, None]) & (key_seq[None, :] == query_seq[:, None])


def masked_scores(queries, keys, seq_kind, query_start, score_scale):
    query_rows = queries.shape[0]
    key_rows = keys.shape[0]
    query_heads = queries.reshape(query_rows, HEADS, HD)
    key_heads = keys.reshape(key_rows, HEADS, HD)
    scores = (
        jnp.einsum("qhd,khd->hqk", query_heads, key_heads, preferred_element_type=jnp.float32)
        * score_scale
    )
    query_pos = query_start + jnp.arange(query_rows, dtype=jnp.int32)
    key_pos = jnp.arange(key_rows, dtype=jnp.int32)
    allowed = mask_between(seq_kind, query_pos, key_pos)
    return jnp.where(allowed[None], scores, -1e30)


def attend_group(queries, keys_whole, values_whole, seq_kind, start_row, score_scale):
    rows_here = queries.shape[0]
    length = keys_whole.shape[0]
    masked = masked_scores(queries, keys_whole, seq_kind, start_row, score_scale)
    row_max = jnp.max(masked, axis=-1, keepdims=True)
    exponent = jnp.exp(masked - row_max)
    row_total = jnp.sum(exponent, axis=-1, keepdims=True)
    probs = (exponent / row_total).astype(jnp.bfloat16)
    value_heads = values_whole.reshape(length, HEADS, HD)
    attended = jnp.einsum("hqk,khd->qhd", probs, value_heads, preferred_element_type=jnp.float32)
    return (
        attended.reshape(rows_here, HEADS * HD).astype(jnp.bfloat16),
        row_max + jnp.log(row_total),
    )


def query_part(
    queries, keys_whole, values_whole, seq_kind, start_row, score_scale, log_totals, grad_att
):
    rows_here = queries.shape[0]
    length = keys_whole.shape[0]
    masked = masked_scores(queries, keys_whole, seq_kind, start_row, score_scale)
    probs = jnp.exp(masked - log_totals)
    key_heads = keys_whole.reshape(length, HEADS, HD)
    value_heads = values_whole.reshape(length, HEADS, HD)
    grad_heads = grad_att.reshape(rows_here, HEADS, HD)
    grad_probs = jnp.einsum(
        "qhd,khd->hqk", grad_heads, value_heads, preferred_element_type=jnp.float32
    )
    row_delta = jnp.sum(probs * grad_probs, axis=-1, keepdims=True)
    grad_scores = (probs * (grad_probs - row_delta)).astype(jnp.bfloat16)
    grad_query = (
        jnp.einsum("hqk,khd->qhd", grad_scores, key_heads, preferred_element_type=jnp.float32)
        * score_scale
    )
    return (grad_query.reshape(rows_here, HEADS * HD), row_delta, probs, grad_scores)


def attend_back(
    queries, keys_whole, values_whole, seq_kind, start_row, score_scale, log_totals, grad_att
):
    rows_here = queries.shape[0]
    grad_query, row_delta, probs, grad_scores = query_part(
        queries, keys_whole, values_whole, seq_kind, start_row, score_scale, log_totals, grad_att
    )
    length = keys_whole.shape[0]
    query_heads = queries.reshape(rows_here, HEADS, HD)
    grad_heads = grad_att.reshape(rows_here, HEADS, HD)
    grad_key = (
        jnp.einsum("hqk,qhd->khd", grad_scores, query_heads, preferred_element_type=jnp.float32)
        * score_scale
    )
    grad_value = jnp.einsum(
        "hqk,qhd->khd", probs.astype(jnp.bfloat16), grad_heads, preferred_element_type=jnp.float32
    )
    return (
        grad_query,
        grad_key.reshape(length, HEADS * HD),
        grad_value.reshape(length, HEADS * HD),
    )


def routing(routes, capacity, experts):
    expert_ids = jnp.arange(experts, dtype=jnp.int32)
    pick_zero = (routes[..., 0:1] == expert_ids).astype(jnp.int32)
    pick_one = (routes[..., 1:2] == expert_ids).astype(jnp.int32)
    named_count = pick_zero + pick_one
    earlier = jnp.cumsum(named_count, axis=1) - named_count
    slot_zero = jnp.sum(earlier * pick_zero, axis=-1)
    slot_one = jnp.sum(earlier * pick_one, axis=-1)
    columns = jnp.arange(experts * capacity, dtype=jnp.int32)
    target_zero = routes[..., 0] * capacity + slot_zero
    target_one = routes[..., 1] * capacity + slot_one
    send_zero = ((target_zero[..., None] == columns) & (slot_zero < capacity)[..., None]).astype(
        jnp.float32
    )
    send_one = ((target_one[..., None] == columns) & (slot_one < capacity)[..., None]).astype(
        jnp.float32
    )
    return (pick_zero.astype(jnp.float32), pick_one.astype(jnp.float32), send_zero, send_one)


def sum_experts(in_grad, out_grad_weights):
    return (
        lax.psum_scatter(
            in_grad[None].astype(jnp.bfloat16), "dp", scatter_dimension=1, tiled=True
        ).astype(jnp.float32),
        lax.psum_scatter(
            out_grad_weights[None].astype(jnp.bfloat16), "dp", scatter_dimension=1, tiled=True
        ).astype(jnp.float32),
    )


def on_device(
    tokens,
    group_kind,
    routes,
    norm1_gain,
    qkv_weight,
    proj_weight,
    norm2_gain,
    router_weight,
    frozen_in,
    frozen_out,
    new_in,
    new_out,
    out_grad,
):
    groups, rows, width = tokens.shape
    count = lax.axis_size("expert")
    experts = 2 * count
    capacity = max(2, 3 * rows * TOP // (2 * experts))
    start_row = lax.axis_index("expert") * rows
    score_scale = HD ** (-0.5)
    inputs = tokens.astype(jnp.float32)
    normed_one, inverse_one = norm_parts(inputs)
    hidden_one = (normed_one * norm1_gain).astype(jnp.bfloat16)
    projected = jnp.einsum(
        "gtd,de->gte", hidden_one, qkv_weight, preferred_element_type=jnp.float32
    ).astype(jnp.bfloat16)
    queries = projected[..., :width]
    keys_local = projected[..., width : 2 * width]
    values_local = projected[..., 2 * width :]
    keys_whole, values_whole = (
        lax.all_gather(keys_local, "expert", axis=1, tiled=True),
        lax.all_gather(values_local, "expert", axis=1, tiled=True),
    )

    def forward_group(group_items):
        query_rows, key_rows, value_rows, seq_kind = group_items
        return attend_group(query_rows, key_rows, value_rows, seq_kind, start_row, score_scale)

    attended, log_totals = lax.map(forward_group, (queries, keys_whole, values_whole, group_kind))
    branch = jnp.einsum("gtd,de->gte", attended, proj_weight, preferred_element_type=jnp.float32)
    residual = inputs + branch
    normed_two, inverse_two = norm_parts(residual)
    hidden_two = (normed_two * norm2_gain).astype(jnp.bfloat16)
    logits = jnp.einsum(
        "gtd,de->gte", hidden_two, router_weight, preferred_element_type=jnp.float32
    )
    pick_zero, pick_one, send_zero, send_one = routing(routes, capacity, experts)
    logit_zero = jnp.sum(logits * pick_zero, axis=-1)
    logit_one = jnp.sum(logits * pick_one, axis=-1)
    gate_zero = jax.nn.sigmoid(logit_zero - logit_one)
    gate_one = jax.nn.sigmoid(logit_one - logit_zero)
    dispatch = (send_zero + send_one).astype(jnp.bfloat16)
    buffers = jnp.einsum(
        "gts,gtd->gsd", dispatch, hidden_two, preferred_element_type=jnp.float32
    ).astype(jnp.bfloat16)
    buffers = buffers.reshape(groups, 2, count, capacity, width)
    received = lax.all_to_all(buffers, "expert", split_axis=2, concat_axis=2, tiled=True)
    pre_frozen = jnp.einsum(
        "gnsd,df->gnsf", received[:, 0], frozen_in[0], preferred_element_type=jnp.float32
    )
    pre_new = jnp.einsum(
        "gnsd,df->gnsf", received[:, 1], new_in[0], preferred_element_type=jnp.float32
    )
    act_frozen = jax.nn.gelu(pre_frozen, approximate=False).astype(jnp.bfloat16)
    act_new = jax.nn.gelu(pre_new, approximate=False).astype(jnp.bfloat16)
    out_frozen = jnp.einsum(
        "gnsf,fd->gnsd", act_frozen, frozen_out[0], preferred_element_type=jnp.float32
    )
    out_new = jnp.einsum("gnsf,fd->gnsd", act_new, new_out[0], preferred_element_type=jnp.float32)
    results = jnp.stack([out_frozen, out_new], axis=1).astype(jnp.bfloat16)
    coming_back = lax.all_to_all(results, "expert", split_axis=2, concat_axis=2, tiled=True)
    returned, received, pre_act, activated = (
        coming_back,
        received,
        jnp.stack([pre_frozen, pre_new], axis=1),
        jnp.stack([act_frozen, act_new], axis=1),
    )
    returned_flat = returned.reshape(groups, experts * capacity, width)
    mixing = (gate_zero[..., None] * send_zero + gate_one[..., None] * send_one).astype(
        jnp.bfloat16
    )
    combined = jnp.einsum("gts,gsd->gtd", mixing, returned_flat, preferred_element_type=jnp.float32)
    mixed = (residual + combined).astype(jnp.bfloat16)
    grad_res = out_grad.astype(jnp.float32)
    grad_mixing = jnp.einsum(
        "gtd,gsd->gts", out_grad, returned_flat, preferred_element_type=jnp.float32
    )
    grad_returned = jnp.einsum(
        "gts,gtd->gsd", mixing, out_grad, preferred_element_type=jnp.float32
    ).astype(jnp.bfloat16)
    grad_returned = grad_returned.reshape(groups, 2, count, capacity, width)
    grad_gap = (
        (jnp.sum(grad_mixing * send_zero, axis=-1) - jnp.sum(grad_mixing * send_one, axis=-1))
        * gate_zero
        * gate_one
    )
    grad_logits = (grad_gap[..., None] * (pick_zero - pick_one)).astype(jnp.bfloat16)
    router_grad = jnp.einsum(
        "gtd,gte->de", hidden_two, grad_logits, preferred_element_type=jnp.float32
    )
    grad_hidden_two = jnp.einsum(
        "gte,de->gtd", grad_logits, router_weight, preferred_element_type=jnp.float32
    )
    arriving = lax.all_to_all(grad_returned, "expert", split_axis=2, concat_axis=2, tiled=True)
    grad_act_frozen = jnp.einsum(
        "gnsd,fd->gnsf", arriving[:, 0], frozen_out[0], preferred_element_type=jnp.float32
    )
    grad_act_new = jnp.einsum(
        "gnsd,fd->gnsf", arriving[:, 1], new_out[0], preferred_element_type=jnp.float32
    )
    grad_pre_frozen = (grad_act_frozen * gelu_slope(pre_act[:, 0])).astype(jnp.bfloat16)
    grad_pre_new = (grad_act_new * gelu_slope(pre_act[:, 1])).astype(jnp.bfloat16)
    new_out_grad = jnp.einsum(
        "gnsf,gnsd->fd", activated[:, 1], arriving[:, 1], preferred_element_type=jnp.float32
    )
    new_in_grad = jnp.einsum(
        "gnsd,gnsf->df", received[:, 1], grad_pre_new, preferred_element_type=jnp.float32
    )
    grad_in_frozen = jnp.einsum(
        "gnsf,df->gnsd", grad_pre_frozen, frozen_in[0], preferred_element_type=jnp.float32
    )
    grad_in_new = jnp.einsum(
        "gnsf,df->gnsd", grad_pre_new, new_in[0], preferred_element_type=jnp.float32
    )
    grad_received = jnp.stack([grad_in_frozen, grad_in_new], axis=1).astype(jnp.bfloat16)
    sent_back = lax.all_to_all(grad_received, "expert", split_axis=2, concat_axis=2, tiled=True)
    grad_hidden_two = grad_hidden_two + jnp.einsum(
        "gts,gsd->gtd",
        dispatch,
        sent_back.reshape(groups, experts * capacity, width),
        preferred_element_type=jnp.float32,
    )
    norm2_gain_grad = jnp.sum(grad_hidden_two * normed_two, axis=(0, 1))
    grad_residual = grad_res + norm_back(grad_hidden_two * norm2_gain, normed_two, inverse_two)
    grad_branch = grad_residual.astype(jnp.bfloat16)
    proj_grad = jnp.einsum("gtd,gte->de", attended, grad_branch, preferred_element_type=jnp.float32)
    grad_attended = jnp.einsum(
        "gte,de->gtd", grad_branch, proj_weight, preferred_element_type=jnp.float32
    ).astype(jnp.bfloat16)
    keys_back, values_back = (keys_whole, values_whole)

    def backward_group(group_items):
        query_rows, key_rows, value_rows, seq_kind, group_totals, grad_rows = group_items
        return attend_back(
            query_rows,
            key_rows,
            value_rows,
            seq_kind,
            start_row,
            score_scale,
            group_totals,
            grad_rows,
        )

    grad_queries, grad_keys_whole, grad_values_whole = lax.map(
        backward_group, (queries, keys_back, values_back, group_kind, log_totals, grad_attended)
    )
    grad_keys, grad_values = (
        lax.psum_scatter(
            grad_keys_whole.astype(jnp.bfloat16), "expert", scatter_dimension=1, tiled=True
        ).astype(jnp.float32),
        lax.psum_scatter(
            grad_values_whole.astype(jnp.bfloat16), "expert", scatter_dimension=1, tiled=True
        ).astype(jnp.float32),
    )
    grad_projected = jnp.concatenate(
        [
            grad_queries.astype(jnp.bfloat16),
            grad_keys.astype(jnp.bfloat16),
            grad_values.astype(jnp.bfloat16),
        ],
        axis=-1,
    )
    qkv_grad = jnp.einsum(
        "gtd,gte->de", hidden_one, grad_projected, preferred_element_type=jnp.float32
    )
    grad_hidden_one = jnp.einsum(
        "gte,de->gtd", grad_projected, qkv_weight, preferred_element_type=jnp.float32
    )
    norm1_gain_grad = jnp.sum(grad_hidden_one * normed_one, axis=(0, 1))
    tokens_grad = grad_residual + norm_back(grad_hidden_one * norm1_gain, normed_one, inverse_one)
    expert_sums = sum_experts(new_in_grad, new_out_grad)
    everyone = lax.axis_size("dp") * count
    own = width // everyone
    matrices = jnp.concatenate([qkv_grad, proj_grad], axis=1).reshape(everyone, own, -1)
    matrices = lax.psum_scatter(matrices, ("dp", "expert"), scatter_dimension=0, tiled=True)[0]
    narrow = jnp.concatenate(
        [router_grad, norm1_gain_grad[:, None], norm2_gain_grad[:, None]], axis=1
    )
    narrow = lax.psum(narrow, ("dp", "expert"))
    first_row = (lax.axis_index("dp") * count + lax.axis_index("expert")) * own
    narrow = lax.dynamic_slice_in_dim(narrow, first_row, own, axis=0)
    dense_sums = (
        narrow[:, -2],
        matrices[:, : 3 * width],
        matrices[:, 3 * width :],
        narrow[:, -1],
        narrow[:, :-2],
    )
    return (
        mixed,
        tokens_grad,
        dense_sums[0],
        dense_sums[1],
        dense_sums[2],
        dense_sums[3],
        dense_sums[4],
        expert_sums[0],
        expert_sums[1],
    )


def solution(mesh):
    return jax.shard_map(
        on_device,
        mesh=mesh,
        in_specs=(
            P("dp", "expert", None),
            P("dp"),
            P("dp", "expert", None),
            P(),
            P(),
            P(),
            P(),
            P(),
            P("expert", None, None),
            P("expert", None, None),
            P("expert", None, None),
            P("expert", None, None),
            P("dp", "expert", None),
        ),
        out_specs=(
            P("dp", "expert", None),
            P("dp", "expert", None),
            P(("dp", "expert")),
            P(("dp", "expert"), None),
            P(("dp", "expert"), None),
            P(("dp", "expert")),
            P(("dp", "expert"), None),
            P("expert", "dp", None),
            P("expert", "dp", None),
        ),
        check_vma=False,
    )
```

```python
import jax
import jax.numpy as jnp
from jax import lax
from jax.experimental import pallas as pl
from jax.experimental.pallas import tpu as pltpu
from jax.sharding import PartitionSpec as P

HEADS = 12
HD = 64
TOP = 2
LONG = 2048


epsilon = 1e-05


def norm_parts(values):
    average = jnp.mean(values, axis=-1, keepdims=True)
    centred = values - average
    variance = jnp.mean(centred * centred, axis=-1, keepdims=True)
    inverse = lax.rsqrt(variance + epsilon)
    return (centred * inverse, inverse)


def norm_back(grad_normed, normed, inverse):
    first_mean = jnp.mean(grad_normed, axis=-1, keepdims=True)
    second_mean = jnp.mean(grad_normed * normed, axis=-1, keepdims=True)
    return inverse * (grad_normed - first_mean - normed * second_mean)


def gelu_slope(pre_act):
    cumulative = 0.5 * (1.0 + lax.erf(pre_act * 0.7071067811865476))
    density = jnp.exp(-0.5 * pre_act * pre_act) * 0.3989422804014327
    return cumulative + pre_act * density


MESH_ID = pl.DeviceIdType.MESH
CHIPS = 4
PAD = 256
BLOCK = 256
CHUNK = 512
CHUNKS = LONG // CHUNK
LOCAL_HEADS = HEADS // CHIPS
STACK = LOCAL_HEADS * BLOCK
NEGATIVE = -1e30


def here():
    position = lax.axis_index("expert")
    return position // 2, lax.rem(position, 2)


def device(z, core):
    return (lax.axis_index("dp"), z * 2 + core)


def greet(barrier):
    position = lax.axis_index("expert")
    for step in range(1, 8):
        pl.semaphore_signal(
            barrier,
            inc=1,
            device_id=(lax.axis_index("dp"), lax.rem(position + step, 8)),
            device_id_type=MESH_ID,
        )


def push(source, target, sends, receives, index_here, index_there, where):
    return pltpu.make_async_remote_copy(
        src_ref=source,
        dst_ref=target,
        send_sem=sends.at[index_here],
        recv_sem=receives.at[index_there],
        device_id=where,
        device_id_type=MESH_ID,
    )


def landed(region, sends, receives, index):
    z, core = here()
    push(region, region, sends, receives, index, index, device(z, 1 - core)).wait_recv()


def dot_nn(left, right):
    return jnp.dot(left, right, preferred_element_type=jnp.float32)


def dot_nt(left, right):
    return lax.dot_general(
        left, right, (((1,), (1,)), ((), ())), preferred_element_type=jnp.float32
    )


def dot_tn(left, right):
    return lax.dot_general(
        left, right, (((0,), (0,)), ((), ())), preferred_element_type=jnp.float32
    )


def head_mask(head, value, dtype):
    lanes = lax.broadcasted_iota(jnp.int32, (1, PAD), 1)
    inside = (lanes >= head * HD) & (lanes < (head + 1) * HD)
    return jnp.where(inside, value, 0.0).astype(dtype)


def lane_tiles(values, combine):
    result = values[:, :128]
    for start in range(128, values.shape[1], 128):
        result = combine(result, values[:, start : start + 128])
    return result


def front_kernel(
    kind_ref,
    tokens_ref,
    gain_ref,
    weight_ref,
    hidden_ref,
    query_ref,
    key_ref,
    value_ref,
    out_ref,
    total_ref,
    attended_ref,
    stacked,
    scores,
    largest,
    sums,
    acc,
    gather_send,
    gather_recv,
    out_send,
    out_recv,
):
    z, core = here()
    mine = z * 2 + core
    up, down, far = lax.rem(z + 1, CHIPS), lax.rem(z + 3, CHIPS), lax.rem(z + 2, CHIPS)
    barrier = pltpu.get_barrier_semaphore()
    greet(barrier)
    normed, _ = norm_parts(tokens_ref[...].astype(jnp.float32))
    hidden_ref[mine] = (normed * gain_ref[...]).astype(jnp.bfloat16)
    pl.semaphore_wait(barrier, 7)

    def send(region, index, where):
        copy = push(region, region, gather_send, gather_recv, index, index, where)
        copy.start()
        return copy

    def arrived(region, index):
        landed(region, gather_send, gather_recv, index)

    def project(block):
        projected = dot_nn(hidden_ref[block], weight_ref[...]).astype(jnp.bfloat16)
        query_ref[block] = projected[:, :PAD]
        rows = pl.ds(pl.multiple_of(block * BLOCK, BLOCK), BLOCK)
        key_ref[rows, :] = projected[:, PAD : 2 * PAD]
        value_ref[rows, :] = projected[:, 2 * PAD :]

    half = BLOCK // 2
    first, second = pl.ds(0, half), pl.ds(half, half)
    block_down, block_up, block_far = down * 2 + core, up * 2 + core, far * 2 + core
    copies = [
        send(hidden_ref.at[mine], 0, device(up, core)),
        send(hidden_ref.at[mine], 1, device(down, core)),
        send(hidden_ref.at[mine], 2, device(z, 1 - core)),
    ]
    project(mine)
    arrived(hidden_ref.at[z * 2 + 1 - core], 2)
    project(z * 2 + 1 - core)
    arrived(hidden_ref.at[block_down], 0)
    copies.append(send(hidden_ref.at[block_down, first], 3, device(up, core)))
    copies.append(send(hidden_ref.at[block_down], 5, device(z, 1 - core)))
    arrived(hidden_ref.at[block_up], 1)
    copies.append(send(hidden_ref.at[block_up, second], 4, device(down, core)))
    copies.append(send(hidden_ref.at[block_up], 6, device(z, 1 - core)))
    project(block_down)
    project(block_up)
    arrived(hidden_ref.at[down * 2 + 1 - core], 5)
    project(down * 2 + 1 - core)
    arrived(hidden_ref.at[up * 2 + 1 - core], 6)
    project(up * 2 + 1 - core)
    arrived(hidden_ref.at[block_far, first], 3)
    arrived(hidden_ref.at[block_far, second], 4)
    copies.append(send(hidden_ref.at[block_far], 7, device(z, 1 - core)))
    project(block_far)
    arrived(hidden_ref.at[far * 2 + 1 - core], 7)
    project(far * 2 + 1 - core)

    kind_bias = kind_ref[0].astype(jnp.float32) * NEGATIVE

    @pl.loop(0, CHIPS)
    def _(step):
        slot = lax.rem(z + step, CHIPS)
        block = slot * 2 + lax.rem(core + slot, 2)
        queries = query_ref[block]
        for head in range(LOCAL_HEADS):
            stacked[head * BLOCK : (head + 1) * BLOCK, :] = queries * head_mask(
                head, HD ** (-0.5), jnp.bfloat16
            )

        def chunk_rows(chunk):
            return pl.ds(pl.multiple_of(chunk * CHUNK, CHUNK), CHUNK)

        def bias_of(chunk):
            return jnp.where((slot >= 2) & (chunk < 2), kind_bias, 0.0)

        masked = dot_nt(stacked[...], key_ref[chunk_rows(slot), :])
        row = lax.broadcasted_iota(jnp.int32, (BLOCK, CHUNK), 0)
        column = lax.broadcasted_iota(jnp.int32, (BLOCK, CHUNK), 1)
        allowed = column - row <= (block - 2 * slot) * BLOCK
        for head in range(LOCAL_HEADS):
            part = slice(head * BLOCK, (head + 1) * BLOCK)
            values = jnp.where(allowed, masked[part], NEGATIVE)
            scores[slot, part, :] = values
            largest[part, :] = lane_tiles(values, jnp.maximum)

        @pl.loop(0, slot)
        def _(chunk):
            values = dot_nt(stacked[...], key_ref[chunk_rows(chunk), :])
            scores[chunk] = values
            largest[...] = jnp.maximum(
                largest[...], lane_tiles(values, jnp.maximum) + bias_of(chunk)
            )

        row_max = jnp.max(largest[...], axis=1, keepdims=True)
        largest[...] = jnp.broadcast_to(row_max, largest.shape)
        sums[...] = jnp.zeros_like(sums)
        acc[...] = jnp.zeros_like(acc)

        @pl.loop(0, slot + 1)
        def _(chunk):
            exponent = jnp.exp(scores[chunk] - (largest[:, :1] - bias_of(chunk)))
            sums[...] += lane_tiles(exponent, jnp.add)
            acc[...] += dot_nn(exponent.astype(jnp.bfloat16), value_ref[chunk_rows(chunk), :])

        total = jnp.sum(sums[...], axis=1, keepdims=True)
        inverse = 1.0 / total
        log_total = largest[...] + jnp.log(total)
        attended = jnp.zeros((BLOCK, PAD), jnp.float32)
        for head in range(LOCAL_HEADS):
            part = slice(head * BLOCK, (head + 1) * BLOCK)
            attended += acc[part, :] * inverse[part] * head_mask(head, 1.0, jnp.float32)
            total_ref[slot, head : head + 1, :] = jnp.transpose(log_total[part, :])[:1, :]
        out_ref[slot] = attended.astype(jnp.bfloat16)

        @pl.when(block != mine)
        def _():
            push(
                out_ref.at[slot],
                attended_ref.at[z],
                out_send,
                out_recv,
                slot,
                z,
                device(slot, lax.rem(core + slot, 2)),
            ).start()

        @pl.when(block == mine)
        def _():
            attended_ref[z] = out_ref[slot]

    for copy in copies:
        copy.wait_send()

    @pl.loop(0, CHIPS)
    def _(slot):
        @pl.when(slot * 2 + lax.rem(core + slot, 2) != mine)
        def _():
            push(
                out_ref.at[slot],
                attended_ref.at[slot],
                out_send,
                out_recv,
                slot,
                slot,
                device(z, 1 - core),
            ).wait_send()

        @pl.when((slot != z) | (lax.rem(core + z, 2) != core))
        def _():
            landed(attended_ref.at[slot], out_send, out_recv, slot)


def vmem():
    return pl.BlockSpec(memory_space=pltpu.VMEM)


def smem():
    return pl.BlockSpec(memory_space=pltpu.SMEM)


def front(kind, tokens, gain, weight):
    half_type = jnp.bfloat16
    shapes = [
        jax.ShapeDtypeStruct((8, BLOCK, 768), half_type),
        jax.ShapeDtypeStruct((8, BLOCK, PAD), half_type),
        jax.ShapeDtypeStruct((LONG, PAD), half_type),
        jax.ShapeDtypeStruct((LONG, PAD), half_type),
        jax.ShapeDtypeStruct((CHIPS, BLOCK, PAD), half_type),
        jax.ShapeDtypeStruct((CHIPS, 8, BLOCK), jnp.float32),
        jax.ShapeDtypeStruct((CHIPS, BLOCK, PAD), half_type),
    ]
    return pl.pallas_call(
        front_kernel,
        out_shape=shapes,
        in_specs=[smem(), vmem(), vmem(), vmem()],
        out_specs=[vmem()] * len(shapes),
        scratch_shapes=[
            pltpu.VMEM((STACK, PAD), half_type),
            pltpu.VMEM((CHUNKS, STACK, CHUNK), jnp.float32),
            pltpu.VMEM((STACK, 128), jnp.float32),
            pltpu.VMEM((STACK, 128), jnp.float32),
            pltpu.VMEM((STACK, PAD), jnp.float32),
            pltpu.SemaphoreType.DMA((8,)),
            pltpu.SemaphoreType.DMA((8,)),
            pltpu.SemaphoreType.DMA((CHIPS,)),
            pltpu.SemaphoreType.DMA((CHIPS,)),
        ],
        compiler_params=pltpu.CompilerParams(
            collective_id=0, has_side_effects=True, vmem_limit_bytes=56 * 2**20
        ),
    )(kind, tokens, gain, weight)


def back_kernel(
    kind_ref,
    grad_ref,
    query_ref,
    key_ref,
    value_ref,
    out_ref,
    total_ref,
    weight_ref,
    hidden_ref,
    result_ref,
    weight_grad_ref,
    grad_out,
    stacked,
    grad_stacked,
    grad_query,
    grad_key,
    grad_value,
    projected,
    part_sib,
    part_own,
    land_sib,
    land_half,
    land_full,
    grad_send,
    grad_recv,
    sib_send,
    sib_recv,
    ring_send,
    ring_recv,
):
    z, core = here()
    mine = z * 2 + core
    up, down, far = lax.rem(z + 1, CHIPS), lax.rem(z + 3, CHIPS), lax.rem(z + 2, CHIPS)
    barrier = pltpu.get_barrier_semaphore()
    greet(barrier)
    grad_key[...] = jnp.zeros_like(grad_key)
    grad_value[...] = jnp.zeros_like(grad_value)
    projected[...] = jnp.zeros_like(projected)
    pl.semaphore_wait(barrier, 7)
    owner_core = lax.rem(core + z, 2)

    @pl.loop(0, CHIPS)
    def _(step):
        chip = lax.rem(z + step, CHIPS)
        mine_too = (chip == z) & (owner_core == core)

        @pl.when(jnp.logical_not(mine_too))
        def _():
            push(
                grad_ref.at[chip],
                grad_out.at[z],
                grad_send,
                grad_recv,
                chip,
                z,
                device(chip, owner_core),
            ).start()

        @pl.when(mine_too)
        def _():
            grad_out[z] = grad_ref[chip]

    kind_bias = kind_ref[0].astype(jnp.float32) * NEGATIVE

    @pl.loop(0, CHIPS)
    def _(step):
        slot = lax.rem(z + step, CHIPS)
        block = slot * 2 + lax.rem(core + slot, 2)

        @pl.when(block != mine)
        def _():
            landed(grad_out.at[slot], grad_send, grad_recv, slot)

        queries = query_ref[block]
        grads = grad_out[slot]
        products = grads.astype(jnp.float32) * out_ref[slot].astype(jnp.float32)
        selector = jnp.concatenate(
            [head_mask(head, 1.0, jnp.float32) for head in range(LOCAL_HEADS)]
            + [jnp.zeros((8 - LOCAL_HEADS, PAD), jnp.float32)],
            axis=0,
        )
        deltas = lax.dot_general(
            selector,
            products,
            (((1,), (1,)), ((), ())),
            preferred_element_type=jnp.float32,
            precision=lax.Precision.HIGHEST,
        )
        for head in range(LOCAL_HEADS):
            part = slice(head * BLOCK, (head + 1) * BLOCK)
            stacked[part, :] = queries * head_mask(head, HD ** (-0.5), jnp.bfloat16)
            grad_stacked[part, :] = grads * head_mask(head, 1.0, jnp.bfloat16)
        totals = total_ref[slot]
        delta_row = jnp.concatenate(
            [deltas[head : head + 1, :] for head in range(LOCAL_HEADS)], axis=1
        )
        total_row = jnp.concatenate(
            [totals[head : head + 1, :] for head in range(LOCAL_HEADS)], axis=1
        )

        def work(chunk, is_last):
            rows = pl.ds(pl.multiple_of(chunk * CHUNK, CHUNK), CHUNK)
            keys, values = key_ref[rows, :], value_ref[rows, :]
            bias = jnp.where((slot >= 2) & (chunk < 2), kind_bias, 0.0)
            probs = jnp.exp(dot_nt(keys, stacked[...]) - (total_row - bias))
            if is_last:
                row = lax.broadcasted_iota(jnp.int32, (CHUNK, STACK), 0)
                column = lax.broadcasted_iota(jnp.int32, (CHUNK, STACK), 1)
                allowed = row - lax.rem(column, BLOCK) <= (block - 2 * slot) * BLOCK
                probs = jnp.where(allowed, probs, 0.0)
            grad_probs = dot_nt(values, grad_stacked[...])
            grad_scores = (probs * (grad_probs - delta_row)).astype(jnp.bfloat16)
            grad_value[rows, :] += dot_nn(probs.astype(jnp.bfloat16), grad_stacked[...])
            grad_key[rows, :] += dot_nn(grad_scores, stacked[...])
            return dot_tn(grad_scores, keys)

        grad_query[...] = work(slot, True)

        @pl.loop(0, slot)
        def _(chunk):
            grad_query[...] += work(chunk, False)

        combined = jnp.zeros((BLOCK, PAD), jnp.float32)
        for head in range(LOCAL_HEADS):
            part = slice(head * BLOCK, (head + 1) * BLOCK)
            combined += grad_query[part, :] * head_mask(head, HD ** (-0.5), jnp.float32)
        rows = pl.ds(pl.multiple_of(block * BLOCK, BLOCK), BLOCK)
        projected[rows, :PAD] = combined.astype(jnp.bfloat16)

    projected[:, PAD : 2 * PAD] = grad_key[...].astype(jnp.bfloat16)
    projected[:, 2 * PAD :] = grad_value[...].astype(jnp.bfloat16)

    def partial(chip, which):
        rows = pl.ds(pl.multiple_of((chip * 2 + which) * BLOCK, BLOCK), BLOCK)
        return dot_nt(projected[rows, :], weight_ref[...])

    def sib_copy(index):
        return push(
            part_sib.at[index],
            land_sib.at[index],
            sib_send,
            sib_recv,
            index,
            index,
            device(z, 1 - core),
        )

    order = (far, up, down, z)
    for index, chip in enumerate(order):
        part_sib[index] = partial(chip, 1 - core).astype(jnp.bfloat16)
        sib_copy(index).start()

    def own(index):
        value = partial(order[index], core)
        landed(land_sib.at[index], sib_send, sib_recv, index)
        return value + land_sib[index].astype(jnp.float32)

    half = BLOCK // 2
    first, second = pl.ds(0, half), pl.ds(half, half)
    part_own[0] = own(0).astype(jnp.bfloat16)

    def ring(source, target, index, where):
        copy = push(source, target, ring_send, ring_recv, index, index, where)
        copy.start()
        return copy

    above, below = device(up, core), device(down, core)
    copies = [
        ring(part_own.at[0, first], land_half.at[0], 0, above),
        ring(part_own.at[0, second], land_half.at[1], 1, below),
    ]
    part_own[1] = own(1).astype(jnp.bfloat16)
    copies.append(ring(part_own.at[1, second], land_full.at[0, second], 2, above))
    part_own[2] = own(2).astype(jnp.bfloat16)
    copies.append(ring(part_own.at[2, first], land_full.at[1, first], 3, below))
    result_ref[...] = own(3)
    landed(land_half.at[0], ring_send, ring_recv, 0)
    part_own[1, first, :] = (
        part_own[1, first, :].astype(jnp.float32) + land_half[0].astype(jnp.float32)
    ).astype(jnp.bfloat16)
    copies.append(ring(part_own.at[1, first], land_full.at[0, first], 4, above))
    landed(land_half.at[1], ring_send, ring_recv, 1)
    part_own[2, second, :] = (
        part_own[2, second, :].astype(jnp.float32) + land_half[1].astype(jnp.float32)
    ).astype(jnp.bfloat16)
    copies.append(ring(part_own.at[2, second], land_full.at[1, second], 5, below))

    for tile in range(3):
        lanes = slice(tile * PAD, (tile + 1) * PAD)
        weight_grad_ref[:, lanes] = dot_tn(hidden_ref[...], projected[:, lanes])

    landed(land_full.at[0, second], ring_send, ring_recv, 2)
    landed(land_full.at[1, first], ring_send, ring_recv, 3)
    landed(land_full.at[0, first], ring_send, ring_recv, 4)
    landed(land_full.at[1, second], ring_send, ring_recv, 5)
    result_ref[...] += land_full[0].astype(jnp.float32) + land_full[1].astype(jnp.float32)
    for copy in copies:
        copy.wait_send()
    for index in range(CHIPS):
        sib_copy(index).wait_send()

    @pl.loop(0, CHIPS)
    def _(chip):
        @pl.when((chip != z) | (owner_core != core))
        def _():
            push(
                grad_ref.at[chip],
                grad_out.at[chip],
                grad_send,
                grad_recv,
                chip,
                chip,
                device(z, 1 - core),
            ).wait_send()


def back(kind, grads, queries, keys, values, out, totals, weight, hidden):
    half_type = jnp.bfloat16
    width = 768
    return pl.pallas_call(
        back_kernel,
        out_shape=[
            jax.ShapeDtypeStruct((BLOCK, width), jnp.float32),
            jax.ShapeDtypeStruct((width, 3 * PAD), jnp.float32),
        ],
        in_specs=[smem()] + [vmem()] * 8,
        out_specs=[vmem()] * 2,
        scratch_shapes=[
            pltpu.VMEM((CHIPS, BLOCK, PAD), half_type),
            pltpu.VMEM((STACK, PAD), half_type),
            pltpu.VMEM((STACK, PAD), half_type),
            pltpu.VMEM((STACK, PAD), jnp.float32),
            pltpu.VMEM((LONG, PAD), jnp.float32),
            pltpu.VMEM((LONG, PAD), jnp.float32),
            pltpu.VMEM((LONG, 3 * PAD), half_type),
            pltpu.VMEM((CHIPS, BLOCK, width), half_type),
            pltpu.VMEM((CHIPS, BLOCK, width), half_type),
            pltpu.VMEM((CHIPS, BLOCK, width), half_type),
            pltpu.VMEM((2, BLOCK // 2, width), half_type),
            pltpu.VMEM((2, BLOCK, width), half_type),
            pltpu.SemaphoreType.DMA((CHIPS,)),
            pltpu.SemaphoreType.DMA((CHIPS,)),
            pltpu.SemaphoreType.DMA((CHIPS,)),
            pltpu.SemaphoreType.DMA((CHIPS,)),
            pltpu.SemaphoreType.DMA((6,)),
            pltpu.SemaphoreType.DMA((6,)),
        ],
        compiler_params=pltpu.CompilerParams(
            collective_id=1, has_side_effects=True, vmem_limit_bytes=56 * 2**20
        ),
    )(kind, grads, queries, keys, values, out, totals, weight, hidden)


def routing(routes, capacity, experts):
    expert_ids = jnp.arange(experts, dtype=jnp.int32)
    pick_zero = (routes[..., 0:1] == expert_ids).astype(jnp.int32)
    pick_one = (routes[..., 1:2] == expert_ids).astype(jnp.int32)
    named_count = pick_zero + pick_one
    earlier = jnp.cumsum(named_count, axis=1) - named_count
    slot_zero = jnp.sum(earlier * pick_zero, axis=-1)
    slot_one = jnp.sum(earlier * pick_one, axis=-1)
    columns = jnp.arange(experts * capacity, dtype=jnp.int32)
    target_zero = routes[..., 0] * capacity + slot_zero
    target_one = routes[..., 1] * capacity + slot_one
    send_zero = ((target_zero[..., None] == columns) & (slot_zero < capacity)[..., None]).astype(
        jnp.float32
    )
    send_one = ((target_one[..., None] == columns) & (slot_one < capacity)[..., None]).astype(
        jnp.float32
    )
    return (pick_zero.astype(jnp.float32), pick_one.astype(jnp.float32), send_zero, send_one)


def sum_experts(in_grad, out_grad_weights):
    return (
        lax.psum_scatter(
            in_grad[None].astype(jnp.bfloat16), "dp", scatter_dimension=1, tiled=True
        ).astype(jnp.float32),
        lax.psum_scatter(
            out_grad_weights[None].astype(jnp.bfloat16), "dp", scatter_dimension=1, tiled=True
        ).astype(jnp.float32),
    )


def on_device(
    tokens,
    group_kind,
    routes,
    norm1_gain,
    qkv_weight,
    proj_weight,
    norm2_gain,
    router_weight,
    frozen_in,
    frozen_out,
    new_in,
    new_out,
    out_grad,
):
    groups, rows, width = tokens.shape
    count = lax.axis_size("expert")
    experts = 2 * count
    capacity = max(2, 3 * rows * TOP // (2 * experts))
    start_row = lax.axis_index("expert") * rows
    score_scale = HD ** (-0.5)
    inputs = tokens.astype(jnp.float32)
    normed_one, inverse_one = norm_parts(inputs)
    chip = lax.axis_index("expert") // 2
    chip_columns = lax.dynamic_index_in_dim(
        qkv_weight.reshape(width, 3, CHIPS, width // CHIPS), chip, axis=2, keepdims=False
    )
    chip_weight = jnp.pad(chip_columns, ((0, 0), (0, 0), (0, PAD - width // CHIPS))).reshape(
        width, 3 * PAD
    )
    proj_chips = jnp.pad(
        proj_weight.reshape(CHIPS, width // CHIPS, width),
        ((0, 0), (0, PAD - width // CHIPS), (0, 0)),
    )
    hidden_all, queries, keys, values, out_heads, totals, attended = front(
        group_kind, tokens[0], norm1_gain[None], chip_weight
    )
    branch = jnp.einsum("ztd,zde->te", attended, proj_chips, preferred_element_type=jnp.float32)[
        None
    ]
    residual = inputs + branch
    normed_two, inverse_two = norm_parts(residual)
    hidden_two = (normed_two * norm2_gain).astype(jnp.bfloat16)
    logits = jnp.einsum(
        "gtd,de->gte", hidden_two, router_weight, preferred_element_type=jnp.float32
    )
    pick_zero, pick_one, send_zero, send_one = routing(routes, capacity, experts)
    logit_zero = jnp.sum(logits * pick_zero, axis=-1)
    logit_one = jnp.sum(logits * pick_one, axis=-1)
    gate_zero = jax.nn.sigmoid(logit_zero - logit_one)
    gate_one = jax.nn.sigmoid(logit_one - logit_zero)
    dispatch = (send_zero + send_one).astype(jnp.bfloat16)
    buffers = jnp.einsum(
        "gts,gtd->gsd", dispatch, hidden_two, preferred_element_type=jnp.float32
    ).astype(jnp.bfloat16)
    buffers = buffers.reshape(groups, 2, count, capacity, width)
    received = lax.all_to_all(buffers, "expert", split_axis=2, concat_axis=2, tiled=True)
    pre_frozen = jnp.einsum(
        "gnsd,df->gnsf", received[:, 0], frozen_in[0], preferred_element_type=jnp.float32
    )
    pre_new = jnp.einsum(
        "gnsd,df->gnsf", received[:, 1], new_in[0], preferred_element_type=jnp.float32
    )
    act_frozen = jax.nn.gelu(pre_frozen, approximate=False).astype(jnp.bfloat16)
    act_new = jax.nn.gelu(pre_new, approximate=False).astype(jnp.bfloat16)
    out_frozen = jnp.einsum(
        "gnsf,fd->gnsd", act_frozen, frozen_out[0], preferred_element_type=jnp.float32
    )
    out_new = jnp.einsum("gnsf,fd->gnsd", act_new, new_out[0], preferred_element_type=jnp.float32)
    results = jnp.stack([out_frozen, out_new], axis=1).astype(jnp.bfloat16)
    coming_back = lax.all_to_all(results, "expert", split_axis=2, concat_axis=2, tiled=True)
    returned, received, pre_act, activated = (
        coming_back,
        received,
        jnp.stack([pre_frozen, pre_new], axis=1),
        jnp.stack([act_frozen, act_new], axis=1),
    )
    returned_flat = returned.reshape(groups, experts * capacity, width)
    mixing = (gate_zero[..., None] * send_zero + gate_one[..., None] * send_one).astype(
        jnp.bfloat16
    )
    combined = jnp.einsum("gts,gsd->gtd", mixing, returned_flat, preferred_element_type=jnp.float32)
    mixed = (residual + combined).astype(jnp.bfloat16)
    grad_res = out_grad.astype(jnp.float32)
    grad_mixing = jnp.einsum(
        "gtd,gsd->gts", out_grad, returned_flat, preferred_element_type=jnp.float32
    )
    grad_returned = jnp.einsum(
        "gts,gtd->gsd", mixing, out_grad, preferred_element_type=jnp.float32
    ).astype(jnp.bfloat16)
    grad_returned = grad_returned.reshape(groups, 2, count, capacity, width)
    grad_gap = (
        (jnp.sum(grad_mixing * send_zero, axis=-1) - jnp.sum(grad_mixing * send_one, axis=-1))
        * gate_zero
        * gate_one
    )
    grad_logits = (grad_gap[..., None] * (pick_zero - pick_one)).astype(jnp.bfloat16)
    router_grad = jnp.einsum(
        "gtd,gte->de", hidden_two, grad_logits, preferred_element_type=jnp.float32
    )
    grad_hidden_two = jnp.einsum(
        "gte,de->gtd", grad_logits, router_weight, preferred_element_type=jnp.float32
    )
    arriving = lax.all_to_all(grad_returned, "expert", split_axis=2, concat_axis=2, tiled=True)
    grad_act_frozen = jnp.einsum(
        "gnsd,fd->gnsf", arriving[:, 0], frozen_out[0], preferred_element_type=jnp.float32
    )
    grad_act_new = jnp.einsum(
        "gnsd,fd->gnsf", arriving[:, 1], new_out[0], preferred_element_type=jnp.float32
    )
    grad_pre_frozen = (grad_act_frozen * gelu_slope(pre_act[:, 0])).astype(jnp.bfloat16)
    grad_pre_new = (grad_act_new * gelu_slope(pre_act[:, 1])).astype(jnp.bfloat16)
    new_out_grad = jnp.einsum(
        "gnsf,gnsd->fd", activated[:, 1], arriving[:, 1], preferred_element_type=jnp.float32
    )
    new_in_grad = jnp.einsum(
        "gnsd,gnsf->df", received[:, 1], grad_pre_new, preferred_element_type=jnp.float32
    )
    grad_in_frozen = jnp.einsum(
        "gnsf,df->gnsd", grad_pre_frozen, frozen_in[0], preferred_element_type=jnp.float32
    )
    grad_in_new = jnp.einsum(
        "gnsf,df->gnsd", grad_pre_new, new_in[0], preferred_element_type=jnp.float32
    )
    grad_received = jnp.stack([grad_in_frozen, grad_in_new], axis=1).astype(jnp.bfloat16)
    sent_back = lax.all_to_all(grad_received, "expert", split_axis=2, concat_axis=2, tiled=True)
    grad_hidden_two = grad_hidden_two + jnp.einsum(
        "gts,gsd->gtd",
        dispatch,
        sent_back.reshape(groups, experts * capacity, width),
        preferred_element_type=jnp.float32,
    )
    norm2_gain_grad = jnp.sum(grad_hidden_two * normed_two, axis=(0, 1))
    grad_residual = grad_res + norm_back(grad_hidden_two * norm2_gain, normed_two, inverse_two)
    grad_branch = grad_residual.astype(jnp.bfloat16)
    proj_grad = jnp.einsum(
        "ztd,te->zde", attended, grad_branch[0], preferred_element_type=jnp.float32
    )[:, : width // CHIPS].reshape(width, width)
    grad_attended = jnp.einsum(
        "te,zde->ztd", grad_branch[0], proj_chips, preferred_element_type=jnp.float32
    ).astype(jnp.bfloat16)
    grad_hidden_one, qkv_grad = back(
        group_kind,
        grad_attended,
        queries,
        keys,
        values,
        out_heads,
        totals,
        chip_weight,
        hidden_all.reshape(LONG, width),
    )
    grad_hidden_one = grad_hidden_one[None]
    norm1_gain_grad = jnp.sum(grad_hidden_one * normed_one, axis=(0, 1))
    tokens_grad = grad_residual + norm_back(grad_hidden_one * norm1_gain, normed_one, inverse_one)
    expert_sums = sum_experts(new_in_grad, new_out_grad)
    own = width // (lax.axis_size("dp") * count)
    matrices = jnp.concatenate([qkv_grad, proj_grad], axis=1)
    matrices = lax.psum_scatter(matrices, "dp", scatter_dimension=0, tiled=True)
    matrices = lax.all_to_all(
        matrices.reshape(count, own, -1), "expert", split_axis=0, concat_axis=0, tiled=True
    )
    proj_sum = jnp.sum(matrices[..., 3 * PAD :], axis=0)
    qkv_sum = jnp.sum(matrices[..., : 3 * PAD].reshape(CHIPS, 2, own, 3, PAD), axis=1)
    qkv_sum = qkv_sum[..., : width // CHIPS].transpose(1, 2, 0, 3).reshape(own, 3 * width)
    narrow = jnp.concatenate(
        [router_grad, norm1_gain_grad[:, None], norm2_gain_grad[:, None]], axis=1
    )
    narrow = lax.psum(narrow, ("dp", "expert"))
    first_row = (lax.axis_index("dp") * count + lax.axis_index("expert")) * own
    narrow = lax.dynamic_slice_in_dim(narrow, first_row, own, axis=0)
    dense_sums = (
        narrow[:, -2],
        qkv_sum,
        proj_sum,
        narrow[:, -1],
        narrow[:, :-2],
    )
    return (
        mixed,
        tokens_grad,
        dense_sums[0],
        dense_sums[1],
        dense_sums[2],
        dense_sums[3],
        dense_sums[4],
        expert_sums[0],
        expert_sums[1],
    )


def solution(mesh):
    return jax.shard_map(
        on_device,
        mesh=mesh,
        in_specs=(
            P("dp", "expert", None),
            P("dp"),
            P("dp", "expert", None),
            P(),
            P(),
            P(),
            P(),
            P(),
            P("expert", None, None),
            P("expert", None, None),
            P("expert", None, None),
            P("expert", None, None),
            P("dp", "expert", None),
        ),
        out_specs=(
            P("dp", "expert", None),
            P("dp", "expert", None),
            P(("dp", "expert")),
            P(("dp", "expert"), None),
            P(("dp", "expert"), None),
            P(("dp", "expert")),
            P(("dp", "expert"), None),
            P("expert", "dp", None),
            P("expert", "dp", None),
        ),
        check_vma=False,
    )
```

```python
import jax
import jax.numpy as jnp
from jax import lax
from jax.experimental import pallas as pl
from jax.experimental.pallas import tpu as pltpu
from jax.sharding import PartitionSpec as P

HEADS = 12
HD = 64
TOP = 2
LONG = 2048


epsilon = 1e-05


def norm_parts(values):
    average = jnp.mean(values, axis=-1, keepdims=True)
    centred = values - average
    variance = jnp.mean(centred * centred, axis=-1, keepdims=True)
    inverse = lax.rsqrt(variance + epsilon)
    return (centred * inverse, inverse)


def norm_back(grad_normed, normed, inverse):
    first_mean = jnp.mean(grad_normed, axis=-1, keepdims=True)
    second_mean = jnp.mean(grad_normed * normed, axis=-1, keepdims=True)
    return inverse * (grad_normed - first_mean - normed * second_mean)


def gelu_slope(pre_act):
    cumulative = 0.5 * (1.0 + lax.erf(pre_act * 0.7071067811865476))
    density = jnp.exp(-0.5 * pre_act * pre_act) * 0.3989422804014327
    return cumulative + pre_act * density


MESH_ID = pl.DeviceIdType.MESH
CHIPS = 4
PAD = 256
BLOCK = 256
CHUNK = 512
CHUNKS = LONG // CHUNK
LOCAL_HEADS = HEADS // CHIPS
STACK = LOCAL_HEADS * BLOCK
NEGATIVE = -1e30


def here():
    position = lax.axis_index("expert")
    return position // 2, lax.rem(position, 2)


def device(z, core):
    return (lax.axis_index("dp"), z * 2 + core)


def greet(barrier):
    position = lax.axis_index("expert")
    for step in range(1, 8):
        pl.semaphore_signal(
            barrier,
            inc=1,
            device_id=(lax.axis_index("dp"), lax.rem(position + step, 8)),
            device_id_type=MESH_ID,
        )


def push(source, target, sends, receives, index_here, index_there, where):
    return pltpu.make_async_remote_copy(
        src_ref=source,
        dst_ref=target,
        send_sem=sends.at[index_here],
        recv_sem=receives.at[index_there],
        device_id=where,
        device_id_type=MESH_ID,
    )


def landed(region, sends, receives, index):
    z, core = here()
    push(region, region, sends, receives, index, index, device(z, 1 - core)).wait_recv()


def dot_nn(left, right):
    return jnp.dot(left, right, preferred_element_type=jnp.float32)


def dot_nt(left, right):
    return lax.dot_general(
        left, right, (((1,), (1,)), ((), ())), preferred_element_type=jnp.float32
    )


def dot_tn(left, right):
    return lax.dot_general(
        left, right, (((0,), (0,)), ((), ())), preferred_element_type=jnp.float32
    )


def plane_device(x, y):
    return (x * 4 + y, lax.axis_index("expert"))


def plane_here():
    group = lax.axis_index("dp")
    return group // 4, lax.rem(group, 4)


def added(left, right):
    return left.astype(jnp.float32) + right.astype(jnp.float32)


class PlaneSum:
    def __init__(self, source, first, full, sends, receives):
        self.source, self.first, self.full = source, first, full
        self.sends, self.receives = sends, receives
        self.x, self.y = plane_here()
        half = source.shape[-1] // 2
        self.left, self.right = pl.ds(0, half), pl.ds(half, half)
        self.low, self.high = pl.ds(0, 2), pl.ds(2, 2)
        self.copies = []

    def x_part(self, x, part):
        return self.source.at[x, part, :, self.left]

    def y_part(self, y, part):
        return self.source.at[part, y, :, self.right]

    def send(self, source, target, index, where):
        copy = push(source, target, self.sends, self.receives, index, index, where)
        copy.start()
        self.copies.append(copy)

    def wait(self, region, index):
        landed(region, self.sends, self.receives, index)

    def neighbours(self, place):
        return lax.rem(place + 1, 4), lax.rem(place + 3, 4), lax.rem(place + 2, 4)

    def start(self):
        low, high = self.low, self.high
        for base, place, part, where in (
            (0, self.x, self.x_part, lambda p: plane_device(p, self.y)),
            (2, self.y, self.y_part, lambda p: plane_device(self.x, p)),
        ):
            up, down, far = self.neighbours(place)
            self.send(part(far, low), self.first.at[base], base, where(up))
            self.send(part(far, high), self.first.at[base + 1], base + 1, where(down))
            self.send(part(up, high), self.full.at[base, high], base + 4, where(up))
            self.send(part(down, low), self.full.at[base + 1, low], base + 5, where(down))

    def second(self):
        low, high = self.low, self.high
        for base, place, part, where in (
            (0, self.x, self.x_part, lambda p: plane_device(p, self.y)),
            (2, self.y, self.y_part, lambda p: plane_device(self.x, p)),
        ):
            up, down, _ = self.neighbours(place)
            for index, piece, chosen, to in (
                (base, low, part(up, low), up),
                (base + 1, high, part(down, high), down),
            ):
                self.wait(self.first.at[index], index)
                chosen[...] = added(chosen[...], self.first[index]).astype(jnp.bfloat16)
                self.send(chosen, self.full.at[index, piece], index + 8, where(to))

    def third(self, x_sum, y_sum):
        low, high = self.low, self.high
        for base, mine, total in (
            (0, self.source.at[self.x, :, :, self.left], x_sum),
            (2, self.source.at[:, self.y, :, self.right], y_sum),
        ):
            self.wait(self.full.at[base, high], base + 4)
            self.wait(self.full.at[base + 1, low], base + 5)
            self.wait(self.full.at[base, low], base + 8)
            self.wait(self.full.at[base + 1, high], base + 9)
            total[...] = (
                added(mine[...], self.full[base]) + self.full[base + 1].astype(jnp.float32)
            ).astype(jnp.bfloat16)

    def drain(self):
        for copy in self.copies:
            copy.wait_send()


class PlaneSpread:
    def __init__(self, x_sum, y_sum, land, sends, receives):
        self.x_sum, self.y_sum, self.land = x_sum, y_sum, land
        self.sends, self.receives = sends, receives
        self.x, self.y = plane_here()
        self.copies = []

    def start(self):
        for step in range(1, 4):
            y, x = lax.rem(self.y + step, 4), lax.rem(self.x + step, 4)
            for index, source, where in (
                (step - 1, self.x_sum.at[y], plane_device(self.x, y)),
                (step + 2, self.y_sum.at[x], plane_device(x, self.y)),
            ):
                copy = push(
                    source, self.land.at[index], self.sends, self.receives, index, index, where
                )
                copy.start()
                self.copies.append(copy)

    def total(self):
        sums = []
        for base, mine in ((0, self.x_sum[self.y]), (3, self.y_sum[self.x])):
            value = mine.astype(jnp.float32)
            for index in range(base, base + 3):
                landed(self.land.at[index], self.sends, self.receives, index)
                value += self.land[index].astype(jnp.float32)
            sums.append(value)
        return sums

    def drain(self):
        for copy in self.copies:
            copy.wait_send()


def greet_plane(barrier):
    x, y = plane_here()
    for step in range(1, 4):
        for where in (plane_device(lax.rem(x + step, 4), y), plane_device(x, lax.rem(y + step, 4))):
            pl.semaphore_signal(barrier, inc=1, device_id=where, device_id_type=MESH_ID)


EXPERT_ROWS = 384
CAPACITY = 48
FF_TILE = 768
FF_TILES = 4
WIDTH = 768


def gelu_parts(u):
    scaled = jnp.abs(u) * 0.7071067811865476
    t = 1.0 / (1.0 + 0.3275911 * scaled)
    poly = t * (
        0.127414796
        + t * (-0.142248368 + t * (0.7107068705 + t * (-0.7265760135 + t * 0.5307027145)))
    )
    density = jnp.exp(-0.5 * u * u)
    tail = poly * density
    cumulative = jnp.where(u >= 0, 1.0 - tail, tail)
    return u * cumulative, cumulative + u * density * 0.3989422804014327


def expert_kernel(
    sent_ref,
    grad_ref,
    in_frozen,
    out_frozen,
    in_new,
    out_new,
    returned_ref,
    grad_back_ref,
    in_grad_ref,
    x_sum_ref,
    y_sum_ref,
    w_in,
    w_out,
    x_land,
    g_land,
    activated,
    slope,
    acc,
    r_send,
    b_send,
    out_grad,
    first,
    full,
    load_sem,
    x_sems,
    g_sems,
    r_sems,
    b_sems,
    plane_send,
    plane_recv,
):
    mine = lax.axis_index("expert")
    barrier = pltpu.get_barrier_semaphore()
    greet(barrier)
    greet_plane(barrier)
    loads = []
    for kind, (first_w, second_w) in ((1, (in_new, out_new)), (0, (in_frozen, out_frozen))):
        for index, (source, target) in enumerate(((first_w, w_in), (second_w, w_out))):
            copy = pltpu.make_async_copy(source, target.at[kind], load_sem.at[kind, index])
            copy.start()
            loads.append(copy)

    def rows_of(place):
        return pl.ds(pl.multiple_of(place * CAPACITY, CAPACITY), CAPACITY)

    own_rows = rows_of(mine)
    x_land[:, own_rows, :] = sent_ref[:, own_rows, :]
    g_land[:, own_rows, :] = grad_ref[:, own_rows, :]
    pl.semaphore_wait(barrier, 13)

    def peer(step):
        return lax.rem(mine + step, 8)

    def group_device(place):
        return (lax.axis_index("dp"), place)

    def exchange(source, target, sems, index, step):
        return pltpu.make_async_remote_copy(
            src_ref=source,
            dst_ref=target,
            send_sem=sems.at[0, index],
            recv_sem=sems.at[1, index],
            device_id=group_device(peer(step)),
            device_id_type=MESH_ID,
        )

    def spread(source, target, sems):
        copies = []
        for step in range(1, 8):
            copy = exchange(
                source.at[:, rows_of(peer(step)), :], target.at[:, own_rows, :], sems, step - 1, step
            )
            copy.start()
            copies.append(copy)
        return copies

    def collect(target, sems):
        for step in range(1, 8):
            region = target.at[:, rows_of(lax.rem(mine + 8 - step, 8)), :]
            exchange(region, region, sems, step - 1, step).wait_recv()

    def spread_kind(kind, source, target, sems):
        target[kind, own_rows, :] = source[kind, own_rows, :]
        copies = []
        for step in range(1, 8):
            copy = exchange(
                source.at[kind, rows_of(peer(step)), :],
                target.at[kind, own_rows, :],
                sems,
                kind * 7 + step - 1,
                step,
            )
            copy.start()
            copies.append(copy)
        return copies

    def collect_kind(kind, target, sems):
        for step in range(1, 8):
            region = target.at[kind, rows_of(lax.rem(mine + 8 - step, 8)), :]
            exchange(region, region, sems, kind * 7 + step - 1, step).wait_recv()

    x_copies = spread(sent_ref, x_land, x_sems)
    for copy in loads:
        copy.wait()
    collect(x_land, x_sems)
    for copy in x_copies:
        copy.wait_send()
    pending = spread(grad_ref, g_land, g_sems)

    def tile_of(index):
        return pl.ds(pl.multiple_of(index * FF_TILE, FF_TILE), FF_TILE)

    for kind in (1, 0):
        acc[...] = jnp.zeros_like(acc)

        @pl.loop(0, FF_TILES)
        def _(index):
            tile = tile_of(index)
            pre = dot_nn(x_land[kind], w_in[kind, :, tile])
            value, steep = gelu_parts(pre)
            value = value.astype(jnp.bfloat16)
            if kind == 1:
                activated[:, tile] = value
            slope[kind, :, tile] = steep.astype(jnp.bfloat16)
            acc[...] += dot_nn(value, w_out[kind, tile, :])

        r_send[kind] = acc[...].astype(jnp.bfloat16)
        pending += spread_kind(kind, r_send, returned_ref, r_sems)

    collect(g_land, g_sems)

    @pl.loop(0, FF_TILES)
    def _(index):
        grads = dot_tn(activated[:, tile_of(index)], g_land[1]).astype(jnp.bfloat16)
        for y in range(4):
            for part in range(4):
                start = (y * 4 + part) * CAPACITY
                out_grad[index, y, :, part * WIDTH : (part + 1) * WIDTH] = grads[
                    start : start + CAPACITY
                ]

    plane = PlaneSum(out_grad, first, full, plane_send, plane_recv)
    plane.start()

    for kind in (1, 0):
        acc[...] = jnp.zeros_like(acc)

        @pl.loop(0, FF_TILES)
        def _(index):
            tile = tile_of(index)
            grads = dot_nt(g_land[kind], w_out[kind, tile, :])
            grads = (grads * slope[kind, :, tile].astype(jnp.float32)).astype(jnp.bfloat16)
            acc[...] += dot_nt(grads, w_in[kind, :, tile])
            if kind == 1:
                weights = dot_tn(x_land[kind], grads).astype(jnp.bfloat16)
                in_grad_ref[:, :, :, tile] = weights.reshape(4, 4, CAPACITY, FF_TILE)

        b_send[kind] = acc[...].astype(jnp.bfloat16)
        pending += spread_kind(kind, b_send, grad_back_ref, b_sems)
        if kind == 1:
            plane.second()

    plane.third(x_sum_ref, y_sum_ref)
    for kind in (1, 0):
        collect_kind(kind, returned_ref, r_sems)
        collect_kind(kind, grad_back_ref, b_sems)
    for copy in pending:
        copy.wait_send()
    plane.drain()


def anywhere():
    return pl.BlockSpec(memory_space=pl.ANY)


def experts_both_ways(sent, grads, in_frozen, out_frozen, in_new, out_new):
    half_type = jnp.bfloat16
    lanes = 4 * WIDTH
    return pl.pallas_call(
        expert_kernel,
        out_shape=[
            jax.ShapeDtypeStruct((2, EXPERT_ROWS, WIDTH), half_type),
            jax.ShapeDtypeStruct((2, EXPERT_ROWS, WIDTH), half_type),
            jax.ShapeDtypeStruct((4, 4, CAPACITY, lanes), half_type),
            jax.ShapeDtypeStruct((4, CAPACITY, lanes // 2), half_type),
            jax.ShapeDtypeStruct((4, CAPACITY, lanes // 2), half_type),
        ],
        in_specs=[vmem()] * 2 + [anywhere()] * 4,
        out_specs=[vmem()] * 5,
        scratch_shapes=[
            pltpu.VMEM((2, WIDTH, lanes), half_type),
            pltpu.VMEM((2, lanes, WIDTH), half_type),
            pltpu.VMEM((2, EXPERT_ROWS, WIDTH), half_type),
            pltpu.VMEM((2, EXPERT_ROWS, WIDTH), half_type),
            pltpu.VMEM((EXPERT_ROWS, lanes), half_type),
            pltpu.VMEM((2, EXPERT_ROWS, lanes), half_type),
            pltpu.VMEM((EXPERT_ROWS, WIDTH), jnp.float32),
            pltpu.VMEM((2, EXPERT_ROWS, WIDTH), half_type),
            pltpu.VMEM((2, EXPERT_ROWS, WIDTH), half_type),
            pltpu.VMEM((4, 4, CAPACITY, lanes), half_type),
            pltpu.VMEM((4, 2, CAPACITY, lanes // 2), half_type),
            pltpu.VMEM((4, 4, CAPACITY, lanes // 2), half_type),
            pltpu.SemaphoreType.DMA((2, 2)),
            pltpu.SemaphoreType.DMA((2, 7)),
            pltpu.SemaphoreType.DMA((2, 7)),
            pltpu.SemaphoreType.DMA((2, 14)),
            pltpu.SemaphoreType.DMA((2, 14)),
            pltpu.SemaphoreType.DMA((12,)),
            pltpu.SemaphoreType.DMA((12,)),
        ],
        compiler_params=pltpu.CompilerParams(
            collective_id=2, has_side_effects=True, vmem_limit_bytes=62 * 2**20
        ),
    )(sent, grads, in_frozen, out_frozen, in_new, out_new)


def head_mask(head, value, dtype):
    lanes = lax.broadcasted_iota(jnp.int32, (1, PAD), 1)
    inside = (lanes >= head * HD) & (lanes < (head + 1) * HD)
    return jnp.where(inside, value, 0.0).astype(dtype)


def lane_tiles(values, combine):
    result = values[:, :128]
    for start in range(128, values.shape[1], 128):
        result = combine(result, values[:, start : start + 128])
    return result


def front_kernel(
    kind_ref,
    tokens_ref,
    gain_ref,
    weight_ref,
    hidden_ref,
    query_ref,
    key_ref,
    value_ref,
    out_ref,
    total_ref,
    attended_ref,
    stacked,
    scores,
    largest,
    sums,
    acc,
    gather_send,
    gather_recv,
    out_send,
    out_recv,
):
    z, core = here()
    mine = z * 2 + core
    up, down, far = lax.rem(z + 1, CHIPS), lax.rem(z + 3, CHIPS), lax.rem(z + 2, CHIPS)
    barrier = pltpu.get_barrier_semaphore()
    greet(barrier)
    normed, _ = norm_parts(tokens_ref[...].astype(jnp.float32))
    hidden_ref[mine] = (normed * gain_ref[...]).astype(jnp.bfloat16)
    pl.semaphore_wait(barrier, 7)

    def send(region, index, where):
        copy = push(region, region, gather_send, gather_recv, index, index, where)
        copy.start()
        return copy

    def arrived(region, index):
        landed(region, gather_send, gather_recv, index)

    def project(block):
        projected = dot_nn(hidden_ref[block], weight_ref[...]).astype(jnp.bfloat16)
        query_ref[block] = projected[:, :PAD]
        rows = pl.ds(pl.multiple_of(block * BLOCK, BLOCK), BLOCK)
        key_ref[rows, :] = projected[:, PAD : 2 * PAD]
        value_ref[rows, :] = projected[:, 2 * PAD :]

    half = BLOCK // 2
    first, second = pl.ds(0, half), pl.ds(half, half)
    block_down, block_up, block_far = down * 2 + core, up * 2 + core, far * 2 + core
    copies = [
        send(hidden_ref.at[mine], 0, device(up, core)),
        send(hidden_ref.at[mine], 1, device(down, core)),
        send(hidden_ref.at[mine], 2, device(z, 1 - core)),
    ]
    project(mine)
    arrived(hidden_ref.at[z * 2 + 1 - core], 2)
    project(z * 2 + 1 - core)
    arrived(hidden_ref.at[block_down], 0)
    copies.append(send(hidden_ref.at[block_down, first], 3, device(up, core)))
    copies.append(send(hidden_ref.at[block_down], 5, device(z, 1 - core)))
    arrived(hidden_ref.at[block_up], 1)
    copies.append(send(hidden_ref.at[block_up, second], 4, device(down, core)))
    copies.append(send(hidden_ref.at[block_up], 6, device(z, 1 - core)))
    project(block_down)
    project(block_up)
    arrived(hidden_ref.at[down * 2 + 1 - core], 5)
    project(down * 2 + 1 - core)
    arrived(hidden_ref.at[up * 2 + 1 - core], 6)
    project(up * 2 + 1 - core)
    arrived(hidden_ref.at[block_far, first], 3)
    arrived(hidden_ref.at[block_far, second], 4)
    copies.append(send(hidden_ref.at[block_far], 7, device(z, 1 - core)))
    project(block_far)
    arrived(hidden_ref.at[far * 2 + 1 - core], 7)
    project(far * 2 + 1 - core)

    kind_bias = kind_ref[0].astype(jnp.float32) * NEGATIVE

    @pl.loop(0, CHIPS)
    def _(step):
        slot = lax.rem(z + step, CHIPS)
        block = slot * 2 + lax.rem(core + slot, 2)
        queries = query_ref[block]
        for head in range(LOCAL_HEADS):
            stacked[head * BLOCK : (head + 1) * BLOCK, :] = queries * head_mask(
                head, HD ** (-0.5), jnp.bfloat16
            )

        def chunk_rows(chunk):
            return pl.ds(pl.multiple_of(chunk * CHUNK, CHUNK), CHUNK)

        def bias_of(chunk):
            return jnp.where((slot >= 2) & (chunk < 2), kind_bias, 0.0)

        masked = dot_nt(stacked[...], key_ref[chunk_rows(slot), :])
        row = lax.broadcasted_iota(jnp.int32, (BLOCK, CHUNK), 0)
        column = lax.broadcasted_iota(jnp.int32, (BLOCK, CHUNK), 1)
        allowed = column - row <= (block - 2 * slot) * BLOCK
        for head in range(LOCAL_HEADS):
            part = slice(head * BLOCK, (head + 1) * BLOCK)
            values = jnp.where(allowed, masked[part], NEGATIVE)
            scores[slot, part, :] = values
            largest[part, :] = lane_tiles(values, jnp.maximum)

        @pl.loop(0, slot)
        def _(chunk):
            values = dot_nt(stacked[...], key_ref[chunk_rows(chunk), :])
            scores[chunk] = values
            largest[...] = jnp.maximum(
                largest[...], lane_tiles(values, jnp.maximum) + bias_of(chunk)
            )

        row_max = jnp.max(largest[...], axis=1, keepdims=True)
        largest[...] = jnp.broadcast_to(row_max, largest.shape)
        sums[...] = jnp.zeros_like(sums)
        acc[...] = jnp.zeros_like(acc)

        @pl.loop(0, slot + 1)
        def _(chunk):
            exponent = jnp.exp(scores[chunk] - (largest[:, :1] - bias_of(chunk)))
            sums[...] += lane_tiles(exponent, jnp.add)
            acc[...] += dot_nn(exponent.astype(jnp.bfloat16), value_ref[chunk_rows(chunk), :])

        total = jnp.sum(sums[...], axis=1, keepdims=True)
        inverse = 1.0 / total
        log_total = largest[...] + jnp.log(total)
        attended = jnp.zeros((BLOCK, PAD), jnp.float32)
        for head in range(LOCAL_HEADS):
            part = slice(head * BLOCK, (head + 1) * BLOCK)
            attended += acc[part, :] * inverse[part] * head_mask(head, 1.0, jnp.float32)
            total_ref[slot, head : head + 1, :] = jnp.transpose(log_total[part, :])[:1, :]
        out_ref[slot] = attended.astype(jnp.bfloat16)

        @pl.when(block != mine)
        def _():
            push(
                out_ref.at[slot],
                attended_ref.at[z],
                out_send,
                out_recv,
                slot,
                z,
                device(slot, lax.rem(core + slot, 2)),
            ).start()

        @pl.when(block == mine)
        def _():
            attended_ref[z] = out_ref[slot]

    for copy in copies:
        copy.wait_send()

    @pl.loop(0, CHIPS)
    def _(slot):
        @pl.when(slot * 2 + lax.rem(core + slot, 2) != mine)
        def _():
            push(
                out_ref.at[slot],
                attended_ref.at[slot],
                out_send,
                out_recv,
                slot,
                slot,
                device(z, 1 - core),
            ).wait_send()

        @pl.when((slot != z) | (lax.rem(core + z, 2) != core))
        def _():
            landed(attended_ref.at[slot], out_send, out_recv, slot)


def vmem():
    return pl.BlockSpec(memory_space=pltpu.VMEM)


def smem():
    return pl.BlockSpec(memory_space=pltpu.SMEM)


def front(kind, tokens, gain, weight):
    half_type = jnp.bfloat16
    shapes = [
        jax.ShapeDtypeStruct((8, BLOCK, 768), half_type),
        jax.ShapeDtypeStruct((8, BLOCK, PAD), half_type),
        jax.ShapeDtypeStruct((LONG, PAD), half_type),
        jax.ShapeDtypeStruct((LONG, PAD), half_type),
        jax.ShapeDtypeStruct((CHIPS, BLOCK, PAD), half_type),
        jax.ShapeDtypeStruct((CHIPS, 8, BLOCK), jnp.float32),
        jax.ShapeDtypeStruct((CHIPS, BLOCK, PAD), half_type),
    ]
    return pl.pallas_call(
        front_kernel,
        out_shape=shapes,
        in_specs=[smem(), vmem(), vmem(), vmem()],
        out_specs=[vmem()] * len(shapes),
        scratch_shapes=[
            pltpu.VMEM((STACK, PAD), half_type),
            pltpu.VMEM((CHUNKS, STACK, CHUNK), jnp.float32),
            pltpu.VMEM((STACK, 128), jnp.float32),
            pltpu.VMEM((STACK, 128), jnp.float32),
            pltpu.VMEM((STACK, PAD), jnp.float32),
            pltpu.SemaphoreType.DMA((8,)),
            pltpu.SemaphoreType.DMA((8,)),
            pltpu.SemaphoreType.DMA((CHIPS,)),
            pltpu.SemaphoreType.DMA((CHIPS,)),
        ],
        compiler_params=pltpu.CompilerParams(
            collective_id=0, has_side_effects=True, vmem_limit_bytes=56 * 2**20
        ),
    )(kind, tokens, gain, weight)


def back_kernel(
    kind_ref,
    grad_ref,
    query_ref,
    key_ref,
    value_ref,
    out_ref,
    total_ref,
    weight_ref,
    hidden_ref,
    in_grad_ref,
    dense_ref,
    x_part_ref,
    y_part_ref,
    result_ref,
    in_sum_ref,
    out_sum_ref,
    dense_land,
    grad_out,
    stacked,
    grad_stacked,
    grad_query,
    grad_key,
    grad_value,
    projected,
    part_sib,
    part_own,
    land_sib,
    land_half,
    land_full,
    grad_send,
    grad_recv,
    sib_send,
    sib_recv,
    ring_send,
    ring_recv,
    big,
    big_first,
    big_full,
    big_x,
    big_y,
    big_land,
    out_land,
    qkv,
    qkv_first,
    qkv_full,
    qkv_x,
    qkv_y,
    qkv_land,
    dense_send,
    load_sem,
    big_sems,
    big_spread,
    out_spread,
    qkv_sems,
    qkv_spread,
    dense_sems,
):
    z, core = here()
    mine = z * 2 + core
    up, down, far = lax.rem(z + 1, CHIPS), lax.rem(z + 3, CHIPS), lax.rem(z + 2, CHIPS)
    barrier = pltpu.get_barrier_semaphore()
    greet(barrier)
    greet_plane(barrier)
    lanes_in = in_grad_ref.shape[-1]
    loads = [
        pltpu.make_async_copy(in_grad_ref, big.at[:, :, :, pl.ds(0, lanes_in)], load_sem.at[0]),
        pltpu.make_async_copy(
            dense_ref, big.at[:, :, :, pl.ds(lanes_in, dense_ref.shape[-1])], load_sem.at[1]
        ),
    ]
    for load in loads:
        load.start()
    grad_key[...] = jnp.zeros_like(grad_key)
    grad_value[...] = jnp.zeros_like(grad_value)
    projected[...] = jnp.zeros_like(projected)
    pl.semaphore_wait(barrier, 13)
    owner_core = lax.rem(core + z, 2)

    @pl.loop(0, CHIPS)
    def _(step):
        chip = lax.rem(z + step, CHIPS)
        mine_too = (chip == z) & (owner_core == core)

        @pl.when(jnp.logical_not(mine_too))
        def _():
            push(
                grad_ref.at[chip],
                grad_out.at[z],
                grad_send,
                grad_recv,
                chip,
                z,
                device(chip, owner_core),
            ).start()

        @pl.when(mine_too)
        def _():
            grad_out[z] = grad_ref[chip]

    for load in loads:
        load.wait()
    big_sum = PlaneSum(big, big_first, big_full, big_sems.at[0], big_sems.at[1])
    big_sum.start()
    out_sum = PlaneSpread(x_part_ref, y_part_ref, out_land, out_spread.at[0], out_spread.at[1])
    out_sum.start()

    kind_bias = kind_ref[0].astype(jnp.float32) * NEGATIVE

    def attend(step):
        slot = lax.rem(z + step, CHIPS)
        block = slot * 2 + lax.rem(core + slot, 2)

        @pl.when(block != mine)
        def _():
            landed(grad_out.at[slot], grad_send, grad_recv, slot)

        queries = query_ref[block]
        grads = grad_out[slot]
        products = grads.astype(jnp.float32) * out_ref[slot].astype(jnp.float32)
        selector = jnp.concatenate(
            [head_mask(head, 1.0, jnp.float32) for head in range(LOCAL_HEADS)]
            + [jnp.zeros((8 - LOCAL_HEADS, PAD), jnp.float32)],
            axis=0,
        )
        deltas = lax.dot_general(
            selector,
            products,
            (((1,), (1,)), ((), ())),
            preferred_element_type=jnp.float32,
            precision=lax.Precision.HIGHEST,
        )
        for head in range(LOCAL_HEADS):
            part = slice(head * BLOCK, (head + 1) * BLOCK)
            stacked[part, :] = queries * head_mask(head, HD ** (-0.5), jnp.bfloat16)
            grad_stacked[part, :] = grads * head_mask(head, 1.0, jnp.bfloat16)
        totals = total_ref[slot]
        delta_row = jnp.concatenate(
            [deltas[head : head + 1, :] for head in range(LOCAL_HEADS)], axis=1
        )
        total_row = jnp.concatenate(
            [totals[head : head + 1, :] for head in range(LOCAL_HEADS)], axis=1
        )

        def work(chunk, is_last):
            rows = pl.ds(pl.multiple_of(chunk * CHUNK, CHUNK), CHUNK)
            keys, values = key_ref[rows, :], value_ref[rows, :]
            bias = jnp.where((slot >= 2) & (chunk < 2), kind_bias, 0.0)
            probs = jnp.exp(dot_nt(keys, stacked[...]) - (total_row - bias))
            if is_last:
                row = lax.broadcasted_iota(jnp.int32, (CHUNK, STACK), 0)
                column = lax.broadcasted_iota(jnp.int32, (CHUNK, STACK), 1)
                allowed = row - lax.rem(column, BLOCK) <= (block - 2 * slot) * BLOCK
                probs = jnp.where(allowed, probs, 0.0)
            grad_probs = dot_nt(values, grad_stacked[...])
            grad_scores = (probs * (grad_probs - delta_row)).astype(jnp.bfloat16)
            grad_value[rows, :] += dot_nn(probs.astype(jnp.bfloat16), grad_stacked[...])
            grad_key[rows, :] += dot_nn(grad_scores, stacked[...])
            return dot_tn(grad_scores, keys)

        grad_query[...] = work(slot, True)

        @pl.loop(0, slot)
        def _(chunk):
            grad_query[...] += work(chunk, False)

        combined = jnp.zeros((BLOCK, PAD), jnp.float32)
        for head in range(LOCAL_HEADS):
            part = slice(head * BLOCK, (head + 1) * BLOCK)
            combined += grad_query[part, :] * head_mask(head, HD ** (-0.5), jnp.float32)
        rows = pl.ds(pl.multiple_of(block * BLOCK, BLOCK), BLOCK)
        projected[rows, :PAD] = combined.astype(jnp.bfloat16)

    pl.loop(0, 2)(attend)
    big_sum.second()
    pl.loop(2, CHIPS)(attend)
    projected[:, PAD : 2 * PAD] = grad_key[...].astype(jnp.bfloat16)
    projected[:, 2 * PAD :] = grad_value[...].astype(jnp.bfloat16)

    for tile in range(3):
        lanes = slice(tile * PAD, (tile + 1) * PAD)
        weights = dot_tn(hidden_ref[...], projected[:, lanes]).astype(jnp.bfloat16)
        qkv[:, :, :, lanes] = weights.reshape(4, 4, CAPACITY, PAD)
    qkv_sum = PlaneSum(qkv, qkv_first, qkv_full, qkv_sems.at[0], qkv_sems.at[1])
    qkv_sum.start()

    def partial(chip, which):
        rows = pl.ds(pl.multiple_of((chip * 2 + which) * BLOCK, BLOCK), BLOCK)
        return dot_nt(projected[rows, :], weight_ref[...])

    def sib_copy(index):
        return push(
            part_sib.at[index],
            land_sib.at[index],
            sib_send,
            sib_recv,
            index,
            index,
            device(z, 1 - core),
        )

    order = (far, up, down, z)
    for index, chip in enumerate(order):
        part_sib[index] = partial(chip, 1 - core).astype(jnp.bfloat16)
        sib_copy(index).start()

    def own(index):
        value = partial(order[index], core)
        landed(land_sib.at[index], sib_send, sib_recv, index)
        return value + land_sib[index].astype(jnp.float32)

    half = BLOCK // 2
    first, second = pl.ds(0, half), pl.ds(half, half)
    part_own[0] = own(0).astype(jnp.bfloat16)

    def ring(source, target, index, where):
        copy = push(source, target, ring_send, ring_recv, index, index, where)
        copy.start()
        return copy

    above, below = device(up, core), device(down, core)
    copies = [
        ring(part_own.at[0, first], land_half.at[0], 0, above),
        ring(part_own.at[0, second], land_half.at[1], 1, below),
    ]
    part_own[1] = own(1).astype(jnp.bfloat16)
    copies.append(ring(part_own.at[1, second], land_full.at[0, second], 2, above))
    part_own[2] = own(2).astype(jnp.bfloat16)
    copies.append(ring(part_own.at[2, first], land_full.at[1, first], 3, below))
    result_ref[...] = own(3)
    landed(land_half.at[0], ring_send, ring_recv, 0)
    part_own[1, first, :] = (
        part_own[1, first, :].astype(jnp.float32) + land_half[0].astype(jnp.float32)
    ).astype(jnp.bfloat16)
    copies.append(ring(part_own.at[1, first], land_full.at[0, first], 4, above))
    landed(land_half.at[1], ring_send, ring_recv, 1)
    part_own[2, second, :] = (
        part_own[2, second, :].astype(jnp.float32) + land_half[1].astype(jnp.float32)
    ).astype(jnp.bfloat16)
    copies.append(ring(part_own.at[2, second], land_full.at[1, second], 5, below))

    qkv_sum.second()
    big_sum.third(big_x, big_y)
    big_total = PlaneSpread(big_x, big_y, big_land, big_spread.at[0], big_spread.at[1])
    big_total.start()

    landed(land_full.at[0, second], ring_send, ring_recv, 2)
    landed(land_full.at[1, first], ring_send, ring_recv, 3)
    landed(land_full.at[0, first], ring_send, ring_recv, 4)
    landed(land_full.at[1, second], ring_send, ring_recv, 5)
    result_ref[...] += land_full[0].astype(jnp.float32) + land_full[1].astype(jnp.float32)

    qkv_sum.third(qkv_x, qkv_y)
    qkv_total = PlaneSpread(qkv_x, qkv_y, qkv_land, qkv_spread.at[0], qkv_spread.at[1])
    qkv_total.start()
    out_left, out_right = out_sum.total()
    out_sum_ref[:, : 2 * WIDTH] = out_left
    out_sum_ref[:, 2 * WIDTH :] = out_right
    left, right = big_total.total()
    half_lanes = left.shape[-1]
    in_sum_ref[:, :half_lanes] = left
    in_sum_ref[:, half_lanes:] = right[:, : lanes_in - half_lanes]
    dense = right[:, lanes_in - half_lanes :]
    dense_lanes = dense.shape[-1]
    own_rows = CAPACITY // 8
    qkv_left, qkv_right = qkv_total.total()
    qkv_lanes = qkv_left.shape[-1]
    for piece in range(8):
        rows = slice(piece * own_rows, (piece + 1) * own_rows)
        dense_send[piece, :own_rows, :dense_lanes] = dense[rows]
        dense_send[piece, :own_rows, dense_lanes : dense_lanes + qkv_lanes] = qkv_left[rows]
        dense_send[piece, :own_rows, dense_lanes + qkv_lanes :] = qkv_right[rows]
    dense_copies = []
    for step in range(1, 8):
        place = lax.rem(mine + step, 8)
        copy = push(
            dense_send.at[place],
            dense_land.at[mine],
            dense_sems.at[0],
            dense_sems.at[1],
            step - 1,
            step - 1,
            (lax.axis_index("dp"), place),
        )
        copy.start()
        dense_copies.append(copy)
    dense_land[mine] = dense_send[mine]
    for step in range(1, 8):
        landed(
            dense_land.at[lax.rem(mine + 8 - step, 8)],
            dense_sems.at[0],
            dense_sems.at[1],
            step - 1,
        )
    for copy in dense_copies:
        copy.wait_send()
    for user in (big_sum, out_sum, big_total, qkv_sum, qkv_total):
        user.drain()
    for copy in copies:
        copy.wait_send()
    for index in range(CHIPS):
        sib_copy(index).wait_send()

    @pl.loop(0, CHIPS)
    def _(chip):
        @pl.when((chip != z) | (owner_core != core))
        def _():
            push(
                grad_ref.at[chip],
                grad_out.at[chip],
                grad_send,
                grad_recv,
                chip,
                chip,
                device(z, 1 - core),
            ).wait_send()


def plane_scratch(lanes):
    half_type = jnp.bfloat16
    return [
        pltpu.VMEM((4, 4, CAPACITY, lanes), half_type),
        pltpu.VMEM((4, 2, CAPACITY, lanes // 2), half_type),
        pltpu.VMEM((4, 4, CAPACITY, lanes // 2), half_type),
        pltpu.VMEM((4, CAPACITY, lanes // 2), half_type),
        pltpu.VMEM((4, CAPACITY, lanes // 2), half_type),
        pltpu.VMEM((6, CAPACITY, lanes // 2), half_type),
    ]


def back(
    kind, grads, queries, keys, values, out, totals, weight, hidden, in_grad, dense, x_part, y_part
):
    half_type = jnp.bfloat16
    width = WIDTH
    lanes_in, lanes_dense = in_grad.shape[-1], dense.shape[-1]
    return pl.pallas_call(
        back_kernel,
        out_shape=[
            jax.ShapeDtypeStruct((BLOCK, width), jnp.float32),
            jax.ShapeDtypeStruct((CAPACITY, lanes_in), jnp.float32),
            jax.ShapeDtypeStruct((CAPACITY, lanes_in), jnp.float32),
            jax.ShapeDtypeStruct((8, 8, lanes_dense + 3 * PAD), jnp.float32),
        ],
        in_specs=[smem()] + [vmem()] * 8 + [anywhere()] * 2 + [vmem()] * 2,
        out_specs=[vmem()] * 4,
        scratch_shapes=[
            pltpu.VMEM((CHIPS, BLOCK, PAD), half_type),
            pltpu.VMEM((STACK, PAD), half_type),
            pltpu.VMEM((STACK, PAD), half_type),
            pltpu.VMEM((STACK, PAD), jnp.float32),
            pltpu.VMEM((LONG, PAD), jnp.float32),
            pltpu.VMEM((LONG, PAD), jnp.float32),
            pltpu.VMEM((LONG, 3 * PAD), half_type),
            pltpu.VMEM((CHIPS, BLOCK, width), half_type),
            pltpu.VMEM((CHIPS, BLOCK, width), half_type),
            pltpu.VMEM((CHIPS, BLOCK, width), half_type),
            pltpu.VMEM((2, BLOCK // 2, width), half_type),
            pltpu.VMEM((2, BLOCK, width), half_type),
            pltpu.SemaphoreType.DMA((CHIPS,)),
            pltpu.SemaphoreType.DMA((CHIPS,)),
            pltpu.SemaphoreType.DMA((CHIPS,)),
            pltpu.SemaphoreType.DMA((CHIPS,)),
            pltpu.SemaphoreType.DMA((6,)),
            pltpu.SemaphoreType.DMA((6,)),
            *plane_scratch(lanes_in + lanes_dense),
            pltpu.VMEM((6, CAPACITY, lanes_in // 2), half_type),
            *plane_scratch(3 * PAD),
            pltpu.VMEM((8, 8, lanes_dense + 3 * PAD), jnp.float32),
            pltpu.SemaphoreType.DMA((2,)),
            pltpu.SemaphoreType.DMA((2, 12)),
            pltpu.SemaphoreType.DMA((2, 6)),
            pltpu.SemaphoreType.DMA((2, 6)),
            pltpu.SemaphoreType.DMA((2, 12)),
            pltpu.SemaphoreType.DMA((2, 6)),
            pltpu.SemaphoreType.DMA((2, 7)),
        ],
        compiler_params=pltpu.CompilerParams(
            collective_id=1, has_side_effects=True, vmem_limit_bytes=60 * 2**20
        ),
    )(kind, grads, queries, keys, values, out, totals, weight, hidden, in_grad, dense, x_part, y_part)


def routing(routes, capacity, experts):
    expert_ids = jnp.arange(experts, dtype=jnp.int32)
    pick_zero = (routes[..., 0:1] == expert_ids).astype(jnp.int32)
    pick_one = (routes[..., 1:2] == expert_ids).astype(jnp.int32)
    named_count = pick_zero + pick_one
    earlier = jnp.cumsum(named_count, axis=1) - named_count
    slot_zero = jnp.sum(earlier * pick_zero, axis=-1)
    slot_one = jnp.sum(earlier * pick_one, axis=-1)
    columns = jnp.arange(experts * capacity, dtype=jnp.int32)
    target_zero = routes[..., 0] * capacity + slot_zero
    target_one = routes[..., 1] * capacity + slot_one
    send_zero = ((target_zero[..., None] == columns) & (slot_zero < capacity)[..., None]).astype(
        jnp.float32
    )
    send_one = ((target_one[..., None] == columns) & (slot_one < capacity)[..., None]).astype(
        jnp.float32
    )
    return (pick_zero.astype(jnp.float32), pick_one.astype(jnp.float32), send_zero, send_one)


def on_device(
    tokens,
    group_kind,
    routes,
    norm1_gain,
    qkv_weight,
    proj_weight,
    norm2_gain,
    router_weight,
    frozen_in,
    frozen_out,
    new_in,
    new_out,
    out_grad,
):
    groups, rows, width = tokens.shape
    count = lax.axis_size("expert")
    experts = 2 * count
    capacity = max(2, 3 * rows * TOP // (2 * experts))
    start_row = lax.axis_index("expert") * rows
    score_scale = HD ** (-0.5)
    inputs = tokens.astype(jnp.float32)
    normed_one, inverse_one = norm_parts(inputs)
    chip = lax.axis_index("expert") // 2
    chip_columns = lax.dynamic_index_in_dim(
        qkv_weight.reshape(width, 3, CHIPS, width // CHIPS), chip, axis=2, keepdims=False
    )
    chip_weight = jnp.pad(chip_columns, ((0, 0), (0, 0), (0, PAD - width // CHIPS))).reshape(
        width, 3 * PAD
    )
    proj_chips = jnp.pad(
        proj_weight.reshape(CHIPS, width // CHIPS, width),
        ((0, 0), (0, PAD - width // CHIPS), (0, 0)),
    )
    hidden_all, queries, keys, values, out_heads, totals, attended = front(
        group_kind, tokens[0], norm1_gain[None], chip_weight
    )
    branch = jnp.einsum("ztd,zde->te", attended, proj_chips, preferred_element_type=jnp.float32)[
        None
    ]
    residual = inputs + branch
    normed_two, inverse_two = norm_parts(residual)
    hidden_two = (normed_two * norm2_gain).astype(jnp.bfloat16)
    logits = jnp.einsum(
        "gtd,de->gte", hidden_two, router_weight, preferred_element_type=jnp.float32
    )
    pick_zero, pick_one, send_zero, send_one = routing(routes, capacity, experts)
    logit_zero = jnp.sum(logits * pick_zero, axis=-1)
    logit_one = jnp.sum(logits * pick_one, axis=-1)
    gate_zero = jax.nn.sigmoid(logit_zero - logit_one)
    gate_one = jax.nn.sigmoid(logit_one - logit_zero)
    dispatch = (send_zero + send_one).astype(jnp.bfloat16)
    buffers = jnp.einsum(
        "gts,gtd->gsd", dispatch, hidden_two, preferred_element_type=jnp.float32
    ).astype(jnp.bfloat16)
    mixing = (gate_zero[..., None] * send_zero + gate_one[..., None] * send_one).astype(
        jnp.bfloat16
    )
    grad_res = out_grad.astype(jnp.float32)
    grad_returned = jnp.einsum(
        "gts,gtd->gsd", mixing, out_grad, preferred_element_type=jnp.float32
    ).astype(jnp.bfloat16)
    returned, sent_back, in_grad, out_grad_x, out_grad_y = experts_both_ways(
        buffers.reshape(2, count * capacity, width),
        grad_returned.reshape(2, count * capacity, width),
        frozen_in[0],
        frozen_out[0],
        new_in[0],
        new_out[0],
    )
    returned_flat = returned.reshape(groups, experts * capacity, width)
    combined = jnp.einsum("gts,gsd->gtd", mixing, returned_flat, preferred_element_type=jnp.float32)
    mixed = (residual + combined).astype(jnp.bfloat16)
    grad_mixing = jnp.einsum(
        "gtd,gsd->gts", out_grad, returned_flat, preferred_element_type=jnp.float32
    )
    grad_gap = (
        (jnp.sum(grad_mixing * send_zero, axis=-1) - jnp.sum(grad_mixing * send_one, axis=-1))
        * gate_zero
        * gate_one
    )
    grad_logits = (grad_gap[..., None] * (pick_zero - pick_one)).astype(jnp.bfloat16)
    router_grad = jnp.einsum(
        "gtd,gte->de", hidden_two, grad_logits, preferred_element_type=jnp.float32
    )
    grad_hidden_two = jnp.einsum(
        "gte,de->gtd", grad_logits, router_weight, preferred_element_type=jnp.float32
    )
    grad_hidden_two = grad_hidden_two + jnp.einsum(
        "gts,gsd->gtd",
        dispatch,
        sent_back.reshape(groups, experts * capacity, width),
        preferred_element_type=jnp.float32,
    )
    norm2_gain_grad = jnp.sum(grad_hidden_two * normed_two, axis=(0, 1))
    grad_residual = grad_res + norm_back(grad_hidden_two * norm2_gain, normed_two, inverse_two)
    grad_branch = grad_residual.astype(jnp.bfloat16)
    proj_grad = jnp.einsum(
        "ztd,te->zde", attended, grad_branch[0], preferred_element_type=jnp.float32
    )[:, : width // CHIPS].reshape(width, width)
    grad_attended = jnp.einsum(
        "te,zde->ztd", grad_branch[0], proj_chips, preferred_element_type=jnp.float32
    ).astype(jnp.bfloat16)
    dense = jnp.concatenate(
        [proj_grad, router_grad, norm2_gain_grad[:, None]], axis=1
    ).astype(jnp.bfloat16)
    dense = jnp.pad(dense, ((0, 0), (0, 1024 - dense.shape[1]))).reshape(4, 4, width // 16, 1024)
    grad_hidden_one, in_sum, out_sum, dense_parts = back(
        group_kind,
        grad_attended,
        queries,
        keys,
        values,
        out_heads,
        totals,
        chip_weight,
        hidden_all.reshape(LONG, width),
        in_grad,
        dense,
        out_grad_x,
        out_grad_y,
    )
    grad_hidden_one = grad_hidden_one[None]
    tokens_grad = grad_residual + norm_back(grad_hidden_one * norm1_gain, normed_one, inverse_one)
    own = width // (lax.axis_size("dp") * count)
    shared = jnp.sum(dense_parts[:, :own, :1024], axis=0)
    qkv_sum = jnp.sum(dense_parts[:, :own, 1024:].reshape(CHIPS, 2, own, 3, PAD), axis=1)
    qkv_sum = qkv_sum[..., : width // CHIPS].transpose(1, 2, 0, 3).reshape(own, 3 * width)
    first_row = (lax.axis_index("dp") * count + lax.axis_index("expert")) * own
    own_weight = lax.dynamic_slice_in_dim(qkv_weight, first_row, own, axis=0)
    own_gain = lax.dynamic_slice_in_dim(norm1_gain, first_row, own, axis=0)
    norm1_gain_grad = jnp.sum(qkv_sum * own_weight.astype(jnp.float32), axis=1) / own_gain
    out_rows = out_sum.reshape(width // 16, 4, width).transpose(1, 0, 2).reshape(1, -1, width)
    return (
        mixed,
        tokens_grad,
        norm1_gain_grad,
        qkv_sum,
        shared[:, :width],
        shared[:, width + experts],
        shared[:, width : width + experts],
        in_sum[None],
        out_rows,
    )


def solution(mesh):
    return jax.shard_map(
        on_device,
        mesh=mesh,
        in_specs=(
            P("dp", "expert", None),
            P("dp"),
            P("dp", "expert", None),
            P(),
            P(),
            P(),
            P(),
            P(),
            P("expert", None, None),
            P("expert", None, None),
            P("expert", None, None),
            P("expert", None, None),
            P("dp", "expert", None),
        ),
        out_specs=(
            P("dp", "expert", None),
            P("dp", "expert", None),
            P(("dp", "expert")),
            P(("dp", "expert"), None),
            P(("dp", "expert"), None),
            P(("dp", "expert")),
            P(("dp", "expert"), None),
            P("expert", "dp", None),
            P("expert", "dp", None),
        ),
        check_vma=False,
    )
```

```python
import jax
import jax.numpy as jnp
from jax import lax
from jax.experimental import pallas as pl
from jax.experimental.pallas import tpu as pltpu
from jax.sharding import PartitionSpec as P

HEADS = 12
HD = 64
LONG = 2048
MESH_ID = pl.DeviceIdType.MESH
CHIPS = 4
PAD = 256
BLOCK = 256
HALF = BLOCK // 2
CHUNK = 512
CHUNKS = LONG // CHUNK
LOCAL_HEADS = HEADS // CHIPS
STACK = LOCAL_HEADS * BLOCK
NEGATIVE = -1e30
WIDTH = 768
EXPERTS = 16
SLOTS = 768
EXPERT_ROWS = 384
CAPACITY = 48
FF = 3072
FF_TILE = 768
FF_TILES = 4
DENSE = 1024
LINE = (DENSE + 3 * PAD) // 2
HALF_TYPE = jnp.bfloat16
FULL_TYPE = jnp.float32

epsilon = 1e-05


def norm_parts(values):
    average = jnp.mean(values, axis=-1, keepdims=True)
    centred = values - average
    variance = jnp.mean(centred * centred, axis=-1, keepdims=True)
    inverse = lax.rsqrt(variance + epsilon)
    return (centred * inverse, inverse)


def norm_back(grad_normed, normed, inverse):
    first_mean = jnp.mean(grad_normed, axis=-1, keepdims=True)
    second_mean = jnp.mean(grad_normed * normed, axis=-1, keepdims=True)
    return inverse * (grad_normed - first_mean - normed * second_mean)


def here():
    position = lax.axis_index("expert")
    return position // 2, lax.rem(position, 2)


def device(z, core):
    return (lax.axis_index("dp"), z * 2 + core)


def greet(barrier):
    position = lax.axis_index("expert")
    for step in range(1, 8):
        pl.semaphore_signal(
            barrier,
            inc=1,
            device_id=(lax.axis_index("dp"), lax.rem(position + step, 8)),
            device_id_type=MESH_ID,
        )


def push(source, target, sends, receives, index_here, index_there, where):
    return pltpu.make_async_remote_copy(
        src_ref=source,
        dst_ref=target,
        send_sem=sends.at[index_here],
        recv_sem=receives.at[index_there],
        device_id=where,
        device_id_type=MESH_ID,
    )


def landed(region, sends, receives, index):
    z, core = here()
    push(region, region, sends, receives, index, index, device(z, 1 - core)).wait_recv()


def dot_nn(left, right):
    return jnp.dot(left, right, preferred_element_type=jnp.float32)


def dot_nt(left, right):
    return lax.dot_general(
        left, right, (((1,), (1,)), ((), ())), preferred_element_type=jnp.float32
    )


def dot_tn(left, right):
    return lax.dot_general(
        left, right, (((0,), (0,)), ((), ())), preferred_element_type=jnp.float32
    )


def window(chip):
    return (chip + chip // 2) * 128, lax.rem(chip, 2) * HD


def head_mask(chip, head, value, dtype):
    start = window(chip)[1] + head * HD
    lanes = lax.broadcasted_iota(jnp.int32, (1, PAD), 1)
    inside = (lanes >= start) & (lanes < start + HD)
    return jnp.where(inside, value, 0.0).astype(dtype)


def lane_tiles(values, combine):
    result = values[:, :128]
    for start in range(128, values.shape[1], 128):
        result = combine(result, values[:, start : start + 128])
    return result


def block_rows(block):
    return pl.ds(pl.multiple_of(block * BLOCK, BLOCK), BLOCK)


def chunk_rows(chunk):
    return pl.ds(pl.multiple_of(chunk * CHUNK, CHUNK), CHUNK)


def load_windows(weight_ref, target, sems, chip):
    copies = []
    for part in range(3):
        first = pl.multiple_of(part * WIDTH + window(chip)[0], 128)
        copies.append(
            pltpu.make_async_copy(
                weight_ref.at[:, pl.ds(first, PAD)],
                target.at[:, pl.ds(part * PAD, PAD)],
                sems.at[part],
            )
        )
    for copy in copies:
        copy.start()
    return copies


class RingGather:
    def __init__(self, ref, sends, receives):
        self.ref, self.sends, self.receives = ref, sends, receives
        self.z, self.core = here()
        self.up, self.down = lax.rem(self.z + 1, CHIPS), lax.rem(self.z + 3, CHIPS)
        self.far = lax.rem(self.z + 2, CHIPS)
        self.copies = []

    def region(self, chip, core, half):
        rows = slice(None) if half is None else pl.ds(half * HALF, HALF)
        return self.ref.at[chip * 2 + core, rows]

    def send(self, index, chip, half, where):
        region = self.region(chip, self.core, half)
        copy = push(region, region, self.sends, self.receives, index, index, where)
        copy.start()
        self.copies.append(copy)

    def wait(self, index, chip, core, half):
        landed(self.region(chip, core, half), self.sends, self.receives, index)

    def above(self):
        return device(self.up, self.core)

    def below(self):
        return device(self.down, self.core)

    def beside(self):
        return device(self.z, 1 - self.core)

    def start(self):
        self.send(0, self.z, 0, self.above())
        self.send(1, self.z, 1, self.below())
        self.send(2, self.z, 1, self.above())
        self.send(3, self.z, 0, self.below())
        self.send(4, self.z, None, self.beside())

    def relay(self):
        self.wait(0, self.down, self.core, 0)
        self.send(5, self.down, 0, self.above())
        self.send(7, self.down, 0, self.beside())
        self.wait(1, self.up, self.core, 1)
        self.send(6, self.up, 1, self.below())
        self.send(8, self.up, 1, self.beside())

    def share(self):
        self.wait(2, self.down, self.core, 1)
        self.send(9, self.down, 1, self.beside())
        self.wait(3, self.up, self.core, 0)
        self.send(10, self.up, 0, self.beside())

    def share_far(self):
        self.wait(5, self.far, self.core, 0)
        self.send(11, self.far, 0, self.beside())
        self.wait(6, self.far, self.core, 1)
        self.send(12, self.far, 1, self.beside())

    def other_own(self):
        self.wait(4, self.z, 1 - self.core, None)

    def other_down(self):
        self.wait(7, self.down, 1 - self.core, 0)
        self.wait(9, self.down, 1 - self.core, 1)

    def other_up(self):
        self.wait(8, self.up, 1 - self.core, 1)
        self.wait(10, self.up, 1 - self.core, 0)

    def other_far(self):
        self.wait(11, self.far, 1 - self.core, 0)
        self.wait(12, self.far, 1 - self.core, 1)

    def drain(self):
        for copy in self.copies:
            copy.wait_send()


def plane_device(x, y):
    return (x * 4 + y, lax.axis_index("expert"))


def plane_here():
    group = lax.axis_index("dp")
    return group // 4, lax.rem(group, 4)


def added(left, right):
    return left.astype(jnp.float32) + right.astype(jnp.float32)


class PlaneSum:
    def __init__(self, source, first, full, sends, receives):
        self.source, self.first, self.full = source, first, full
        self.sends, self.receives = sends, receives
        self.x, self.y = plane_here()
        half = source.shape[-1] // 2
        self.left, self.right = pl.ds(0, half), pl.ds(half, half)
        self.low, self.high = pl.ds(0, 2), pl.ds(2, 2)
        self.copies = []

    def x_part(self, x, part):
        return self.source.at[x, part, :, self.left]

    def y_part(self, y, part):
        return self.source.at[part, y, :, self.right]

    def send(self, source, target, index, where):
        copy = push(source, target, self.sends, self.receives, index, index, where)
        copy.start()
        self.copies.append(copy)

    def wait(self, region, index):
        landed(region, self.sends, self.receives, index)

    def neighbours(self, place):
        return lax.rem(place + 1, 4), lax.rem(place + 3, 4), lax.rem(place + 2, 4)

    def start(self):
        low, high = self.low, self.high
        for base, place, part, where in (
            (0, self.x, self.x_part, lambda p: plane_device(p, self.y)),
            (2, self.y, self.y_part, lambda p: plane_device(self.x, p)),
        ):
            up, down, far = self.neighbours(place)
            self.send(part(far, low), self.first.at[base], base, where(up))
            self.send(part(far, high), self.first.at[base + 1], base + 1, where(down))
            self.send(part(up, high), self.full.at[base, high], base + 4, where(up))
            self.send(part(down, low), self.full.at[base + 1, low], base + 5, where(down))

    def second(self):
        low, high = self.low, self.high
        for base, place, part, where in (
            (0, self.x, self.x_part, lambda p: plane_device(p, self.y)),
            (2, self.y, self.y_part, lambda p: plane_device(self.x, p)),
        ):
            up, down, _ = self.neighbours(place)
            for index, piece, chosen, to in (
                (base, low, part(up, low), up),
                (base + 1, high, part(down, high), down),
            ):
                self.wait(self.first.at[index], index)
                chosen[...] = added(chosen[...], self.first[index]).astype(jnp.bfloat16)
                self.send(chosen, self.full.at[index, piece], index + 8, where(to))

    def third(self, x_sum, y_sum):
        low, high = self.low, self.high
        for base, mine, total in (
            (0, self.source.at[self.x, :, :, self.left], x_sum),
            (2, self.source.at[:, self.y, :, self.right], y_sum),
        ):
            self.wait(self.full.at[base, high], base + 4)
            self.wait(self.full.at[base + 1, low], base + 5)
            self.wait(self.full.at[base, low], base + 8)
            self.wait(self.full.at[base + 1, high], base + 9)
            total[...] = (
                added(mine[...], self.full[base]) + self.full[base + 1].astype(jnp.float32)
            ).astype(jnp.bfloat16)

    def drain(self):
        for copy in self.copies:
            copy.wait_send()


class PlaneSpread:
    def __init__(self, x_sum, y_sum, land, sends, receives):
        self.x_sum, self.y_sum, self.land = x_sum, y_sum, land
        self.sends, self.receives = sends, receives
        self.x, self.y = plane_here()
        self.copies = []

    def start(self):
        for step in range(1, 4):
            y, x = lax.rem(self.y + step, 4), lax.rem(self.x + step, 4)
            for index, source, where in (
                (step - 1, self.x_sum.at[y], plane_device(self.x, y)),
                (step + 2, self.y_sum.at[x], plane_device(x, self.y)),
            ):
                copy = push(
                    source, self.land.at[index], self.sends, self.receives, index, index, where
                )
                copy.start()
                self.copies.append(copy)

    def total(self):
        sums = []
        for base, mine in ((0, self.x_sum[self.y]), (3, self.y_sum[self.x])):
            value = mine.astype(jnp.float32)
            for index in range(base, base + 3):
                landed(self.land.at[index], self.sends, self.receives, index)
                value += self.land[index].astype(jnp.float32)
            sums.append(value)
        return sums

    def drain(self):
        for copy in self.copies:
            copy.wait_send()


def greet_plane(barrier):
    x, y = plane_here()
    for step in range(1, 4):
        for where in (plane_device(lax.rem(x + step, 4), y), plane_device(x, lax.rem(y + step, 4))):
            pl.semaphore_signal(barrier, inc=1, device_id=where, device_id_type=MESH_ID)


def gelu_parts(u):
    scaled = jnp.abs(u) * 0.7071067811865476
    t = 1.0 / (1.0 + 0.3275911 * scaled)
    poly = t * (
        0.127414796
        + t * (-0.142248368 + t * (0.7107068705 + t * (-0.7265760135 + t * 0.5307027145)))
    )
    density = jnp.exp(-0.5 * u * u)
    tail = poly * density
    cumulative = jnp.where(u >= 0, 1.0 - tail, tail)
    return u * cumulative, cumulative + u * density * 0.3989422804014327


def vmem():
    return pl.BlockSpec(memory_space=pltpu.VMEM)


def smem():
    return pl.BlockSpec(memory_space=pltpu.SMEM)


def anywhere():
    return pl.BlockSpec(memory_space=pl.ANY)


def front_kernel(
    kind_ref,
    tokens_ref,
    gain_ref,
    weight_ref,
    grad_ref,
    routes_ref,
    proj_ref,
    gain_two_ref,
    router_ref,
    hidden_out,
    query_out,
    key_out,
    value_out,
    heads_out,
    grads_out,
    total_ref,
    attended_ref,
    residual_ref,
    hidden_two_ref,
    sent_ref,
    info_ref,
    hidden_ref,
    query_ref,
    key_ref,
    value_ref,
    out_ref,
    grads_ref,
    weight,
    stacked,
    scores,
    largest,
    sums,
    acc,
    gather_sems,
    grads_sems,
    out_sems,
    weight_sems,
    store_sems,
):
    z, core = here()
    mine = z * 2 + core
    up, down, far = lax.rem(z + 1, CHIPS), lax.rem(z + 3, CHIPS), lax.rem(z + 2, CHIPS)
    barrier = pltpu.get_barrier_semaphore()
    greet(barrier)
    loads = load_windows(weight_ref, weight, weight_sems, z)
    tokens = tokens_ref[...].astype(jnp.float32)
    normed, _ = norm_parts(tokens)
    hidden_ref[mine] = (normed * gain_ref[...]).astype(jnp.bfloat16)
    grads_ref[mine] = grad_ref[...]
    pl.semaphore_wait(barrier, 7)
    gather = RingGather(hidden_ref, gather_sems.at[0], gather_sems.at[1])
    grads_gather = RingGather(grads_ref, grads_sems.at[0], grads_sems.at[1])
    stores = []

    def store(source, target):
        copy = pltpu.make_async_copy(source, target, store_sems.at[len(stores)])
        copy.start()
        stores.append(copy)

    def project(block):
        projected = dot_nn(hidden_ref[block], weight[...]).astype(jnp.bfloat16)
        query_ref[block] = projected[:, :PAD]
        key_ref[block_rows(block), :] = projected[:, PAD : 2 * PAD]
        value_ref[block_rows(block), :] = projected[:, 2 * PAD :]

    gather.start()
    for load in loads:
        load.wait()
    project(mine)
    routes = routes_ref[...].astype(jnp.float32)
    names = lax.broadcasted_iota(jnp.int32, (EXPERTS, BLOCK), 0).astype(jnp.float32)
    pick_zero = jnp.where(names == routes[0:1, :], 1.0, 0.0)
    pick_one = jnp.where(names == routes[1:2, :], 1.0, 0.0)
    row = lax.broadcasted_iota(jnp.int32, (BLOCK, BLOCK), 0)
    column = lax.broadcasted_iota(jnp.int32, (BLOCK, BLOCK), 1)
    before = jnp.where(row < column, 1.0, 0.0).astype(jnp.bfloat16)
    earlier = dot_nn((pick_zero + pick_one).astype(jnp.bfloat16), before)
    places = []
    for index, pick in enumerate((pick_zero, pick_one)):
        slot = jnp.sum(earlier * pick, axis=0, keepdims=True)
        place = routes[index : index + 1, :] * CAPACITY + slot
        places.append(jnp.where(slot < CAPACITY, place, -1.0))
    gather.relay()
    gather.other_own()
    project(z * 2 + 1 - core)
    gather.share()
    project(down * 2 + core)
    project(up * 2 + core)
    gather.share_far()
    grads_gather.start()
    project(far * 2 + core)
    gather.other_down()
    project(down * 2 + 1 - core)
    gather.other_up()
    project(up * 2 + 1 - core)
    gather.other_far()
    project(far * 2 + 1 - core)
    store(hidden_ref, hidden_out)
    store(query_ref, query_out)
    store(key_ref, key_out)
    store(value_ref, value_out)

    kind_bias = kind_ref[0].astype(jnp.float32) * NEGATIVE
    out_send, out_recv = out_sems.at[0], out_sems.at[1]

    def attend(step):
        slot = lax.rem(z + step, CHIPS)
        block = slot * 2 + lax.rem(core + slot, 2)
        queries = query_ref[block]
        for head in range(LOCAL_HEADS):
            stacked[head * BLOCK : (head + 1) * BLOCK, :] = queries * head_mask(
                z, head, HD ** (-0.5), jnp.bfloat16
            )

        def bias_of(chunk):
            return jnp.where((slot >= 2) & (chunk < 2), kind_bias, 0.0)

        masked = dot_nt(stacked[...], key_ref[chunk_rows(slot), :])
        row = lax.broadcasted_iota(jnp.int32, (BLOCK, CHUNK), 0)
        column = lax.broadcasted_iota(jnp.int32, (BLOCK, CHUNK), 1)
        allowed = column - row <= (block - 2 * slot) * BLOCK
        for head in range(LOCAL_HEADS):
            part = slice(head * BLOCK, (head + 1) * BLOCK)
            values = jnp.where(allowed, masked[part], NEGATIVE)
            scores[slot, part, :] = values
            largest[part, :] = lane_tiles(values, jnp.maximum)

        @pl.loop(0, slot)
        def _(chunk):
            values = dot_nt(stacked[...], key_ref[chunk_rows(chunk), :])
            scores[chunk] = values
            largest[...] = jnp.maximum(
                largest[...], lane_tiles(values, jnp.maximum) + bias_of(chunk)
            )

        row_max = jnp.max(largest[...], axis=1, keepdims=True)
        largest[...] = jnp.broadcast_to(row_max, largest.shape)
        sums[...] = jnp.zeros_like(sums)
        acc[...] = jnp.zeros_like(acc)

        @pl.loop(0, slot + 1)
        def _(chunk):
            exponent = jnp.exp(scores[chunk] - (largest[:, :1] - bias_of(chunk)))
            sums[...] += lane_tiles(exponent, jnp.add)
            acc[...] += dot_nn(exponent.astype(jnp.bfloat16), value_ref[chunk_rows(chunk), :])

        total = jnp.sum(sums[...], axis=1, keepdims=True)
        inverse = 1.0 / total
        log_total = largest[...] + jnp.log(total)
        attended = jnp.zeros((BLOCK, PAD), jnp.float32)
        for head in range(LOCAL_HEADS):
            part = slice(head * BLOCK, (head + 1) * BLOCK)
            attended += acc[part, :] * inverse[part] * head_mask(z, head, 1.0, jnp.float32)
            total_ref[slot, head : head + 1, :] = jnp.transpose(log_total[part, :])[:1, :]
        out_ref[slot] = attended.astype(jnp.bfloat16)

        @pl.when(block != mine)
        def _():
            push(
                out_ref.at[slot],
                attended_ref.at[z],
                out_send,
                out_recv,
                slot,
                z,
                device(slot, lax.rem(core + slot, 2)),
            ).start()

        @pl.when(block == mine)
        def _():
            attended_ref[z] = out_ref[slot]

    pl.loop(0, CHIPS - 1)(attend)
    grads_gather.relay()
    grads_gather.share()
    pl.loop(CHIPS - 1, CHIPS)(attend)
    store(out_ref, heads_out)

    @pl.loop(0, CHIPS)
    def _(slot):
        @pl.when((slot != z) | (lax.rem(core + z, 2) != core))
        def _():
            landed(attended_ref.at[slot], out_send, out_recv, slot)

    grads_gather.share_far()
    residual = tokens_ref[...].astype(jnp.float32)
    for chip in range(CHIPS):
        first = (chip + chip // 2) * 128
        residual += dot_nn(attended_ref[chip], proj_ref[first : first + PAD, :])
    residual_ref[...] = residual
    normed_two, _ = norm_parts(residual)
    hidden_two = (normed_two * gain_two_ref[...]).astype(jnp.bfloat16)
    hidden_two_ref[...] = hidden_two
    logits = dot_nt(router_ref[...], hidden_two)
    logit_zero = jnp.sum(logits * pick_zero, axis=0, keepdims=True)
    logit_one = jnp.sum(logits * pick_one, axis=0, keepdims=True)
    gate_zero = 1.0 / (1.0 + jnp.exp(logit_one - logit_zero))
    gate_one = 1.0 / (1.0 + jnp.exp(logit_zero - logit_one))
    for index, line in enumerate((*places, gate_zero, gate_one, routes[0:1], routes[1:2])):
        info_ref[index : index + 1, :] = line
    info_ref[6:8, :] = jnp.zeros((2, BLOCK), jnp.float32)
    ids = lax.broadcasted_iota(jnp.int32, (SLOTS, BLOCK), 0).astype(jnp.float32)
    chosen = jnp.where((ids == places[0]) | (ids == places[1]), 1.0, 0.0).astype(jnp.bfloat16)
    sent = dot_nn(chosen, hidden_two).astype(jnp.bfloat16)
    sent_ref[0] = sent[:EXPERT_ROWS]
    sent_ref[1] = sent[EXPERT_ROWS:]
    grads_gather.other_own()
    grads_gather.other_down()
    grads_gather.other_up()
    grads_gather.other_far()
    store(grads_ref, grads_out)
    gather.drain()
    grads_gather.drain()

    @pl.loop(0, CHIPS)
    def _(slot):
        @pl.when(slot * 2 + lax.rem(core + slot, 2) != mine)
        def _():
            push(
                out_ref.at[slot],
                attended_ref.at[slot],
                out_send,
                out_recv,
                slot,
                slot,
                device(z, 1 - core),
            ).wait_send()

    for copy in stores:
        copy.wait()


def front(kind, tokens, gain, weight, grads, routes, proj, gain_two, router):
    def shape(*dims, dtype=HALF_TYPE):
        return jax.ShapeDtypeStruct(dims, dtype)

    shapes = [
        shape(8, BLOCK, WIDTH),
        shape(8, BLOCK, PAD),
        shape(LONG, PAD),
        shape(LONG, PAD),
        shape(CHIPS, BLOCK, PAD),
        shape(8, BLOCK, WIDTH),
        shape(CHIPS, 8, BLOCK, dtype=FULL_TYPE),
        shape(CHIPS, BLOCK, PAD),
        shape(BLOCK, WIDTH, dtype=FULL_TYPE),
        shape(BLOCK, WIDTH),
        shape(2, EXPERT_ROWS, WIDTH),
        shape(8, BLOCK, dtype=FULL_TYPE),
    ]
    return pl.pallas_call(
        front_kernel,
        out_shape=shapes,
        in_specs=[smem(), vmem(), vmem(), anywhere()] + [vmem()] * 5,
        out_specs=[anywhere()] * 6 + [vmem()] * 6,
        scratch_shapes=[
            pltpu.VMEM((8, BLOCK, WIDTH), HALF_TYPE),
            pltpu.VMEM((8, BLOCK, PAD), HALF_TYPE),
            pltpu.VMEM((LONG, PAD), HALF_TYPE),
            pltpu.VMEM((LONG, PAD), HALF_TYPE),
            pltpu.VMEM((CHIPS, BLOCK, PAD), HALF_TYPE),
            pltpu.VMEM((8, BLOCK, WIDTH), HALF_TYPE),
            pltpu.VMEM((WIDTH, 3 * PAD), HALF_TYPE),
            pltpu.VMEM((STACK, PAD), HALF_TYPE),
            pltpu.VMEM((CHUNKS, STACK, CHUNK), FULL_TYPE),
            pltpu.VMEM((STACK, 128), FULL_TYPE),
            pltpu.VMEM((STACK, 128), FULL_TYPE),
            pltpu.VMEM((STACK, PAD), FULL_TYPE),
            pltpu.SemaphoreType.DMA((2, 13)),
            pltpu.SemaphoreType.DMA((2, 13)),
            pltpu.SemaphoreType.DMA((2, CHIPS)),
            pltpu.SemaphoreType.DMA((3,)),
            pltpu.SemaphoreType.DMA((6,)),
        ],
        compiler_params=pltpu.CompilerParams(
            collective_id=0, has_side_effects=True, vmem_limit_bytes=56 * 2**20
        ),
    )(kind, tokens, gain, weight, grads, routes, proj, gain_two, router)


def expert_kernel(
    sent_ref,
    info_ref,
    grads_ref,
    in_frozen,
    out_frozen,
    in_new,
    out_new,
    returned_ref,
    grad_back_ref,
    in_grad_ref,
    out_sum_ref,
    w_in,
    w_out,
    grads,
    info,
    x_land,
    gated,
    activated,
    change,
    slope,
    acc,
    r_send,
    b_send,
    in_grad,
    out_grad,
    first,
    full,
    x_sum,
    y_sum,
    out_land,
    load_sems,
    info_sems,
    x_sems,
    r_sems,
    b_sems,
    plane_sems,
    plane_spread,
    store_sems,
):
    mine = lax.axis_index("expert")
    barrier = pltpu.get_barrier_semaphore()
    greet(barrier)
    greet_plane(barrier)
    loads = []
    for index, (source, target) in enumerate(
        (
            (grads_ref, grads),
            (in_new, w_in.at[1]),
            (out_new, w_out.at[1]),
            (in_frozen, w_in.at[0]),
            (out_frozen, w_out.at[0]),
        )
    ):
        copy = pltpu.make_async_copy(source, target, load_sems.at[index])
        copy.start()
        loads.append(copy)

    def rows_of(place):
        return pl.ds(pl.multiple_of(place * CAPACITY, CAPACITY), CAPACITY)

    own_rows = rows_of(mine)
    info[mine] = info_ref[...]
    pl.semaphore_wait(barrier, 13)

    def peer(step):
        return lax.rem(mine + step, 8)

    def exchange(source, target, sems, index, step):
        return push(
            source, target, sems.at[0], sems.at[1], index, index, (lax.axis_index("dp"), peer(step))
        )

    pending = []

    def begin(copy):
        copy.start()
        pending.append(copy)

    for step in range(1, 8):
        begin(exchange(info_ref, info.at[mine], info_sems, step - 1, step))

    def spread_kind(kind, source, target, sems):
        target[kind, own_rows, :] = source[kind, own_rows, :]
        for step in range(1, 8):
            begin(
                exchange(
                    source.at[kind, rows_of(peer(step)), :],
                    target.at[kind, own_rows, :],
                    sems,
                    kind * 7 + step - 1,
                    step,
                )
            )

    def collect_kind(kind, target, sems):
        for step in range(1, 8):
            region = target.at[kind, rows_of(lax.rem(mine + 8 - step, 8)), :]
            exchange(region, region, sems, kind * 7 + step - 1, step).wait_recv()

    for kind in (1, 0):
        spread_kind(kind, sent_ref, x_land, x_sems)
    for step in range(1, 8):
        region = info.at[lax.rem(mine + 8 - step, 8)]
        exchange(region, region, info_sems, step - 1, step).wait_recv()
    loads[0].wait()
    ids = lax.broadcasted_iota(jnp.int32, (2 * CAPACITY, BLOCK), 0)
    ids = jnp.where(ids < CAPACITY, mine * CAPACITY + ids, (mine + 7) * CAPACITY + ids)
    ids = ids.astype(jnp.float32)

    @pl.loop(0, 8)
    def _(block):
        lines = info[block]
        at_zero, at_one = ids == lines[0:1, :], ids == lines[1:2, :]
        chosen = jnp.where(at_zero | at_one, 1.0, 0.0).astype(jnp.bfloat16)
        gates = jnp.where(at_zero, lines[2:3, :], 0.0) + jnp.where(at_one, lines[3:4, :], 0.0)
        gate = jnp.sum(gates, axis=1, keepdims=True).astype(jnp.bfloat16).astype(jnp.float32)
        values = dot_nn(chosen, grads[block])
        scaled = (values * gate).astype(jnp.bfloat16)
        for kind in range(2):
            part = slice(kind * CAPACITY, (kind + 1) * CAPACITY)
            gated[kind, rows_of(block), :] = scaled[part]

    def tile_of(index):
        return pl.ds(pl.multiple_of(index * FF_TILE, FF_TILE), FF_TILE)

    plane = PlaneSum(out_grad, first, full, plane_sems.at[0], plane_sems.at[1])
    for kind in (1, 0):
        collect_kind(kind, x_land, x_sems)
        loads[1 if kind == 1 else 3].wait()
        loads[2 if kind == 1 else 4].wait()
        acc[...] = jnp.zeros_like(acc)

        @pl.loop(0, FF_TILES, unroll=True)
        def _(index):
            tile = tile_of(index)
            pre = dot_nn(x_land[kind], w_in[kind, :, tile])
            value, steep = gelu_parts(pre)
            value = value.astype(jnp.bfloat16)
            if kind == 1:
                activated[:, tile] = value
            slope[:, tile] = steep.astype(jnp.bfloat16)
            acc[...] += dot_nn(value, w_out[kind, tile, :])

        r_send[kind] = acc[...].astype(jnp.bfloat16)
        spread_kind(kind, r_send, returned_ref, r_sems)
        if kind == 1:

            @pl.loop(0, FF_TILES, unroll=True)
            def _(index):
                weights = dot_tn(activated[:, tile_of(index)], gated[1]).astype(jnp.bfloat16)
                for y in range(4):
                    for part in range(4):
                        start = (y * 4 + part) * CAPACITY
                        out_grad[index, y, :, part * WIDTH : (part + 1) * WIDTH] = weights[
                            start : start + CAPACITY
                        ]

            plane.start()
        else:
            plane.second()

        acc[...] = jnp.zeros_like(acc)

        @pl.loop(0, FF_TILES, unroll=True)
        def _(index):
            tile = tile_of(index)
            grad = dot_nt(gated[kind], w_out[kind, tile, :])
            grad = (grad * slope[:, tile].astype(jnp.float32)).astype(jnp.bfloat16)
            acc[...] += dot_nt(grad, w_in[kind, :, tile])
            if kind == 1:
                change[:, tile] = grad

        b_send[kind] = acc[...].astype(jnp.bfloat16)
        spread_kind(kind, b_send, grad_back_ref, b_sems)
        if kind == 0:
            plane.third(x_sum, y_sum)
            spread = PlaneSpread(x_sum, y_sum, out_land, plane_spread.at[0], plane_spread.at[1])
            spread.start()


    def in_store(index):
        tile = tile_of(index)
        return pltpu.make_async_copy(
            in_grad.at[:, :, :, tile], in_grad_ref.at[:, :, :, tile], store_sems.at[index]
        )

    @pl.loop(0, FF_TILES, unroll=True)
    def _(index):
        weights = dot_tn(x_land[1], change[:, tile_of(index)]).astype(jnp.bfloat16)
        in_grad[:, :, :, tile_of(index)] = weights.reshape(4, 4, CAPACITY, FF_TILE)
        in_store(index).start()

    for kind in (1, 0):
        collect_kind(kind, returned_ref, r_sems)
        collect_kind(kind, grad_back_ref, b_sems)
    left, right = spread.total()
    out_sum_ref[:, : FF // 2] = left
    out_sum_ref[:, FF // 2 :] = right
    for copy in pending:
        copy.wait_send()
    plane.drain()
    spread.drain()
    for index in range(FF_TILES):
        in_store(index).wait()


def experts_both_ways(sent, info, grads, in_frozen, out_frozen, in_new, out_new):
    def shape(*dims, dtype=HALF_TYPE):
        return jax.ShapeDtypeStruct(dims, dtype)

    return pl.pallas_call(
        expert_kernel,
        out_shape=[
            shape(2, EXPERT_ROWS, WIDTH),
            shape(2, EXPERT_ROWS, WIDTH),
            shape(4, 4, CAPACITY, FF),
            shape(CAPACITY, FF, dtype=FULL_TYPE),
        ],
        in_specs=[vmem()] * 2 + [anywhere()] * 5,
        out_specs=[vmem()] * 2 + [anywhere(), vmem()],
        scratch_shapes=[
            pltpu.VMEM((2, WIDTH, FF), HALF_TYPE),
            pltpu.VMEM((2, FF, WIDTH), HALF_TYPE),
            pltpu.VMEM((8, BLOCK, WIDTH), HALF_TYPE),
            pltpu.VMEM((8, 8, BLOCK), FULL_TYPE),
            pltpu.VMEM((2, EXPERT_ROWS, WIDTH), HALF_TYPE),
            pltpu.VMEM((2, EXPERT_ROWS, WIDTH), HALF_TYPE),
            pltpu.VMEM((EXPERT_ROWS, FF), HALF_TYPE),
            pltpu.VMEM((EXPERT_ROWS, FF), HALF_TYPE),
            pltpu.VMEM((EXPERT_ROWS, FF), HALF_TYPE),
            pltpu.VMEM((EXPERT_ROWS, WIDTH), FULL_TYPE),
            pltpu.VMEM((2, EXPERT_ROWS, WIDTH), HALF_TYPE),
            pltpu.VMEM((2, EXPERT_ROWS, WIDTH), HALF_TYPE),
            pltpu.VMEM((4, 4, CAPACITY, FF), HALF_TYPE),
            pltpu.VMEM((4, 4, CAPACITY, FF), HALF_TYPE),
            pltpu.VMEM((4, 2, CAPACITY, FF // 2), HALF_TYPE),
            pltpu.VMEM((4, 4, CAPACITY, FF // 2), HALF_TYPE),
            pltpu.VMEM((4, CAPACITY, FF // 2), HALF_TYPE),
            pltpu.VMEM((4, CAPACITY, FF // 2), HALF_TYPE),
            pltpu.VMEM((6, CAPACITY, FF // 2), HALF_TYPE),
            pltpu.SemaphoreType.DMA((5,)),
            pltpu.SemaphoreType.DMA((2, 7)),
            pltpu.SemaphoreType.DMA((2, 14)),
            pltpu.SemaphoreType.DMA((2, 14)),
            pltpu.SemaphoreType.DMA((2, 14)),
            pltpu.SemaphoreType.DMA((2, 12)),
            pltpu.SemaphoreType.DMA((2, 6)),
            pltpu.SemaphoreType.DMA((FF_TILES,)),
        ],
        compiler_params=pltpu.CompilerParams(
            collective_id=2, has_side_effects=True, vmem_limit_bytes=62 * 2**20
        ),
    )(sent, info, grads, in_frozen, out_frozen, in_new, out_new)


def back_kernel(
    kind_ref,
    tokens_ref,
    gain_ref,
    gain_two_ref,
    grad_ref,
    residual_ref,
    info_ref,
    returned_ref,
    grad_back_ref,
    router_ref,
    proj_ref,
    hidden_two_ref,
    total_ref,
    query_hbm,
    key_hbm,
    value_hbm,
    heads_hbm,
    weight_hbm,
    hidden_hbm,
    attended_hbm,
    in_grad_hbm,
    mixed_ref,
    tokens_grad_ref,
    in_sum_ref,
    dense_sum_ref,
    qkv_sum_ref,
    dense_land,
    query_ref,
    key_ref,
    value_ref,
    heads_ref,
    weight,
    hidden_ref,
    attended_ref,
    grad_residual,
    grad_sent,
    grad_out,
    stacked,
    grad_stacked,
    grad_query,
    grad_key,
    grad_value,
    projected,
    part_sib,
    part_own,
    land_sib,
    land_half,
    land_full,
    big,
    big_first,
    big_full,
    big_x,
    big_y,
    big_land,
    mid,
    mid_first,
    mid_full,
    mid_x,
    mid_y,
    mid_land,
    qkv,
    qkv_first,
    qkv_full,
    qkv_x,
    qkv_y,
    qkv_land,
    dense_send,
    weight_sems,
    load_sems,
    grad_sems,
    sib_sems,
    ring_sems,
    big_sems,
    big_spread,
    mid_sems,
    mid_spread,
    qkv_sems,
    qkv_spread,
    dense_sems,
):
    z, core = here()
    mine = z * 2 + core
    up, down, far = lax.rem(z + 1, CHIPS), lax.rem(z + 3, CHIPS), lax.rem(z + 2, CHIPS)
    barrier = pltpu.get_barrier_semaphore()
    greet(barrier)
    greet_plane(barrier)
    loads = []
    for index, (source, target) in enumerate(
        (
            (in_grad_hbm, big),
            (attended_hbm, attended_ref),
            (query_hbm, query_ref),
            (key_hbm, key_ref),
            (value_hbm, value_ref),
            (heads_hbm, heads_ref),
            (hidden_hbm, hidden_ref),
        )
    ):
        copy = pltpu.make_async_copy(source, target, load_sems.at[index])
        copy.start()
        loads.append(copy)
    weight_loads = load_windows(weight_hbm, weight, weight_sems, z)

    info = info_ref[...]
    columns = jnp.transpose(
        jnp.concatenate([info, jnp.zeros((120, BLOCK), jnp.float32)], axis=0)
    )
    lane_ids = lax.broadcasted_iota(jnp.int32, (BLOCK, SLOTS), 1).astype(jnp.float32)
    at_zero, at_one = lane_ids == columns[:, 0:1], lane_ids == columns[:, 1:2]
    match = jnp.concatenate(
        [dot_nt(grad_ref[...], returned_ref[0]), dot_nt(grad_ref[...], returned_ref[1])], axis=1
    )
    match = jnp.where(at_zero, match, 0.0) - jnp.where(at_one, match, 0.0)
    match = jnp.broadcast_to(jnp.sum(match, axis=1, keepdims=True), (BLOCK, 128))
    gap = jnp.transpose(match)[:1, :] * info[2:3, :] * info[3:4, :]
    names = lax.broadcasted_iota(jnp.int32, (EXPERTS, BLOCK), 0).astype(jnp.float32)
    pick_zero = jnp.where(names == info[4:5, :], 1.0, 0.0)
    pick_one = jnp.where(names == info[5:6, :], 1.0, 0.0)
    grad_logits = (gap * (pick_zero - pick_one)).astype(jnp.bfloat16)
    chosen = jnp.where(at_zero | at_one, 1.0, 0.0).astype(jnp.bfloat16)
    grad_two = (
        dot_tn(grad_logits, router_ref[...])
        + dot_nn(chosen[:, :EXPERT_ROWS], grad_back_ref[0])
        + dot_nn(chosen[:, EXPERT_ROWS:], grad_back_ref[1])
    )
    pl.semaphore_wait(barrier, 13)
    loads[0].wait()
    big_sum = PlaneSum(big, big_first, big_full, big_sems.at[0], big_sems.at[1])
    big_sum.start()
    normed_two, inverse_two = norm_parts(residual_ref[...])
    gain_two_grad = jnp.sum(grad_two * normed_two, axis=0, keepdims=True)
    grad_residual[...] = grad_ref[...].astype(jnp.float32) + norm_back(
        grad_two * gain_two_ref[...], normed_two, inverse_two
    )
    grad_branch = grad_residual[...].astype(jnp.bfloat16)
    for chip in range(CHIPS):
        first = (chip + chip // 2) * 128
        grad_sent[chip] = dot_nt(grad_branch, proj_ref[first : first + PAD, :]).astype(
            jnp.bfloat16
        )
    owner_core = lax.rem(core + z, 2)
    grad_send, grad_recv = grad_sems.at[0], grad_sems.at[1]

    @pl.loop(0, CHIPS)
    def _(step):
        chip = lax.rem(z + step, CHIPS)
        mine_too = (chip == z) & (owner_core == core)

        @pl.when(jnp.logical_not(mine_too))
        def _():
            push(
                grad_sent.at[chip],
                grad_out.at[z],
                grad_send,
                grad_recv,
                chip,
                z,
                device(chip, owner_core),
            ).start()

        @pl.when(mine_too)
        def _():
            grad_out[z] = grad_sent[chip]

    loads[1].wait()
    for chip in range(CHIPS):
        grads = dot_tn(attended_ref[chip], grad_branch).astype(jnp.bfloat16)
        first = (chip % 2) * HD
        for y in range(4):
            start = first + y * CAPACITY
            mid[chip, y, :, :WIDTH] = grads[start : start + CAPACITY]
    narrow = jnp.concatenate(
        [
            dot_nn(grad_logits, hidden_two_ref[...]),
            gain_two_grad,
            jnp.zeros((111, WIDTH), jnp.float32),
        ],
        axis=0,
    )
    mid[:, :, :, WIDTH : WIDTH + 128] = (
        jnp.transpose(narrow).astype(jnp.bfloat16).reshape(4, 4, CAPACITY, 128)
    )
    mid[:, :, :, WIDTH + 128 :] = jnp.zeros((4, 4, CAPACITY, 128), jnp.bfloat16)
    mid_sum = PlaneSum(mid, mid_first, mid_full, mid_sems.at[0], mid_sems.at[1])
    mid_sum.start()

    mixing = (
        jnp.where(at_zero, columns[:, 2:3], 0.0) + jnp.where(at_one, columns[:, 3:4], 0.0)
    ).astype(jnp.bfloat16)
    mixed_ref[...] = (
        residual_ref[...]
        + dot_nn(mixing[:, :EXPERT_ROWS], returned_ref[0])
        + dot_nn(mixing[:, EXPERT_ROWS:], returned_ref[1])
    ).astype(jnp.bfloat16)

    grad_key[...] = jnp.zeros_like(grad_key)
    grad_value[...] = jnp.zeros_like(grad_value)
    projected[...] = jnp.zeros_like(projected)
    for load in loads[2:6]:
        load.wait()
    kind_bias = kind_ref[0].astype(jnp.float32) * NEGATIVE

    def attend(step):
        slot = lax.rem(z + step, CHIPS)
        block = slot * 2 + lax.rem(core + slot, 2)

        @pl.when(block != mine)
        def _():
            landed(grad_out.at[slot], grad_send, grad_recv, slot)

        queries = query_ref[block]
        grads = grad_out[slot]
        products = grads.astype(jnp.float32) * heads_ref[slot].astype(jnp.float32)
        selector = jnp.concatenate(
            [head_mask(z, head, 1.0, jnp.float32) for head in range(LOCAL_HEADS)]
            + [jnp.zeros((8 - LOCAL_HEADS, PAD), jnp.float32)],
            axis=0,
        )
        deltas = lax.dot_general(
            selector,
            products,
            (((1,), (1,)), ((), ())),
            preferred_element_type=jnp.float32,
            precision=lax.Precision.HIGHEST,
        )
        for head in range(LOCAL_HEADS):
            part = slice(head * BLOCK, (head + 1) * BLOCK)
            stacked[part, :] = queries * head_mask(z, head, HD ** (-0.5), jnp.bfloat16)
            grad_stacked[part, :] = grads * head_mask(z, head, 1.0, jnp.bfloat16)
        totals = total_ref[slot]
        delta_row = jnp.concatenate(
            [deltas[head : head + 1, :] for head in range(LOCAL_HEADS)], axis=1
        )
        total_row = jnp.concatenate(
            [totals[head : head + 1, :] for head in range(LOCAL_HEADS)], axis=1
        )

        def work(chunk, is_last):
            rows = chunk_rows(chunk)
            keys, values = key_ref[rows, :], value_ref[rows, :]
            bias = jnp.where((slot >= 2) & (chunk < 2), kind_bias, 0.0)
            probs = jnp.exp(dot_nt(keys, stacked[...]) - (total_row - bias))
            if is_last:
                row = lax.broadcasted_iota(jnp.int32, (CHUNK, STACK), 0)
                column = lax.broadcasted_iota(jnp.int32, (CHUNK, STACK), 1)
                allowed = row - lax.rem(column, BLOCK) <= (block - 2 * slot) * BLOCK
                probs = jnp.where(allowed, probs, 0.0)
            grad_probs = dot_nt(values, grad_stacked[...])
            grad_scores = (probs * (grad_probs - delta_row)).astype(jnp.bfloat16)
            grad_value[rows, :] += dot_nn(probs.astype(jnp.bfloat16), grad_stacked[...])
            grad_key[rows, :] += dot_nn(grad_scores, stacked[...])
            return dot_tn(grad_scores, keys)

        grad_query[...] = work(slot, True)

        @pl.loop(0, slot)
        def _(chunk):
            grad_query[...] += work(chunk, False)

        combined = jnp.zeros((BLOCK, PAD), jnp.float32)
        for head in range(LOCAL_HEADS):
            part = slice(head * BLOCK, (head + 1) * BLOCK)
            combined += grad_query[part, :] * head_mask(z, head, HD ** (-0.5), jnp.float32)
        projected[block_rows(block), :PAD] = combined.astype(jnp.bfloat16)

    pl.loop(0, CHIPS)(attend)
    big_sum.second()
    mid_sum.second()
    projected[:, PAD : 2 * PAD] = grad_key[...].astype(jnp.bfloat16)
    projected[:, 2 * PAD :] = grad_value[...].astype(jnp.bfloat16)
    loads[6].wait()
    for load in weight_loads:
        load.wait()
    for tile in range(3):
        lanes = slice(tile * PAD, (tile + 1) * PAD)
        weights = dot_tn(hidden_ref[...], projected[:, lanes]).astype(jnp.bfloat16)
        qkv[:, :, :, lanes] = weights.reshape(4, 4, CAPACITY, PAD)
    qkv_sum = PlaneSum(qkv, qkv_first, qkv_full, qkv_sems.at[0], qkv_sems.at[1])
    qkv_sum.start()


    def partial(chip, which):
        return dot_nt(projected[block_rows(chip * 2 + which), :], weight[...])

    sib_send, sib_recv = sib_sems.at[0], sib_sems.at[1]

    def sib_copy(index):
        return push(
            part_sib.at[index],
            land_sib.at[index],
            sib_send,
            sib_recv,
            index,
            index,
            device(z, 1 - core),
        )

    order = (far, up, down, z)
    for index, chip in enumerate(order):
        part_sib[index] = partial(chip, 1 - core).astype(jnp.bfloat16)
        sib_copy(index).start()


    def own(index):
        value = partial(order[index], core)
        landed(land_sib.at[index], sib_send, sib_recv, index)
        return value + land_sib[index].astype(jnp.float32)

    first, second = pl.ds(0, HALF), pl.ds(HALF, HALF)
    ring_send, ring_recv = ring_sems.at[0], ring_sems.at[1]
    copies = []

    def ring(source, target, index, where):
        copy = push(source, target, ring_send, ring_recv, index, index, where)
        copy.start()
        copies.append(copy)

    above, below = device(up, core), device(down, core)
    part_own[0] = own(0).astype(jnp.bfloat16)
    ring(part_own.at[0, first], land_half.at[0], 0, above)
    ring(part_own.at[0, second], land_half.at[1], 1, below)
    part_own[1] = own(1).astype(jnp.bfloat16)
    ring(part_own.at[1, second], land_full.at[0, second], 2, above)
    part_own[2] = own(2).astype(jnp.bfloat16)
    ring(part_own.at[2, first], land_full.at[1, first], 3, below)
    grad_one = own(3)
    big_sum.third(big_x, big_y)
    big_total = PlaneSpread(big_x, big_y, big_land, big_spread.at[0], big_spread.at[1])
    big_total.start()
    landed(land_half.at[0], ring_send, ring_recv, 0)
    part_own[1, first, :] = added(part_own[1, first, :], land_half[0]).astype(jnp.bfloat16)
    ring(part_own.at[1, first], land_full.at[0, first], 4, above)
    landed(land_half.at[1], ring_send, ring_recv, 1)
    part_own[2, second, :] = added(part_own[2, second, :], land_half[1]).astype(jnp.bfloat16)
    ring(part_own.at[2, second], land_full.at[1, second], 5, below)
    qkv_sum.second()
    mid_sum.third(mid_x, mid_y)
    mid_total = PlaneSpread(mid_x, mid_y, mid_land, mid_spread.at[0], mid_spread.at[1])
    mid_total.start()
    qkv_sum.third(qkv_x, qkv_y)
    qkv_total = PlaneSpread(qkv_x, qkv_y, qkv_land, qkv_spread.at[0], qkv_spread.at[1])
    qkv_total.start()

    landed(land_full.at[0, second], ring_send, ring_recv, 2)
    landed(land_full.at[1, first], ring_send, ring_recv, 3)
    landed(land_full.at[0, first], ring_send, ring_recv, 4)
    landed(land_full.at[1, second], ring_send, ring_recv, 5)
    grad_one += added(land_full[0], land_full[1])
    normed_one, inverse_one = norm_parts(tokens_ref[...].astype(jnp.float32))
    tokens_grad_ref[...] = grad_residual[...] + norm_back(
        grad_one * gain_ref[...], normed_one, inverse_one
    )

    left, right = big_total.total()
    in_sum_ref[:, : FF // 2] = left
    in_sum_ref[:, FF // 2 :] = right
    mid_left, mid_right = mid_total.total()
    qkv_left, qkv_right = qkv_total.total()
    share = CAPACITY // 8
    line = jnp.concatenate([mid_left, mid_right, qkv_left, qkv_right], axis=1)
    for piece in range(8):
        rows = slice(piece * share, (piece + 1) * share)
        dense_send[piece] = jnp.concatenate(
            [line[rows, :LINE], line[rows, LINE:], jnp.zeros((16 - 2 * share, LINE), jnp.float32)],
            axis=0,
        ).astype(jnp.bfloat16)
    dense_copies = []
    for step in range(1, 8):
        place = lax.rem(mine + step, 8)
        copy = push(
            dense_send.at[place],
            dense_land.at[mine],
            dense_sems.at[0],
            dense_sems.at[1],
            step - 1,
            step - 1,
            (lax.axis_index("dp"), place),
        )
        copy.start()
        dense_copies.append(copy)
    dense_land[mine] = dense_send[mine]
    for step in range(1, 8):
        landed(
            dense_land.at[lax.rem(mine + 8 - step, 8)],
            dense_sems.at[0],
            dense_sems.at[1],
            step - 1,
        )
    lines = [dense_land[place].astype(jnp.float32) for place in range(8)]
    total = sum(lines[1:], lines[0])
    total = jnp.concatenate([total[:share], total[share : 2 * share]], axis=1)
    dense_sum_ref[...] = total[:, :DENSE]
    qkv_sum_ref[...] = jnp.zeros_like(qkv_sum_ref)
    for chip in range(CHIPS):
        line = lines[2 * chip] + lines[2 * chip + 1]
        line = jnp.concatenate([line[:share], line[share : 2 * share]], axis=1)[:, DENSE:]
        for part in range(3):
            start = part * WIDTH + (chip + chip // 2) * 128
            qkv_sum_ref[:, start : start + PAD] += line[:, part * PAD : (part + 1) * PAD]
    for copy in dense_copies + copies:
        copy.wait_send()
    for user in (big_sum, big_total, mid_sum, mid_total, qkv_sum, qkv_total):
        user.drain()
    for index in range(CHIPS):
        sib_copy(index).wait_send()

    @pl.loop(0, CHIPS)
    def _(chip):
        @pl.when((chip != z) | (owner_core != core))
        def _():
            push(
                grad_sent.at[chip],
                grad_out.at[chip],
                grad_send,
                grad_recv,
                chip,
                chip,
                device(z, 1 - core),
            ).wait_send()


def plane_scratch(lanes):
    return [
        pltpu.VMEM((4, 4, CAPACITY, lanes), HALF_TYPE),
        pltpu.VMEM((4, 2, CAPACITY, lanes // 2), HALF_TYPE),
        pltpu.VMEM((4, 4, CAPACITY, lanes // 2), HALF_TYPE),
        pltpu.VMEM((4, CAPACITY, lanes // 2), HALF_TYPE),
        pltpu.VMEM((4, CAPACITY, lanes // 2), HALF_TYPE),
        pltpu.VMEM((6, CAPACITY, lanes // 2), HALF_TYPE),
    ]


def back(*operands):
    def shape(*dims, dtype=FULL_TYPE):
        return jax.ShapeDtypeStruct(dims, dtype)

    def pair(count):
        return pltpu.SemaphoreType.DMA((2, count))

    return pl.pallas_call(
        back_kernel,
        out_shape=[
            shape(BLOCK, WIDTH, dtype=HALF_TYPE),
            shape(BLOCK, WIDTH),
            shape(CAPACITY, FF),
            shape(CAPACITY // 8, DENSE),
            shape(CAPACITY // 8, 3 * WIDTH),
        ],
        in_specs=[smem()] + [vmem()] * 12 + [anywhere()] * 8,
        out_specs=[vmem()] * 5,
        scratch_shapes=[
            pltpu.VMEM((8, 16, LINE), HALF_TYPE),
            pltpu.VMEM((8, BLOCK, PAD), HALF_TYPE),
            pltpu.VMEM((LONG, PAD), HALF_TYPE),
            pltpu.VMEM((LONG, PAD), HALF_TYPE),
            pltpu.VMEM((CHIPS, BLOCK, PAD), HALF_TYPE),
            pltpu.VMEM((WIDTH, 3 * PAD), HALF_TYPE),
            pltpu.VMEM((LONG, WIDTH), HALF_TYPE),
            pltpu.VMEM((CHIPS, BLOCK, PAD), HALF_TYPE),
            pltpu.VMEM((BLOCK, WIDTH), FULL_TYPE),
            pltpu.VMEM((CHIPS, BLOCK, PAD), HALF_TYPE),
            pltpu.VMEM((CHIPS, BLOCK, PAD), HALF_TYPE),
            pltpu.VMEM((STACK, PAD), HALF_TYPE),
            pltpu.VMEM((STACK, PAD), HALF_TYPE),
            pltpu.VMEM((STACK, PAD), FULL_TYPE),
            pltpu.VMEM((LONG, PAD), FULL_TYPE),
            pltpu.VMEM((LONG, PAD), FULL_TYPE),
            pltpu.VMEM((LONG, 3 * PAD), HALF_TYPE),
            pltpu.VMEM((CHIPS, BLOCK, WIDTH), HALF_TYPE),
            pltpu.VMEM((CHIPS - 1, BLOCK, WIDTH), HALF_TYPE),
            pltpu.VMEM((CHIPS, BLOCK, WIDTH), HALF_TYPE),
            pltpu.VMEM((2, HALF, WIDTH), HALF_TYPE),
            pltpu.VMEM((2, BLOCK, WIDTH), HALF_TYPE),
            *plane_scratch(FF),
            *plane_scratch(DENSE),
            *plane_scratch(3 * PAD),
            pltpu.VMEM((8, 16, LINE), HALF_TYPE),
            pltpu.SemaphoreType.DMA((3,)),
            pltpu.SemaphoreType.DMA((7,)),
            pair(CHIPS),
            pair(CHIPS),
            pair(6),
            pair(12),
            pair(6),
            pair(12),
            pair(6),
            pair(12),
            pair(6),
            pair(7),
        ],
        compiler_params=pltpu.CompilerParams(
            collective_id=1, has_side_effects=True, vmem_limit_bytes=60 * 2**20
        ),
    )(*operands)


def finish_kernel(
    mixed_ref,
    tokens_grad_ref,
    in_sum_ref,
    out_sum_ref,
    dense_ref,
    qkv_ref,
    weight_ref,
    gain_ref,
    mixed_out,
    tokens_grad_out,
    gain_out,
    qkv_out,
    proj_out,
    gain_two_out,
    router_out,
    in_out,
    out_out,
):
    mixed_out[0] = mixed_ref[...]
    tokens_grad_out[0] = tokens_grad_ref[...]
    in_out[0] = in_sum_ref[...]
    for part in range(4):
        rows = slice(part * CAPACITY, (part + 1) * CAPACITY)
        out_out[0, rows, :] = out_sum_ref[:, part * WIDTH : (part + 1) * WIDTH]
    dense = dense_ref[...]
    qkv_out[...] = qkv_ref[...]
    proj_out[...] = dense[:, :WIDTH]
    router_out[...] = dense[:, WIDTH : WIDTH + EXPERTS]
    gain_two_out[...] = dense[:, WIDTH + EXPERTS : WIDTH + EXPERTS + 1]
    products = qkv_ref[...] * weight_ref[...].astype(jnp.float32)
    gain_out[...] = jnp.sum(products, axis=1, keepdims=True) / gain_ref[...]


def finish(*operands):
    def shape(*dims, dtype=FULL_TYPE):
        return jax.ShapeDtypeStruct(dims, dtype)

    share = CAPACITY // 8
    shapes = [
        shape(1, BLOCK, WIDTH, dtype=HALF_TYPE),
        shape(1, BLOCK, WIDTH),
        shape(share, 1),
        shape(share, 3 * WIDTH),
        shape(share, WIDTH),
        shape(share, 1),
        shape(share, EXPERTS),
        shape(1, CAPACITY, FF),
        shape(1, 4 * CAPACITY, WIDTH),
    ]
    return pl.pallas_call(
        finish_kernel,
        out_shape=shapes,
        in_specs=[vmem()] * 8,
        out_specs=[vmem()] * 9,
        compiler_params=pltpu.CompilerParams(vmem_limit_bytes=32 * 2**20),
    )(*operands)


def on_device(
    tokens,
    group_kind,
    routes,
    norm1_gain,
    qkv_weight,
    proj_weight,
    norm2_gain,
    router_weight,
    frozen_in,
    frozen_out,
    new_in,
    new_out,
    out_grad,
):
    width = WIDTH
    gain_one, gain_two = norm1_gain[None], norm2_gain[None]
    router = router_weight.T
    (
        hidden,
        queries,
        keys,
        values,
        heads,
        all_grads,
        totals,
        attended,
        residual,
        hidden_two,
        sent,
        info,
    ) = front(
        group_kind,
        tokens[0],
        gain_one,
        qkv_weight,
        out_grad[0],
        routes[0].T,
        proj_weight,
        gain_two,
        router,
    )
    returned, grad_back, in_grad, out_sum = experts_both_ways(
        sent, info, all_grads, frozen_in[0], frozen_out[0], new_in[0], new_out[0]
    )
    mixed, tokens_grad, in_sum, dense_sum, qkv_sum = back(
        group_kind,
        tokens[0],
        gain_one,
        gain_two,
        out_grad[0],
        residual,
        info,
        returned,
        grad_back,
        router,
        proj_weight,
        hidden_two,
        totals,
        queries,
        keys,
        values,
        heads,
        qkv_weight,
        hidden.reshape(LONG, width),
        attended,
        in_grad,
    )
    own = width // (lax.axis_size("dp") * lax.axis_size("expert"))
    first_row = (lax.axis_index("dp") * lax.axis_size("expert") + lax.axis_index("expert")) * own
    own_weight = lax.dynamic_slice_in_dim(qkv_weight, first_row, own, axis=0)
    own_gain = lax.dynamic_slice_in_dim(norm1_gain, first_row, own, axis=0)
    outputs = finish(
        mixed, tokens_grad, in_sum, out_sum, dense_sum, qkv_sum, own_weight, own_gain[:, None]
    )
    return tuple(
        value[:, 0] if index in (2, 5) else value for index, value in enumerate(outputs)
    )


def solution(mesh):
    return jax.shard_map(
        on_device,
        mesh=mesh,
        in_specs=(
            P("dp", "expert", None),
            P("dp"),
            P("dp", "expert", None),
            P(),
            P(),
            P(),
            P(),
            P(),
            P("expert", None, None),
            P("expert", None, None),
            P("expert", None, None),
            P("expert", None, None),
            P("dp", "expert", None),
        ),
        out_specs=(
            P("dp", "expert", None),
            P("dp", "expert", None),
            P(("dp", "expert")),
            P(("dp", "expert"), None),
            P(("dp", "expert"), None),
            P(("dp", "expert")),
            P(("dp", "expert"), None),
            P("expert", "dp", None),
            P("expert", "dp", None),
        ),
        check_vma=False,
    )
```

```python
import jax
import jax.numpy as jnp
from jax import lax
from jax.experimental import pallas as pl
from jax.experimental.pallas import tpu as pltpu
from jax.sharding import PartitionSpec as P

HEADS = 12
HD = 64
LONG = 2048
MESH_ID = pl.DeviceIdType.MESH
CHIPS = 4
PAD = 256
BLOCK = 256
HALF = BLOCK // 2
CHUNK = 512
CHUNKS = LONG // CHUNK
LOCAL_HEADS = HEADS // CHIPS
STACK = LOCAL_HEADS * BLOCK
NEGATIVE = -1e30
WIDTH = 768
EXPERTS = 16
SLOTS = 768
EXPERT_ROWS = 384
CAPACITY = 48
FF = 3072
FF_TILE = 768
FF_TILES = 4
DENSE = 1024
LINE = (DENSE + 3 * PAD) // 2
HALF_TYPE = jnp.bfloat16
FULL_TYPE = jnp.float32

epsilon = 1e-05


def norm_parts(values):
    average = jnp.mean(values, axis=-1, keepdims=True)
    centred = values - average
    variance = jnp.mean(centred * centred, axis=-1, keepdims=True)
    inverse = lax.rsqrt(variance + epsilon)
    return (centred * inverse, inverse)


def norm_back(grad_normed, normed, inverse):
    first_mean = jnp.mean(grad_normed, axis=-1, keepdims=True)
    second_mean = jnp.mean(grad_normed * normed, axis=-1, keepdims=True)
    return inverse * (grad_normed - first_mean - normed * second_mean)


def here():
    position = lax.axis_index("expert")
    return position // 2, lax.rem(position, 2)


def device(z, core):
    return (lax.axis_index("dp"), z * 2 + core)


def greet(barrier):
    position = lax.axis_index("expert")
    for step in range(1, 8):
        pl.semaphore_signal(
            barrier,
            inc=1,
            device_id=(lax.axis_index("dp"), lax.rem(position + step, 8)),
            device_id_type=MESH_ID,
        )


def push(source, target, sends, receives, index_here, index_there, where):
    return pltpu.make_async_remote_copy(
        src_ref=source,
        dst_ref=target,
        send_sem=sends.at[index_here],
        recv_sem=receives.at[index_there],
        device_id=where,
        device_id_type=MESH_ID,
    )


def landed(region, sends, receives, index):
    z, core = here()
    push(region, region, sends, receives, index, index, device(z, 1 - core)).wait_recv()


def dot_nn(left, right):
    return jnp.dot(left, right, preferred_element_type=jnp.float32)


def dot_nt(left, right):
    return lax.dot_general(
        left, right, (((1,), (1,)), ((), ())), preferred_element_type=jnp.float32
    )


def dot_tn(left, right):
    return lax.dot_general(
        left, right, (((0,), (0,)), ((), ())), preferred_element_type=jnp.float32
    )


def window(chip):
    return (chip + chip // 2) * 128, lax.rem(chip, 2) * HD


def head_mask(chip, head, value, dtype):
    start = window(chip)[1] + head * HD
    lanes = lax.broadcasted_iota(jnp.int32, (1, PAD), 1)
    inside = (lanes >= start) & (lanes < start + HD)
    return jnp.where(inside, value, 0.0).astype(dtype)


def lane_tiles(values, combine):
    result = values[:, :128]
    for start in range(128, values.shape[1], 128):
        result = combine(result, values[:, start : start + 128])
    return result


def block_rows(block):
    return pl.ds(pl.multiple_of(block * BLOCK, BLOCK), BLOCK)


def chunk_rows(chunk):
    return pl.ds(pl.multiple_of(chunk * CHUNK, CHUNK), CHUNK)


def load_windows(weight_ref, target, sems, chip):
    copies = []
    for part in range(3):
        first = pl.multiple_of(part * WIDTH + window(chip)[0], 128)
        copies.append(
            pltpu.make_async_copy(
                weight_ref.at[:, pl.ds(first, PAD)],
                target.at[:, pl.ds(part * PAD, PAD)],
                sems.at[part],
            )
        )
    for copy in copies:
        copy.start()
    return copies


class RingGather:
    def __init__(self, ref, sends, receives):
        self.ref, self.sends, self.receives = ref, sends, receives
        self.z, self.core = here()
        self.up, self.down = lax.rem(self.z + 1, CHIPS), lax.rem(self.z + 3, CHIPS)
        self.far = lax.rem(self.z + 2, CHIPS)
        self.copies = []

    def region(self, chip, core, half):
        rows = slice(None) if half is None else pl.ds(half * HALF, HALF)
        return self.ref.at[chip * 2 + core, rows]

    def send(self, index, chip, half, where):
        region = self.region(chip, self.core, half)
        copy = push(region, region, self.sends, self.receives, index, index, where)
        copy.start()
        self.copies.append(copy)

    def wait(self, index, chip, core, half):
        landed(self.region(chip, core, half), self.sends, self.receives, index)

    def above(self):
        return device(self.up, self.core)

    def below(self):
        return device(self.down, self.core)

    def beside(self):
        return device(self.z, 1 - self.core)

    def start(self):
        self.send(0, self.z, 0, self.above())
        self.send(1, self.z, 1, self.below())
        self.send(2, self.z, 1, self.above())
        self.send(3, self.z, 0, self.below())
        self.send(4, self.z, None, self.beside())

    def relay(self):
        self.wait(0, self.down, self.core, 0)
        self.send(5, self.down, 0, self.above())
        self.send(7, self.down, 0, self.beside())
        self.wait(1, self.up, self.core, 1)
        self.send(6, self.up, 1, self.below())
        self.send(8, self.up, 1, self.beside())

    def share(self):
        self.wait(2, self.down, self.core, 1)
        self.send(9, self.down, 1, self.beside())
        self.wait(3, self.up, self.core, 0)
        self.send(10, self.up, 0, self.beside())

    def share_far(self):
        self.wait(5, self.far, self.core, 0)
        self.send(11, self.far, 0, self.beside())
        self.wait(6, self.far, self.core, 1)
        self.send(12, self.far, 1, self.beside())

    def other_own(self):
        self.wait(4, self.z, 1 - self.core, None)

    def other_down(self):
        self.wait(7, self.down, 1 - self.core, 0)
        self.wait(9, self.down, 1 - self.core, 1)

    def other_up(self):
        self.wait(8, self.up, 1 - self.core, 1)
        self.wait(10, self.up, 1 - self.core, 0)

    def other_far(self):
        self.wait(11, self.far, 1 - self.core, 0)
        self.wait(12, self.far, 1 - self.core, 1)

    def drain(self):
        for copy in self.copies:
            copy.wait_send()


def plane_device(x, y):
    return (x * 4 + y, lax.axis_index("expert"))


def plane_here():
    group = lax.axis_index("dp")
    return group // 4, lax.rem(group, 4)


def added(left, right):
    return left.astype(jnp.float32) + right.astype(jnp.float32)


class PlaneSum:
    def __init__(self, source, first, direct, combined, sends, receives):
        self.source, self.first = source, first
        self.direct, self.combined = direct, combined
        self.sends, self.receives = sends, receives
        self.x, self.y = plane_here()
        half = source.shape[-1] // 2
        self.left, self.right = pl.ds(0, half), pl.ds(half, half)
        self.low, self.high = pl.ds(0, 2), pl.ds(2, 2)
        self.copies = []

    def x_part(self, x, part):
        return self.source.at[x, part, :, self.left]

    def y_part(self, y, part):
        return self.source.at[part, y, :, self.right]

    def sides(self):
        return (
            (0, self.x, self.x_part, lambda p: plane_device(p, self.y)),
            (2, self.y, self.y_part, lambda p: plane_device(self.x, p)),
        )

    def send(self, source, target, index, where):
        copy = push(source, target, self.sends, self.receives, index, index, where)
        copy.start()
        self.copies.append(copy)

    def wait(self, region, index):
        landed(region, self.sends, self.receives, index)

    def neighbours(self, place):
        return lax.rem(place + 1, 4), lax.rem(place + 3, 4), lax.rem(place + 2, 4)

    def start_far(self):
        for base, place, part, where in self.sides():
            up, down, far = self.neighbours(place)
            self.send(part(far, self.low), self.first.at[base], base, where(up))
            self.send(part(far, self.high), self.first.at[base + 1], base + 1, where(down))

    def start_near(self):
        for base, place, part, where in self.sides():
            up, down, _ = self.neighbours(place)
            self.send(part(up, self.high), self.direct.at[base], base + 4, where(up))
            self.send(part(down, self.low), self.direct.at[base + 1], base + 5, where(down))

    def start(self):
        self.start_far()
        self.start_near()

    def settle_far(self):
        for index in range(4):
            self.wait(self.first.at[index], index)

    def second(self, waits=True):
        low, high = self.low, self.high
        for base, place, part, where in self.sides():
            up, down, _ = self.neighbours(place)
            for index, chosen, to in (
                (base, part(up, low), up),
                (base + 1, part(down, high), down),
            ):
                if waits:
                    self.wait(self.first.at[index], index)
                chosen[...] = added(chosen[...], self.first[index]).astype(jnp.bfloat16)
                self.send(chosen, self.combined.at[index], index + 8, where(to))

    def third(self, x_sum, y_sum):
        low, high = self.low, self.high
        for base, place, part, total in (
            (0, self.x, self.x_part, x_sum),
            (2, self.y, self.y_part, y_sum),
        ):
            self.wait(self.direct.at[base], base + 4)
            self.wait(self.direct.at[base + 1], base + 5)
            self.wait(self.combined.at[base], base + 8)
            self.wait(self.combined.at[base + 1], base + 9)
            total[low] = (
                added(part(place, low)[...], self.combined[base])
                + self.direct[base + 1].astype(jnp.float32)
            ).astype(jnp.bfloat16)
            total[high] = (
                added(part(place, high)[...], self.direct[base])
                + self.combined[base + 1].astype(jnp.float32)
            ).astype(jnp.bfloat16)

    def drain(self):
        for copy in self.copies:
            copy.wait_send()


class PlaneSpread:
    def __init__(self, x_sum, y_sum, land, sends, receives):
        self.x_sum, self.y_sum, self.land = x_sum, y_sum, land
        self.sends, self.receives = sends, receives
        self.x, self.y = plane_here()
        self.copies = []

    def start(self):
        for step in range(1, 4):
            y, x = lax.rem(self.y + step, 4), lax.rem(self.x + step, 4)
            for index, source, where in (
                (step - 1, self.x_sum.at[y], plane_device(self.x, y)),
                (step + 2, self.y_sum.at[x], plane_device(x, self.y)),
            ):
                copy = push(
                    source, self.land.at[index], self.sends, self.receives, index, index, where
                )
                copy.start()
                self.copies.append(copy)

    def total(self):
        sums = []
        for base, mine in ((0, self.x_sum[self.y]), (3, self.y_sum[self.x])):
            value = mine.astype(jnp.float32)
            for index in range(base, base + 3):
                landed(self.land.at[index], self.sends, self.receives, index)
                value += self.land[index].astype(jnp.float32)
            sums.append(value)
        return sums

    def drain(self):
        for copy in self.copies:
            copy.wait_send()


def greet_plane(barrier):
    x, y = plane_here()
    for step in range(1, 4):
        for where in (plane_device(lax.rem(x + step, 4), y), plane_device(x, lax.rem(y + step, 4))):
            pl.semaphore_signal(barrier, inc=1, device_id=where, device_id_type=MESH_ID)


def gelu_parts(u):
    scaled = jnp.abs(u) * 0.7071067811865476
    t = 1.0 / (1.0 + 0.3275911 * scaled)
    poly = t * (
        0.127414796
        + t * (-0.142248368 + t * (0.7107068705 + t * (-0.7265760135 + t * 0.5307027145)))
    )
    density = jnp.exp(-0.5 * u * u)
    tail = poly * density
    cumulative = jnp.where(u >= 0, 1.0 - tail, tail)
    return u * cumulative, cumulative + u * density * 0.3989422804014327


def vmem():
    return pl.BlockSpec(memory_space=pltpu.VMEM)


def smem():
    return pl.BlockSpec(memory_space=pltpu.SMEM)


def anywhere():
    return pl.BlockSpec(memory_space=pl.ANY)


def front_kernel(
    kind_ref,
    tokens_ref,
    gain_ref,
    weight_ref,
    grad_ref,
    routes_ref,
    proj_ref,
    gain_two_ref,
    router_ref,
    hidden_out,
    query_out,
    key_out,
    value_out,
    heads_out,
    total_ref,
    attended_ref,
    residual_ref,
    hidden_two_ref,
    sent_ref,
    grad_rows_ref,
    info_ref,
    hidden_ref,
    query_ref,
    key_ref,
    value_ref,
    out_ref,
    weight,
    stacked,
    diagonal,
    beside,
    scores,
    largest,
    sums,
    acc,
    gather_sems,
    out_sems,
    weight_sems,
    store_sems,
):
    z, core = here()
    mine = z * 2 + core
    up, down, far = lax.rem(z + 1, CHIPS), lax.rem(z + 3, CHIPS), lax.rem(z + 2, CHIPS)
    barrier = pltpu.get_barrier_semaphore()
    greet(barrier)
    loads = load_windows(weight_ref, weight, weight_sems, z)
    tokens = tokens_ref[...].astype(jnp.float32)
    normed, _ = norm_parts(tokens)
    hidden_ref[mine] = (normed * gain_ref[...][None]).astype(jnp.bfloat16)
    pl.semaphore_wait(barrier, 7)
    gather = RingGather(hidden_ref, gather_sems.at[0], gather_sems.at[1])
    stores = []

    def store(source, target):
        copy = pltpu.make_async_copy(source, target, store_sems.at[len(stores)])
        copy.start()
        stores.append(copy)

    def project(block):
        projected = dot_nn(hidden_ref[block], weight[...]).astype(jnp.bfloat16)
        query_ref[block] = projected[:, :PAD]
        key_ref[block_rows(block), :] = projected[:, PAD : 2 * PAD]
        value_ref[block_rows(block), :] = projected[:, 2 * PAD :]

    gather.start()
    for load in loads:
        load.wait()
    project(mine)
    routes = routes_ref[...].astype(jnp.float32)
    names = lax.broadcasted_iota(jnp.int32, (EXPERTS, BLOCK), 0).astype(jnp.float32)
    pick_zero = jnp.where(names == routes[0:1, :], 1.0, 0.0)
    pick_one = jnp.where(names == routes[1:2, :], 1.0, 0.0)
    row = lax.broadcasted_iota(jnp.int32, (BLOCK, BLOCK), 0)
    column = lax.broadcasted_iota(jnp.int32, (BLOCK, BLOCK), 1)
    before = jnp.where(row < column, 1.0, 0.0).astype(jnp.bfloat16)
    earlier = dot_nn((pick_zero + pick_one).astype(jnp.bfloat16), before)
    places = []
    for index, pick in enumerate((pick_zero, pick_one)):
        slot = jnp.sum(earlier * pick, axis=0, keepdims=True)
        place = routes[index : index + 1, :] * CAPACITY + slot
        places.append(jnp.where(slot < CAPACITY, place, -1.0))
    gather.relay()
    gather.other_own()
    project(z * 2 + 1 - core)
    gather.share()
    project(down * 2 + core)
    project(up * 2 + core)
    gather.share_far()
    project(far * 2 + core)
    gather.other_down()
    project(down * 2 + 1 - core)
    gather.other_up()
    project(up * 2 + 1 - core)
    gather.other_far()
    project(far * 2 + 1 - core)
    store(hidden_ref, hidden_out)
    store(query_ref, query_out)
    store(key_ref, key_out)
    store(value_ref, value_out)

    kind_bias = kind_ref[0].astype(jnp.float32) * NEGATIVE
    out_send, out_recv = out_sems.at[0], out_sems.at[1]

    def attend(step):
        slot = lax.rem(z + step, CHIPS)
        block = slot * 2 + lax.rem(core + slot, 2)
        queries = query_ref[block]
        for head in range(LOCAL_HEADS):
            stacked[head * BLOCK : (head + 1) * BLOCK, :] = queries * head_mask(
                z, head, HD ** (-0.5), jnp.bfloat16
            )

        def bias_of(chunk):
            return jnp.where((slot >= 2) & (chunk < 2), kind_bias, 0.0)

        masked = dot_nt(stacked[...], key_ref[block_rows(block), :])
        row = lax.broadcasted_iota(jnp.int32, (BLOCK, BLOCK), 0)
        column = lax.broadcasted_iota(jnp.int32, (BLOCK, BLOCK), 1)
        for head in range(LOCAL_HEADS):
            part = slice(head * BLOCK, (head + 1) * BLOCK)
            values = jnp.where(column <= row, masked[part], NEGATIVE)
            diagonal[part, :] = values
            largest[part, :] = lane_tiles(values, jnp.maximum)
        is_odd = block != 2 * slot

        @pl.when(is_odd)
        def _():
            values = dot_nt(stacked[...], key_ref[block_rows(block - 1), :])
            beside[...] = values
            largest[...] = jnp.maximum(largest[...], lane_tiles(values, jnp.maximum))

        @pl.loop(0, slot)
        def _(chunk):
            values = dot_nt(stacked[...], key_ref[chunk_rows(chunk), :])
            scores[chunk] = values
            largest[...] = jnp.maximum(
                largest[...], lane_tiles(values, jnp.maximum) + bias_of(chunk)
            )

        row_max = jnp.max(largest[...], axis=1, keepdims=True)
        largest[...] = jnp.broadcast_to(row_max, largest.shape)
        exponent = jnp.exp(diagonal[...] - row_max)
        sums[...] = lane_tiles(exponent, jnp.add)
        acc[...] = dot_nn(exponent.astype(jnp.bfloat16), value_ref[block_rows(block), :])

        @pl.when(is_odd)
        def _():
            exponent = jnp.exp(beside[...] - largest[:, :1])
            sums[...] += lane_tiles(exponent, jnp.add)
            acc[...] += dot_nn(exponent.astype(jnp.bfloat16), value_ref[block_rows(block - 1), :])

        @pl.loop(0, slot)
        def _(chunk):
            exponent = jnp.exp(scores[chunk] - (largest[:, :1] - bias_of(chunk)))
            sums[...] += lane_tiles(exponent, jnp.add)
            acc[...] += dot_nn(exponent.astype(jnp.bfloat16), value_ref[chunk_rows(chunk), :])

        total = jnp.sum(sums[...], axis=1, keepdims=True)
        inverse = 1.0 / total
        log_total = largest[...] + jnp.log(total)
        attended = jnp.zeros((BLOCK, PAD), jnp.float32)
        for head in range(LOCAL_HEADS):
            part = slice(head * BLOCK, (head + 1) * BLOCK)
            attended += acc[part, :] * inverse[part] * head_mask(z, head, 1.0, jnp.float32)
            total_ref[slot, head : head + 1, :] = jnp.transpose(log_total[part, :])[:1, :]
        out_ref[slot] = attended.astype(jnp.bfloat16)

        @pl.when(block != mine)
        def _():
            push(
                out_ref.at[slot],
                attended_ref.at[z],
                out_send,
                out_recv,
                slot,
                z,
                device(slot, lax.rem(core + slot, 2)),
            ).start()

        @pl.when(block == mine)
        def _():
            attended_ref[z] = out_ref[slot]

    pl.loop(0, CHIPS)(attend)
    store(out_ref, heads_out)

    @pl.loop(0, CHIPS)
    def _(slot):
        @pl.when((slot != z) | (lax.rem(core + z, 2) != core))
        def _():
            landed(attended_ref.at[slot], out_send, out_recv, slot)

    residual = tokens_ref[...].astype(jnp.float32)
    for chip in range(CHIPS):
        first = (chip + chip // 2) * 128
        residual += dot_nn(attended_ref[chip], proj_ref[first : first + PAD, :])
    residual_ref[...] = residual
    normed_two, _ = norm_parts(residual)
    hidden_two = (normed_two * gain_two_ref[...][None]).astype(jnp.bfloat16)
    hidden_two_ref[...] = hidden_two
    logits = dot_nt(router_ref[...], hidden_two)
    logit_zero = jnp.sum(logits * pick_zero, axis=0, keepdims=True)
    logit_one = jnp.sum(logits * pick_one, axis=0, keepdims=True)
    gate_zero = 1.0 / (1.0 + jnp.exp(logit_one - logit_zero))
    gate_one = 1.0 / (1.0 + jnp.exp(logit_zero - logit_one))
    for index, line in enumerate((*places, gate_zero, gate_one, routes[0:1], routes[1:2])):
        info_ref[index : index + 1, :] = line
    info_ref[6:8, :] = jnp.zeros((2, BLOCK), jnp.float32)
    ids = lax.broadcasted_iota(jnp.int32, (SLOTS, BLOCK), 0).astype(jnp.float32)
    chosen = jnp.where((ids == places[0]) | (ids == places[1]), 1.0, 0.0).astype(jnp.bfloat16)
    sent = dot_nn(chosen, hidden_two).astype(jnp.bfloat16)
    sent_ref[0] = sent[:EXPERT_ROWS]
    sent_ref[1] = sent[EXPERT_ROWS:]
    mixing = (
        jnp.where(ids == places[0], gate_zero, 0.0) + jnp.where(ids == places[1], gate_one, 0.0)
    ).astype(jnp.bfloat16)
    rows = dot_nn(mixing, grad_ref[...]).astype(jnp.bfloat16)
    grad_rows_ref[0] = rows[:EXPERT_ROWS]
    grad_rows_ref[1] = rows[EXPERT_ROWS:]
    gather.drain()

    @pl.loop(0, CHIPS)
    def _(slot):
        @pl.when(slot * 2 + lax.rem(core + slot, 2) != mine)
        def _():
            push(
                out_ref.at[slot],
                attended_ref.at[slot],
                out_send,
                out_recv,
                slot,
                slot,
                device(z, 1 - core),
            ).wait_send()

    for copy in stores:
        copy.wait()


def front(kind, tokens, gain, weight, grads, routes, proj, gain_two, router):
    def shape(*dims, dtype=HALF_TYPE):
        return jax.ShapeDtypeStruct(dims, dtype)

    shapes = [
        shape(8, BLOCK, WIDTH),
        shape(8, BLOCK, PAD),
        shape(LONG, PAD),
        shape(LONG, PAD),
        shape(CHIPS, BLOCK, PAD),
        shape(CHIPS, 8, BLOCK, dtype=FULL_TYPE),
        shape(CHIPS, BLOCK, PAD),
        shape(BLOCK, WIDTH, dtype=FULL_TYPE),
        shape(BLOCK, WIDTH),
        shape(2, EXPERT_ROWS, WIDTH),
        shape(2, EXPERT_ROWS, WIDTH),
        shape(8, BLOCK, dtype=FULL_TYPE),
    ]
    return pl.pallas_call(
        front_kernel,
        out_shape=shapes,
        in_specs=[smem(), vmem(), vmem(), anywhere()] + [vmem()] * 5,
        out_specs=[anywhere()] * 5 + [vmem()] * 7,
        scratch_shapes=[
            pltpu.VMEM((8, BLOCK, WIDTH), HALF_TYPE),
            pltpu.VMEM((8, BLOCK, PAD), HALF_TYPE),
            pltpu.VMEM((LONG, PAD), HALF_TYPE),
            pltpu.VMEM((LONG, PAD), HALF_TYPE),
            pltpu.VMEM((CHIPS, BLOCK, PAD), HALF_TYPE),
            pltpu.VMEM((WIDTH, 3 * PAD), HALF_TYPE),
            pltpu.VMEM((STACK, PAD), HALF_TYPE),
            pltpu.VMEM((STACK, BLOCK), FULL_TYPE),
            pltpu.VMEM((STACK, BLOCK), FULL_TYPE),
            pltpu.VMEM((CHUNKS - 1, STACK, CHUNK), FULL_TYPE),
            pltpu.VMEM((STACK, 128), FULL_TYPE),
            pltpu.VMEM((STACK, 128), FULL_TYPE),
            pltpu.VMEM((STACK, PAD), FULL_TYPE),
            pltpu.SemaphoreType.DMA((2, 13)),
            pltpu.SemaphoreType.DMA((2, CHIPS)),
            pltpu.SemaphoreType.DMA((3,)),
            pltpu.SemaphoreType.DMA((5,)),
        ],
        compiler_params=pltpu.CompilerParams(
            collective_id=0, has_side_effects=True, vmem_limit_bytes=56 * 2**20
        ),
    )(kind, tokens, gain, weight, grads, routes, proj, gain_two, router)


def expert_kernel(
    sent_ref,
    grad_rows_ref,
    in_frozen,
    out_frozen,
    in_new,
    out_new,
    returned_ref,
    in_grad_ref,
    in_first_ref,
    grad_back_ref,
    match_ref,
    x_sum_ref,
    y_sum_ref,
    w_in,
    w_out,
    x_land,
    g_land,
    activated,
    slope,
    acc,
    r_send,
    b_send,
    in_grad,
    out_grad,
    first,
    direct,
    combined,
    in_first,
    match_send,
    load_sems,
    x_sems,
    g_sems,
    b_sems,
    match_sems,
    plane_sems,
    in_sems,
    store_sems,
):
    mine = lax.axis_index("expert")
    barrier = pltpu.get_barrier_semaphore()
    greet(barrier)
    greet_plane(barrier)
    loads = []
    for index, (source, target) in enumerate(
        (
            (in_new, w_in.at[1]),
            (out_new, w_out.at[1]),
            (in_frozen, w_in.at[0]),
            (out_frozen, w_out.at[0]),
        )
    ):
        copy = pltpu.make_async_copy(source, target, load_sems.at[index])
        copy.start()
        loads.append(copy)

    def rows_of(place):
        return pl.ds(pl.multiple_of(place * CAPACITY, CAPACITY), CAPACITY)

    own_rows = rows_of(mine)
    own_loads = []
    for index, (source, target) in enumerate(((sent_ref, x_land), (grad_rows_ref, g_land))):
        copy = pltpu.make_async_copy(
            source.at[:, own_rows, :], target.at[:, own_rows, :], load_sems.at[4 + index]
        )
        copy.start()
        own_loads.append(copy)
    pl.semaphore_wait(barrier, 13)

    def peer(step):
        return lax.rem(mine + step, 8)

    def exchange(source, target, sems, index, step):
        return push(
            source, target, sems.at[0], sems.at[1], index, index, (lax.axis_index("dp"), peer(step))
        )

    stores, used = [], []

    def store(source, target):
        copy = pltpu.make_async_copy(source, target, store_sems.at[len(stores)])
        copy.start()
        stores.append(copy)

    def seven(ref, sem):
        region = ref.at[0, pl.ds(0, 7 * CAPACITY), :]
        return pltpu.make_async_copy(region, region, sem)

    def spread_kind(kind, source, target, sems):
        for step in range(1, 8):
            exchange(
                source.at[kind, rows_of(peer(step)), :],
                target.at[kind, own_rows, :],
                sems,
                kind,
                step,
            ).start()
        used.append((target, sems.at[0, kind]))

    def collect_kind(kind, target, sems):
        seven(target, sems.at[1, kind]).wait()

    for kind in (1, 0):
        spread_kind(kind, sent_ref, x_land, x_sems)
        spread_kind(kind, grad_rows_ref, g_land, g_sems)
    for copy in own_loads:
        copy.wait()

    def tile_of(index):
        return pl.ds(pl.multiple_of(index * FF_TILE, FF_TILE), FF_TILE)

    plane = PlaneSum(out_grad, first, direct, combined, plane_sems.at[0], plane_sems.at[1])
    in_plane = PlaneSum(in_grad, in_first, None, None, in_sems.at[0], in_sems.at[1])
    matches = [None, None]
    for kind in (1, 0):
        collect_kind(kind, x_land, x_sems)
        loads[0 if kind == 1 else 2].wait()
        loads[1 if kind == 1 else 3].wait()
        acc[...] = jnp.zeros_like(acc)

        @pl.loop(0, FF_TILES, unroll=True)
        def _(index):
            tile = tile_of(index)
            pre = dot_nn(x_land[kind], w_in[kind, :, tile])
            value, steep = gelu_parts(pre)
            value = value.astype(jnp.bfloat16)
            if kind == 1:
                activated[:, tile] = value
            slope[:, tile] = steep.astype(jnp.bfloat16)
            acc[...] += dot_nn(value, w_out[kind, tile, :])

        collect_kind(kind, g_land, g_sems)
        result = acc[...].astype(jnp.bfloat16)
        r_send[kind] = result
        store(r_send.at[kind], returned_ref.at[kind])
        products = result.astype(jnp.float32) * g_land[kind].astype(jnp.float32)
        matches[kind] = jnp.sum(products, axis=1, keepdims=True)
        if kind == 1:

            @pl.loop(0, FF_TILES, unroll=True)
            def _(index):
                weights = dot_tn(activated[:, tile_of(index)], g_land[1]).astype(jnp.bfloat16)
                for y in range(4):
                    for part in range(4):
                        start = (y * 4 + part) * CAPACITY
                        out_grad[index, y, :, part * WIDTH : (part + 1) * WIDTH] = weights[
                            start : start + CAPACITY
                        ]

            plane.start()

        acc[...] = jnp.zeros_like(acc)

        @pl.loop(0, FF_TILES, unroll=True)
        def _(index):
            tile = tile_of(index)
            grad = dot_nt(g_land[kind], w_out[kind, tile, :])
            grad = (grad * slope[:, tile].astype(jnp.float32)).astype(jnp.bfloat16)
            acc[...] += dot_nt(grad, w_in[kind, :, tile])
            if kind == 1:
                activated[:, tile] = grad

        b_send[kind] = acc[...].astype(jnp.bfloat16)
        grad_back_ref[kind, own_rows, :] = b_send[kind, own_rows, :]
        spread_kind(kind, b_send, grad_back_ref, b_sems)
    lanes = lax.broadcasted_iota(jnp.int32, (EXPERT_ROWS, 128), 1)
    match_send[0] = jnp.where(lanes < 64, matches[0], matches[1])
    match_ref[0, own_rows, :] = match_send[0, own_rows, :]
    spread_kind(0, match_send, match_ref, match_sems)
    plane.second()

    @pl.loop(0, FF_TILES, unroll=True)
    def _(index):
        tile = tile_of(index)
        weights = dot_tn(x_land[1], activated[:, tile]).astype(jnp.bfloat16)
        in_grad[:, :, :, tile] = weights.reshape(4, 4, CAPACITY, FF_TILE)

    in_plane.start_far()
    store(in_grad, in_grad_ref)
    plane.third(x_sum_ref, y_sum_ref)
    collect_kind(0, match_ref, match_sems)
    for kind in (1, 0):
        collect_kind(kind, grad_back_ref, b_sems)
    in_plane.settle_far()
    store(in_first, in_first_ref)
    for target, sem in used:
        seven(target, sem).wait()
    plane.drain()
    in_plane.drain()
    for copy in stores:
        copy.wait()


def experts_both_ways(sent, grad_rows, in_frozen, out_frozen, in_new, out_new):
    def shape(*dims, dtype=HALF_TYPE):
        return jax.ShapeDtypeStruct(dims, dtype)

    return pl.pallas_call(
        expert_kernel,
        out_shape=[
            shape(2, EXPERT_ROWS, WIDTH),
            shape(4, 4, CAPACITY, FF),
            shape(4, 2, CAPACITY, FF // 2),
            shape(2, EXPERT_ROWS, WIDTH),
            shape(1, EXPERT_ROWS, 128, dtype=FULL_TYPE),
            shape(4, CAPACITY, FF // 2),
            shape(4, CAPACITY, FF // 2),
        ],
        in_specs=[anywhere()] * 6,
        out_specs=[anywhere()] * 3 + [vmem()] * 4,
        scratch_shapes=[
            pltpu.VMEM((2, WIDTH, FF), HALF_TYPE),
            pltpu.VMEM((2, FF, WIDTH), HALF_TYPE),
            pltpu.VMEM((2, EXPERT_ROWS, WIDTH), HALF_TYPE),
            pltpu.VMEM((2, EXPERT_ROWS, WIDTH), HALF_TYPE),
            pltpu.VMEM((EXPERT_ROWS, FF), HALF_TYPE),
            pltpu.VMEM((EXPERT_ROWS, FF), HALF_TYPE),
            pltpu.VMEM((EXPERT_ROWS, WIDTH), FULL_TYPE),
            pltpu.VMEM((2, EXPERT_ROWS, WIDTH), HALF_TYPE),
            pltpu.VMEM((2, EXPERT_ROWS, WIDTH), HALF_TYPE),
            pltpu.VMEM((4, 4, CAPACITY, FF), HALF_TYPE),
            pltpu.VMEM((4, 4, CAPACITY, FF), HALF_TYPE),
            pltpu.VMEM((4, 2, CAPACITY, FF // 2), HALF_TYPE),
            pltpu.VMEM((4, 2, CAPACITY, FF // 2), HALF_TYPE),
            pltpu.VMEM((4, 2, CAPACITY, FF // 2), HALF_TYPE),
            pltpu.VMEM((4, 2, CAPACITY, FF // 2), HALF_TYPE),
            pltpu.VMEM((1, EXPERT_ROWS, 128), FULL_TYPE),
            pltpu.SemaphoreType.DMA((6,)),
            pltpu.SemaphoreType.DMA((2, 2)),
            pltpu.SemaphoreType.DMA((2, 2)),
            pltpu.SemaphoreType.DMA((2, 2)),
            pltpu.SemaphoreType.DMA((2, 2)),
            pltpu.SemaphoreType.DMA((2, 12)),
            pltpu.SemaphoreType.DMA((2, 4)),
            pltpu.SemaphoreType.DMA((4,)),
        ],
        compiler_params=pltpu.CompilerParams(
            collective_id=2, has_side_effects=True, vmem_limit_bytes=62 * 2**20
        ),
    )(sent, grad_rows, in_frozen, out_frozen, in_new, out_new)


def slot_rows(place):
    return pl.ds(pl.multiple_of(place * CAPACITY, CAPACITY), CAPACITY)


def back_kernel(
    kind_ref,
    tokens_ref,
    gain_ref,
    gain_two_ref,
    grad_ref,
    residual_ref,
    info_ref,
    match_ref,
    grad_back_ref,
    router_ref,
    proj_ref,
    hidden_two_ref,
    total_ref,
    query_hbm,
    key_hbm,
    value_hbm,
    heads_hbm,
    weight_hbm,
    hidden_hbm,
    attended_hbm,
    in_grad_hbm,
    in_first_hbm,
    returned_hbm,
    x_part_hbm,
    y_part_hbm,
    mixed_ref,
    tokens_grad_ref,
    in_sum_ref,
    out_sum_ref,
    dense_sum_ref,
    qkv_sum_ref,
    dense_land,
    query_ref,
    key_ref,
    value_ref,
    heads_ref,
    weight,
    hidden_ref,
    attended_ref,
    x_part,
    y_part,
    out_land,
    returned,
    grad_residual,
    grad_sent,
    grad_out,
    stacked,
    grad_stacked,
    grad_query,
    grad_key,
    grad_value,
    projected,
    part_sib,
    part_own,
    land_sib,
    land_half,
    land_full,
    big,
    big_first,
    big_direct,
    big_combined,
    big_x,
    big_y,
    big_land,
    mid,
    mid_first,
    mid_direct,
    mid_combined,
    mid_x,
    mid_y,
    mid_land,
    qkv,
    qkv_first,
    qkv_direct,
    qkv_combined,
    qkv_x,
    qkv_y,
    qkv_land,
    dense_send,
    weight_sems,
    load_sems,
    grad_sems,
    sib_sems,
    ring_sems,
    big_sems,
    out_spread,
    big_spread,
    mid_sems,
    mid_spread,
    qkv_sems,
    qkv_spread,
    dense_sems,
    returned_sems,
):
    z, core = here()
    mine = z * 2 + core
    up, down, far = lax.rem(z + 1, CHIPS), lax.rem(z + 3, CHIPS), lax.rem(z + 2, CHIPS)
    barrier = pltpu.get_barrier_semaphore()
    greet(barrier)
    greet_plane(barrier)
    loads = []
    for index, (source, target) in enumerate(
        (
            (in_grad_hbm, big),
            (in_first_hbm, big_first),
            (x_part_hbm, x_part),
            (y_part_hbm, y_part),
            (
                returned_hbm.at[:, slot_rows(mine), :],
                returned.at[:, slot_rows(mine), :],
            ),
            (attended_hbm, attended_ref),
            (query_hbm, query_ref),
            (key_hbm, key_ref),
            (value_hbm, value_ref),
            (heads_hbm, heads_ref),
            (hidden_hbm, hidden_ref),
        )
    ):
        copy = pltpu.make_async_copy(source, target, load_sems.at[index])
        copy.start()
        loads.append(copy)
    weight_loads = load_windows(weight_hbm, weight, weight_sems, z)

    info = info_ref[...]
    columns = jnp.transpose(
        jnp.concatenate([info, jnp.zeros((120, BLOCK), jnp.float32)], axis=0)
    )
    lane_ids = lax.broadcasted_iota(jnp.int32, (BLOCK, SLOTS), 1).astype(jnp.float32)
    at_zero, at_one = lane_ids == columns[:, 0:1], lane_ids == columns[:, 1:2]
    ids = lax.broadcasted_iota(jnp.int32, (SLOTS, BLOCK), 0).astype(jnp.float32)
    lines = match_ref[0]
    match = jnp.concatenate(
        [jnp.broadcast_to(lines[:, lane : lane + 1], (EXPERT_ROWS, BLOCK)) for lane in (0, 64)],
        axis=0,
    )
    parts = []
    for place, gate in ((0, 2), (1, 3)):
        value = jnp.sum(
            jnp.where(ids == info[place : place + 1, :], match, 0.0), axis=0, keepdims=True
        )
        used = info[gate : gate + 1, :].astype(jnp.bfloat16).astype(jnp.float32)
        ratio = jnp.where(used > 0.0, info[gate : gate + 1, :] / jnp.where(used > 0.0, used, 1.0), 1.0)
        parts.append(value * ratio)
    gap = parts[0] * info[3:4, :] - parts[1] * info[2:3, :]
    names = lax.broadcasted_iota(jnp.int32, (EXPERTS, BLOCK), 0).astype(jnp.float32)
    pick_zero = jnp.where(names == info[4:5, :], 1.0, 0.0)
    pick_one = jnp.where(names == info[5:6, :], 1.0, 0.0)
    grad_logits = (gap * (pick_zero - pick_one)).astype(jnp.bfloat16)
    chosen = jnp.where(at_zero | at_one, 1.0, 0.0).astype(jnp.bfloat16)
    grad_two = (
        dot_tn(grad_logits, router_ref[...])
        + dot_nn(chosen[:, :EXPERT_ROWS], grad_back_ref[0])
        + dot_nn(chosen[:, EXPERT_ROWS:], grad_back_ref[1])
    )
    normed_two, inverse_two = norm_parts(residual_ref[...])
    gain_two_grad = jnp.sum(grad_two * normed_two, axis=0, keepdims=True)
    grad_residual[...] = grad_ref[...].astype(jnp.float32) + norm_back(
        grad_two * gain_two_ref[...][None], normed_two, inverse_two
    )
    grad_branch = grad_residual[...].astype(jnp.bfloat16)
    for chip in range(CHIPS):
        first = (chip + chip // 2) * 128
        grad_sent[chip] = dot_nt(grad_branch, proj_ref[first : first + PAD, :]).astype(
            jnp.bfloat16
        )
    pl.semaphore_wait(barrier, 13)
    owner_core = lax.rem(core + z, 2)
    grad_send, grad_recv = grad_sems.at[0], grad_sems.at[1]

    @pl.loop(0, CHIPS)
    def _(step):
        chip = lax.rem(z + step, CHIPS)
        mine_too = (chip == z) & (owner_core == core)

        @pl.when(jnp.logical_not(mine_too))
        def _():
            push(
                grad_sent.at[chip],
                grad_out.at[z],
                grad_send,
                grad_recv,
                chip,
                z,
                device(chip, owner_core),
            ).start()

        @pl.when(mine_too)
        def _():
            grad_out[z] = grad_sent[chip]

    for step in range(1, 8):
        place = lax.rem(mine + step, 8)
        copy = push(
            returned_hbm.at[:, slot_rows(place), :],
            returned.at[:, slot_rows(mine), :],
            returned_sems.at[0],
            returned_sems.at[1],
            0,
            0,
            (lax.axis_index("dp"), place),
        )
        copy.start()
    for load in loads[:4]:
        load.wait()
    big_sum = PlaneSum(big, big_first, big_direct, big_combined, big_sems.at[0], big_sems.at[1])
    big_sum.start_near()
    big_sum.second(waits=False)
    loads[5].wait()
    for chip in range(CHIPS):
        grads = dot_tn(attended_ref[chip], grad_branch).astype(jnp.bfloat16)
        first = (chip % 2) * HD
        for y in range(4):
            start = first + y * CAPACITY
            mid[chip, y, :, :WIDTH] = grads[start : start + CAPACITY]
    narrow = jnp.concatenate(
        [
            dot_nn(grad_logits, hidden_two_ref[...]),
            gain_two_grad,
            jnp.zeros((111, WIDTH), jnp.float32),
        ],
        axis=0,
    )
    mid[:, :, :, WIDTH : WIDTH + 128] = (
        jnp.transpose(narrow).astype(jnp.bfloat16).reshape(4, 4, CAPACITY, 128)
    )
    mid[:, :, :, WIDTH + 128 :] = jnp.zeros((4, 4, CAPACITY, 128), jnp.bfloat16)
    mid_sum = PlaneSum(mid, mid_first, mid_direct, mid_combined, mid_sems.at[0], mid_sems.at[1])
    mid_sum.start()
    out_sum = PlaneSpread(x_part, y_part, out_land, out_spread.at[0], out_spread.at[1])
    out_sum.start()

    grad_key[...] = jnp.zeros_like(grad_key)
    grad_value[...] = jnp.zeros_like(grad_value)
    projected[...] = jnp.zeros_like(projected)
    for load in loads[6:10]:
        load.wait()
    kind_bias = kind_ref[0].astype(jnp.float32) * NEGATIVE

    def attend(step):
        slot = lax.rem(z + step, CHIPS)
        block = slot * 2 + lax.rem(core + slot, 2)

        @pl.when(block != mine)
        def _():
            landed(grad_out.at[slot], grad_send, grad_recv, slot)

        queries = query_ref[block]
        grads = grad_out[slot]
        products = grads.astype(jnp.float32) * heads_ref[slot].astype(jnp.float32)
        selector = jnp.concatenate(
            [head_mask(z, head, 1.0, jnp.float32) for head in range(LOCAL_HEADS)]
            + [jnp.zeros((8 - LOCAL_HEADS, PAD), jnp.float32)],
            axis=0,
        )
        deltas = lax.dot_general(
            selector,
            products,
            (((1,), (1,)), ((), ())),
            preferred_element_type=jnp.float32,
            precision=lax.Precision.HIGHEST,
        )
        for head in range(LOCAL_HEADS):
            part = slice(head * BLOCK, (head + 1) * BLOCK)
            stacked[part, :] = queries * head_mask(z, head, HD ** (-0.5), jnp.bfloat16)
            grad_stacked[part, :] = grads * head_mask(z, head, 1.0, jnp.bfloat16)
        totals = total_ref[slot]
        delta_row = jnp.concatenate(
            [deltas[head : head + 1, :] for head in range(LOCAL_HEADS)], axis=1
        )
        total_row = jnp.concatenate(
            [totals[head : head + 1, :] for head in range(LOCAL_HEADS)], axis=1
        )

        def work(rows, bias, is_diagonal):
            keys, values = key_ref[rows, :], value_ref[rows, :]
            probs = jnp.exp(dot_nt(keys, stacked[...]) - (total_row - bias))
            if is_diagonal:
                row = lax.broadcasted_iota(jnp.int32, (BLOCK, STACK), 0)
                column = lax.broadcasted_iota(jnp.int32, (BLOCK, STACK), 1)
                probs = jnp.where(row <= lax.rem(column, BLOCK), probs, 0.0)
            grad_probs = dot_nt(values, grad_stacked[...])
            grad_scores = (probs * (grad_probs - delta_row)).astype(jnp.bfloat16)
            grad_value[rows, :] += dot_nn(probs.astype(jnp.bfloat16), grad_stacked[...])
            grad_key[rows, :] += dot_nn(grad_scores, stacked[...])
            return dot_tn(grad_scores, keys)

        grad_query[...] = work(block_rows(block), 0.0, True)

        @pl.when(block != 2 * slot)
        def _():
            grad_query[...] += work(block_rows(block - 1), 0.0, False)

        @pl.loop(0, slot)
        def _(chunk):
            bias = jnp.where((slot >= 2) & (chunk < 2), kind_bias, 0.0)
            grad_query[...] += work(chunk_rows(chunk), bias, False)

        combined = jnp.zeros((BLOCK, PAD), jnp.float32)
        for head in range(LOCAL_HEADS):
            part = slice(head * BLOCK, (head + 1) * BLOCK)
            combined += grad_query[part, :] * head_mask(z, head, HD ** (-0.5), jnp.float32)
        projected[block_rows(block), :PAD] = combined.astype(jnp.bfloat16)

    pl.loop(0, CHIPS)(attend)
    projected[:, PAD : 2 * PAD] = grad_key[...].astype(jnp.bfloat16)
    projected[:, 2 * PAD :] = grad_value[...].astype(jnp.bfloat16)
    for load in weight_loads:
        load.wait()

    def partial(chip, which):
        return dot_nt(projected[block_rows(chip * 2 + which), :], weight[...])

    sib_send, sib_recv = sib_sems.at[0], sib_sems.at[1]

    def sib_copy(index):
        return push(
            part_sib.at[index],
            land_sib.at[index],
            sib_send,
            sib_recv,
            index,
            index,
            device(z, 1 - core),
        )

    order = (far, up, down, z)
    for index, chip in enumerate(order):
        part_sib[index] = partial(chip, 1 - core).astype(jnp.bfloat16)
        sib_copy(index).start()

    loads[10].wait()
    for tile in range(3):
        lanes = slice(tile * PAD, (tile + 1) * PAD)
        weights = dot_tn(hidden_ref[...], projected[:, lanes]).astype(jnp.bfloat16)
        qkv[:, :, :, lanes] = weights.reshape(4, 4, CAPACITY, PAD)
    qkv_sum = PlaneSum(
        qkv, qkv_first, qkv_direct, qkv_combined, qkv_sems.at[0], qkv_sems.at[1]
    )
    qkv_sum.start()
    mid_sum.second()


    def own(index):
        value = partial(order[index], core)
        landed(land_sib.at[index], sib_send, sib_recv, index)
        return value + land_sib[index].astype(jnp.float32)

    first, second = pl.ds(0, HALF), pl.ds(HALF, HALF)
    ring_send, ring_recv = ring_sems.at[0], ring_sems.at[1]
    copies = []

    def ring(source, target, index, where):
        copy = push(source, target, ring_send, ring_recv, index, index, where)
        copy.start()
        copies.append(copy)

    above, below = device(up, core), device(down, core)
    part_own[0] = own(0).astype(jnp.bfloat16)
    ring(part_own.at[0, first], land_half.at[0], 0, above)
    ring(part_own.at[0, second], land_half.at[1], 1, below)
    part_own[1] = own(1).astype(jnp.bfloat16)
    ring(part_own.at[1, second], land_full.at[0, second], 2, above)
    part_own[2] = own(2).astype(jnp.bfloat16)
    ring(part_own.at[2, first], land_full.at[1, first], 3, below)
    grad_one = own(3)
    qkv_sum.second()
    landed(land_half.at[0], ring_send, ring_recv, 0)
    part_own[1, first, :] = added(part_own[1, first, :], land_half[0]).astype(jnp.bfloat16)
    ring(part_own.at[1, first], land_full.at[0, first], 4, above)
    landed(land_half.at[1], ring_send, ring_recv, 1)
    part_own[2, second, :] = added(part_own[2, second, :], land_half[1]).astype(jnp.bfloat16)
    ring(part_own.at[2, second], land_full.at[1, second], 5, below)
    mid_sum.third(mid_x, mid_y)
    mid_total = PlaneSpread(mid_x, mid_y, mid_land, mid_spread.at[0], mid_spread.at[1])
    mid_total.start()
    qkv_sum.third(qkv_x, qkv_y)
    qkv_total = PlaneSpread(qkv_x, qkv_y, qkv_land, qkv_spread.at[0], qkv_spread.at[1])
    qkv_total.start()
    big_sum.third(big_x, big_y)
    big_total = PlaneSpread(big_x, big_y, big_land, big_spread.at[0], big_spread.at[1])
    big_total.start()
    loads[4].wait()
    seven = returned.at[:, pl.ds(0, 7 * CAPACITY), :]
    pltpu.make_async_copy(seven, seven, returned_sems.at[1, 0]).wait()
    mixing = (
        jnp.where(at_zero, columns[:, 2:3], 0.0) + jnp.where(at_one, columns[:, 3:4], 0.0)
    ).astype(jnp.bfloat16)
    mixed_ref[...] = (
        residual_ref[...]
        + dot_nn(mixing[:, :EXPERT_ROWS], returned[0])
        + dot_nn(mixing[:, EXPERT_ROWS:], returned[1])
    ).astype(jnp.bfloat16)
    out_left, out_right = out_sum.total()
    out_sum_ref[:, : FF // 2] = out_left
    out_sum_ref[:, FF // 2 :] = out_right
    mid_left, mid_right = mid_total.total()
    qkv_left, qkv_right = qkv_total.total()
    share = CAPACITY // 8
    line = jnp.concatenate([mid_left, mid_right, qkv_left, qkv_right], axis=1)
    for piece in range(8):
        rows = slice(piece * share, (piece + 1) * share)
        dense_send[piece] = jnp.concatenate(
            [line[rows, :LINE], line[rows, LINE:], jnp.zeros((16 - 2 * share, LINE), jnp.float32)],
            axis=0,
        ).astype(jnp.bfloat16)
    dense_copies = []
    for step in range(1, 8):
        place = lax.rem(mine + step, 8)
        copy = push(
            dense_send.at[place],
            dense_land.at[mine],
            dense_sems.at[0],
            dense_sems.at[1],
            step - 1,
            step - 1,
            (lax.axis_index("dp"), place),
        )
        copy.start()
        dense_copies.append(copy)
    dense_land[mine] = dense_send[mine]
    landed(land_full.at[0, second], ring_send, ring_recv, 2)
    landed(land_full.at[1, first], ring_send, ring_recv, 3)
    landed(land_full.at[0, first], ring_send, ring_recv, 4)
    landed(land_full.at[1, second], ring_send, ring_recv, 5)
    grad_one += added(land_full[0], land_full[1])
    normed_one, inverse_one = norm_parts(tokens_ref[...].astype(jnp.float32))
    tokens_grad_ref[...] = grad_residual[...] + norm_back(
        grad_one * gain_ref[...][None], normed_one, inverse_one
    )
    left, right = big_total.total()
    in_sum_ref[:, : FF // 2] = left
    in_sum_ref[:, FF // 2 :] = right
    for step in range(1, 8):
        landed(
            dense_land.at[lax.rem(mine + 8 - step, 8)],
            dense_sems.at[0],
            dense_sems.at[1],
            step - 1,
        )
    lines = [dense_land[place].astype(jnp.float32) for place in range(8)]
    total = sum(lines[1:], lines[0])
    total = jnp.concatenate([total[:share], total[share : 2 * share]], axis=1)
    dense_sum_ref[...] = total[:, :DENSE]
    qkv_sum_ref[...] = jnp.zeros_like(qkv_sum_ref)
    for chip in range(CHIPS):
        line = lines[2 * chip] + lines[2 * chip + 1]
        line = jnp.concatenate([line[:share], line[share : 2 * share]], axis=1)[:, DENSE:]
        for part in range(3):
            start = part * WIDTH + (chip + chip // 2) * 128
            qkv_sum_ref[:, start : start + PAD] += line[:, part * PAD : (part + 1) * PAD]
    pltpu.make_async_copy(seven, seven, returned_sems.at[0, 0]).wait()
    for copy in dense_copies + copies:
        copy.wait_send()
    for user in (big_sum, out_sum, big_total, mid_sum, mid_total, qkv_sum, qkv_total):
        user.drain()
    for index in range(CHIPS):
        sib_copy(index).wait_send()

    @pl.loop(0, CHIPS)
    def _(chip):
        @pl.when((chip != z) | (owner_core != core))
        def _():
            push(
                grad_sent.at[chip],
                grad_out.at[chip],
                grad_send,
                grad_recv,
                chip,
                chip,
                device(z, 1 - core),
            ).wait_send()


def plane_scratch(lanes):
    return [
        pltpu.VMEM((4, 4, CAPACITY, lanes), HALF_TYPE),
        pltpu.VMEM((4, 2, CAPACITY, lanes // 2), HALF_TYPE),
        pltpu.VMEM((4, 2, CAPACITY, lanes // 2), HALF_TYPE),
        pltpu.VMEM((4, 2, CAPACITY, lanes // 2), HALF_TYPE),
        pltpu.VMEM((4, CAPACITY, lanes // 2), HALF_TYPE),
        pltpu.VMEM((4, CAPACITY, lanes // 2), HALF_TYPE),
        pltpu.VMEM((6, CAPACITY, lanes // 2), HALF_TYPE),
    ]


def back(*operands):
    def shape(*dims, dtype=FULL_TYPE):
        return jax.ShapeDtypeStruct(dims, dtype)

    def pair(count):
        return pltpu.SemaphoreType.DMA((2, count))

    return pl.pallas_call(
        back_kernel,
        out_shape=[
            shape(BLOCK, WIDTH, dtype=HALF_TYPE),
            shape(BLOCK, WIDTH),
            shape(CAPACITY, FF),
            shape(CAPACITY, FF),
            shape(CAPACITY // 8, DENSE),
            shape(CAPACITY // 8, 3 * WIDTH),
        ],
        in_specs=[smem()] + [vmem()] * 12 + [anywhere()] * 12,
        out_specs=[vmem()] * 6,
        scratch_shapes=[
            pltpu.VMEM((8, 16, LINE), HALF_TYPE),
            pltpu.VMEM((8, BLOCK, PAD), HALF_TYPE),
            pltpu.VMEM((LONG, PAD), HALF_TYPE),
            pltpu.VMEM((LONG, PAD), HALF_TYPE),
            pltpu.VMEM((CHIPS, BLOCK, PAD), HALF_TYPE),
            pltpu.VMEM((WIDTH, 3 * PAD), HALF_TYPE),
            pltpu.VMEM((LONG, WIDTH), HALF_TYPE),
            pltpu.VMEM((CHIPS, BLOCK, PAD), HALF_TYPE),
            pltpu.VMEM((4, CAPACITY, FF // 2), HALF_TYPE),
            pltpu.VMEM((4, CAPACITY, FF // 2), HALF_TYPE),
            pltpu.VMEM((6, CAPACITY, FF // 2), HALF_TYPE),
            pltpu.VMEM((2, EXPERT_ROWS, WIDTH), HALF_TYPE),
            pltpu.VMEM((BLOCK, WIDTH), FULL_TYPE),
            pltpu.VMEM((CHIPS, BLOCK, PAD), HALF_TYPE),
            pltpu.VMEM((CHIPS, BLOCK, PAD), HALF_TYPE),
            pltpu.VMEM((STACK, PAD), HALF_TYPE),
            pltpu.VMEM((STACK, PAD), HALF_TYPE),
            pltpu.VMEM((STACK, PAD), FULL_TYPE),
            pltpu.VMEM((LONG, PAD), FULL_TYPE),
            pltpu.VMEM((LONG, PAD), FULL_TYPE),
            pltpu.VMEM((LONG, 3 * PAD), HALF_TYPE),
            pltpu.VMEM((CHIPS, BLOCK, WIDTH), HALF_TYPE),
            pltpu.VMEM((CHIPS - 1, BLOCK, WIDTH), HALF_TYPE),
            pltpu.VMEM((CHIPS, BLOCK, WIDTH), HALF_TYPE),
            pltpu.VMEM((2, HALF, WIDTH), HALF_TYPE),
            pltpu.VMEM((2, BLOCK, WIDTH), HALF_TYPE),
            *plane_scratch(FF),
            *plane_scratch(DENSE),
            *plane_scratch(3 * PAD),
            pltpu.VMEM((8, 16, LINE), HALF_TYPE),
            pltpu.SemaphoreType.DMA((3,)),
            pltpu.SemaphoreType.DMA((11,)),
            pair(CHIPS),
            pair(CHIPS),
            pair(6),
            pair(12),
            pair(6),
            pair(6),
            pair(12),
            pair(6),
            pair(12),
            pair(6),
            pair(7),
            pair(1),
        ],
        compiler_params=pltpu.CompilerParams(
            collective_id=1, has_side_effects=True, vmem_limit_bytes=60 * 2**20
        ),
    )(*operands)


def finish_kernel(
    mixed_ref,
    tokens_grad_ref,
    in_sum_ref,
    out_sum_ref,
    dense_ref,
    qkv_ref,
    weight_ref,
    gain_ref,
    mixed_out,
    tokens_grad_out,
    gain_out,
    qkv_out,
    proj_out,
    gain_two_out,
    router_out,
    in_out,
    out_out,
    weight,
    sem,
):
    mixed_out[0] = mixed_ref[...]
    tokens_grad_out[0] = tokens_grad_ref[...]
    in_out[0] = in_sum_ref[...]
    for part in range(4):
        rows = slice(part * CAPACITY, (part + 1) * CAPACITY)
        out_out[0, rows, :] = out_sum_ref[:, part * WIDTH : (part + 1) * WIDTH]
    share = CAPACITY // 8
    first = (lax.axis_index("dp") * 8 + lax.axis_index("expert")) * share
    start = pl.multiple_of(jnp.minimum(first // 16, WIDTH // 16 - 2) * 16, 16)
    load = pltpu.make_async_copy(weight_ref.at[pl.ds(start, 32), :], weight, sem)
    load.start()
    qkv_out[...] = qkv_ref[...]
    dense = dense_ref[...]
    proj_out[...] = dense[:, :WIDTH]
    router_out[...] = dense[:, WIDTH : WIDTH + EXPERTS]
    gain_two_out[...] = dense[:, WIDTH + EXPERTS : WIDTH + EXPERTS + 1]
    row = lax.broadcasted_iota(jnp.int32, (share, 32), 0)
    column = lax.broadcasted_iota(jnp.int32, (share, 32), 1)
    chosen = jnp.where(column == row + (first - start), 1.0, 0.0).astype(jnp.bfloat16)
    row = lax.broadcasted_iota(jnp.int32, (share, WIDTH), 0)
    column = lax.broadcasted_iota(jnp.int32, (share, WIDTH), 1)
    gain = jnp.sum(
        jnp.where(column == row + first, gain_ref[...][None], 0.0), axis=1, keepdims=True
    )
    load.wait()
    products = qkv_ref[...] * dot_nn(chosen, weight[...])
    gain_out[...] = jnp.sum(products, axis=1, keepdims=True) / gain


def finish(*operands):
    def shape(*dims, dtype=FULL_TYPE):
        return jax.ShapeDtypeStruct(dims, dtype)

    share = CAPACITY // 8
    shapes = [
        shape(1, BLOCK, WIDTH, dtype=HALF_TYPE),
        shape(1, BLOCK, WIDTH),
        shape(share, 1),
        shape(share, 3 * WIDTH),
        shape(share, WIDTH),
        shape(share, 1),
        shape(share, EXPERTS),
        shape(1, CAPACITY, FF),
        shape(1, 4 * CAPACITY, WIDTH),
    ]
    return pl.pallas_call(
        finish_kernel,
        out_shape=shapes,
        in_specs=[vmem()] * 6 + [anywhere(), vmem()],
        out_specs=[vmem()] * 9,
        scratch_shapes=[
            pltpu.VMEM((32, 3 * WIDTH), HALF_TYPE),
            pltpu.SemaphoreType.DMA,
        ],
        compiler_params=pltpu.CompilerParams(vmem_limit_bytes=62 * 2**20),
    )(*operands)


def on_device(
    tokens,
    group_kind,
    routes,
    norm1_gain,
    qkv_weight,
    proj_weight,
    norm2_gain,
    router_weight,
    frozen_in,
    frozen_out,
    new_in,
    new_out,
    out_grad,
):
    width = WIDTH
    router = router_weight.T
    (
        hidden,
        queries,
        keys,
        values,
        heads,
        totals,
        attended,
        residual,
        hidden_two,
        sent,
        grad_rows,
        info,
    ) = front(
        group_kind,
        tokens[0],
        norm1_gain,
        qkv_weight,
        out_grad[0],
        routes[0].T,
        proj_weight,
        norm2_gain,
        router,
    )
    returned, in_grad, in_first, grad_back, match, x_part, y_part = experts_both_ways(
        sent, grad_rows, frozen_in[0], frozen_out[0], new_in[0], new_out[0]
    )
    mixed, tokens_grad, in_sum, out_sum, dense_sum, qkv_sum = back(
        group_kind,
        tokens[0],
        norm1_gain,
        norm2_gain,
        out_grad[0],
        residual,
        info,
        match,
        grad_back,
        router,
        proj_weight,
        hidden_two,
        totals,
        queries,
        keys,
        values,
        heads,
        qkv_weight,
        hidden.reshape(LONG, width),
        attended,
        in_grad,
        in_first,
        returned,
        x_part,
        y_part,
    )
    outputs = finish(
        mixed, tokens_grad, in_sum, out_sum, dense_sum, qkv_sum, qkv_weight, norm1_gain
    )
    return tuple(
        value[:, 0] if index in (2, 5) else value for index, value in enumerate(outputs)
    )


def solution(mesh):
    return jax.shard_map(
        on_device,
        mesh=mesh,
        in_specs=(
            P("dp", "expert", None),
            P("dp"),
            P("dp", "expert", None),
            P(),
            P(),
            P(),
            P(),
            P(),
            P("expert", None, None),
            P("expert", None, None),
            P("expert", None, None),
            P("expert", None, None),
            P("dp", "expert", None),
        ),
        out_specs=(
            P("dp", "expert", None),
            P("dp", "expert", None),
            P(("dp", "expert")),
            P(("dp", "expert"), None),
            P(("dp", "expert"), None),
            P(("dp", "expert")),
            P(("dp", "expert"), None),
            P("expert", "dp", None),
            P("expert", "dp", None),
        ),
        check_vma=False,
    )
```

```python
import jax
import jax.numpy as jnp
from jax import lax
from jax.experimental import pallas as pl
from jax.experimental.pallas import tpu as pltpu
from jax.sharding import PartitionSpec as P

HEADS = 12
HD = 64
LONG = 2048
MESH_ID = pl.DeviceIdType.MESH
CHIPS = 4
PAD = 256
BLOCK = 256
HALF = BLOCK // 2
CHUNK = 512
CHUNKS = LONG // CHUNK
LOCAL_HEADS = HEADS // CHIPS
STACK = LOCAL_HEADS * BLOCK
NEGATIVE = -1e30
WIDTH = 768
EXPERTS = 16
SLOTS = 768
EXPERT_ROWS = 384
CAPACITY = 48
FF = 3072
FF_TILE = 768
FF_TILES = 4
DENSE = 1024
LINE = (DENSE + 3 * PAD) // 2
HALF_TYPE = jnp.bfloat16
FULL_TYPE = jnp.float32

epsilon = 1e-05


def norm_parts(values):
    average = jnp.mean(values, axis=-1, keepdims=True)
    centred = values - average
    variance = jnp.mean(centred * centred, axis=-1, keepdims=True)
    inverse = lax.rsqrt(variance + epsilon)
    return (centred * inverse, inverse)


def norm_back(grad_normed, normed, inverse):
    first_mean = jnp.mean(grad_normed, axis=-1, keepdims=True)
    second_mean = jnp.mean(grad_normed * normed, axis=-1, keepdims=True)
    return inverse * (grad_normed - first_mean - normed * second_mean)


def here():
    position = lax.axis_index("expert")
    return position // 2, lax.rem(position, 2)


def device(z, core):
    return (lax.axis_index("dp"), z * 2 + core)


def greet(barrier):
    position = lax.axis_index("expert")
    for step in range(1, 8):
        pl.semaphore_signal(
            barrier,
            inc=1,
            device_id=(lax.axis_index("dp"), lax.rem(position + step, 8)),
            device_id_type=MESH_ID,
        )


def push(source, target, sends, receives, index_here, index_there, where):
    return pltpu.make_async_remote_copy(
        src_ref=source,
        dst_ref=target,
        send_sem=sends.at[index_here],
        recv_sem=receives.at[index_there],
        device_id=where,
        device_id_type=MESH_ID,
    )


def landed(region, sends, receives, index):
    z, core = here()
    push(region, region, sends, receives, index, index, device(z, 1 - core)).wait_recv()


def dot_nn(left, right):
    return jnp.dot(left, right, preferred_element_type=jnp.float32)


def dot_nt(left, right):
    return lax.dot_general(
        left, right, (((1,), (1,)), ((), ())), preferred_element_type=jnp.float32
    )


def dot_tn(left, right):
    return lax.dot_general(
        left, right, (((0,), (0,)), ((), ())), preferred_element_type=jnp.float32
    )


def window(chip):
    return (chip + chip // 2) * 128, lax.rem(chip, 2) * HD


def head_mask(chip, head, value, dtype):
    start = window(chip)[1] + head * HD
    lanes = lax.broadcasted_iota(jnp.int32, (1, PAD), 1)
    inside = (lanes >= start) & (lanes < start + HD)
    return jnp.where(inside, value, 0.0).astype(dtype)


def lane_tiles(values, combine):
    result = values[:, :128]
    for start in range(128, values.shape[1], 128):
        result = combine(result, values[:, start : start + 128])
    return result


def block_rows(block):
    return pl.ds(pl.multiple_of(block * BLOCK, BLOCK), BLOCK)


def chunk_rows(chunk):
    return pl.ds(pl.multiple_of(chunk * CHUNK, CHUNK), CHUNK)


def load_windows(weight_ref, target, sems, chip):
    copies = []
    for part in range(3):
        first = pl.multiple_of(part * WIDTH + window(chip)[0], 128)
        copies.append(
            pltpu.make_async_copy(
                weight_ref.at[:, pl.ds(first, PAD)],
                target.at[:, pl.ds(part * PAD, PAD)],
                sems.at[part],
            )
        )
    for copy in copies:
        copy.start()
    return copies


class RingGather:
    def __init__(self, ref, sends, receives):
        self.ref, self.sends, self.receives = ref, sends, receives
        self.z, self.core = here()
        self.up, self.down = lax.rem(self.z + 1, CHIPS), lax.rem(self.z + 3, CHIPS)
        self.far = lax.rem(self.z + 2, CHIPS)
        self.copies = []

    def region(self, chip, core, half):
        rows = slice(None) if half is None else pl.ds(half * HALF, HALF)
        return self.ref.at[chip * 2 + core, rows]

    def send(self, index, chip, half, where):
        region = self.region(chip, self.core, half)
        copy = push(region, region, self.sends, self.receives, index, index, where)
        copy.start()
        self.copies.append(copy)

    def wait(self, index, chip, core, half):
        landed(self.region(chip, core, half), self.sends, self.receives, index)

    def above(self):
        return device(self.up, self.core)

    def below(self):
        return device(self.down, self.core)

    def beside(self):
        return device(self.z, 1 - self.core)

    def start(self):
        self.send(0, self.z, 0, self.above())
        self.send(1, self.z, 1, self.below())
        self.send(2, self.z, 1, self.above())
        self.send(3, self.z, 0, self.below())
        self.send(4, self.z, None, self.beside())

    def relay(self):
        self.wait(0, self.down, self.core, 0)
        self.send(5, self.down, 0, self.above())
        self.send(7, self.down, 0, self.beside())
        self.wait(1, self.up, self.core, 1)
        self.send(6, self.up, 1, self.below())
        self.send(8, self.up, 1, self.beside())

    def share(self):
        self.wait(2, self.down, self.core, 1)
        self.send(9, self.down, 1, self.beside())
        self.wait(3, self.up, self.core, 0)
        self.send(10, self.up, 0, self.beside())

    def share_far(self):
        self.wait(5, self.far, self.core, 0)
        self.send(11, self.far, 0, self.beside())
        self.wait(6, self.far, self.core, 1)
        self.send(12, self.far, 1, self.beside())

    def other_own(self):
        self.wait(4, self.z, 1 - self.core, None)

    def other_down(self):
        self.wait(7, self.down, 1 - self.core, 0)
        self.wait(9, self.down, 1 - self.core, 1)

    def other_up(self):
        self.wait(8, self.up, 1 - self.core, 1)
        self.wait(10, self.up, 1 - self.core, 0)

    def other_far(self):
        self.wait(11, self.far, 1 - self.core, 0)
        self.wait(12, self.far, 1 - self.core, 1)

    def drain(self):
        for copy in self.copies:
            copy.wait_send()


def plane_device(x, y):
    return (x * 4 + y, lax.axis_index("expert"))


def plane_here():
    group = lax.axis_index("dp")
    return group // 4, lax.rem(group, 4)


def added(left, right):
    return left.astype(jnp.float32) + right.astype(jnp.float32)


class PlaneSum:
    def __init__(self, source, first, direct, combined, sends, receives):
        self.source, self.first = source, first
        self.direct, self.combined = direct, combined
        self.sends, self.receives = sends, receives
        self.x, self.y = plane_here()
        half = source.shape[-1] // 2
        self.left, self.right = pl.ds(0, half), pl.ds(half, half)
        self.low, self.high = pl.ds(0, 2), pl.ds(2, 2)
        self.copies = []

    def x_part(self, x, part):
        return self.source.at[x, part, :, self.left]

    def y_part(self, y, part):
        return self.source.at[part, y, :, self.right]

    def sides(self):
        return (
            (0, self.x, self.x_part, lambda p: plane_device(p, self.y)),
            (2, self.y, self.y_part, lambda p: plane_device(self.x, p)),
        )

    def send(self, source, target, index, where):
        copy = push(source, target, self.sends, self.receives, index, index, where)
        copy.start()
        self.copies.append(copy)

    def wait(self, region, index):
        landed(region, self.sends, self.receives, index)

    def neighbours(self, place):
        return lax.rem(place + 1, 4), lax.rem(place + 3, 4), lax.rem(place + 2, 4)

    def start_far(self):
        for base, place, part, where in self.sides():
            up, down, far = self.neighbours(place)
            self.send(part(far, self.low), self.first.at[base], base, where(up))
            self.send(part(far, self.high), self.first.at[base + 1], base + 1, where(down))

    def start_near(self):
        for base, place, part, where in self.sides():
            up, down, _ = self.neighbours(place)
            self.send(part(up, self.high), self.direct.at[base], base + 4, where(up))
            self.send(part(down, self.low), self.direct.at[base + 1], base + 5, where(down))

    def start(self):
        self.start_far()
        self.start_near()

    def settle_far(self):
        for index in range(4):
            self.wait(self.first.at[index], index)

    def second(self, waits=True):
        low, high = self.low, self.high
        for base, place, part, where in self.sides():
            up, down, _ = self.neighbours(place)
            for index, chosen, to in (
                (base, part(up, low), up),
                (base + 1, part(down, high), down),
            ):
                if waits:
                    self.wait(self.first.at[index], index)
                chosen[...] = added(chosen[...], self.first[index]).astype(jnp.bfloat16)
                self.send(chosen, self.combined.at[index], index + 8, where(to))

    def third(self, x_sum, y_sum):
        low, high = self.low, self.high
        for base, place, part, total in (
            (0, self.x, self.x_part, x_sum),
            (2, self.y, self.y_part, y_sum),
        ):
            self.wait(self.direct.at[base], base + 4)
            self.wait(self.direct.at[base + 1], base + 5)
            self.wait(self.combined.at[base], base + 8)
            self.wait(self.combined.at[base + 1], base + 9)
            total[low] = (
                added(part(place, low)[...], self.combined[base])
                + self.direct[base + 1].astype(jnp.float32)
            ).astype(jnp.bfloat16)
            total[high] = (
                added(part(place, high)[...], self.direct[base])
                + self.combined[base + 1].astype(jnp.float32)
            ).astype(jnp.bfloat16)

    def drain(self):
        for copy in self.copies:
            copy.wait_send()


class PlaneSpread:
    def __init__(self, x_sum, y_sum, land, sends, receives):
        self.x_sum, self.y_sum, self.land = x_sum, y_sum, land
        self.sends, self.receives = sends, receives
        self.x, self.y = plane_here()
        self.copies = []

    def start(self):
        for step in range(1, 4):
            y, x = lax.rem(self.y + step, 4), lax.rem(self.x + step, 4)
            for index, source, where in (
                (step - 1, self.x_sum.at[y], plane_device(self.x, y)),
                (step + 2, self.y_sum.at[x], plane_device(x, self.y)),
            ):
                copy = push(
                    source, self.land.at[index], self.sends, self.receives, index, index, where
                )
                copy.start()
                self.copies.append(copy)

    def total(self):
        sums = []
        for base, mine in ((0, self.x_sum[self.y]), (3, self.y_sum[self.x])):
            value = mine.astype(jnp.float32)
            for index in range(base, base + 3):
                landed(self.land.at[index], self.sends, self.receives, index)
                value += self.land[index].astype(jnp.float32)
            sums.append(value)
        return sums

    def drain(self):
        for copy in self.copies:
            copy.wait_send()


def greet_plane(barrier):
    x, y = plane_here()
    for step in range(1, 4):
        for where in (plane_device(lax.rem(x + step, 4), y), plane_device(x, lax.rem(y + step, 4))):
            pl.semaphore_signal(barrier, inc=1, device_id=where, device_id_type=MESH_ID)


def gelu_parts(u):
    scaled = jnp.abs(u) * 0.7071067811865476
    t = 1.0 / (1.0 + 0.3275911 * scaled)
    poly = t * (
        0.127414796
        + t * (-0.142248368 + t * (0.7107068705 + t * (-0.7265760135 + t * 0.5307027145)))
    )
    density = jnp.exp(-0.5 * u * u)
    tail = poly * density
    cumulative = jnp.where(u >= 0, 1.0 - tail, tail)
    return u * cumulative, cumulative + u * density * 0.3989422804014327


def vmem():
    return pl.BlockSpec(memory_space=pltpu.VMEM)


def smem():
    return pl.BlockSpec(memory_space=pltpu.SMEM)


def anywhere():
    return pl.BlockSpec(memory_space=pl.ANY)


def front_kernel(
    kind_ref,
    tokens_ref,
    gain_ref,
    weight_ref,
    grad_hbm,
    routes_ref,
    proj_hbm,
    gain_two_ref,
    router_ref,
    hidden_out,
    query_out,
    key_out,
    value_out,
    heads_out,
    attended_out,
    residual_out,
    hidden_two_out,
    sent_out,
    grad_rows_out,
    total_ref,
    info_ref,
    hidden_ref,
    query_ref,
    key_ref,
    value_ref,
    out_ref,
    attended_ref,
    residual_ref,
    hidden_two_ref,
    sent_ref,
    grad_rows_ref,
    grad_ref,
    proj_ref,
    weight,
    stacked,
    diagonal,
    beside,
    scores,
    largest,
    sums,
    acc,
    gather_sems,
    out_sems,
    weight_sems,
    store_sems,
):
    z, core = here()
    mine = z * 2 + core
    up, down, far = lax.rem(z + 1, CHIPS), lax.rem(z + 3, CHIPS), lax.rem(z + 2, CHIPS)
    barrier = pltpu.get_barrier_semaphore()
    greet(barrier)
    loads = load_windows(weight_ref, weight, weight_sems, z)
    late_loads = [
        pltpu.make_async_copy(grad_hbm, grad_ref, weight_sems.at[3]),
        pltpu.make_async_copy(proj_hbm, proj_ref, weight_sems.at[4]),
    ]
    for load in late_loads:
        load.start()
    tokens = tokens_ref[...].astype(jnp.float32)
    normed, _ = norm_parts(tokens)
    hidden_ref[mine] = (normed * gain_ref[...][None]).astype(jnp.bfloat16)
    pl.semaphore_wait(barrier, 7)
    gather = RingGather(hidden_ref, gather_sems.at[0], gather_sems.at[1])
    stores = []

    def store(source, target):
        copy = pltpu.make_async_copy(source, target, store_sems.at[len(stores)])
        copy.start()
        stores.append(copy)

    def project(block):
        projected = dot_nn(hidden_ref[block], weight[...]).astype(jnp.bfloat16)
        query_ref[block] = projected[:, :PAD]
        key_ref[block_rows(block), :] = projected[:, PAD : 2 * PAD]
        value_ref[block_rows(block), :] = projected[:, 2 * PAD :]

    gather.start()
    for load in loads:
        load.wait()
    project(mine)
    routes = routes_ref[...].astype(jnp.float32)
    names = lax.broadcasted_iota(jnp.int32, (EXPERTS, BLOCK), 0).astype(jnp.float32)
    pick_zero = jnp.where(names == routes[0:1, :], 1.0, 0.0)
    pick_one = jnp.where(names == routes[1:2, :], 1.0, 0.0)
    row = lax.broadcasted_iota(jnp.int32, (BLOCK, BLOCK), 0)
    column = lax.broadcasted_iota(jnp.int32, (BLOCK, BLOCK), 1)
    before = jnp.where(row < column, 1.0, 0.0).astype(jnp.bfloat16)
    earlier = dot_nn((pick_zero + pick_one).astype(jnp.bfloat16), before)
    places = []
    for index, pick in enumerate((pick_zero, pick_one)):
        slot = jnp.sum(earlier * pick, axis=0, keepdims=True)
        place = routes[index : index + 1, :] * CAPACITY + slot
        places.append(jnp.where(slot < CAPACITY, place, -1.0))
    gather.relay()
    gather.other_own()
    project(z * 2 + 1 - core)
    gather.share()
    project(down * 2 + core)
    project(up * 2 + core)
    gather.other_down()
    project(down * 2 + 1 - core)
    gather.other_up()
    project(up * 2 + 1 - core)
    gather.share_far()
    project(far * 2 + core)
    gather.other_far()
    project(far * 2 + 1 - core)
    store(hidden_ref, hidden_out)
    store(query_ref, query_out)
    store(key_ref, key_out)
    store(value_ref, value_out)

    kind_bias = kind_ref[0].astype(jnp.float32) * NEGATIVE
    out_send, out_recv = out_sems.at[0], out_sems.at[1]

    def attend(step):
        slot = lax.rem(z + CHIPS - 1 - step, CHIPS)
        block = slot * 2 + lax.rem(core + slot, 2)
        queries = query_ref[block]
        for head in range(LOCAL_HEADS):
            stacked[head * BLOCK : (head + 1) * BLOCK, :] = queries * head_mask(
                z, head, HD ** (-0.5), jnp.bfloat16
            )

        def bias_of(chunk):
            return jnp.where((slot >= 2) & (chunk < 2), kind_bias, 0.0)

        masked = dot_nt(stacked[...], key_ref[block_rows(block), :])
        row = lax.broadcasted_iota(jnp.int32, (BLOCK, BLOCK), 0)
        column = lax.broadcasted_iota(jnp.int32, (BLOCK, BLOCK), 1)
        for head in range(LOCAL_HEADS):
            part = slice(head * BLOCK, (head + 1) * BLOCK)
            values = jnp.where(column <= row, masked[part], NEGATIVE)
            diagonal[part, :] = values
            largest[part, :] = lane_tiles(values, jnp.maximum)
        is_odd = block != 2 * slot

        @pl.when(is_odd)
        def _():
            values = dot_nt(stacked[...], key_ref[block_rows(block - 1), :])
            beside[...] = values
            largest[...] = jnp.maximum(largest[...], lane_tiles(values, jnp.maximum))

        @pl.loop(0, slot)
        def _(chunk):
            values = dot_nt(stacked[...], key_ref[chunk_rows(chunk), :])
            scores[chunk] = values
            largest[...] = jnp.maximum(
                largest[...], lane_tiles(values, jnp.maximum) + bias_of(chunk)
            )

        row_max = jnp.max(largest[...], axis=1, keepdims=True)
        largest[...] = jnp.broadcast_to(row_max, largest.shape)
        exponent = jnp.exp(diagonal[...] - row_max)
        sums[...] = lane_tiles(exponent, jnp.add)
        acc[...] = dot_nn(exponent.astype(jnp.bfloat16), value_ref[block_rows(block), :])

        @pl.when(is_odd)
        def _():
            exponent = jnp.exp(beside[...] - largest[:, :1])
            sums[...] += lane_tiles(exponent, jnp.add)
            acc[...] += dot_nn(exponent.astype(jnp.bfloat16), value_ref[block_rows(block - 1), :])

        @pl.loop(0, slot)
        def _(chunk):
            exponent = jnp.exp(scores[chunk] - (largest[:, :1] - bias_of(chunk)))
            sums[...] += lane_tiles(exponent, jnp.add)
            acc[...] += dot_nn(exponent.astype(jnp.bfloat16), value_ref[chunk_rows(chunk), :])

        total = jnp.sum(sums[...], axis=1, keepdims=True)
        inverse = 1.0 / total
        log_total = largest[...] + jnp.log(total)
        attended = jnp.zeros((BLOCK, PAD), jnp.float32)
        for head in range(LOCAL_HEADS):
            part = slice(head * BLOCK, (head + 1) * BLOCK)
            attended += acc[part, :] * inverse[part] * head_mask(z, head, 1.0, jnp.float32)
            total_ref[slot, head : head + 1, :] = jnp.transpose(log_total[part, :])[:1, :]
        out_ref[slot] = attended.astype(jnp.bfloat16)

        @pl.when(block != mine)
        def _():
            push(
                out_ref.at[slot],
                attended_ref.at[z],
                out_send,
                out_recv,
                slot,
                z,
                device(slot, lax.rem(core + slot, 2)),
            ).start()

        @pl.when(block == mine)
        def _():
            attended_ref[z] = out_ref[slot]

    pl.loop(0, CHIPS)(attend)
    store(out_ref, heads_out)

    @pl.loop(0, CHIPS)
    def _(slot):
        @pl.when((slot != z) | (lax.rem(core + z, 2) != core))
        def _():
            landed(attended_ref.at[slot], out_send, out_recv, slot)

    store(attended_ref, attended_out)
    for load in late_loads:
        load.wait()
    residual = tokens_ref[...].astype(jnp.float32)
    for chip in range(CHIPS):
        first = (chip + chip // 2) * 128
        residual += dot_nn(attended_ref[chip], proj_ref[first : first + PAD, :])
    residual_ref[...] = residual
    normed_two, _ = norm_parts(residual)
    hidden_two = (normed_two * gain_two_ref[...][None]).astype(jnp.bfloat16)
    hidden_two_ref[...] = hidden_two
    store(residual_ref, residual_out)
    store(hidden_two_ref, hidden_two_out)
    logits = dot_nt(router_ref[...], hidden_two)
    logit_zero = jnp.sum(logits * pick_zero, axis=0, keepdims=True)
    logit_one = jnp.sum(logits * pick_one, axis=0, keepdims=True)
    gate_zero = 1.0 / (1.0 + jnp.exp(logit_one - logit_zero))
    gate_one = 1.0 / (1.0 + jnp.exp(logit_zero - logit_one))
    for index, line in enumerate((*places, gate_zero, gate_one, routes[0:1], routes[1:2])):
        info_ref[index : index + 1, :] = line
    info_ref[6:8, :] = jnp.zeros((2, BLOCK), jnp.float32)
    ids = lax.broadcasted_iota(jnp.int32, (SLOTS, BLOCK), 0).astype(jnp.float32)
    chosen = jnp.where((ids == places[0]) | (ids == places[1]), 1.0, 0.0).astype(jnp.bfloat16)
    sent = dot_nn(chosen, hidden_two).astype(jnp.bfloat16)
    sent_ref[0] = sent[:EXPERT_ROWS]
    sent_ref[1] = sent[EXPERT_ROWS:]
    store(sent_ref, sent_out)
    mixing = (
        jnp.where(ids == places[0], gate_zero, 0.0) + jnp.where(ids == places[1], gate_one, 0.0)
    ).astype(jnp.bfloat16)
    rows = dot_nn(mixing, grad_ref[...]).astype(jnp.bfloat16)
    grad_rows_ref[0] = rows[:EXPERT_ROWS]
    grad_rows_ref[1] = rows[EXPERT_ROWS:]
    store(grad_rows_ref, grad_rows_out)
    gather.drain()

    @pl.loop(0, CHIPS)
    def _(slot):
        @pl.when(slot * 2 + lax.rem(core + slot, 2) != mine)
        def _():
            push(
                out_ref.at[slot],
                attended_ref.at[slot],
                out_send,
                out_recv,
                slot,
                slot,
                device(z, 1 - core),
            ).wait_send()

    for copy in stores:
        copy.wait()


def front(kind, tokens, gain, weight, grads, routes, proj, gain_two, router):
    def shape(*dims, dtype=HALF_TYPE):
        return jax.ShapeDtypeStruct(dims, dtype)

    shapes = [
        shape(8, BLOCK, WIDTH),
        shape(8, BLOCK, PAD),
        shape(LONG, PAD),
        shape(LONG, PAD),
        shape(CHIPS, BLOCK, PAD),
        shape(CHIPS, BLOCK, PAD),
        shape(BLOCK, WIDTH, dtype=FULL_TYPE),
        shape(BLOCK, WIDTH),
        shape(2, EXPERT_ROWS, WIDTH),
        shape(2, EXPERT_ROWS, WIDTH),
        shape(CHIPS, 8, BLOCK, dtype=FULL_TYPE),
        shape(8, BLOCK, dtype=FULL_TYPE),
    ]
    return pl.pallas_call(
        front_kernel,
        out_shape=shapes,
        in_specs=[
            smem(),
            vmem(),
            vmem(),
            anywhere(),
            anywhere(),
            vmem(),
            anywhere(),
            vmem(),
            vmem(),
        ],
        out_specs=[anywhere()] * 10 + [vmem()] * 2,
        scratch_shapes=[
            pltpu.VMEM((8, BLOCK, WIDTH), HALF_TYPE),
            pltpu.VMEM((8, BLOCK, PAD), HALF_TYPE),
            pltpu.VMEM((LONG, PAD), HALF_TYPE),
            pltpu.VMEM((LONG, PAD), HALF_TYPE),
            pltpu.VMEM((CHIPS, BLOCK, PAD), HALF_TYPE),
            pltpu.VMEM((CHIPS, BLOCK, PAD), HALF_TYPE),
            pltpu.VMEM((BLOCK, WIDTH), FULL_TYPE),
            pltpu.VMEM((BLOCK, WIDTH), HALF_TYPE),
            pltpu.VMEM((2, EXPERT_ROWS, WIDTH), HALF_TYPE),
            pltpu.VMEM((2, EXPERT_ROWS, WIDTH), HALF_TYPE),
            pltpu.VMEM((BLOCK, WIDTH), HALF_TYPE),
            pltpu.VMEM((WIDTH, WIDTH), HALF_TYPE),
            pltpu.VMEM((WIDTH, 3 * PAD), HALF_TYPE),
            pltpu.VMEM((STACK, PAD), HALF_TYPE),
            pltpu.VMEM((STACK, BLOCK), FULL_TYPE),
            pltpu.VMEM((STACK, BLOCK), FULL_TYPE),
            pltpu.VMEM((CHUNKS - 1, STACK, CHUNK), FULL_TYPE),
            pltpu.VMEM((STACK, 128), FULL_TYPE),
            pltpu.VMEM((STACK, 128), FULL_TYPE),
            pltpu.VMEM((STACK, PAD), FULL_TYPE),
            pltpu.SemaphoreType.DMA((2, 13)),
            pltpu.SemaphoreType.DMA((2, CHIPS)),
            pltpu.SemaphoreType.DMA((5,)),
            pltpu.SemaphoreType.DMA((10,)),
        ],
        compiler_params=pltpu.CompilerParams(
            collective_id=0, has_side_effects=True, vmem_limit_bytes=56 * 2**20
        ),
    )(kind, tokens, gain, weight, grads, routes, proj, gain_two, router)


def expert_kernel(
    sent_ref,
    grad_rows_ref,
    in_frozen,
    out_frozen,
    in_new,
    out_new,
    returned_ref,
    in_grad_ref,
    in_first_ref,
    grad_back_ref,
    match_ref,
    x_sum_ref,
    y_sum_ref,
    w_in,
    w_out,
    x_land,
    g_land,
    activated,
    slope,
    acc,
    r_send,
    b_send,
    in_grad,
    out_grad,
    first,
    direct,
    combined,
    in_first,
    match_send,
    load_sems,
    x_sems,
    g_sems,
    b_sems,
    match_sems,
    plane_sems,
    in_sems,
    store_sems,
):
    mine = lax.axis_index("expert")
    barrier = pltpu.get_barrier_semaphore()
    greet(barrier)
    greet_plane(barrier)
    loads = []
    for index, (source, target) in enumerate(
        (
            (in_new, w_in.at[1]),
            (out_new, w_out.at[1]),
            (in_frozen, w_in.at[0]),
            (out_frozen, w_out.at[0]),
        )
    ):
        copy = pltpu.make_async_copy(source, target, load_sems.at[index])
        copy.start()
        loads.append(copy)

    def rows_of(place):
        return pl.ds(pl.multiple_of(place * CAPACITY, CAPACITY), CAPACITY)

    own_rows = rows_of(mine)
    own_loads = []
    for index, (source, target) in enumerate(((sent_ref, x_land), (grad_rows_ref, g_land))):
        copy = pltpu.make_async_copy(
            source.at[:, own_rows, :], target.at[:, own_rows, :], load_sems.at[4 + index]
        )
        copy.start()
        own_loads.append(copy)
    pl.semaphore_wait(barrier, 13)

    def peer(step):
        return lax.rem(mine + step, 8)

    def exchange(source, target, sems, index, step):
        return push(
            source, target, sems.at[0], sems.at[1], index, index, (lax.axis_index("dp"), peer(step))
        )

    stores, used = [], []

    def store(source, target):
        copy = pltpu.make_async_copy(source, target, store_sems.at[len(stores)])
        copy.start()
        stores.append(copy)

    def seven(ref, sem):
        region = ref.at[0, pl.ds(0, 7 * CAPACITY), :]
        return pltpu.make_async_copy(region, region, sem)

    def spread_kind(kind, source, target, sems):
        for step in range(1, 8):
            exchange(
                source.at[kind, rows_of(peer(step)), :],
                target.at[kind, own_rows, :],
                sems,
                kind,
                step,
            ).start()
        used.append((target, sems.at[0, kind]))

    def collect_kind(kind, target, sems):
        seven(target, sems.at[1, kind]).wait()

    for kind in (1, 0):
        spread_kind(kind, sent_ref, x_land, x_sems)
        spread_kind(kind, grad_rows_ref, g_land, g_sems)
    for copy in own_loads:
        copy.wait()

    def tile_of(index):
        return pl.ds(pl.multiple_of(index * FF_TILE, FF_TILE), FF_TILE)

    plane = PlaneSum(out_grad, first, direct, combined, plane_sems.at[0], plane_sems.at[1])
    in_plane = PlaneSum(in_grad, in_first, None, None, in_sems.at[0], in_sems.at[1])
    matches = [None, None]
    for kind in (1, 0):
        collect_kind(kind, x_land, x_sems)
        loads[0 if kind == 1 else 2].wait()
        loads[1 if kind == 1 else 3].wait()
        acc[...] = jnp.zeros_like(acc)

        @pl.loop(0, FF_TILES, unroll=True)
        def _(index):
            tile = tile_of(index)
            pre = dot_nn(x_land[kind], w_in[kind, :, tile])
            value, steep = gelu_parts(pre)
            value = value.astype(jnp.bfloat16)
            if kind == 1:
                activated[:, tile] = value
            slope[:, tile] = steep.astype(jnp.bfloat16)
            acc[...] += dot_nn(value, w_out[kind, tile, :])

        collect_kind(kind, g_land, g_sems)
        result = acc[...].astype(jnp.bfloat16)
        r_send[kind] = result
        store(r_send.at[kind], returned_ref.at[kind])
        products = result.astype(jnp.float32) * g_land[kind].astype(jnp.float32)
        matches[kind] = jnp.sum(products, axis=1, keepdims=True)
        if kind == 1:

            @pl.loop(0, FF_TILES, unroll=True)
            def _(index):
                weights = dot_tn(activated[:, tile_of(index)], g_land[1]).astype(jnp.bfloat16)
                for y in range(4):
                    for part in range(4):
                        start = (y * 4 + part) * CAPACITY
                        out_grad[index, y, :, part * WIDTH : (part + 1) * WIDTH] = weights[
                            start : start + CAPACITY
                        ]

            plane.start()

        acc[...] = jnp.zeros_like(acc)

        @pl.loop(0, FF_TILES, unroll=True)
        def _(index):
            tile = tile_of(index)
            grad = dot_nt(g_land[kind], w_out[kind, tile, :])
            grad = (grad * slope[:, tile].astype(jnp.float32)).astype(jnp.bfloat16)
            acc[...] += dot_nt(grad, w_in[kind, :, tile])
            if kind == 1:
                activated[:, tile] = grad

        b_send[kind] = acc[...].astype(jnp.bfloat16)
        grad_back_ref[kind, own_rows, :] = b_send[kind, own_rows, :]
        spread_kind(kind, b_send, grad_back_ref, b_sems)
        if kind == 1:

            @pl.loop(0, FF_TILES, unroll=True)
            def _(index):
                tile = tile_of(index)
                weights = dot_tn(x_land[1], activated[:, tile]).astype(jnp.bfloat16)
                in_grad[:, :, :, tile] = weights.reshape(4, 4, CAPACITY, FF_TILE)

            in_plane.start_far()
            store(in_grad, in_grad_ref)
    lanes = lax.broadcasted_iota(jnp.int32, (EXPERT_ROWS, 128), 1)
    match_send[0] = jnp.where(lanes < 64, matches[0], matches[1])
    match_ref[0, own_rows, :] = match_send[0, own_rows, :]
    spread_kind(0, match_send, match_ref, match_sems)
    plane.second()
    plane.third(x_sum_ref, y_sum_ref)
    collect_kind(0, match_ref, match_sems)
    for kind in (1, 0):
        collect_kind(kind, grad_back_ref, b_sems)
    in_plane.settle_far()
    store(in_first, in_first_ref)
    for target, sem in used:
        seven(target, sem).wait()
    plane.drain()
    in_plane.drain()
    for copy in stores:
        copy.wait()


def experts_both_ways(sent, grad_rows, in_frozen, out_frozen, in_new, out_new):
    def shape(*dims, dtype=HALF_TYPE):
        return jax.ShapeDtypeStruct(dims, dtype)

    return pl.pallas_call(
        expert_kernel,
        out_shape=[
            shape(2, EXPERT_ROWS, WIDTH),
            shape(4, 4, CAPACITY, FF),
            shape(4, 2, CAPACITY, FF // 2),
            shape(2, EXPERT_ROWS, WIDTH),
            shape(1, EXPERT_ROWS, 128, dtype=FULL_TYPE),
            shape(4, CAPACITY, FF // 2),
            shape(4, CAPACITY, FF // 2),
        ],
        in_specs=[anywhere()] * 6,
        out_specs=[anywhere()] * 3 + [vmem()] * 4,
        scratch_shapes=[
            pltpu.VMEM((2, WIDTH, FF), HALF_TYPE),
            pltpu.VMEM((2, FF, WIDTH), HALF_TYPE),
            pltpu.VMEM((2, EXPERT_ROWS, WIDTH), HALF_TYPE),
            pltpu.VMEM((2, EXPERT_ROWS, WIDTH), HALF_TYPE),
            pltpu.VMEM((EXPERT_ROWS, FF), HALF_TYPE),
            pltpu.VMEM((EXPERT_ROWS, FF), HALF_TYPE),
            pltpu.VMEM((EXPERT_ROWS, WIDTH), FULL_TYPE),
            pltpu.VMEM((2, EXPERT_ROWS, WIDTH), HALF_TYPE),
            pltpu.VMEM((2, EXPERT_ROWS, WIDTH), HALF_TYPE),
            pltpu.VMEM((4, 4, CAPACITY, FF), HALF_TYPE),
            pltpu.VMEM((4, 4, CAPACITY, FF), HALF_TYPE),
            pltpu.VMEM((4, 2, CAPACITY, FF // 2), HALF_TYPE),
            pltpu.VMEM((4, 2, CAPACITY, FF // 2), HALF_TYPE),
            pltpu.VMEM((4, 2, CAPACITY, FF // 2), HALF_TYPE),
            pltpu.VMEM((4, 2, CAPACITY, FF // 2), HALF_TYPE),
            pltpu.VMEM((1, EXPERT_ROWS, 128), FULL_TYPE),
            pltpu.SemaphoreType.DMA((6,)),
            pltpu.SemaphoreType.DMA((2, 2)),
            pltpu.SemaphoreType.DMA((2, 2)),
            pltpu.SemaphoreType.DMA((2, 2)),
            pltpu.SemaphoreType.DMA((2, 2)),
            pltpu.SemaphoreType.DMA((2, 12)),
            pltpu.SemaphoreType.DMA((2, 4)),
            pltpu.SemaphoreType.DMA((4,)),
        ],
        compiler_params=pltpu.CompilerParams(
            collective_id=2, has_side_effects=True, vmem_limit_bytes=62 * 2**20
        ),
    )(sent, grad_rows, in_frozen, out_frozen, in_new, out_new)


def slot_rows(place):
    return pl.ds(pl.multiple_of(place * CAPACITY, CAPACITY), CAPACITY)


def back_kernel(
    kind_ref,
    tokens_ref,
    gain_ref,
    gain_two_ref,
    grad_ref,
    residual_ref,
    info_ref,
    match_ref,
    grad_back_ref,
    router_ref,
    proj_ref,
    hidden_two_ref,
    total_ref,
    query_hbm,
    key_hbm,
    value_hbm,
    heads_hbm,
    weight_hbm,
    hidden_hbm,
    attended_hbm,
    in_grad_hbm,
    in_first_hbm,
    returned_hbm,
    x_part_hbm,
    y_part_hbm,
    mixed_ref,
    tokens_grad_ref,
    in_sum_ref,
    out_sum_ref,
    dense_sum_ref,
    qkv_sum_ref,
    dense_land,
    query_ref,
    key_ref,
    value_ref,
    heads_ref,
    weight,
    hidden_ref,
    attended_ref,
    x_part,
    y_part,
    out_land,
    returned,
    grad_residual,
    grad_sent,
    grad_out,
    stacked,
    grad_stacked,
    grad_query,
    grad_key,
    grad_value,
    projected,
    part_sib,
    part_own,
    land_sib,
    land_half,
    land_full,
    big,
    big_first,
    big_direct,
    big_combined,
    big_x,
    big_y,
    big_land,
    mid,
    mid_first,
    mid_direct,
    mid_combined,
    mid_x,
    mid_y,
    mid_land,
    qkv,
    qkv_first,
    qkv_direct,
    qkv_combined,
    qkv_x,
    qkv_y,
    qkv_land,
    dense_send,
    weight_sems,
    load_sems,
    grad_sems,
    sib_sems,
    ring_sems,
    big_sems,
    out_spread,
    big_spread,
    mid_sems,
    mid_spread,
    qkv_sems,
    qkv_spread,
    dense_sems,
    returned_sems,
):
    z, core = here()
    mine = z * 2 + core
    up, down, far = lax.rem(z + 1, CHIPS), lax.rem(z + 3, CHIPS), lax.rem(z + 2, CHIPS)
    barrier = pltpu.get_barrier_semaphore()
    greet(barrier)
    greet_plane(barrier)
    loads = []
    for index, (source, target) in enumerate(
        (
            (in_grad_hbm, big),
            (in_first_hbm, big_first),
            (x_part_hbm, x_part),
            (y_part_hbm, y_part),
            (
                returned_hbm.at[:, slot_rows(mine), :],
                returned.at[:, slot_rows(mine), :],
            ),
            (attended_hbm, attended_ref),
            (query_hbm, query_ref),
            (key_hbm, key_ref),
            (value_hbm, value_ref),
            (heads_hbm, heads_ref),
            (hidden_hbm, hidden_ref),
        )
    ):
        copy = pltpu.make_async_copy(source, target, load_sems.at[index])
        copy.start()
        loads.append(copy)
    weight_loads = load_windows(weight_hbm, weight, weight_sems, z)

    info = info_ref[...]
    columns = jnp.transpose(
        jnp.concatenate([info, jnp.zeros((120, BLOCK), jnp.float32)], axis=0)
    )
    lane_ids = lax.broadcasted_iota(jnp.int32, (BLOCK, SLOTS), 1).astype(jnp.float32)
    at_zero, at_one = lane_ids == columns[:, 0:1], lane_ids == columns[:, 1:2]
    ids = lax.broadcasted_iota(jnp.int32, (SLOTS, BLOCK), 0).astype(jnp.float32)
    lines = match_ref[0]
    match = jnp.concatenate(
        [jnp.broadcast_to(lines[:, lane : lane + 1], (EXPERT_ROWS, BLOCK)) for lane in (0, 64)],
        axis=0,
    )
    parts = []
    for place, gate in ((0, 2), (1, 3)):
        value = jnp.sum(
            jnp.where(ids == info[place : place + 1, :], match, 0.0), axis=0, keepdims=True
        )
        used = info[gate : gate + 1, :].astype(jnp.bfloat16).astype(jnp.float32)
        ratio = jnp.where(used > 0.0, info[gate : gate + 1, :] / jnp.where(used > 0.0, used, 1.0), 1.0)
        parts.append(value * ratio)
    gap = parts[0] * info[3:4, :] - parts[1] * info[2:3, :]
    names = lax.broadcasted_iota(jnp.int32, (EXPERTS, BLOCK), 0).astype(jnp.float32)
    pick_zero = jnp.where(names == info[4:5, :], 1.0, 0.0)
    pick_one = jnp.where(names == info[5:6, :], 1.0, 0.0)
    grad_logits = (gap * (pick_zero - pick_one)).astype(jnp.bfloat16)
    chosen = jnp.where(at_zero | at_one, 1.0, 0.0).astype(jnp.bfloat16)
    grad_two = (
        dot_tn(grad_logits, router_ref[...])
        + dot_nn(chosen[:, :EXPERT_ROWS], grad_back_ref[0])
        + dot_nn(chosen[:, EXPERT_ROWS:], grad_back_ref[1])
    )
    normed_two, inverse_two = norm_parts(residual_ref[...])
    gain_two_grad = jnp.sum(grad_two * normed_two, axis=0, keepdims=True)
    grad_residual[...] = grad_ref[...].astype(jnp.float32) + norm_back(
        grad_two * gain_two_ref[...][None], normed_two, inverse_two
    )
    grad_branch = grad_residual[...].astype(jnp.bfloat16)
    for chip in range(CHIPS):
        first = (chip + chip // 2) * 128
        grad_sent[chip] = dot_nt(grad_branch, proj_ref[first : first + PAD, :]).astype(
            jnp.bfloat16
        )
    pl.semaphore_wait(barrier, 13)
    owner_core = lax.rem(core + z, 2)
    grad_send, grad_recv = grad_sems.at[0], grad_sems.at[1]

    @pl.loop(0, CHIPS)
    def _(step):
        chip = lax.rem(z + step, CHIPS)
        mine_too = (chip == z) & (owner_core == core)

        @pl.when(jnp.logical_not(mine_too))
        def _():
            push(
                grad_sent.at[chip],
                grad_out.at[z],
                grad_send,
                grad_recv,
                chip,
                z,
                device(chip, owner_core),
            ).start()

        @pl.when(mine_too)
        def _():
            grad_out[z] = grad_sent[chip]

    for step in range(1, 8):
        place = lax.rem(mine + step, 8)
        copy = push(
            returned_hbm.at[:, slot_rows(place), :],
            returned.at[:, slot_rows(mine), :],
            returned_sems.at[0],
            returned_sems.at[1],
            0,
            0,
            (lax.axis_index("dp"), place),
        )
        copy.start()
    for load in loads[:4]:
        load.wait()
    big_sum = PlaneSum(big, big_first, big_direct, big_combined, big_sems.at[0], big_sems.at[1])
    big_sum.start_near()
    big_sum.second(waits=False)
    loads[5].wait()
    for chip in range(CHIPS):
        grads = dot_tn(attended_ref[chip], grad_branch).astype(jnp.bfloat16)
        first = (chip % 2) * HD
        for y in range(4):
            start = first + y * CAPACITY
            mid[chip, y, :, :WIDTH] = grads[start : start + CAPACITY]
    narrow = jnp.concatenate(
        [
            dot_nn(grad_logits, hidden_two_ref[...]),
            gain_two_grad,
            jnp.zeros((111, WIDTH), jnp.float32),
        ],
        axis=0,
    )
    mid[:, :, :, WIDTH : WIDTH + 128] = (
        jnp.transpose(narrow).astype(jnp.bfloat16).reshape(4, 4, CAPACITY, 128)
    )
    mid[:, :, :, WIDTH + 128 :] = jnp.zeros((4, 4, CAPACITY, 128), jnp.bfloat16)
    mid_sum = PlaneSum(mid, mid_first, mid_direct, mid_combined, mid_sems.at[0], mid_sems.at[1])
    mid_sum.start()
    out_sum = PlaneSpread(x_part, y_part, out_land, out_spread.at[0], out_spread.at[1])
    out_sum.start()

    grad_key[...] = jnp.zeros_like(grad_key)
    grad_value[...] = jnp.zeros_like(grad_value)
    projected[...] = jnp.zeros_like(projected)
    for load in loads[6:10]:
        load.wait()
    kind_bias = kind_ref[0].astype(jnp.float32) * NEGATIVE

    def attend(step):
        slot = lax.rem(z + step, CHIPS)
        block = slot * 2 + lax.rem(core + slot, 2)

        @pl.when(block != mine)
        def _():
            landed(grad_out.at[slot], grad_send, grad_recv, slot)

        queries = query_ref[block]
        grads = grad_out[slot]
        products = grads.astype(jnp.float32) * heads_ref[slot].astype(jnp.float32)
        selector = jnp.concatenate(
            [head_mask(z, head, 1.0, jnp.float32) for head in range(LOCAL_HEADS)]
            + [jnp.zeros((8 - LOCAL_HEADS, PAD), jnp.float32)],
            axis=0,
        )
        deltas = lax.dot_general(
            selector,
            products,
            (((1,), (1,)), ((), ())),
            preferred_element_type=jnp.float32,
            precision=lax.Precision.HIGHEST,
        )
        for head in range(LOCAL_HEADS):
            part = slice(head * BLOCK, (head + 1) * BLOCK)
            stacked[part, :] = queries * head_mask(z, head, HD ** (-0.5), jnp.bfloat16)
            grad_stacked[part, :] = grads * head_mask(z, head, 1.0, jnp.bfloat16)
        totals = total_ref[slot]
        delta_row = jnp.concatenate(
            [deltas[head : head + 1, :] for head in range(LOCAL_HEADS)], axis=1
        )
        total_row = jnp.concatenate(
            [totals[head : head + 1, :] for head in range(LOCAL_HEADS)], axis=1
        )

        def work(rows, bias, is_diagonal):
            keys, values = key_ref[rows, :], value_ref[rows, :]
            probs = jnp.exp(dot_nt(keys, stacked[...]) - (total_row - bias))
            if is_diagonal:
                row = lax.broadcasted_iota(jnp.int32, (BLOCK, STACK), 0)
                column = lax.broadcasted_iota(jnp.int32, (BLOCK, STACK), 1)
                probs = jnp.where(row <= lax.rem(column, BLOCK), probs, 0.0)
            grad_probs = dot_nt(values, grad_stacked[...])
            grad_scores = (probs * (grad_probs - delta_row)).astype(jnp.bfloat16)
            grad_value[rows, :] += dot_nn(probs.astype(jnp.bfloat16), grad_stacked[...])
            grad_key[rows, :] += dot_nn(grad_scores, stacked[...])
            return dot_tn(grad_scores, keys)

        grad_query[...] = work(block_rows(block), 0.0, True)

        @pl.when(block != 2 * slot)
        def _():
            grad_query[...] += work(block_rows(block - 1), 0.0, False)

        @pl.loop(0, slot)
        def _(chunk):
            bias = jnp.where((slot >= 2) & (chunk < 2), kind_bias, 0.0)
            grad_query[...] += work(chunk_rows(chunk), bias, False)

        combined = jnp.zeros((BLOCK, PAD), jnp.float32)
        for head in range(LOCAL_HEADS):
            part = slice(head * BLOCK, (head + 1) * BLOCK)
            combined += grad_query[part, :] * head_mask(z, head, HD ** (-0.5), jnp.float32)
        projected[block_rows(block), :PAD] = combined.astype(jnp.bfloat16)

    pl.loop(0, CHIPS)(attend)
    projected[:, PAD : 2 * PAD] = grad_key[...].astype(jnp.bfloat16)
    projected[:, 2 * PAD :] = grad_value[...].astype(jnp.bfloat16)
    for load in weight_loads:
        load.wait()

    def partial(chip, which):
        return dot_nt(projected[block_rows(chip * 2 + which), :], weight[...])

    sib_send, sib_recv = sib_sems.at[0], sib_sems.at[1]

    def sib_copy(index):
        return push(
            part_sib.at[index],
            land_sib.at[index],
            sib_send,
            sib_recv,
            index,
            index,
            device(z, 1 - core),
        )

    order = (far, up, down, z)
    for index, chip in enumerate(order):
        part_sib[index] = partial(chip, 1 - core).astype(jnp.bfloat16)
        sib_copy(index).start()

    loads[10].wait()
    for tile in range(3):
        lanes = slice(tile * PAD, (tile + 1) * PAD)
        weights = dot_tn(hidden_ref[...], projected[:, lanes]).astype(jnp.bfloat16)
        qkv[:, :, :, lanes] = weights.reshape(4, 4, CAPACITY, PAD)
    qkv_sum = PlaneSum(
        qkv, qkv_first, qkv_direct, qkv_combined, qkv_sems.at[0], qkv_sems.at[1]
    )
    qkv_sum.start()
    mid_sum.second()


    def own(index):
        value = partial(order[index], core)
        landed(land_sib.at[index], sib_send, sib_recv, index)
        return value + land_sib[index].astype(jnp.float32)

    first, second = pl.ds(0, HALF), pl.ds(HALF, HALF)
    ring_send, ring_recv = ring_sems.at[0], ring_sems.at[1]
    copies = []

    def ring(source, target, index, where):
        copy = push(source, target, ring_send, ring_recv, index, index, where)
        copy.start()
        copies.append(copy)

    above, below = device(up, core), device(down, core)
    part_own[0] = own(0).astype(jnp.bfloat16)
    ring(part_own.at[0, first], land_half.at[0], 0, above)
    ring(part_own.at[0, second], land_half.at[1], 1, below)
    part_own[1] = own(1).astype(jnp.bfloat16)
    ring(part_own.at[1, second], land_full.at[0, second], 2, above)
    part_own[2] = own(2).astype(jnp.bfloat16)
    ring(part_own.at[2, first], land_full.at[1, first], 3, below)
    grad_one = own(3)
    qkv_sum.second()
    landed(land_half.at[0], ring_send, ring_recv, 0)
    part_own[1, first, :] = added(part_own[1, first, :], land_half[0]).astype(jnp.bfloat16)
    ring(part_own.at[1, first], land_full.at[0, first], 4, above)
    landed(land_half.at[1], ring_send, ring_recv, 1)
    part_own[2, second, :] = added(part_own[2, second, :], land_half[1]).astype(jnp.bfloat16)
    ring(part_own.at[2, second], land_full.at[1, second], 5, below)
    mid_sum.third(mid_x, mid_y)
    mid_total = PlaneSpread(mid_x, mid_y, mid_land, mid_spread.at[0], mid_spread.at[1])
    mid_total.start()
    qkv_sum.third(qkv_x, qkv_y)
    qkv_total = PlaneSpread(qkv_x, qkv_y, qkv_land, qkv_spread.at[0], qkv_spread.at[1])
    qkv_total.start()
    big_sum.third(big_x, big_y)
    big_total = PlaneSpread(big_x, big_y, big_land, big_spread.at[0], big_spread.at[1])
    big_total.start()
    loads[4].wait()
    seven = returned.at[:, pl.ds(0, 7 * CAPACITY), :]
    pltpu.make_async_copy(seven, seven, returned_sems.at[1, 0]).wait()
    mixing = (
        jnp.where(at_zero, columns[:, 2:3], 0.0) + jnp.where(at_one, columns[:, 3:4], 0.0)
    ).astype(jnp.bfloat16)
    mixed_ref[...] = (
        residual_ref[...]
        + dot_nn(mixing[:, :EXPERT_ROWS], returned[0])
        + dot_nn(mixing[:, EXPERT_ROWS:], returned[1])
    ).astype(jnp.bfloat16)
    out_left, out_right = out_sum.total()
    out_sum_ref[:, : FF // 2] = out_left
    out_sum_ref[:, FF // 2 :] = out_right
    mid_left, mid_right = mid_total.total()
    qkv_left, qkv_right = qkv_total.total()
    share = CAPACITY // 8
    line = jnp.concatenate([mid_left, mid_right, qkv_left, qkv_right], axis=1)
    for piece in range(8):
        rows = slice(piece * share, (piece + 1) * share)
        dense_send[piece] = jnp.concatenate(
            [line[rows, :LINE], line[rows, LINE:], jnp.zeros((16 - 2 * share, LINE), jnp.float32)],
            axis=0,
        ).astype(jnp.bfloat16)
    dense_copies = []
    for step in range(1, 8):
        place = lax.rem(mine + step, 8)
        copy = push(
            dense_send.at[place],
            dense_land.at[mine],
            dense_sems.at[0],
            dense_sems.at[1],
            step - 1,
            step - 1,
            (lax.axis_index("dp"), place),
        )
        copy.start()
        dense_copies.append(copy)
    dense_land[mine] = dense_send[mine]
    landed(land_full.at[0, second], ring_send, ring_recv, 2)
    landed(land_full.at[1, first], ring_send, ring_recv, 3)
    landed(land_full.at[0, first], ring_send, ring_recv, 4)
    landed(land_full.at[1, second], ring_send, ring_recv, 5)
    grad_one += added(land_full[0], land_full[1])
    normed_one, inverse_one = norm_parts(tokens_ref[...].astype(jnp.float32))
    tokens_grad_ref[...] = grad_residual[...] + norm_back(
        grad_one * gain_ref[...][None], normed_one, inverse_one
    )
    left, right = big_total.total()
    in_sum_ref[:, : FF // 2] = left
    in_sum_ref[:, FF // 2 :] = right
    for step in range(1, 8):
        landed(
            dense_land.at[lax.rem(mine + 8 - step, 8)],
            dense_sems.at[0],
            dense_sems.at[1],
            step - 1,
        )
    lines = [dense_land[place].astype(jnp.float32) for place in range(8)]
    total = sum(lines[1:], lines[0])
    total = jnp.concatenate([total[:share], total[share : 2 * share]], axis=1)
    dense_sum_ref[...] = total[:, :DENSE]
    qkv_sum_ref[...] = jnp.zeros_like(qkv_sum_ref)
    for chip in range(CHIPS):
        line = lines[2 * chip] + lines[2 * chip + 1]
        line = jnp.concatenate([line[:share], line[share : 2 * share]], axis=1)[:, DENSE:]
        for part in range(3):
            start = part * WIDTH + (chip + chip // 2) * 128
            qkv_sum_ref[:, start : start + PAD] += line[:, part * PAD : (part + 1) * PAD]
    pltpu.make_async_copy(seven, seven, returned_sems.at[0, 0]).wait()
    for copy in dense_copies + copies:
        copy.wait_send()
    for user in (big_sum, out_sum, big_total, mid_sum, mid_total, qkv_sum, qkv_total):
        user.drain()
    for index in range(CHIPS):
        sib_copy(index).wait_send()

    @pl.loop(0, CHIPS)
    def _(chip):
        @pl.when((chip != z) | (owner_core != core))
        def _():
            push(
                grad_sent.at[chip],
                grad_out.at[chip],
                grad_send,
                grad_recv,
                chip,
                chip,
                device(z, 1 - core),
            ).wait_send()


def plane_scratch(lanes):
    return [
        pltpu.VMEM((4, 4, CAPACITY, lanes), HALF_TYPE),
        pltpu.VMEM((4, 2, CAPACITY, lanes // 2), HALF_TYPE),
        pltpu.VMEM((4, 2, CAPACITY, lanes // 2), HALF_TYPE),
        pltpu.VMEM((4, 2, CAPACITY, lanes // 2), HALF_TYPE),
        pltpu.VMEM((4, CAPACITY, lanes // 2), HALF_TYPE),
        pltpu.VMEM((4, CAPACITY, lanes // 2), HALF_TYPE),
        pltpu.VMEM((6, CAPACITY, lanes // 2), HALF_TYPE),
    ]


def back(*operands):
    def shape(*dims, dtype=FULL_TYPE):
        return jax.ShapeDtypeStruct(dims, dtype)

    def pair(count):
        return pltpu.SemaphoreType.DMA((2, count))

    return pl.pallas_call(
        back_kernel,
        out_shape=[
            shape(BLOCK, WIDTH, dtype=HALF_TYPE),
            shape(BLOCK, WIDTH),
            shape(CAPACITY, FF),
            shape(CAPACITY, FF),
            shape(CAPACITY // 8, DENSE),
            shape(CAPACITY // 8, 3 * WIDTH),
        ],
        in_specs=[smem()] + [vmem()] * 12 + [anywhere()] * 12,
        out_specs=[vmem()] * 6,
        scratch_shapes=[
            pltpu.VMEM((8, 16, LINE), HALF_TYPE),
            pltpu.VMEM((8, BLOCK, PAD), HALF_TYPE),
            pltpu.VMEM((LONG, PAD), HALF_TYPE),
            pltpu.VMEM((LONG, PAD), HALF_TYPE),
            pltpu.VMEM((CHIPS, BLOCK, PAD), HALF_TYPE),
            pltpu.VMEM((WIDTH, 3 * PAD), HALF_TYPE),
            pltpu.VMEM((LONG, WIDTH), HALF_TYPE),
            pltpu.VMEM((CHIPS, BLOCK, PAD), HALF_TYPE),
            pltpu.VMEM((4, CAPACITY, FF // 2), HALF_TYPE),
            pltpu.VMEM((4, CAPACITY, FF // 2), HALF_TYPE),
            pltpu.VMEM((6, CAPACITY, FF // 2), HALF_TYPE),
            pltpu.VMEM((2, EXPERT_ROWS, WIDTH), HALF_TYPE),
            pltpu.VMEM((BLOCK, WIDTH), FULL_TYPE),
            pltpu.VMEM((CHIPS, BLOCK, PAD), HALF_TYPE),
            pltpu.VMEM((CHIPS, BLOCK, PAD), HALF_TYPE),
            pltpu.VMEM((STACK, PAD), HALF_TYPE),
            pltpu.VMEM((STACK, PAD), HALF_TYPE),
            pltpu.VMEM((STACK, PAD), FULL_TYPE),
            pltpu.VMEM((LONG, PAD), FULL_TYPE),
            pltpu.VMEM((LONG, PAD), FULL_TYPE),
            pltpu.VMEM((LONG, 3 * PAD), HALF_TYPE),
            pltpu.VMEM((CHIPS, BLOCK, WIDTH), HALF_TYPE),
            pltpu.VMEM((CHIPS - 1, BLOCK, WIDTH), HALF_TYPE),
            pltpu.VMEM((CHIPS, BLOCK, WIDTH), HALF_TYPE),
            pltpu.VMEM((2, HALF, WIDTH), HALF_TYPE),
            pltpu.VMEM((2, BLOCK, WIDTH), HALF_TYPE),
            *plane_scratch(FF),
            *plane_scratch(DENSE),
            *plane_scratch(3 * PAD),
            pltpu.VMEM((8, 16, LINE), HALF_TYPE),
            pltpu.SemaphoreType.DMA((3,)),
            pltpu.SemaphoreType.DMA((11,)),
            pair(CHIPS),
            pair(CHIPS),
            pair(6),
            pair(12),
            pair(6),
            pair(6),
            pair(12),
            pair(6),
            pair(12),
            pair(6),
            pair(7),
            pair(1),
        ],
        compiler_params=pltpu.CompilerParams(
            collective_id=1, has_side_effects=True, vmem_limit_bytes=60 * 2**20
        ),
    )(*operands)


def as_row(column):
    size = column.shape[0]
    row = lax.broadcasted_iota(jnp.int32, (size, size), 0)
    lane = lax.broadcasted_iota(jnp.int32, (size, size), 1)
    return jnp.sum(jnp.where(row == lane, column, 0.0), axis=0, keepdims=True)


def finish_kernel(
    mixed_ref,
    tokens_grad_ref,
    in_sum_ref,
    out_sum_ref,
    dense_ref,
    qkv_ref,
    weight_ref,
    gain_ref,
    mixed_out,
    tokens_grad_out,
    gain_out,
    qkv_out,
    proj_out,
    gain_two_out,
    router_out,
    in_out,
    out_out,
    weight,
    sem,
):
    mixed_out[0] = mixed_ref[...]
    tokens_grad_out[0] = tokens_grad_ref[...]
    in_out[0] = in_sum_ref[...]
    for part in range(4):
        rows = slice(part * CAPACITY, (part + 1) * CAPACITY)
        out_out[0, rows, :] = out_sum_ref[:, part * WIDTH : (part + 1) * WIDTH]
    share = CAPACITY // 8
    first = (lax.axis_index("dp") * 8 + lax.axis_index("expert")) * share
    start = pl.multiple_of(jnp.minimum(first // 16, WIDTH // 16 - 2) * 16, 16)
    load = pltpu.make_async_copy(weight_ref.at[pl.ds(start, 32), :], weight, sem)
    load.start()
    qkv_out[...] = qkv_ref[...]
    dense = dense_ref[...]
    proj_out[...] = dense[:, :WIDTH]
    router_out[...] = dense[:, WIDTH : WIDTH + EXPERTS]
    gain_two_out[...] = as_row(dense[:, WIDTH + EXPERTS : WIDTH + EXPERTS + 1])
    row = lax.broadcasted_iota(jnp.int32, (share, 32), 0)
    column = lax.broadcasted_iota(jnp.int32, (share, 32), 1)
    chosen = jnp.where(column == row + (first - start), 1.0, 0.0).astype(jnp.bfloat16)
    row = lax.broadcasted_iota(jnp.int32, (share, WIDTH), 0)
    column = lax.broadcasted_iota(jnp.int32, (share, WIDTH), 1)
    gain = jnp.sum(
        jnp.where(column == row + first, gain_ref[...][None], 0.0), axis=1, keepdims=True
    )
    load.wait()
    products = qkv_ref[...] * dot_nn(chosen, weight[...])
    gain_out[...] = as_row(jnp.sum(products, axis=1, keepdims=True) / gain)


def finish(*operands):
    def shape(*dims, dtype=FULL_TYPE):
        return jax.ShapeDtypeStruct(dims, dtype)

    share = CAPACITY // 8
    shapes = [
        shape(1, BLOCK, WIDTH, dtype=HALF_TYPE),
        shape(1, BLOCK, WIDTH),
        shape(1, share),
        shape(share, 3 * WIDTH),
        shape(share, WIDTH),
        shape(1, share),
        shape(share, EXPERTS),
        shape(1, CAPACITY, FF),
        shape(1, 4 * CAPACITY, WIDTH),
    ]
    return pl.pallas_call(
        finish_kernel,
        out_shape=shapes,
        in_specs=[vmem()] * 6 + [anywhere(), vmem()],
        out_specs=[vmem()] * 9,
        scratch_shapes=[
            pltpu.VMEM((32, 3 * WIDTH), HALF_TYPE),
            pltpu.SemaphoreType.DMA,
        ],
        compiler_params=pltpu.CompilerParams(vmem_limit_bytes=62 * 2**20),
    )(*operands)


def on_device(
    tokens,
    group_kind,
    routes,
    norm1_gain,
    qkv_weight,
    proj_weight,
    norm2_gain,
    router_weight,
    frozen_in,
    frozen_out,
    new_in,
    new_out,
    out_grad,
):
    width = WIDTH
    router = router_weight.T
    (
        hidden,
        queries,
        keys,
        values,
        heads,
        attended,
        residual,
        hidden_two,
        sent,
        grad_rows,
        totals,
        info,
    ) = front(
        group_kind,
        tokens[0],
        norm1_gain,
        qkv_weight,
        out_grad[0],
        routes[0].T,
        proj_weight,
        norm2_gain,
        router,
    )
    returned, in_grad, in_first, grad_back, match, x_part, y_part = experts_both_ways(
        sent, grad_rows, frozen_in[0], frozen_out[0], new_in[0], new_out[0]
    )
    mixed, tokens_grad, in_sum, out_sum, dense_sum, qkv_sum = back(
        group_kind,
        tokens[0],
        norm1_gain,
        norm2_gain,
        out_grad[0],
        residual,
        info,
        match,
        grad_back,
        router,
        proj_weight,
        hidden_two,
        totals,
        queries,
        keys,
        values,
        heads,
        qkv_weight,
        hidden.reshape(LONG, width),
        attended,
        in_grad,
        in_first,
        returned,
        x_part,
        y_part,
    )
    outputs = finish(
        mixed, tokens_grad, in_sum, out_sum, dense_sum, qkv_sum, qkv_weight, norm1_gain
    )
    return tuple(
        value[0] if index in (2, 5) else value for index, value in enumerate(outputs)
    )


def solution(mesh):
    return jax.shard_map(
        on_device,
        mesh=mesh,
        in_specs=(
            P("dp", "expert", None),
            P("dp"),
            P("dp", "expert", None),
            P(),
            P(),
            P(),
            P(),
            P(),
            P("expert", None, None),
            P("expert", None, None),
            P("expert", None, None),
            P("expert", None, None),
            P("dp", "expert", None),
        ),
        out_specs=(
            P("dp", "expert", None),
            P("dp", "expert", None),
            P(("dp", "expert")),
            P(("dp", "expert"), None),
            P(("dp", "expert"), None),
            P(("dp", "expert")),
            P(("dp", "expert"), None),
            P("expert", "dp", None),
            P("expert", "dp", None),
        ),
        check_vma=False,
    )
```

```python
import jax
import jax.numpy as jnp
from jax import lax
from jax.experimental import pallas as pl
from jax.experimental.pallas import tpu as pltpu
from jax.sharding import PartitionSpec as P

HEADS = 12
HD = 64
LONG = 2048
MESH_ID = pl.DeviceIdType.MESH
CHIPS = 4
PAD = 256
BLOCK = 256
HALF = BLOCK // 2
CHUNK = 512
CHUNKS = LONG // CHUNK
LOCAL_HEADS = HEADS // CHIPS
STACK = LOCAL_HEADS * BLOCK
NEGATIVE = -1e30
WIDTH = 768
EXPERTS = 16
SLOTS = 768
EXPERT_ROWS = 384
CAPACITY = 48
FF = 3072
FF_TILE = 768
FF_TILES = 4
DENSE = 1024
LINE = (DENSE + 3 * PAD) // 2
HALF_TYPE = jnp.bfloat16
FULL_TYPE = jnp.float32

epsilon = 1e-05


def norm_parts(values):
    average = jnp.mean(values, axis=-1, keepdims=True)
    centred = values - average
    variance = jnp.mean(centred * centred, axis=-1, keepdims=True)
    inverse = lax.rsqrt(variance + epsilon)
    return (centred * inverse, inverse)


def norm_back(grad_normed, normed, inverse):
    first_mean = jnp.mean(grad_normed, axis=-1, keepdims=True)
    second_mean = jnp.mean(grad_normed * normed, axis=-1, keepdims=True)
    return inverse * (grad_normed - first_mean - normed * second_mean)


def here():
    position = lax.axis_index("expert")
    return position // 2, lax.rem(position, 2)


def device(z, core):
    return (lax.axis_index("dp"), z * 2 + core)


def greet(barrier):
    position = lax.axis_index("expert")
    for step in range(1, 8):
        pl.semaphore_signal(
            barrier,
            inc=1,
            device_id=(lax.axis_index("dp"), lax.rem(position + step, 8)),
            device_id_type=MESH_ID,
        )


def push(source, target, sends, receives, index_here, index_there, where):
    return pltpu.make_async_remote_copy(
        src_ref=source,
        dst_ref=target,
        send_sem=sends.at[index_here],
        recv_sem=receives.at[index_there],
        device_id=where,
        device_id_type=MESH_ID,
    )


def landed(region, sends, receives, index):
    z, core = here()
    push(region, region, sends, receives, index, index, device(z, 1 - core)).wait_recv()


def dot_nn(left, right):
    return jnp.dot(left, right, preferred_element_type=jnp.float32)


def dot_nt(left, right):
    return lax.dot_general(
        left, right, (((1,), (1,)), ((), ())), preferred_element_type=jnp.float32
    )


def dot_tn(left, right):
    return lax.dot_general(
        left, right, (((0,), (0,)), ((), ())), preferred_element_type=jnp.float32
    )


def window(chip):
    return (chip + chip // 2) * 128, lax.rem(chip, 2) * HD


def head_mask(chip, head, value, dtype):
    start = window(chip)[1] + head * HD
    lanes = lax.broadcasted_iota(jnp.int32, (1, PAD), 1)
    inside = (lanes >= start) & (lanes < start + HD)
    return jnp.where(inside, value, 0.0).astype(dtype)


def lane_tiles(values, combine):
    result = values[:, :128]
    for start in range(128, values.shape[1], 128):
        result = combine(result, values[:, start : start + 128])
    return result


def block_rows(block):
    return pl.ds(pl.multiple_of(block * BLOCK, BLOCK), BLOCK)


def chunk_rows(chunk):
    return pl.ds(pl.multiple_of(chunk * CHUNK, CHUNK), CHUNK)


def load_windows(weight_ref, target, sems, chip):
    copies = []
    for part in range(3):
        first = pl.multiple_of(part * WIDTH + window(chip)[0], 128)
        copies.append(
            pltpu.make_async_copy(
                weight_ref.at[:, pl.ds(first, PAD)],
                target.at[:, pl.ds(part * PAD, PAD)],
                sems.at[part],
            )
        )
    for copy in copies:
        copy.start()
    return copies


class RingGather:
    def __init__(self, ref, sends, receives):
        self.ref, self.sends, self.receives = ref, sends, receives
        self.z, self.core = here()
        self.up, self.down = lax.rem(self.z + 1, CHIPS), lax.rem(self.z + 3, CHIPS)
        self.far = lax.rem(self.z + 2, CHIPS)
        self.copies = []

    def region(self, chip, core, half):
        rows = slice(None) if half is None else pl.ds(half * HALF, HALF)
        return self.ref.at[chip * 2 + core, rows]

    def send(self, index, chip, half, where):
        region = self.region(chip, self.core, half)
        copy = push(region, region, self.sends, self.receives, index, index, where)
        copy.start()
        self.copies.append(copy)

    def wait(self, index, chip, core, half):
        landed(self.region(chip, core, half), self.sends, self.receives, index)

    def above(self):
        return device(self.up, self.core)

    def below(self):
        return device(self.down, self.core)

    def beside(self):
        return device(self.z, 1 - self.core)

    def start(self):
        self.send(0, self.z, 0, self.above())
        self.send(1, self.z, 1, self.below())
        self.send(2, self.z, 1, self.above())
        self.send(3, self.z, 0, self.below())
        self.send(4, self.z, None, self.beside())

    def relay(self):
        self.wait(0, self.down, self.core, 0)
        self.send(5, self.down, 0, self.above())
        self.send(7, self.down, 0, self.beside())
        self.wait(1, self.up, self.core, 1)
        self.send(6, self.up, 1, self.below())
        self.send(8, self.up, 1, self.beside())

    def share(self):
        self.wait(2, self.down, self.core, 1)
        self.send(9, self.down, 1, self.beside())
        self.wait(3, self.up, self.core, 0)
        self.send(10, self.up, 0, self.beside())

    def share_far(self):
        self.wait(5, self.far, self.core, 0)
        self.send(11, self.far, 0, self.beside())
        self.wait(6, self.far, self.core, 1)
        self.send(12, self.far, 1, self.beside())

    def other_own(self):
        self.wait(4, self.z, 1 - self.core, None)

    def other_down(self):
        self.wait(7, self.down, 1 - self.core, 0)
        self.wait(9, self.down, 1 - self.core, 1)

    def other_up(self):
        self.wait(8, self.up, 1 - self.core, 1)
        self.wait(10, self.up, 1 - self.core, 0)

    def other_far(self):
        self.wait(11, self.far, 1 - self.core, 0)
        self.wait(12, self.far, 1 - self.core, 1)

    def drain(self):
        for copy in self.copies:
            copy.wait_send()


def plane_device(x, y):
    return (x * 4 + y, lax.axis_index("expert"))


def plane_here():
    group = lax.axis_index("dp")
    return group // 4, lax.rem(group, 4)


def added(left, right):
    return left.astype(jnp.float32) + right.astype(jnp.float32)


class PlaneSum:
    def __init__(self, source, first, direct, combined, sends, receives):
        self.source, self.first = source, first
        self.direct, self.combined = direct, combined
        self.sends, self.receives = sends, receives
        self.x, self.y = plane_here()
        half = source.shape[-1] // 2
        self.left, self.right = pl.ds(0, half), pl.ds(half, half)
        self.low, self.high = pl.ds(0, 2), pl.ds(2, 2)
        self.copies = []

    def x_part(self, x, part):
        return self.source.at[x, part, :, self.left]

    def y_part(self, y, part):
        return self.source.at[part, y, :, self.right]

    def sides(self):
        return (
            (0, self.x, self.x_part, lambda p: plane_device(p, self.y)),
            (2, self.y, self.y_part, lambda p: plane_device(self.x, p)),
        )

    def send(self, source, target, index, where):
        copy = push(source, target, self.sends, self.receives, index, index, where)
        copy.start()
        self.copies.append(copy)

    def wait(self, region, index):
        landed(region, self.sends, self.receives, index)

    def neighbours(self, place):
        return lax.rem(place + 1, 4), lax.rem(place + 3, 4), lax.rem(place + 2, 4)

    def start_far(self):
        for base, place, part, where in self.sides():
            up, down, far = self.neighbours(place)
            self.send(part(far, self.low), self.first.at[base], base, where(up))
            self.send(part(far, self.high), self.first.at[base + 1], base + 1, where(down))

    def start_near(self):
        for base, place, part, where in self.sides():
            up, down, _ = self.neighbours(place)
            self.send(part(up, self.high), self.direct.at[base], base + 4, where(up))
            self.send(part(down, self.low), self.direct.at[base + 1], base + 5, where(down))

    def start(self):
        self.start_far()
        self.start_near()

    def settle_far(self):
        for index in range(4):
            self.wait(self.first.at[index], index)

    def second(self, waits=True):
        low, high = self.low, self.high
        for base, place, part, where in self.sides():
            up, down, _ = self.neighbours(place)
            for index, chosen, to in (
                (base, part(up, low), up),
                (base + 1, part(down, high), down),
            ):
                if waits:
                    self.wait(self.first.at[index], index)
                chosen[...] = added(chosen[...], self.first[index]).astype(jnp.bfloat16)
                self.send(chosen, self.combined.at[index], index + 8, where(to))

    def third(self, x_sum, y_sum):
        low, high = self.low, self.high
        for base, place, part, total in (
            (0, self.x, self.x_part, x_sum),
            (2, self.y, self.y_part, y_sum),
        ):
            self.wait(self.direct.at[base], base + 4)
            self.wait(self.direct.at[base + 1], base + 5)
            self.wait(self.combined.at[base], base + 8)
            self.wait(self.combined.at[base + 1], base + 9)
            total[low] = (
                added(part(place, low)[...], self.combined[base])
                + self.direct[base + 1].astype(jnp.float32)
            ).astype(jnp.bfloat16)
            total[high] = (
                added(part(place, high)[...], self.direct[base])
                + self.combined[base + 1].astype(jnp.float32)
            ).astype(jnp.bfloat16)

    def drain(self):
        for copy in self.copies:
            copy.wait_send()


class PlaneSpread:
    def __init__(self, x_sum, y_sum, land, sends, receives):
        self.x_sum, self.y_sum, self.land = x_sum, y_sum, land
        self.sends, self.receives = sends, receives
        self.x, self.y = plane_here()
        self.copies = []

    def start(self):
        for step in range(1, 4):
            y, x = lax.rem(self.y + step, 4), lax.rem(self.x + step, 4)
            for index, source, where in (
                (step - 1, self.x_sum.at[y], plane_device(self.x, y)),
                (step + 2, self.y_sum.at[x], plane_device(x, self.y)),
            ):
                copy = push(
                    source, self.land.at[index], self.sends, self.receives, index, index, where
                )
                copy.start()
                self.copies.append(copy)

    def total(self):
        sums = []
        for base, mine in ((0, self.x_sum[self.y]), (3, self.y_sum[self.x])):
            value = mine.astype(jnp.float32)
            for index in range(base, base + 3):
                landed(self.land.at[index], self.sends, self.receives, index)
                value += self.land[index].astype(jnp.float32)
            sums.append(value)
        return sums

    def drain(self):
        for copy in self.copies:
            copy.wait_send()


def greet_plane(barrier):
    x, y = plane_here()
    for step in range(1, 4):
        for where in (plane_device(lax.rem(x + step, 4), y), plane_device(x, lax.rem(y + step, 4))):
            pl.semaphore_signal(barrier, inc=1, device_id=where, device_id_type=MESH_ID)


def gelu_parts(u):
    scaled = jnp.abs(u) * 0.7071067811865476
    t = 1.0 / (1.0 + 0.3275911 * scaled)
    poly = t * (
        0.127414796
        + t * (-0.142248368 + t * (0.7107068705 + t * (-0.7265760135 + t * 0.5307027145)))
    )
    density = jnp.exp(-0.5 * u * u)
    tail = poly * density
    cumulative = jnp.where(u >= 0, 1.0 - tail, tail)
    return u * cumulative, cumulative + u * density * 0.3989422804014327


def vmem():
    return pl.BlockSpec(memory_space=pltpu.VMEM)


def smem():
    return pl.BlockSpec(memory_space=pltpu.SMEM)


def anywhere():
    return pl.BlockSpec(memory_space=pl.ANY)


def front_part(
    kind_ref,
    tokens_ref,
    gain_ref,
    weight_ref,
    grad_hbm,
    routes_ref,
    proj_hbm,
    gain_two_ref,
    router_ref,
    hidden_out,
    query_out,
    key_out,
    value_out,
    heads_out,
    attended_out,
    residual_out,
    hidden_two_out,
    total_ref,
    info_ref,
    hidden_ref,
    out_ref,
    attended_ref,
    residual_ref,
    hidden_two_ref,
    sent_ref,
    grad_rows_ref,
    grad_ref,
    proj_ref,
    gather_sems,
    out_sems,
    weight_sems,
    store_sems,
    begin_rows,
):
    z, core = here()
    mine = z * 2 + core
    up, down, far = lax.rem(z + 1, CHIPS), lax.rem(z + 3, CHIPS), lax.rem(z + 2, CHIPS)
    barrier = pltpu.get_barrier_semaphore()
    greet(barrier)
    greet_plane(barrier)
    late_loads = [
        pltpu.make_async_copy(grad_hbm, grad_ref, weight_sems.at[3]),
        pltpu.make_async_copy(proj_hbm, proj_ref, weight_sems.at[4]),
    ]
    for load in late_loads:
        load.start()
    tokens = tokens_ref[...].astype(jnp.float32)
    normed, _ = norm_parts(tokens)
    hidden_ref[mine] = (normed * gain_ref[...][None]).astype(jnp.bfloat16)
    pl.semaphore_wait(barrier, 13)
    gather = RingGather(hidden_ref, gather_sems.at[0], gather_sems.at[1])
    stores, store_count = [], [0]

    def store(source, target):
        copy = pltpu.make_async_copy(source, target, store_sems.at[store_count[0]])
        copy.start()
        store_count[0] += 1
        stores.append(copy)

    out_send, out_recv = out_sems.at[0], out_sems.at[1]
    gather.start()
    routes = routes_ref[...].astype(jnp.float32)
    names = lax.broadcasted_iota(jnp.int32, (EXPERTS, BLOCK), 0).astype(jnp.float32)
    pick_zero = jnp.where(names == routes[0:1, :], 1.0, 0.0)
    pick_one = jnp.where(names == routes[1:2, :], 1.0, 0.0)
    row = lax.broadcasted_iota(jnp.int32, (BLOCK, BLOCK), 0)
    column = lax.broadcasted_iota(jnp.int32, (BLOCK, BLOCK), 1)
    before = jnp.where(row < column, 1.0, 0.0).astype(jnp.bfloat16)
    earlier = dot_nn((pick_zero + pick_one).astype(jnp.bfloat16), before)
    places = []
    for index, pick in enumerate((pick_zero, pick_one)):
        slot = jnp.sum(earlier * pick, axis=0, keepdims=True)
        place = routes[index : index + 1, :] * CAPACITY + slot
        places.append(jnp.where(slot < CAPACITY, place, -1.0))

    def attention(
        query_ref,
        key_ref,
        value_ref,
        weight,
        stacked,
        diagonal,
        beside,
        scores,
        largest,
        sums,
        acc,
    ):
        loads = load_windows(weight_ref, weight, weight_sems, z)

        def project(block):
            projected = dot_nn(hidden_ref[block], weight[...]).astype(jnp.bfloat16)
            query_ref[block] = projected[:, :PAD]
            key_ref[block_rows(block), :] = projected[:, PAD : 2 * PAD]
            value_ref[block_rows(block), :] = projected[:, 2 * PAD :]

        for load in loads:
            load.wait()
        project(mine)
        gather.relay()
        gather.other_own()
        project(z * 2 + 1 - core)
        gather.share()
        project(down * 2 + core)
        project(up * 2 + core)
        gather.other_down()
        project(down * 2 + 1 - core)
        gather.other_up()
        project(up * 2 + 1 - core)
        gather.share_far()
        project(far * 2 + core)
        gather.other_far()
        project(far * 2 + 1 - core)
        store(hidden_ref, hidden_out)
        store(query_ref, query_out)
        store(key_ref, key_out)
        store(value_ref, value_out)

        kind_bias = kind_ref[0].astype(jnp.float32) * NEGATIVE

        def attend(step):
            slot = lax.rem(z + CHIPS - 1 - step, CHIPS)
            block = slot * 2 + lax.rem(core + slot, 2)
            queries = query_ref[block]
            for head in range(LOCAL_HEADS):
                stacked[head * BLOCK : (head + 1) * BLOCK, :] = queries * head_mask(
                    z, head, HD ** (-0.5), jnp.bfloat16
                )

            def bias_of(chunk):
                return jnp.where((slot >= 2) & (chunk < 2), kind_bias, 0.0)

            masked = dot_nt(stacked[...], key_ref[block_rows(block), :])
            row = lax.broadcasted_iota(jnp.int32, (BLOCK, BLOCK), 0)
            column = lax.broadcasted_iota(jnp.int32, (BLOCK, BLOCK), 1)
            for head in range(LOCAL_HEADS):
                part = slice(head * BLOCK, (head + 1) * BLOCK)
                values = jnp.where(column <= row, masked[part], NEGATIVE)
                diagonal[part, :] = values
                largest[part, :] = lane_tiles(values, jnp.maximum)
            is_odd = block != 2 * slot

            @pl.when(is_odd)
            def _():
                values = dot_nt(stacked[...], key_ref[block_rows(block - 1), :])
                beside[...] = values
                largest[...] = jnp.maximum(largest[...], lane_tiles(values, jnp.maximum))

            @pl.loop(0, slot)
            def _(chunk):
                values = dot_nt(stacked[...], key_ref[chunk_rows(chunk), :])
                scores[chunk] = values
                largest[...] = jnp.maximum(
                    largest[...], lane_tiles(values, jnp.maximum) + bias_of(chunk)
                )

            row_max = jnp.max(largest[...], axis=1, keepdims=True)
            largest[...] = jnp.broadcast_to(row_max, largest.shape)
            exponent = jnp.exp(diagonal[...] - row_max)
            sums[...] = lane_tiles(exponent, jnp.add)
            acc[...] = dot_nn(exponent.astype(jnp.bfloat16), value_ref[block_rows(block), :])

            @pl.when(is_odd)
            def _():
                exponent = jnp.exp(beside[...] - largest[:, :1])
                sums[...] += lane_tiles(exponent, jnp.add)
                acc[...] += dot_nn(exponent.astype(jnp.bfloat16), value_ref[block_rows(block - 1), :])

            @pl.loop(0, slot)
            def _(chunk):
                exponent = jnp.exp(scores[chunk] - (largest[:, :1] - bias_of(chunk)))
                sums[...] += lane_tiles(exponent, jnp.add)
                acc[...] += dot_nn(exponent.astype(jnp.bfloat16), value_ref[chunk_rows(chunk), :])

            total = jnp.sum(sums[...], axis=1, keepdims=True)
            inverse = 1.0 / total
            log_total = largest[...] + jnp.log(total)
            attended = jnp.zeros((BLOCK, PAD), jnp.float32)
            for head in range(LOCAL_HEADS):
                part = slice(head * BLOCK, (head + 1) * BLOCK)
                attended += acc[part, :] * inverse[part] * head_mask(z, head, 1.0, jnp.float32)
                total_ref[slot, head : head + 1, :] = jnp.transpose(log_total[part, :])[:1, :]
            out_ref[slot] = attended.astype(jnp.bfloat16)

            @pl.when(block != mine)
            def _():
                push(
                    out_ref.at[slot],
                    attended_ref.at[z],
                    out_send,
                    out_recv,
                    slot,
                    z,
                    device(slot, lax.rem(core + slot, 2)),
                ).start()

            @pl.when(block == mine)
            def _():
                attended_ref[z] = out_ref[slot]

        pl.loop(0, CHIPS)(attend)
        gather.drain()
        for copy in stores:
            copy.wait()

    pl.run_scoped(
        attention,
        pltpu.VMEM((8, BLOCK, PAD), HALF_TYPE),
        pltpu.VMEM((LONG, PAD), HALF_TYPE),
        pltpu.VMEM((LONG, PAD), HALF_TYPE),
        pltpu.VMEM((WIDTH, 3 * PAD), HALF_TYPE),
        pltpu.VMEM((STACK, PAD), HALF_TYPE),
        pltpu.VMEM((STACK, BLOCK), FULL_TYPE),
        pltpu.VMEM((STACK, BLOCK), FULL_TYPE),
        pltpu.VMEM((CHUNKS - 1, STACK, CHUNK), FULL_TYPE),
        pltpu.VMEM((STACK, 128), FULL_TYPE),
        pltpu.VMEM((STACK, 128), FULL_TYPE),
        pltpu.VMEM((STACK, PAD), FULL_TYPE),
    )
    stores.clear()
    store(out_ref, heads_out)

    @pl.loop(0, CHIPS)
    def _(slot):
        @pl.when((slot != z) | (lax.rem(core + z, 2) != core))
        def _():
            landed(attended_ref.at[slot], out_send, out_recv, slot)

    store(attended_ref, attended_out)
    for load in late_loads:
        load.wait()
    residual = tokens_ref[...].astype(jnp.float32)
    for chip in range(CHIPS):
        first = (chip + chip // 2) * 128
        residual += dot_nn(attended_ref[chip], proj_ref[first : first + PAD, :])
    residual_ref[...] = residual
    normed_two, _ = norm_parts(residual)
    hidden_two = (normed_two * gain_two_ref[...][None]).astype(jnp.bfloat16)
    hidden_two_ref[...] = hidden_two
    store(residual_ref, residual_out)
    store(hidden_two_ref, hidden_two_out)
    logits = dot_nt(router_ref[...], hidden_two)
    logit_zero = jnp.sum(logits * pick_zero, axis=0, keepdims=True)
    logit_one = jnp.sum(logits * pick_one, axis=0, keepdims=True)
    gate_zero = 1.0 / (1.0 + jnp.exp(logit_one - logit_zero))
    gate_one = 1.0 / (1.0 + jnp.exp(logit_zero - logit_one))
    for index, line in enumerate((*places, gate_zero, gate_one, routes[0:1], routes[1:2])):
        info_ref[index : index + 1, :] = line
    info_ref[6:8, :] = jnp.zeros((2, BLOCK), jnp.float32)
    ids = lax.broadcasted_iota(jnp.int32, (SLOTS, BLOCK), 0).astype(jnp.float32)
    chosen = jnp.where((ids == places[0]) | (ids == places[1]), 1.0, 0.0).astype(jnp.bfloat16)
    sent = dot_nn(chosen, hidden_two).astype(jnp.bfloat16)
    sent_ref[0] = sent[:EXPERT_ROWS]
    sent_ref[1] = sent[EXPERT_ROWS:]
    begin_rows(0)
    mixing = (
        jnp.where(ids == places[0], gate_zero, 0.0) + jnp.where(ids == places[1], gate_one, 0.0)
    ).astype(jnp.bfloat16)
    rows = dot_nn(mixing, grad_ref[...]).astype(jnp.bfloat16)
    grad_rows_ref[0] = rows[:EXPERT_ROWS]
    grad_rows_ref[1] = rows[EXPERT_ROWS:]
    begin_rows(1)

    def finish_front():

        @pl.loop(0, CHIPS)
        def _(slot):
            @pl.when(slot * 2 + lax.rem(core + slot, 2) != mine)
            def _():
                push(
                    out_ref.at[slot],
                    attended_ref.at[slot],
                    out_send,
                    out_recv,
                    slot,
                    slot,
                    device(z, 1 - core),
                ).wait_send()

        for copy in stores:
            copy.wait()

    return finish_front


def expert_part(
    sent_ref,
    grad_rows_ref,
    in_frozen,
    out_frozen,
    in_new,
    out_new,
    returned_ref,
    in_grad_ref,
    in_first_ref,
    grad_back_ref,
    match_ref,
    x_sum_ref,
    y_sum_ref,
    x_land,
    g_land,
    r_send,
    b_send,
    in_grad,
    out_grad,
    first,
    direct,
    combined,
    in_first,
    match_send,
    load_sems,
    x_sems,
    g_sems,
    b_sems,
    match_sems,
    plane_sems,
    in_sems,
    store_sems,
):
    mine = lax.axis_index("expert")

    def rows_of(place):
        return pl.ds(pl.multiple_of(place * CAPACITY, CAPACITY), CAPACITY)

    own_rows = rows_of(mine)

    def peer(step):
        return lax.rem(mine + step, 8)

    def exchange(source, target, sems, index, step):
        return push(
            source, target, sems.at[0], sems.at[1], index, index, (lax.axis_index("dp"), peer(step))
        )

    stores, used = [], []

    def store(source, target):
        copy = pltpu.make_async_copy(source, target, store_sems.at[len(stores)])
        copy.start()
        stores.append(copy)

    def seven(ref, sem):
        region = ref.at[0, pl.ds(0, 7 * CAPACITY), :]
        return pltpu.make_async_copy(region, region, sem)

    def spread_kind(kind, source, target, sems):
        for step in range(1, 8):
            exchange(
                source.at[kind, rows_of(peer(step)), :],
                target.at[kind, own_rows, :],
                sems,
                kind,
                step,
            ).start()
        used.append((target, sems.at[0, kind]))

    def collect_kind(kind, target, sems):
        seven(target, sems.at[1, kind]).wait()

    def begin_rows(which):
        source, target, sems = ((sent_ref, x_land, x_sems), (grad_rows_ref, g_land, g_sems))[which]
        if which == 1:
            spread_kind(1, source, target, sems)
            spread_kind(0, sent_ref, x_land, x_sems)
            spread_kind(0, source, target, sems)
        else:
            spread_kind(1, source, target, sems)
        target[:, own_rows, :] = source[:, own_rows, :]

    def work(w_in, w_out, activated, slope, acc):
        loads = []
        for index, (source, target) in enumerate(
            (
                (in_new, w_in.at[1]),
                (out_new, w_out.at[1]),
                (in_frozen, w_in.at[0]),
                (out_frozen, w_out.at[0]),
            )
        ):
            copy = pltpu.make_async_copy(source, target, load_sems.at[index])
            copy.start()
            loads.append(copy)

        def tile_of(index):
            return pl.ds(pl.multiple_of(index * FF_TILE, FF_TILE), FF_TILE)

        plane = PlaneSum(out_grad, first, direct, combined, plane_sems.at[0], plane_sems.at[1])
        in_plane = PlaneSum(in_grad, in_first, None, None, in_sems.at[0], in_sems.at[1])
        matches = [None, None]
        for kind in (1, 0):
            collect_kind(kind, x_land, x_sems)
            loads[0 if kind == 1 else 2].wait()
            loads[1 if kind == 1 else 3].wait()
            acc[...] = jnp.zeros_like(acc)

            @pl.loop(0, FF_TILES, unroll=True)
            def _(index):
                tile = tile_of(index)
                pre = dot_nn(x_land[kind], w_in[kind, :, tile])
                value, steep = gelu_parts(pre)
                value = value.astype(jnp.bfloat16)
                if kind == 1:
                    activated[:, tile] = value
                slope[:, tile] = steep.astype(jnp.bfloat16)
                acc[...] += dot_nn(value, w_out[kind, tile, :])

            collect_kind(kind, g_land, g_sems)
            result = acc[...].astype(jnp.bfloat16)
            r_send[kind] = result
            store(r_send.at[kind], returned_ref.at[kind])
            products = result.astype(jnp.float32) * g_land[kind].astype(jnp.float32)
            matches[kind] = jnp.sum(products, axis=1, keepdims=True)
            if kind == 1:

                @pl.loop(0, FF_TILES, unroll=True)
                def _(index):
                    weights = dot_tn(activated[:, tile_of(index)], g_land[1]).astype(jnp.bfloat16)
                    for y in range(4):
                        for part in range(4):
                            start = (y * 4 + part) * CAPACITY
                            out_grad[index, y, :, part * WIDTH : (part + 1) * WIDTH] = weights[
                                start : start + CAPACITY
                            ]

                plane.start()

            acc[...] = jnp.zeros_like(acc)

            @pl.loop(0, FF_TILES, unroll=True)
            def _(index):
                tile = tile_of(index)
                grad = dot_nt(g_land[kind], w_out[kind, tile, :])
                grad = (grad * slope[:, tile].astype(jnp.float32)).astype(jnp.bfloat16)
                acc[...] += dot_nt(grad, w_in[kind, :, tile])
                if kind == 1:
                    activated[:, tile] = grad

            b_send[kind] = acc[...].astype(jnp.bfloat16)
            grad_back_ref[kind, own_rows, :] = b_send[kind, own_rows, :]
            spread_kind(kind, b_send, grad_back_ref, b_sems)
            if kind == 1:

                @pl.loop(0, FF_TILES, unroll=True)
                def _(index):
                    tile = tile_of(index)
                    weights = dot_tn(x_land[1], activated[:, tile]).astype(jnp.bfloat16)
                    in_grad[:, :, :, tile] = weights.reshape(4, 4, CAPACITY, FF_TILE)

                in_plane.start_far()
                store(in_grad, in_grad_ref)
        lanes = lax.broadcasted_iota(jnp.int32, (EXPERT_ROWS, 128), 1)
        match_send[0] = jnp.where(lanes < 64, matches[0], matches[1])
        match_ref[0, own_rows, :] = match_send[0, own_rows, :]
        spread_kind(0, match_send, match_ref, match_sems)
        plane.second()
        plane.third(x_sum_ref, y_sum_ref)
        collect_kind(0, match_ref, match_sems)
        for kind in (1, 0):
            collect_kind(kind, grad_back_ref, b_sems)
        in_plane.settle_far()
        store(in_first, in_first_ref)
        for target, sem in used:
            seven(target, sem).wait()
        plane.drain()
        in_plane.drain()
        for copy in stores:
            copy.wait()

    def run():
        pl.run_scoped(
            work,
            pltpu.VMEM((2, WIDTH, FF), HALF_TYPE),
            pltpu.VMEM((2, FF, WIDTH), HALF_TYPE),
            pltpu.VMEM((EXPERT_ROWS, FF), HALF_TYPE),
            pltpu.VMEM((EXPERT_ROWS, FF), HALF_TYPE),
            pltpu.VMEM((EXPERT_ROWS, WIDTH), FULL_TYPE),
        )

    return begin_rows, run


def layer_kernel(*refs):
    front_in, rest = refs[:9], refs[9:]
    expert_in, rest = rest[:4], rest[4:]
    front_out, rest = rest[:10], rest[10:]
    expert_out, rest = rest[:7], rest[7:]
    front_scratch, expert_scratch = rest[:13], rest[13:]
    sent, grad_rows = front_scratch[5:7]
    begin_rows, run_experts = expert_part(sent, grad_rows, *expert_in, *expert_out, *expert_scratch)
    finish_front = front_part(*front_in, *front_out, *front_scratch, begin_rows)
    run_experts()
    finish_front()


def layer(*operands):
    def shape(*dims, dtype=HALF_TYPE):
        return jax.ShapeDtypeStruct(dims, dtype)

    def pair(count):
        return pltpu.SemaphoreType.DMA((2, count))

    shapes = [
        shape(8, BLOCK, WIDTH),
        shape(8, BLOCK, PAD),
        shape(LONG, PAD),
        shape(LONG, PAD),
        shape(CHIPS, BLOCK, PAD),
        shape(CHIPS, BLOCK, PAD),
        shape(BLOCK, WIDTH, dtype=FULL_TYPE),
        shape(BLOCK, WIDTH),
        shape(CHIPS, 8, BLOCK, dtype=FULL_TYPE),
        shape(8, BLOCK, dtype=FULL_TYPE),
        shape(2, EXPERT_ROWS, WIDTH),
        shape(4, 4, CAPACITY, FF),
        shape(4, 2, CAPACITY, FF // 2),
        shape(2, EXPERT_ROWS, WIDTH),
        shape(1, EXPERT_ROWS, 128, dtype=FULL_TYPE),
        shape(4, CAPACITY, FF // 2),
        shape(4, CAPACITY, FF // 2),
    ]
    return pl.pallas_call(
        layer_kernel,
        out_shape=shapes,
        in_specs=[
            smem(),
            vmem(),
            vmem(),
            anywhere(),
            anywhere(),
            vmem(),
            anywhere(),
            vmem(),
            vmem(),
        ]
        + [anywhere()] * 4,
        out_specs=[anywhere()] * 8 + [vmem()] * 2 + [anywhere()] * 3 + [vmem()] * 4,
        scratch_shapes=[
            pltpu.VMEM((8, BLOCK, WIDTH), HALF_TYPE),
            pltpu.VMEM((CHIPS, BLOCK, PAD), HALF_TYPE),
            pltpu.VMEM((CHIPS, BLOCK, PAD), HALF_TYPE),
            pltpu.VMEM((BLOCK, WIDTH), FULL_TYPE),
            pltpu.VMEM((BLOCK, WIDTH), HALF_TYPE),
            pltpu.VMEM((2, EXPERT_ROWS, WIDTH), HALF_TYPE),
            pltpu.VMEM((2, EXPERT_ROWS, WIDTH), HALF_TYPE),
            pltpu.VMEM((BLOCK, WIDTH), HALF_TYPE),
            pltpu.VMEM((WIDTH, WIDTH), HALF_TYPE),
            pair(13),
            pair(CHIPS),
            pltpu.SemaphoreType.DMA((5,)),
            pltpu.SemaphoreType.DMA((8,)),
            pltpu.VMEM((2, EXPERT_ROWS, WIDTH), HALF_TYPE),
            pltpu.VMEM((2, EXPERT_ROWS, WIDTH), HALF_TYPE),
            pltpu.VMEM((2, EXPERT_ROWS, WIDTH), HALF_TYPE),
            pltpu.VMEM((2, EXPERT_ROWS, WIDTH), HALF_TYPE),
            pltpu.VMEM((4, 4, CAPACITY, FF), HALF_TYPE),
            pltpu.VMEM((4, 4, CAPACITY, FF), HALF_TYPE),
            pltpu.VMEM((4, 2, CAPACITY, FF // 2), HALF_TYPE),
            pltpu.VMEM((4, 2, CAPACITY, FF // 2), HALF_TYPE),
            pltpu.VMEM((4, 2, CAPACITY, FF // 2), HALF_TYPE),
            pltpu.VMEM((4, 2, CAPACITY, FF // 2), HALF_TYPE),
            pltpu.VMEM((1, EXPERT_ROWS, 128), FULL_TYPE),
            pltpu.SemaphoreType.DMA((4,)),
            pair(2),
            pair(2),
            pair(2),
            pair(2),
            pair(12),
            pair(4),
            pltpu.SemaphoreType.DMA((4,)),
        ],
        compiler_params=pltpu.CompilerParams(
            collective_id=0, has_side_effects=True, vmem_limit_bytes=62 * 2**20
        ),
    )(*operands)


def slot_rows(place):
    return pl.ds(pl.multiple_of(place * CAPACITY, CAPACITY), CAPACITY)


def back_kernel(
    kind_ref,
    tokens_ref,
    gain_ref,
    gain_two_ref,
    grad_ref,
    residual_ref,
    info_ref,
    match_ref,
    grad_back_ref,
    router_ref,
    proj_ref,
    hidden_two_ref,
    total_ref,
    query_hbm,
    key_hbm,
    value_hbm,
    heads_hbm,
    weight_hbm,
    hidden_hbm,
    attended_hbm,
    in_grad_hbm,
    in_first_hbm,
    returned_hbm,
    x_part_hbm,
    y_part_hbm,
    mixed_ref,
    tokens_grad_ref,
    in_sum_ref,
    out_sum_ref,
    dense_sum_ref,
    qkv_sum_ref,
    dense_land,
    query_ref,
    key_ref,
    value_ref,
    heads_ref,
    weight,
    hidden_ref,
    attended_ref,
    x_part,
    y_part,
    out_land,
    returned,
    grad_residual,
    grad_sent,
    grad_out,
    stacked,
    grad_stacked,
    grad_query,
    grad_key,
    grad_value,
    projected,
    part_sib,
    part_own,
    land_sib,
    land_half,
    land_full,
    big,
    big_first,
    big_direct,
    big_combined,
    big_x,
    big_y,
    big_land,
    mid,
    mid_first,
    mid_direct,
    mid_combined,
    mid_x,
    mid_y,
    mid_land,
    qkv,
    qkv_first,
    qkv_direct,
    qkv_combined,
    qkv_x,
    qkv_y,
    qkv_land,
    dense_send,
    weight_sems,
    load_sems,
    grad_sems,
    sib_sems,
    ring_sems,
    big_sems,
    out_spread,
    big_spread,
    mid_sems,
    mid_spread,
    qkv_sems,
    qkv_spread,
    dense_sems,
    returned_sems,
):
    z, core = here()
    mine = z * 2 + core
    up, down, far = lax.rem(z + 1, CHIPS), lax.rem(z + 3, CHIPS), lax.rem(z + 2, CHIPS)
    barrier = pltpu.get_barrier_semaphore()
    greet(barrier)
    greet_plane(barrier)
    loads = []
    for index, (source, target) in enumerate(
        (
            (in_grad_hbm, big),
            (in_first_hbm, big_first),
            (x_part_hbm, x_part),
            (y_part_hbm, y_part),
            (
                returned_hbm.at[:, slot_rows(mine), :],
                returned.at[:, slot_rows(mine), :],
            ),
            (attended_hbm, attended_ref),
            (query_hbm, query_ref),
            (key_hbm, key_ref),
            (value_hbm, value_ref),
            (heads_hbm, heads_ref),
            (hidden_hbm, hidden_ref),
        )
    ):
        copy = pltpu.make_async_copy(source, target, load_sems.at[index])
        copy.start()
        loads.append(copy)
    weight_loads = load_windows(weight_hbm, weight, weight_sems, z)

    info = info_ref[...]
    columns = jnp.transpose(
        jnp.concatenate([info, jnp.zeros((120, BLOCK), jnp.float32)], axis=0)
    )
    lane_ids = lax.broadcasted_iota(jnp.int32, (BLOCK, SLOTS), 1).astype(jnp.float32)
    at_zero, at_one = lane_ids == columns[:, 0:1], lane_ids == columns[:, 1:2]
    ids = lax.broadcasted_iota(jnp.int32, (SLOTS, BLOCK), 0).astype(jnp.float32)
    lines = match_ref[0]
    match = jnp.concatenate(
        [jnp.broadcast_to(lines[:, lane : lane + 1], (EXPERT_ROWS, BLOCK)) for lane in (0, 64)],
        axis=0,
    )
    parts = []
    for place, gate in ((0, 2), (1, 3)):
        value = jnp.sum(
            jnp.where(ids == info[place : place + 1, :], match, 0.0), axis=0, keepdims=True
        )
        used = info[gate : gate + 1, :].astype(jnp.bfloat16).astype(jnp.float32)
        ratio = jnp.where(used > 0.0, info[gate : gate + 1, :] / jnp.where(used > 0.0, used, 1.0), 1.0)
        parts.append(value * ratio)
    gap = parts[0] * info[3:4, :] - parts[1] * info[2:3, :]
    names = lax.broadcasted_iota(jnp.int32, (EXPERTS, BLOCK), 0).astype(jnp.float32)
    pick_zero = jnp.where(names == info[4:5, :], 1.0, 0.0)
    pick_one = jnp.where(names == info[5:6, :], 1.0, 0.0)
    grad_logits = (gap * (pick_zero - pick_one)).astype(jnp.bfloat16)
    chosen = jnp.where(at_zero | at_one, 1.0, 0.0).astype(jnp.bfloat16)
    grad_two = (
        dot_tn(grad_logits, router_ref[...])
        + dot_nn(chosen[:, :EXPERT_ROWS], grad_back_ref[0])
        + dot_nn(chosen[:, EXPERT_ROWS:], grad_back_ref[1])
    )
    normed_two, inverse_two = norm_parts(residual_ref[...])
    gain_two_grad = jnp.sum(grad_two * normed_two, axis=0, keepdims=True)
    grad_residual[...] = grad_ref[...].astype(jnp.float32) + norm_back(
        grad_two * gain_two_ref[...][None], normed_two, inverse_two
    )
    grad_branch = grad_residual[...].astype(jnp.bfloat16)
    for chip in range(CHIPS):
        first = (chip + chip // 2) * 128
        grad_sent[chip] = dot_nt(grad_branch, proj_ref[first : first + PAD, :]).astype(
            jnp.bfloat16
        )
    pl.semaphore_wait(barrier, 13)
    owner_core = lax.rem(core + z, 2)
    grad_send, grad_recv = grad_sems.at[0], grad_sems.at[1]

    @pl.loop(0, CHIPS)
    def _(step):
        chip = lax.rem(z + step, CHIPS)
        mine_too = (chip == z) & (owner_core == core)

        @pl.when(jnp.logical_not(mine_too))
        def _():
            push(
                grad_sent.at[chip],
                grad_out.at[z],
                grad_send,
                grad_recv,
                chip,
                z,
                device(chip, owner_core),
            ).start()

        @pl.when(mine_too)
        def _():
            grad_out[z] = grad_sent[chip]

    for step in range(1, 8):
        place = lax.rem(mine + step, 8)
        copy = push(
            returned_hbm.at[:, slot_rows(place), :],
            returned.at[:, slot_rows(mine), :],
            returned_sems.at[0],
            returned_sems.at[1],
            0,
            0,
            (lax.axis_index("dp"), place),
        )
        copy.start()
    for load in loads[:4]:
        load.wait()
    big_sum = PlaneSum(big, big_first, big_direct, big_combined, big_sems.at[0], big_sems.at[1])
    big_sum.start_near()
    big_sum.second(waits=False)
    loads[5].wait()
    for chip in range(CHIPS):
        grads = dot_tn(attended_ref[chip], grad_branch).astype(jnp.bfloat16)
        first = (chip % 2) * HD
        for y in range(4):
            start = first + y * CAPACITY
            mid[chip, y, :, :WIDTH] = grads[start : start + CAPACITY]
    narrow = jnp.concatenate(
        [
            dot_nn(grad_logits, hidden_two_ref[...]),
            gain_two_grad,
            jnp.zeros((111, WIDTH), jnp.float32),
        ],
        axis=0,
    )
    mid[:, :, :, WIDTH : WIDTH + 128] = (
        jnp.transpose(narrow).astype(jnp.bfloat16).reshape(4, 4, CAPACITY, 128)
    )
    mid[:, :, :, WIDTH + 128 :] = jnp.zeros((4, 4, CAPACITY, 128), jnp.bfloat16)
    mid_sum = PlaneSum(mid, mid_first, mid_direct, mid_combined, mid_sems.at[0], mid_sems.at[1])
    mid_sum.start()
    out_sum = PlaneSpread(x_part, y_part, out_land, out_spread.at[0], out_spread.at[1])
    out_sum.start()

    grad_key[...] = jnp.zeros_like(grad_key)
    grad_value[...] = jnp.zeros_like(grad_value)
    projected[...] = jnp.zeros_like(projected)
    for load in loads[6:10]:
        load.wait()
    kind_bias = kind_ref[0].astype(jnp.float32) * NEGATIVE

    def attend(step):
        slot = lax.rem(z + step, CHIPS)
        block = slot * 2 + lax.rem(core + slot, 2)

        @pl.when(block != mine)
        def _():
            landed(grad_out.at[slot], grad_send, grad_recv, slot)

        queries = query_ref[block]
        grads = grad_out[slot]
        products = grads.astype(jnp.float32) * heads_ref[slot].astype(jnp.float32)
        selector = jnp.concatenate(
            [head_mask(z, head, 1.0, jnp.float32) for head in range(LOCAL_HEADS)]
            + [jnp.zeros((8 - LOCAL_HEADS, PAD), jnp.float32)],
            axis=0,
        )
        deltas = lax.dot_general(
            selector,
            products,
            (((1,), (1,)), ((), ())),
            preferred_element_type=jnp.float32,
            precision=lax.Precision.HIGHEST,
        )
        for head in range(LOCAL_HEADS):
            part = slice(head * BLOCK, (head + 1) * BLOCK)
            stacked[part, :] = queries * head_mask(z, head, HD ** (-0.5), jnp.bfloat16)
            grad_stacked[part, :] = grads * head_mask(z, head, 1.0, jnp.bfloat16)
        totals = total_ref[slot]
        delta_row = jnp.concatenate(
            [deltas[head : head + 1, :] for head in range(LOCAL_HEADS)], axis=1
        )
        total_row = jnp.concatenate(
            [totals[head : head + 1, :] for head in range(LOCAL_HEADS)], axis=1
        )

        def work(rows, bias, is_diagonal):
            keys, values = key_ref[rows, :], value_ref[rows, :]
            probs = jnp.exp(dot_nt(keys, stacked[...]) - (total_row - bias))
            if is_diagonal:
                row = lax.broadcasted_iota(jnp.int32, (BLOCK, STACK), 0)
                column = lax.broadcasted_iota(jnp.int32, (BLOCK, STACK), 1)
                probs = jnp.where(row <= lax.rem(column, BLOCK), probs, 0.0)
            grad_probs = dot_nt(values, grad_stacked[...])
            grad_scores = (probs * (grad_probs - delta_row)).astype(jnp.bfloat16)
            grad_value[rows, :] += dot_nn(probs.astype(jnp.bfloat16), grad_stacked[...])
            grad_key[rows, :] += dot_nn(grad_scores, stacked[...])
            return dot_tn(grad_scores, keys)

        grad_query[...] = work(block_rows(block), 0.0, True)

        @pl.when(block != 2 * slot)
        def _():
            grad_query[...] += work(block_rows(block - 1), 0.0, False)

        @pl.loop(0, slot)
        def _(chunk):
            bias = jnp.where((slot >= 2) & (chunk < 2), kind_bias, 0.0)
            grad_query[...] += work(chunk_rows(chunk), bias, False)

        combined = jnp.zeros((BLOCK, PAD), jnp.float32)
        for head in range(LOCAL_HEADS):
            part = slice(head * BLOCK, (head + 1) * BLOCK)
            combined += grad_query[part, :] * head_mask(z, head, HD ** (-0.5), jnp.float32)
        projected[block_rows(block), :PAD] = combined.astype(jnp.bfloat16)

    pl.loop(0, CHIPS)(attend)
    projected[:, PAD : 2 * PAD] = grad_key[...].astype(jnp.bfloat16)
    projected[:, 2 * PAD :] = grad_value[...].astype(jnp.bfloat16)
    for load in weight_loads:
        load.wait()

    def partial(chip, which):
        return dot_nt(projected[block_rows(chip * 2 + which), :], weight[...])

    sib_send, sib_recv = sib_sems.at[0], sib_sems.at[1]

    def sib_copy(index):
        return push(
            part_sib.at[index],
            land_sib.at[index],
            sib_send,
            sib_recv,
            index,
            index,
            device(z, 1 - core),
        )

    order = (far, up, down, z)
    for index, chip in enumerate(order):
        part_sib[index] = partial(chip, 1 - core).astype(jnp.bfloat16)
        sib_copy(index).start()

    loads[10].wait()
    for tile in range(3):
        lanes = slice(tile * PAD, (tile + 1) * PAD)
        weights = dot_tn(hidden_ref[...], projected[:, lanes]).astype(jnp.bfloat16)
        qkv[:, :, :, lanes] = weights.reshape(4, 4, CAPACITY, PAD)
    qkv_sum = PlaneSum(
        qkv, qkv_first, qkv_direct, qkv_combined, qkv_sems.at[0], qkv_sems.at[1]
    )
    qkv_sum.start()
    mid_sum.second()


    def own(index):
        value = partial(order[index], core)
        landed(land_sib.at[index], sib_send, sib_recv, index)
        return value + land_sib[index].astype(jnp.float32)

    first, second = pl.ds(0, HALF), pl.ds(HALF, HALF)
    ring_send, ring_recv = ring_sems.at[0], ring_sems.at[1]
    copies = []

    def ring(source, target, index, where):
        copy = push(source, target, ring_send, ring_recv, index, index, where)
        copy.start()
        copies.append(copy)

    above, below = device(up, core), device(down, core)
    part_own[0] = own(0).astype(jnp.bfloat16)
    ring(part_own.at[0, first], land_half.at[0], 0, above)
    ring(part_own.at[0, second], land_half.at[1], 1, below)
    part_own[1] = own(1).astype(jnp.bfloat16)
    ring(part_own.at[1, second], land_full.at[0, second], 2, above)
    part_own[2] = own(2).astype(jnp.bfloat16)
    ring(part_own.at[2, first], land_full.at[1, first], 3, below)
    grad_one = own(3)
    qkv_sum.second()
    landed(land_half.at[0], ring_send, ring_recv, 0)
    part_own[1, first, :] = added(part_own[1, first, :], land_half[0]).astype(jnp.bfloat16)
    ring(part_own.at[1, first], land_full.at[0, first], 4, above)
    landed(land_half.at[1], ring_send, ring_recv, 1)
    part_own[2, second, :] = added(part_own[2, second, :], land_half[1]).astype(jnp.bfloat16)
    ring(part_own.at[2, second], land_full.at[1, second], 5, below)
    mid_sum.third(mid_x, mid_y)
    mid_total = PlaneSpread(mid_x, mid_y, mid_land, mid_spread.at[0], mid_spread.at[1])
    mid_total.start()
    qkv_sum.third(qkv_x, qkv_y)
    qkv_total = PlaneSpread(qkv_x, qkv_y, qkv_land, qkv_spread.at[0], qkv_spread.at[1])
    qkv_total.start()
    big_sum.third(big_x, big_y)
    big_total = PlaneSpread(big_x, big_y, big_land, big_spread.at[0], big_spread.at[1])
    big_total.start()
    loads[4].wait()
    seven = returned.at[:, pl.ds(0, 7 * CAPACITY), :]
    pltpu.make_async_copy(seven, seven, returned_sems.at[1, 0]).wait()
    mixing = (
        jnp.where(at_zero, columns[:, 2:3], 0.0) + jnp.where(at_one, columns[:, 3:4], 0.0)
    ).astype(jnp.bfloat16)
    mixed_ref[...] = (
        residual_ref[...]
        + dot_nn(mixing[:, :EXPERT_ROWS], returned[0])
        + dot_nn(mixing[:, EXPERT_ROWS:], returned[1])
    ).astype(jnp.bfloat16)
    out_left, out_right = out_sum.total()
    out_sum_ref[:, : FF // 2] = out_left
    out_sum_ref[:, FF // 2 :] = out_right
    mid_left, mid_right = mid_total.total()
    qkv_left, qkv_right = qkv_total.total()
    share = CAPACITY // 8
    line = jnp.concatenate([mid_left, mid_right, qkv_left, qkv_right], axis=1)
    for piece in range(8):
        rows = slice(piece * share, (piece + 1) * share)
        dense_send[piece] = jnp.concatenate(
            [line[rows, :LINE], line[rows, LINE:], jnp.zeros((16 - 2 * share, LINE), jnp.float32)],
            axis=0,
        ).astype(jnp.bfloat16)
    dense_copies = []
    for step in range(1, 8):
        place = lax.rem(mine + step, 8)
        copy = push(
            dense_send.at[place],
            dense_land.at[mine],
            dense_sems.at[0],
            dense_sems.at[1],
            step - 1,
            step - 1,
            (lax.axis_index("dp"), place),
        )
        copy.start()
        dense_copies.append(copy)
    dense_land[mine] = dense_send[mine]
    landed(land_full.at[0, second], ring_send, ring_recv, 2)
    landed(land_full.at[1, first], ring_send, ring_recv, 3)
    landed(land_full.at[0, first], ring_send, ring_recv, 4)
    landed(land_full.at[1, second], ring_send, ring_recv, 5)
    grad_one += added(land_full[0], land_full[1])
    normed_one, inverse_one = norm_parts(tokens_ref[...].astype(jnp.float32))
    tokens_grad_ref[...] = grad_residual[...] + norm_back(
        grad_one * gain_ref[...][None], normed_one, inverse_one
    )
    left, right = big_total.total()
    in_sum_ref[:, : FF // 2] = left
    in_sum_ref[:, FF // 2 :] = right
    for step in range(1, 8):
        landed(
            dense_land.at[lax.rem(mine + 8 - step, 8)],
            dense_sems.at[0],
            dense_sems.at[1],
            step - 1,
        )
    lines = [dense_land[place].astype(jnp.float32) for place in range(8)]
    total = sum(lines[1:], lines[0])
    total = jnp.concatenate([total[:share], total[share : 2 * share]], axis=1)
    dense_sum_ref[...] = total[:, :DENSE]
    qkv_sum_ref[...] = jnp.zeros_like(qkv_sum_ref)
    for chip in range(CHIPS):
        line = lines[2 * chip] + lines[2 * chip + 1]
        line = jnp.concatenate([line[:share], line[share : 2 * share]], axis=1)[:, DENSE:]
        for part in range(3):
            start = part * WIDTH + (chip + chip // 2) * 128
            qkv_sum_ref[:, start : start + PAD] += line[:, part * PAD : (part + 1) * PAD]
    pltpu.make_async_copy(seven, seven, returned_sems.at[0, 0]).wait()
    for copy in dense_copies + copies:
        copy.wait_send()
    for user in (big_sum, out_sum, big_total, mid_sum, mid_total, qkv_sum, qkv_total):
        user.drain()
    for index in range(CHIPS):
        sib_copy(index).wait_send()

    @pl.loop(0, CHIPS)
    def _(chip):
        @pl.when((chip != z) | (owner_core != core))
        def _():
            push(
                grad_sent.at[chip],
                grad_out.at[chip],
                grad_send,
                grad_recv,
                chip,
                chip,
                device(z, 1 - core),
            ).wait_send()


def plane_scratch(lanes):
    return [
        pltpu.VMEM((4, 4, CAPACITY, lanes), HALF_TYPE),
        pltpu.VMEM((4, 2, CAPACITY, lanes // 2), HALF_TYPE),
        pltpu.VMEM((4, 2, CAPACITY, lanes // 2), HALF_TYPE),
        pltpu.VMEM((4, 2, CAPACITY, lanes // 2), HALF_TYPE),
        pltpu.VMEM((4, CAPACITY, lanes // 2), HALF_TYPE),
        pltpu.VMEM((4, CAPACITY, lanes // 2), HALF_TYPE),
        pltpu.VMEM((6, CAPACITY, lanes // 2), HALF_TYPE),
    ]


def back(*operands):
    def shape(*dims, dtype=FULL_TYPE):
        return jax.ShapeDtypeStruct(dims, dtype)

    def pair(count):
        return pltpu.SemaphoreType.DMA((2, count))

    return pl.pallas_call(
        back_kernel,
        out_shape=[
            shape(BLOCK, WIDTH, dtype=HALF_TYPE),
            shape(BLOCK, WIDTH),
            shape(CAPACITY, FF),
            shape(CAPACITY, FF),
            shape(CAPACITY // 8, DENSE),
            shape(CAPACITY // 8, 3 * WIDTH),
        ],
        in_specs=[smem()] + [vmem()] * 12 + [anywhere()] * 12,
        out_specs=[vmem()] * 6,
        scratch_shapes=[
            pltpu.VMEM((8, 16, LINE), HALF_TYPE),
            pltpu.VMEM((8, BLOCK, PAD), HALF_TYPE),
            pltpu.VMEM((LONG, PAD), HALF_TYPE),
            pltpu.VMEM((LONG, PAD), HALF_TYPE),
            pltpu.VMEM((CHIPS, BLOCK, PAD), HALF_TYPE),
            pltpu.VMEM((WIDTH, 3 * PAD), HALF_TYPE),
            pltpu.VMEM((LONG, WIDTH), HALF_TYPE),
            pltpu.VMEM((CHIPS, BLOCK, PAD), HALF_TYPE),
            pltpu.VMEM((4, CAPACITY, FF // 2), HALF_TYPE),
            pltpu.VMEM((4, CAPACITY, FF // 2), HALF_TYPE),
            pltpu.VMEM((6, CAPACITY, FF // 2), HALF_TYPE),
            pltpu.VMEM((2, EXPERT_ROWS, WIDTH), HALF_TYPE),
            pltpu.VMEM((BLOCK, WIDTH), FULL_TYPE),
            pltpu.VMEM((CHIPS, BLOCK, PAD), HALF_TYPE),
            pltpu.VMEM((CHIPS, BLOCK, PAD), HALF_TYPE),
            pltpu.VMEM((STACK, PAD), HALF_TYPE),
            pltpu.VMEM((STACK, PAD), HALF_TYPE),
            pltpu.VMEM((STACK, PAD), FULL_TYPE),
            pltpu.VMEM((LONG, PAD), FULL_TYPE),
            pltpu.VMEM((LONG, PAD), FULL_TYPE),
            pltpu.VMEM((LONG, 3 * PAD), HALF_TYPE),
            pltpu.VMEM((CHIPS, BLOCK, WIDTH), HALF_TYPE),
            pltpu.VMEM((CHIPS - 1, BLOCK, WIDTH), HALF_TYPE),
            pltpu.VMEM((CHIPS, BLOCK, WIDTH), HALF_TYPE),
            pltpu.VMEM((2, HALF, WIDTH), HALF_TYPE),
            pltpu.VMEM((2, BLOCK, WIDTH), HALF_TYPE),
            *plane_scratch(FF),
            *plane_scratch(DENSE),
            *plane_scratch(3 * PAD),
            pltpu.VMEM((8, 16, LINE), HALF_TYPE),
            pltpu.SemaphoreType.DMA((3,)),
            pltpu.SemaphoreType.DMA((11,)),
            pair(CHIPS),
            pair(CHIPS),
            pair(6),
            pair(12),
            pair(6),
            pair(6),
            pair(12),
            pair(6),
            pair(12),
            pair(6),
            pair(7),
            pair(1),
        ],
        compiler_params=pltpu.CompilerParams(
            collective_id=1, has_side_effects=True, vmem_limit_bytes=60 * 2**20
        ),
    )(*operands)


def as_row(column):
    size = column.shape[0]
    row = lax.broadcasted_iota(jnp.int32, (size, size), 0)
    lane = lax.broadcasted_iota(jnp.int32, (size, size), 1)
    return jnp.sum(jnp.where(row == lane, column, 0.0), axis=0, keepdims=True)


def finish_kernel(
    mixed_ref,
    tokens_grad_ref,
    in_sum_ref,
    out_sum_ref,
    dense_ref,
    qkv_ref,
    weight_ref,
    gain_ref,
    mixed_out,
    tokens_grad_out,
    gain_out,
    qkv_out,
    proj_out,
    gain_two_out,
    router_out,
    in_out,
    out_out,
    weight,
    sem,
):
    mixed_out[0] = mixed_ref[...]
    tokens_grad_out[0] = tokens_grad_ref[...]
    in_out[0] = in_sum_ref[...]
    for part in range(4):
        rows = slice(part * CAPACITY, (part + 1) * CAPACITY)
        out_out[0, rows, :] = out_sum_ref[:, part * WIDTH : (part + 1) * WIDTH]
    share = CAPACITY // 8
    first = (lax.axis_index("dp") * 8 + lax.axis_index("expert")) * share
    start = pl.multiple_of(jnp.minimum(first // 16, WIDTH // 16 - 2) * 16, 16)
    load = pltpu.make_async_copy(weight_ref.at[pl.ds(start, 32), :], weight, sem)
    load.start()
    qkv_out[...] = qkv_ref[...]
    dense = dense_ref[...]
    proj_out[...] = dense[:, :WIDTH]
    router_out[...] = dense[:, WIDTH : WIDTH + EXPERTS]
    gain_two_out[...] = as_row(dense[:, WIDTH + EXPERTS : WIDTH + EXPERTS + 1])
    row = lax.broadcasted_iota(jnp.int32, (share, 32), 0)
    column = lax.broadcasted_iota(jnp.int32, (share, 32), 1)
    chosen = jnp.where(column == row + (first - start), 1.0, 0.0).astype(jnp.bfloat16)
    row = lax.broadcasted_iota(jnp.int32, (share, WIDTH), 0)
    column = lax.broadcasted_iota(jnp.int32, (share, WIDTH), 1)
    gain = jnp.sum(
        jnp.where(column == row + first, gain_ref[...][None], 0.0), axis=1, keepdims=True
    )
    load.wait()
    products = qkv_ref[...] * dot_nn(chosen, weight[...])
    gain_out[...] = as_row(jnp.sum(products, axis=1, keepdims=True) / gain)


def finish(*operands):
    def shape(*dims, dtype=FULL_TYPE):
        return jax.ShapeDtypeStruct(dims, dtype)

    share = CAPACITY // 8
    shapes = [
        shape(1, BLOCK, WIDTH, dtype=HALF_TYPE),
        shape(1, BLOCK, WIDTH),
        shape(1, share),
        shape(share, 3 * WIDTH),
        shape(share, WIDTH),
        shape(1, share),
        shape(share, EXPERTS),
        shape(1, CAPACITY, FF),
        shape(1, 4 * CAPACITY, WIDTH),
    ]
    return pl.pallas_call(
        finish_kernel,
        out_shape=shapes,
        in_specs=[vmem()] * 6 + [anywhere(), vmem()],
        out_specs=[vmem()] * 9,
        scratch_shapes=[
            pltpu.VMEM((32, 3 * WIDTH), HALF_TYPE),
            pltpu.SemaphoreType.DMA,
        ],
        compiler_params=pltpu.CompilerParams(vmem_limit_bytes=62 * 2**20),
    )(*operands)


def on_device(
    tokens,
    group_kind,
    routes,
    norm1_gain,
    qkv_weight,
    proj_weight,
    norm2_gain,
    router_weight,
    frozen_in,
    frozen_out,
    new_in,
    new_out,
    out_grad,
):
    width = WIDTH
    router = router_weight.T
    (
        hidden,
        queries,
        keys,
        values,
        heads,
        attended,
        residual,
        hidden_two,
        totals,
        info,
        returned,
        in_grad,
        in_first,
        grad_back,
        match,
        x_part,
        y_part,
    ) = layer(
        group_kind,
        tokens[0],
        norm1_gain,
        qkv_weight,
        out_grad[0],
        routes[0].T,
        proj_weight,
        norm2_gain,
        router,
        frozen_in[0],
        frozen_out[0],
        new_in[0],
        new_out[0],
    )
    mixed, tokens_grad, in_sum, out_sum, dense_sum, qkv_sum = back(
        group_kind,
        tokens[0],
        norm1_gain,
        norm2_gain,
        out_grad[0],
        residual,
        info,
        match,
        grad_back,
        router,
        proj_weight,
        hidden_two,
        totals,
        queries,
        keys,
        values,
        heads,
        qkv_weight,
        hidden.reshape(LONG, width),
        attended,
        in_grad,
        in_first,
        returned,
        x_part,
        y_part,
    )
    outputs = finish(
        mixed, tokens_grad, in_sum, out_sum, dense_sum, qkv_sum, qkv_weight, norm1_gain
    )
    return tuple(
        value[0] if index in (2, 5) else value for index, value in enumerate(outputs)
    )


def solution(mesh):
    return jax.shard_map(
        on_device,
        mesh=mesh,
        in_specs=(
            P("dp", "expert", None),
            P("dp"),
            P("dp", "expert", None),
            P(),
            P(),
            P(),
            P(),
            P(),
            P("expert", None, None),
            P("expert", None, None),
            P("expert", None, None),
            P("expert", None, None),
            P("dp", "expert", None),
        ),
        out_specs=(
            P("dp", "expert", None),
            P("dp", "expert", None),
            P(("dp", "expert")),
            P(("dp", "expert"), None),
            P(("dp", "expert"), None),
            P(("dp", "expert")),
            P(("dp", "expert"), None),
            P("expert", "dp", None),
            P("expert", "dp", None),
        ),
        check_vma=False,
    )
```

```python
import jax
import jax.numpy as jnp
from jax import lax
from jax.experimental import pallas as pl
from jax.experimental.pallas import tpu as pltpu
from jax.sharding import PartitionSpec as P

HEADS = 12
HD = 64
LONG = 2048
MESH_ID = pl.DeviceIdType.MESH
CHIPS = 4
PAD = 256
BLOCK = 256
HALF = BLOCK // 2
CHUNK = 512
CHUNKS = LONG // CHUNK
LOCAL_HEADS = HEADS // CHIPS
STACK = LOCAL_HEADS * BLOCK
NEGATIVE = -1e30
WIDTH = 768
EXPERTS = 16
SLOTS = 768
EXPERT_ROWS = 384
CAPACITY = 48
FF = 3072
FF_TILE = 768
FF_TILES = 4
DENSE = 1024
LINE = (DENSE + 3 * PAD) // 2
HALF_TYPE = jnp.bfloat16
FULL_TYPE = jnp.float32

epsilon = 1e-05


def norm_parts(values):
    average = jnp.mean(values, axis=-1, keepdims=True)
    centred = values - average
    variance = jnp.mean(centred * centred, axis=-1, keepdims=True)
    inverse = lax.rsqrt(variance + epsilon)
    return (centred * inverse, inverse)


def norm_back(grad_normed, normed, inverse):
    first_mean = jnp.mean(grad_normed, axis=-1, keepdims=True)
    second_mean = jnp.mean(grad_normed * normed, axis=-1, keepdims=True)
    return inverse * (grad_normed - first_mean - normed * second_mean)


def here():
    position = lax.axis_index("expert")
    return position // 2, lax.rem(position, 2)


def device(z, core):
    return (lax.axis_index("dp"), z * 2 + core)


def greet(barrier):
    position = lax.axis_index("expert")
    for step in range(1, 8):
        pl.semaphore_signal(
            barrier,
            inc=1,
            device_id=(lax.axis_index("dp"), lax.rem(position + step, 8)),
            device_id_type=MESH_ID,
        )


def push(source, target, sends, receives, index_here, index_there, where):
    return pltpu.make_async_remote_copy(
        src_ref=source,
        dst_ref=target,
        send_sem=sends.at[index_here],
        recv_sem=receives.at[index_there],
        device_id=where,
        device_id_type=MESH_ID,
    )


def landed(region, sends, receives, index):
    z, core = here()
    push(region, region, sends, receives, index, index, device(z, 1 - core)).wait_recv()


def dot_nn(left, right):
    return jnp.dot(left, right, preferred_element_type=jnp.float32)


def dot_nt(left, right):
    return lax.dot_general(
        left, right, (((1,), (1,)), ((), ())), preferred_element_type=jnp.float32
    )


def dot_tn(left, right):
    return lax.dot_general(
        left, right, (((0,), (0,)), ((), ())), preferred_element_type=jnp.float32
    )


def window(chip):
    return (chip + chip // 2) * 128, lax.rem(chip, 2) * HD


def head_mask(chip, head, value, dtype):
    start = window(chip)[1] + head * HD
    lanes = lax.broadcasted_iota(jnp.int32, (1, PAD), 1)
    inside = (lanes >= start) & (lanes < start + HD)
    return jnp.where(inside, value, 0.0).astype(dtype)


def lane_tiles(values, combine):
    result = values[:, :128]
    for start in range(128, values.shape[1], 128):
        result = combine(result, values[:, start : start + 128])
    return result


def block_rows(block):
    return pl.ds(pl.multiple_of(block * BLOCK, BLOCK), BLOCK)


def chunk_rows(chunk):
    return pl.ds(pl.multiple_of(chunk * CHUNK, CHUNK), CHUNK)


def load_windows(weight_ref, target, sems, chip):
    copies = []
    for part in range(3):
        first = pl.multiple_of(part * WIDTH + window(chip)[0], 128)
        copies.append(
            pltpu.make_async_copy(
                weight_ref.at[:, pl.ds(first, PAD)],
                target.at[:, pl.ds(part * PAD, PAD)],
                sems.at[part],
            )
        )
    for copy in copies:
        copy.start()
    return copies


class RingGather:
    def __init__(self, ref, sends, receives):
        self.ref, self.sends, self.receives = ref, sends, receives
        self.z, self.core = here()
        self.up, self.down = lax.rem(self.z + 1, CHIPS), lax.rem(self.z + 3, CHIPS)
        self.far = lax.rem(self.z + 2, CHIPS)
        self.copies = []

    def region(self, chip, core, half):
        rows = slice(None) if half is None else pl.ds(half * HALF, HALF)
        return self.ref.at[chip * 2 + core, rows]

    def send(self, index, chip, half, where):
        region = self.region(chip, self.core, half)
        copy = push(region, region, self.sends, self.receives, index, index, where)
        copy.start()
        self.copies.append(copy)

    def wait(self, index, chip, core, half):
        landed(self.region(chip, core, half), self.sends, self.receives, index)

    def above(self):
        return device(self.up, self.core)

    def below(self):
        return device(self.down, self.core)

    def beside(self):
        return device(self.z, 1 - self.core)

    def start(self):
        self.send(0, self.z, 0, self.above())
        self.send(1, self.z, 1, self.below())
        self.send(2, self.z, 1, self.above())
        self.send(3, self.z, 0, self.below())
        self.send(4, self.z, None, self.beside())

    def relay(self):
        self.wait(0, self.down, self.core, 0)
        self.send(5, self.down, 0, self.above())
        self.send(7, self.down, 0, self.beside())
        self.wait(1, self.up, self.core, 1)
        self.send(6, self.up, 1, self.below())
        self.send(8, self.up, 1, self.beside())

    def share(self):
        self.wait(2, self.down, self.core, 1)
        self.send(9, self.down, 1, self.beside())
        self.wait(3, self.up, self.core, 0)
        self.send(10, self.up, 0, self.beside())

    def share_far(self):
        self.wait(5, self.far, self.core, 0)
        self.send(11, self.far, 0, self.beside())
        self.wait(6, self.far, self.core, 1)
        self.send(12, self.far, 1, self.beside())

    def other_own(self):
        self.wait(4, self.z, 1 - self.core, None)

    def other_down(self):
        self.wait(7, self.down, 1 - self.core, 0)
        self.wait(9, self.down, 1 - self.core, 1)

    def other_up(self):
        self.wait(8, self.up, 1 - self.core, 1)
        self.wait(10, self.up, 1 - self.core, 0)

    def other_far(self):
        self.wait(11, self.far, 1 - self.core, 0)
        self.wait(12, self.far, 1 - self.core, 1)

    def drain(self):
        for copy in self.copies:
            copy.wait_send()


def plane_device(x, y):
    return (x * 4 + y, lax.axis_index("expert"))


def plane_here():
    group = lax.axis_index("dp")
    return group // 4, lax.rem(group, 4)


def added(left, right):
    return left.astype(jnp.float32) + right.astype(jnp.float32)


class PlaneSum:
    def __init__(self, source, first, direct, combined, sends, receives):
        self.source, self.first = source, first
        self.direct, self.combined = direct, combined
        self.sends, self.receives = sends, receives
        self.x, self.y = plane_here()
        half = source.shape[-1] // 2
        self.left, self.right = pl.ds(0, half), pl.ds(half, half)
        self.low, self.high = pl.ds(0, 2), pl.ds(2, 2)
        self.copies = []

    def x_part(self, x, part):
        return self.source.at[x, part, :, self.left]

    def y_part(self, y, part):
        return self.source.at[part, y, :, self.right]

    def sides(self):
        return (
            (0, self.x, self.x_part, lambda p: plane_device(p, self.y)),
            (2, self.y, self.y_part, lambda p: plane_device(self.x, p)),
        )

    def send(self, source, target, index, where):
        copy = push(source, target, self.sends, self.receives, index, index, where)
        copy.start()
        self.copies.append(copy)

    def wait(self, region, index):
        landed(region, self.sends, self.receives, index)

    def neighbours(self, place):
        return lax.rem(place + 1, 4), lax.rem(place + 3, 4), lax.rem(place + 2, 4)

    def start_far(self):
        for base, place, part, where in self.sides():
            up, down, far = self.neighbours(place)
            self.send(part(far, self.low), self.first.at[base], base, where(up))
            self.send(part(far, self.high), self.first.at[base + 1], base + 1, where(down))

    def start_near(self):
        for base, place, part, where in self.sides():
            up, down, _ = self.neighbours(place)
            self.send(part(up, self.high), self.direct.at[base], base + 4, where(up))
            self.send(part(down, self.low), self.direct.at[base + 1], base + 5, where(down))

    def start(self):
        self.start_far()
        self.start_near()

    def settle_far(self):
        for index in range(4):
            self.wait(self.first.at[index], index)

    def second(self, waits=True):
        low, high = self.low, self.high
        for base, place, part, where in self.sides():
            up, down, _ = self.neighbours(place)
            for index, chosen, to in (
                (base, part(up, low), up),
                (base + 1, part(down, high), down),
            ):
                if waits:
                    self.wait(self.first.at[index], index)
                chosen[...] = added(chosen[...], self.first[index]).astype(jnp.bfloat16)
                self.send(chosen, self.combined.at[index], index + 8, where(to))

    def third(self, x_sum, y_sum):
        low, high = self.low, self.high
        for base, place, part, total in (
            (0, self.x, self.x_part, x_sum),
            (2, self.y, self.y_part, y_sum),
        ):
            self.wait(self.direct.at[base], base + 4)
            self.wait(self.direct.at[base + 1], base + 5)
            self.wait(self.combined.at[base], base + 8)
            self.wait(self.combined.at[base + 1], base + 9)
            total[low] = (
                added(part(place, low)[...], self.combined[base])
                + self.direct[base + 1].astype(jnp.float32)
            ).astype(jnp.bfloat16)
            total[high] = (
                added(part(place, high)[...], self.direct[base])
                + self.combined[base + 1].astype(jnp.float32)
            ).astype(jnp.bfloat16)

    def drain(self):
        for copy in self.copies:
            copy.wait_send()


class PlaneSpread:
    def __init__(self, x_sum, y_sum, land, sends, receives):
        self.x_sum, self.y_sum, self.land = x_sum, y_sum, land
        self.sends, self.receives = sends, receives
        self.x, self.y = plane_here()
        self.copies = []

    def start(self):
        for step in range(1, 4):
            y, x = lax.rem(self.y + step, 4), lax.rem(self.x + step, 4)
            for index, source, where in (
                (step - 1, self.x_sum.at[y], plane_device(self.x, y)),
                (step + 2, self.y_sum.at[x], plane_device(x, self.y)),
            ):
                copy = push(
                    source, self.land.at[index], self.sends, self.receives, index, index, where
                )
                copy.start()
                self.copies.append(copy)

    def total(self):
        sums = []
        for base, mine in ((0, self.x_sum[self.y]), (3, self.y_sum[self.x])):
            value = mine.astype(jnp.float32)
            for index in range(base, base + 3):
                landed(self.land.at[index], self.sends, self.receives, index)
                value += self.land[index].astype(jnp.float32)
            sums.append(value)
        return sums

    def drain(self):
        for copy in self.copies:
            copy.wait_send()


def greet_plane(barrier):
    x, y = plane_here()
    for step in range(1, 4):
        for where in (plane_device(lax.rem(x + step, 4), y), plane_device(x, lax.rem(y + step, 4))):
            pl.semaphore_signal(barrier, inc=1, device_id=where, device_id_type=MESH_ID)


def gelu_parts(u):
    scaled = jnp.abs(u) * 0.7071067811865476
    t = 1.0 / (1.0 + 0.3275911 * scaled)
    poly = t * (
        0.127414796
        + t * (-0.142248368 + t * (0.7107068705 + t * (-0.7265760135 + t * 0.5307027145)))
    )
    density = jnp.exp(-0.5 * u * u)
    tail = poly * density
    cumulative = jnp.where(u >= 0, 1.0 - tail, tail)
    return u * cumulative, cumulative + u * density * 0.3989422804014327


def vmem():
    return pl.BlockSpec(memory_space=pltpu.VMEM)


def smem():
    return pl.BlockSpec(memory_space=pltpu.SMEM)


def anywhere():
    return pl.BlockSpec(memory_space=pl.ANY)


def front_part(
    kind_ref,
    tokens_ref,
    gain_ref,
    weight_ref,
    grad_hbm,
    routes_ref,
    proj_hbm,
    gain_two_ref,
    router_ref,
    hidden_out,
    query_out,
    key_out,
    value_out,
    heads_out,
    attended_out,
    residual_out,
    hidden_two_out,
    total_ref,
    info_ref,
    hidden_ref,
    out_ref,
    attended_ref,
    residual_ref,
    hidden_two_ref,
    sent_ref,
    grad_rows_ref,
    grad_ref,
    proj_ref,
    gather_sems,
    out_sems,
    weight_sems,
    store_sems,
    begin_rows,
):
    z, core = here()
    mine = z * 2 + core
    up, down, far = lax.rem(z + 1, CHIPS), lax.rem(z + 3, CHIPS), lax.rem(z + 2, CHIPS)
    barrier = pltpu.get_barrier_semaphore()
    greet(barrier)
    greet_plane(barrier)
    late_loads = [
        pltpu.make_async_copy(grad_hbm, grad_ref, weight_sems.at[3]),
        pltpu.make_async_copy(proj_hbm, proj_ref, weight_sems.at[4]),
    ]
    for load in late_loads:
        load.start()
    tokens = tokens_ref[...].astype(jnp.float32)
    normed, _ = norm_parts(tokens)
    hidden_ref[mine] = (normed * gain_ref[...][None]).astype(jnp.bfloat16)
    pl.semaphore_wait(barrier, 13)
    gather = RingGather(hidden_ref, gather_sems.at[0], gather_sems.at[1])
    stores, store_count = [], [0]

    def store(source, target):
        copy = pltpu.make_async_copy(source, target, store_sems.at[store_count[0]])
        copy.start()
        store_count[0] += 1
        stores.append(copy)

    out_send, out_recv = out_sems.at[0], out_sems.at[1]
    gather.start()
    routes = routes_ref[...].astype(jnp.float32)
    names = lax.broadcasted_iota(jnp.int32, (EXPERTS, BLOCK), 0).astype(jnp.float32)
    pick_zero = jnp.where(names == routes[0:1, :], 1.0, 0.0)
    pick_one = jnp.where(names == routes[1:2, :], 1.0, 0.0)
    row = lax.broadcasted_iota(jnp.int32, (BLOCK, BLOCK), 0)
    column = lax.broadcasted_iota(jnp.int32, (BLOCK, BLOCK), 1)
    before = jnp.where(row < column, 1.0, 0.0).astype(jnp.bfloat16)
    earlier = dot_nn((pick_zero + pick_one).astype(jnp.bfloat16), before)
    places = []
    for index, pick in enumerate((pick_zero, pick_one)):
        slot = jnp.sum(earlier * pick, axis=0, keepdims=True)
        place = routes[index : index + 1, :] * CAPACITY + slot
        places.append(jnp.where(slot < CAPACITY, place, -1.0))

    def attention(
        query_ref,
        key_ref,
        value_ref,
        weight,
        stacked,
        diagonal,
        beside,
        scores,
        largest,
        sums,
        acc,
    ):
        loads = load_windows(weight_ref, weight, weight_sems, z)

        def project(block):
            projected = dot_nn(hidden_ref[block], weight[...]).astype(jnp.bfloat16)
            query_ref[block] = projected[:, :PAD]
            key_ref[block_rows(block), :] = projected[:, PAD : 2 * PAD]
            value_ref[block_rows(block), :] = projected[:, 2 * PAD :]

        for load in loads:
            load.wait()
        project(mine)
        gather.relay()
        gather.other_own()
        project(z * 2 + 1 - core)
        gather.share()
        project(down * 2 + core)
        project(up * 2 + core)
        gather.other_down()
        project(down * 2 + 1 - core)
        gather.other_up()
        project(up * 2 + 1 - core)
        gather.share_far()
        project(far * 2 + core)
        gather.other_far()
        project(far * 2 + 1 - core)
        store(hidden_ref, hidden_out)
        store(query_ref, query_out)
        store(key_ref, key_out)
        store(value_ref, value_out)

        kind_bias = kind_ref[0].astype(jnp.float32) * NEGATIVE

        def attend(step):
            slot = lax.rem(z + CHIPS - 1 - step, CHIPS)
            block = slot * 2 + lax.rem(core + slot, 2)
            queries = query_ref[block]
            for head in range(LOCAL_HEADS):
                stacked[head * BLOCK : (head + 1) * BLOCK, :] = queries * head_mask(
                    z, head, HD ** (-0.5), jnp.bfloat16
                )

            def bias_of(chunk):
                return jnp.where((slot >= 2) & (chunk < 2), kind_bias, 0.0)

            masked = dot_nt(stacked[...], key_ref[block_rows(block), :])
            row = lax.broadcasted_iota(jnp.int32, (BLOCK, BLOCK), 0)
            column = lax.broadcasted_iota(jnp.int32, (BLOCK, BLOCK), 1)
            for head in range(LOCAL_HEADS):
                part = slice(head * BLOCK, (head + 1) * BLOCK)
                values = jnp.where(column <= row, masked[part], NEGATIVE)
                diagonal[part, :] = values
                largest[part, :] = lane_tiles(values, jnp.maximum)
            is_odd = block != 2 * slot

            @pl.when(is_odd)
            def _():
                values = dot_nt(stacked[...], key_ref[block_rows(block - 1), :])
                beside[...] = values
                largest[...] = jnp.maximum(largest[...], lane_tiles(values, jnp.maximum))

            @pl.loop(0, slot)
            def _(chunk):
                values = dot_nt(stacked[...], key_ref[chunk_rows(chunk), :])
                scores[chunk] = values
                largest[...] = jnp.maximum(
                    largest[...], lane_tiles(values, jnp.maximum) + bias_of(chunk)
                )

            row_max = jnp.max(largest[...], axis=1, keepdims=True)
            largest[...] = jnp.broadcast_to(row_max, largest.shape)
            exponent = jnp.exp(diagonal[...] - row_max)
            sums[...] = lane_tiles(exponent, jnp.add)
            acc[...] = dot_nn(exponent.astype(jnp.bfloat16), value_ref[block_rows(block), :])

            @pl.when(is_odd)
            def _():
                exponent = jnp.exp(beside[...] - largest[:, :1])
                sums[...] += lane_tiles(exponent, jnp.add)
                acc[...] += dot_nn(exponent.astype(jnp.bfloat16), value_ref[block_rows(block - 1), :])

            @pl.loop(0, slot)
            def _(chunk):
                exponent = jnp.exp(scores[chunk] - (largest[:, :1] - bias_of(chunk)))
                sums[...] += lane_tiles(exponent, jnp.add)
                acc[...] += dot_nn(exponent.astype(jnp.bfloat16), value_ref[chunk_rows(chunk), :])

            total = jnp.sum(sums[...], axis=1, keepdims=True)
            inverse = 1.0 / total
            log_total = largest[...] + jnp.log(total)
            attended = jnp.zeros((BLOCK, PAD), jnp.float32)
            for head in range(LOCAL_HEADS):
                part = slice(head * BLOCK, (head + 1) * BLOCK)
                attended += acc[part, :] * inverse[part] * head_mask(z, head, 1.0, jnp.float32)
                total_ref[slot, head : head + 1, :] = jnp.transpose(log_total[part, :])[:1, :]
            out_ref[slot] = attended.astype(jnp.bfloat16)

            @pl.when(block != mine)
            def _():
                push(
                    out_ref.at[slot],
                    attended_ref.at[z],
                    out_send,
                    out_recv,
                    slot,
                    z,
                    device(slot, lax.rem(core + slot, 2)),
                ).start()

            @pl.when(block == mine)
            def _():
                attended_ref[z] = out_ref[slot]

        pl.loop(0, CHIPS)(attend)
        gather.drain()
        for copy in stores:
            copy.wait()

    pl.run_scoped(
        attention,
        pltpu.VMEM((8, BLOCK, PAD), HALF_TYPE),
        pltpu.VMEM((LONG, PAD), HALF_TYPE),
        pltpu.VMEM((LONG, PAD), HALF_TYPE),
        pltpu.VMEM((WIDTH, 3 * PAD), HALF_TYPE),
        pltpu.VMEM((STACK, PAD), HALF_TYPE),
        pltpu.VMEM((STACK, BLOCK), FULL_TYPE),
        pltpu.VMEM((STACK, BLOCK), FULL_TYPE),
        pltpu.VMEM((CHUNKS - 1, STACK, CHUNK), FULL_TYPE),
        pltpu.VMEM((STACK, 128), FULL_TYPE),
        pltpu.VMEM((STACK, 128), FULL_TYPE),
        pltpu.VMEM((STACK, PAD), FULL_TYPE),
    )
    stores.clear()
    store(out_ref, heads_out)

    @pl.loop(0, CHIPS)
    def _(slot):
        @pl.when((slot != z) | (lax.rem(core + z, 2) != core))
        def _():
            landed(attended_ref.at[slot], out_send, out_recv, slot)

    store(attended_ref, attended_out)
    for load in late_loads:
        load.wait()
    residual = tokens_ref[...].astype(jnp.float32)
    for chip in range(CHIPS):
        first = (chip + chip // 2) * 128
        residual += dot_nn(attended_ref[chip], proj_ref[first : first + PAD, :])
    residual_ref[...] = residual
    normed_two, _ = norm_parts(residual)
    hidden_two = (normed_two * gain_two_ref[...][None]).astype(jnp.bfloat16)
    hidden_two_ref[...] = hidden_two
    store(residual_ref, residual_out)
    store(hidden_two_ref, hidden_two_out)
    logits = dot_nt(router_ref[...], hidden_two)
    logit_zero = jnp.sum(logits * pick_zero, axis=0, keepdims=True)
    logit_one = jnp.sum(logits * pick_one, axis=0, keepdims=True)
    gate_zero = 1.0 / (1.0 + jnp.exp(logit_one - logit_zero))
    gate_one = 1.0 / (1.0 + jnp.exp(logit_zero - logit_one))
    for index, line in enumerate((*places, gate_zero, gate_one, routes[0:1], routes[1:2])):
        info_ref[index : index + 1, :] = line
    info_ref[6:8, :] = jnp.zeros((2, BLOCK), jnp.float32)
    ids = lax.broadcasted_iota(jnp.int32, (SLOTS, BLOCK), 0).astype(jnp.float32)
    chosen = jnp.where((ids == places[0]) | (ids == places[1]), 1.0, 0.0).astype(jnp.bfloat16)
    sent = dot_nn(chosen, hidden_two).astype(jnp.bfloat16)
    sent_ref[0] = sent[:EXPERT_ROWS]
    sent_ref[1] = sent[EXPERT_ROWS:]
    begin_rows(0)
    mixing = (
        jnp.where(ids == places[0], gate_zero, 0.0) + jnp.where(ids == places[1], gate_one, 0.0)
    ).astype(jnp.bfloat16)
    rows = dot_nn(mixing, grad_ref[...]).astype(jnp.bfloat16)
    grad_rows_ref[0] = rows[:EXPERT_ROWS]
    grad_rows_ref[1] = rows[EXPERT_ROWS:]
    begin_rows(1)

    def finish_front():

        @pl.loop(0, CHIPS)
        def _(slot):
            @pl.when(slot * 2 + lax.rem(core + slot, 2) != mine)
            def _():
                push(
                    out_ref.at[slot],
                    attended_ref.at[slot],
                    out_send,
                    out_recv,
                    slot,
                    slot,
                    device(z, 1 - core),
                ).wait_send()

        for copy in stores:
            copy.wait()

    return finish_front


def expert_part(
    sent_ref,
    grad_rows_ref,
    in_frozen,
    out_frozen,
    in_new,
    out_new,
    returned_ref,
    in_grad_ref,
    in_first_ref,
    grad_back_ref,
    match_ref,
    x_sum_ref,
    y_sum_ref,
    x_land,
    g_land,
    r_send,
    b_send,
    in_grad,
    out_grad,
    first,
    direct,
    combined,
    in_first,
    match_send,
    load_sems,
    x_sems,
    g_sems,
    b_sems,
    match_sems,
    plane_sems,
    in_sems,
    store_sems,
):
    mine = lax.axis_index("expert")

    def rows_of(place):
        return pl.ds(pl.multiple_of(place * CAPACITY, CAPACITY), CAPACITY)

    own_rows = rows_of(mine)

    def peer(step):
        return lax.rem(mine + step, 8)

    def exchange(source, target, sems, index, step):
        return push(
            source, target, sems.at[0], sems.at[1], index, index, (lax.axis_index("dp"), peer(step))
        )

    stores, used = [], []

    def store(source, target):
        copy = pltpu.make_async_copy(source, target, store_sems.at[len(stores)])
        copy.start()
        stores.append(copy)

    def seven(ref, sem):
        region = ref.at[0, pl.ds(0, 7 * CAPACITY), :]
        return pltpu.make_async_copy(region, region, sem)

    def spread_kind(kind, source, target, sems):
        for step in range(1, 8):
            exchange(
                source.at[kind, rows_of(peer(step)), :],
                target.at[kind, own_rows, :],
                sems,
                kind,
                step,
            ).start()
        used.append((target, sems.at[0, kind]))

    def collect_kind(kind, target, sems):
        seven(target, sems.at[1, kind]).wait()

    def begin_rows(which):
        source, target, sems = ((sent_ref, x_land, x_sems), (grad_rows_ref, g_land, g_sems))[which]
        if which == 1:
            spread_kind(1, source, target, sems)
            spread_kind(0, sent_ref, x_land, x_sems)
            spread_kind(0, source, target, sems)
        else:
            spread_kind(1, source, target, sems)
        target[:, own_rows, :] = source[:, own_rows, :]

    def work(w_in, w_out, activated, slope, acc):
        loads = []
        for index, (source, target) in enumerate(
            (
                (in_new, w_in.at[1]),
                (out_new, w_out.at[1]),
                (in_frozen, w_in.at[0]),
                (out_frozen, w_out.at[0]),
            )
        ):
            copy = pltpu.make_async_copy(source, target, load_sems.at[index])
            copy.start()
            loads.append(copy)

        def tile_of(index):
            return pl.ds(pl.multiple_of(index * FF_TILE, FF_TILE), FF_TILE)

        plane = PlaneSum(out_grad, first, direct, combined, plane_sems.at[0], plane_sems.at[1])
        in_plane = PlaneSum(in_grad, in_first, None, None, in_sems.at[0], in_sems.at[1])
        matches = [None, None]
        for kind in (1, 0):
            collect_kind(kind, x_land, x_sems)
            loads[0 if kind == 1 else 2].wait()
            loads[1 if kind == 1 else 3].wait()
            acc[...] = jnp.zeros_like(acc)

            @pl.loop(0, FF_TILES, unroll=True)
            def _(index):
                tile = tile_of(index)
                pre = dot_nn(x_land[kind], w_in[kind, :, tile])
                value, steep = gelu_parts(pre)
                value = value.astype(jnp.bfloat16)
                if kind == 1:
                    activated[:, tile] = value
                slope[:, tile] = steep.astype(jnp.bfloat16)
                acc[...] += dot_nn(value, w_out[kind, tile, :])

            collect_kind(kind, g_land, g_sems)
            result = acc[...].astype(jnp.bfloat16)
            r_send[kind] = result
            store(r_send.at[kind], returned_ref.at[kind])
            products = result.astype(jnp.float32) * g_land[kind].astype(jnp.float32)
            matches[kind] = jnp.sum(products, axis=1, keepdims=True)
            if kind == 1:

                @pl.loop(0, FF_TILES, unroll=True)
                def _(index):
                    weights = dot_tn(activated[:, tile_of(index)], g_land[1]).astype(jnp.bfloat16)
                    for y in range(4):
                        for part in range(4):
                            start = (y * 4 + part) * CAPACITY
                            out_grad[index, y, :, part * WIDTH : (part + 1) * WIDTH] = weights[
                                start : start + CAPACITY
                            ]

                plane.start()

            acc[...] = jnp.zeros_like(acc)

            @pl.loop(0, FF_TILES, unroll=True)
            def _(index):
                tile = tile_of(index)
                grad = dot_nt(g_land[kind], w_out[kind, tile, :])
                grad = (grad * slope[:, tile].astype(jnp.float32)).astype(jnp.bfloat16)
                acc[...] += dot_nt(grad, w_in[kind, :, tile])
                if kind == 1:
                    activated[:, tile] = grad

            b_send[kind] = acc[...].astype(jnp.bfloat16)
            grad_back_ref[kind, own_rows, :] = b_send[kind, own_rows, :]
            spread_kind(kind, b_send, grad_back_ref, b_sems)
            if kind == 1:

                @pl.loop(0, FF_TILES, unroll=True)
                def _(index):
                    tile = tile_of(index)
                    weights = dot_tn(x_land[1], activated[:, tile]).astype(jnp.bfloat16)
                    in_grad[:, :, :, tile] = weights.reshape(4, 4, CAPACITY, FF_TILE)

                in_plane.start_far()
                store(in_grad, in_grad_ref)
        lanes = lax.broadcasted_iota(jnp.int32, (EXPERT_ROWS, 128), 1)
        match_send[0] = jnp.where(lanes < 64, matches[0], matches[1])
        match_ref[0, own_rows, :] = match_send[0, own_rows, :]
        spread_kind(0, match_send, match_ref, match_sems)
        plane.second()
        plane.third(x_sum_ref, y_sum_ref)
        collect_kind(0, match_ref, match_sems)
        for kind in (1, 0):
            collect_kind(kind, grad_back_ref, b_sems)
        in_plane.settle_far()
        store(in_first, in_first_ref)
        for target, sem in used:
            seven(target, sem).wait()
        plane.drain()
        in_plane.drain()
        for copy in stores:
            copy.wait()

    def run():
        pl.run_scoped(
            work,
            pltpu.VMEM((2, WIDTH, FF), HALF_TYPE),
            pltpu.VMEM((2, FF, WIDTH), HALF_TYPE),
            pltpu.VMEM((EXPERT_ROWS, FF), HALF_TYPE),
            pltpu.VMEM((EXPERT_ROWS, FF), HALF_TYPE),
            pltpu.VMEM((EXPERT_ROWS, WIDTH), FULL_TYPE),
        )

    return begin_rows, run


def layer_kernel(*refs):
    front_in, rest = refs[:9], refs[9:]
    expert_in, rest = rest[:4], rest[4:]
    front_out, rest = rest[:10], rest[10:]
    expert_out, rest = rest[:7], rest[7:]
    front_scratch, expert_scratch = rest[:13], rest[13:]
    sent, grad_rows = front_scratch[5:7]
    begin_rows, run_experts = expert_part(sent, grad_rows, *expert_in, *expert_out, *expert_scratch)
    finish_front = front_part(*front_in, *front_out, *front_scratch, begin_rows)
    run_experts()
    finish_front()


def layer(*operands):
    def shape(*dims, dtype=HALF_TYPE):
        return jax.ShapeDtypeStruct(dims, dtype)

    def pair(count):
        return pltpu.SemaphoreType.DMA((2, count))

    shapes = [
        shape(8, BLOCK, WIDTH),
        shape(8, BLOCK, PAD),
        shape(LONG, PAD),
        shape(LONG, PAD),
        shape(CHIPS, BLOCK, PAD),
        shape(CHIPS, BLOCK, PAD),
        shape(BLOCK, WIDTH, dtype=FULL_TYPE),
        shape(BLOCK, WIDTH),
        shape(CHIPS, 8, BLOCK, dtype=FULL_TYPE),
        shape(8, BLOCK, dtype=FULL_TYPE),
        shape(2, EXPERT_ROWS, WIDTH),
        shape(4, 4, CAPACITY, FF),
        shape(4, 2, CAPACITY, FF // 2),
        shape(2, EXPERT_ROWS, WIDTH),
        shape(1, EXPERT_ROWS, 128, dtype=FULL_TYPE),
        shape(4, CAPACITY, FF // 2),
        shape(4, CAPACITY, FF // 2),
    ]
    return pl.pallas_call(
        layer_kernel,
        out_shape=shapes,
        in_specs=[
            smem(),
            vmem(),
            vmem(),
            anywhere(),
            anywhere(),
            vmem(),
            anywhere(),
            vmem(),
            vmem(),
        ]
        + [anywhere()] * 4,
        out_specs=[anywhere()] * 8 + [vmem()] * 2 + [anywhere()] * 3 + [vmem()] * 4,
        scratch_shapes=[
            pltpu.VMEM((8, BLOCK, WIDTH), HALF_TYPE),
            pltpu.VMEM((CHIPS, BLOCK, PAD), HALF_TYPE),
            pltpu.VMEM((CHIPS, BLOCK, PAD), HALF_TYPE),
            pltpu.VMEM((BLOCK, WIDTH), FULL_TYPE),
            pltpu.VMEM((BLOCK, WIDTH), HALF_TYPE),
            pltpu.VMEM((2, EXPERT_ROWS, WIDTH), HALF_TYPE),
            pltpu.VMEM((2, EXPERT_ROWS, WIDTH), HALF_TYPE),
            pltpu.VMEM((BLOCK, WIDTH), HALF_TYPE),
            pltpu.VMEM((WIDTH, WIDTH), HALF_TYPE),
            pair(13),
            pair(CHIPS),
            pltpu.SemaphoreType.DMA((5,)),
            pltpu.SemaphoreType.DMA((8,)),
            pltpu.VMEM((2, EXPERT_ROWS, WIDTH), HALF_TYPE),
            pltpu.VMEM((2, EXPERT_ROWS, WIDTH), HALF_TYPE),
            pltpu.VMEM((2, EXPERT_ROWS, WIDTH), HALF_TYPE),
            pltpu.VMEM((2, EXPERT_ROWS, WIDTH), HALF_TYPE),
            pltpu.VMEM((4, 4, CAPACITY, FF), HALF_TYPE),
            pltpu.VMEM((4, 4, CAPACITY, FF), HALF_TYPE),
            pltpu.VMEM((4, 2, CAPACITY, FF // 2), HALF_TYPE),
            pltpu.VMEM((4, 2, CAPACITY, FF // 2), HALF_TYPE),
            pltpu.VMEM((4, 2, CAPACITY, FF // 2), HALF_TYPE),
            pltpu.VMEM((4, 2, CAPACITY, FF // 2), HALF_TYPE),
            pltpu.VMEM((1, EXPERT_ROWS, 128), FULL_TYPE),
            pltpu.SemaphoreType.DMA((4,)),
            pair(2),
            pair(2),
            pair(2),
            pair(2),
            pair(12),
            pair(4),
            pltpu.SemaphoreType.DMA((4,)),
        ],
        compiler_params=pltpu.CompilerParams(
            collective_id=0, has_side_effects=True, vmem_limit_bytes=62 * 2**20
        ),
    )(*operands)


def slot_rows(place):
    return pl.ds(pl.multiple_of(place * CAPACITY, CAPACITY), CAPACITY)


def back_kernel(
    kind_ref,
    tokens_ref,
    gain_ref,
    gain_two_ref,
    grad_ref,
    residual_ref,
    info_ref,
    match_ref,
    grad_back_ref,
    router_ref,
    proj_ref,
    hidden_two_ref,
    total_ref,
    query_hbm,
    key_hbm,
    value_hbm,
    heads_hbm,
    weight_hbm,
    hidden_hbm,
    attended_hbm,
    in_grad_hbm,
    in_first_hbm,
    returned_hbm,
    x_part_hbm,
    y_part_hbm,
    mixed_ref,
    tokens_grad_ref,
    in_sum_ref,
    out_sum_ref,
    dense_sum_ref,
    qkv_sum_ref,
    dense_land,
    query_ref,
    key_ref,
    value_ref,
    heads_ref,
    weight,
    hidden_ref,
    attended_ref,
    x_part,
    y_part,
    out_land,
    returned,
    grad_residual,
    grad_sent,
    grad_out,
    stacked,
    grad_stacked,
    grad_query,
    grad_key,
    grad_value,
    projected,
    part_sib,
    part_own,
    land_sib,
    land_half,
    land_full,
    big,
    big_first,
    big_direct,
    big_combined,
    big_x,
    big_y,
    big_land,
    mid,
    mid_first,
    mid_direct,
    mid_combined,
    mid_x,
    mid_y,
    mid_land,
    qkv,
    qkv_first,
    qkv_direct,
    qkv_combined,
    qkv_x,
    qkv_y,
    qkv_land,
    dense_send,
    weight_sems,
    load_sems,
    grad_sems,
    sib_sems,
    ring_sems,
    big_sems,
    out_spread,
    big_spread,
    mid_sems,
    mid_spread,
    qkv_sems,
    qkv_spread,
    dense_sems,
    returned_sems,
):
    z, core = here()
    mine = z * 2 + core
    up, down, far = lax.rem(z + 1, CHIPS), lax.rem(z + 3, CHIPS), lax.rem(z + 2, CHIPS)
    barrier = pltpu.get_barrier_semaphore()
    greet(barrier)
    greet_plane(barrier)
    loads = []
    for index, (source, target) in enumerate(
        (
            (in_grad_hbm, big),
            (in_first_hbm, big_first),
            (x_part_hbm, x_part),
            (y_part_hbm, y_part),
            (
                returned_hbm.at[:, slot_rows(mine), :],
                returned.at[:, slot_rows(mine), :],
            ),
            (attended_hbm, attended_ref),
            (query_hbm, query_ref),
            (key_hbm, key_ref),
            (value_hbm, value_ref),
            (heads_hbm, heads_ref),
            (hidden_hbm, hidden_ref),
        )
    ):
        copy = pltpu.make_async_copy(source, target, load_sems.at[index])
        copy.start()
        loads.append(copy)
    weight_loads = load_windows(weight_hbm, weight, weight_sems, z)

    info = info_ref[...]
    columns = jnp.transpose(
        jnp.concatenate([info, jnp.zeros((120, BLOCK), jnp.float32)], axis=0)
    )
    lane_ids = lax.broadcasted_iota(jnp.int32, (BLOCK, SLOTS), 1).astype(jnp.float32)
    at_zero, at_one = lane_ids == columns[:, 0:1], lane_ids == columns[:, 1:2]
    ids = lax.broadcasted_iota(jnp.int32, (SLOTS, BLOCK), 0).astype(jnp.float32)
    lines = match_ref[0]
    match = jnp.concatenate(
        [jnp.broadcast_to(lines[:, lane : lane + 1], (EXPERT_ROWS, BLOCK)) for lane in (0, 64)],
        axis=0,
    )
    parts = []
    for place, gate in ((0, 2), (1, 3)):
        value = jnp.sum(
            jnp.where(ids == info[place : place + 1, :], match, 0.0), axis=0, keepdims=True
        )
        used = info[gate : gate + 1, :].astype(jnp.bfloat16).astype(jnp.float32)
        ratio = jnp.where(used > 0.0, info[gate : gate + 1, :] / jnp.where(used > 0.0, used, 1.0), 1.0)
        parts.append(value * ratio)
    gap = parts[0] * info[3:4, :] - parts[1] * info[2:3, :]
    names = lax.broadcasted_iota(jnp.int32, (EXPERTS, BLOCK), 0).astype(jnp.float32)
    pick_zero = jnp.where(names == info[4:5, :], 1.0, 0.0)
    pick_one = jnp.where(names == info[5:6, :], 1.0, 0.0)
    grad_logits = (gap * (pick_zero - pick_one)).astype(jnp.bfloat16)
    chosen = jnp.where(at_zero | at_one, 1.0, 0.0).astype(jnp.bfloat16)
    grad_two = (
        dot_tn(grad_logits, router_ref[...])
        + dot_nn(chosen[:, :EXPERT_ROWS], grad_back_ref[0])
        + dot_nn(chosen[:, EXPERT_ROWS:], grad_back_ref[1])
    )
    normed_two, inverse_two = norm_parts(residual_ref[...])
    gain_two_grad = jnp.sum(grad_two * normed_two, axis=0, keepdims=True)
    grad_residual[...] = grad_ref[...].astype(jnp.float32) + norm_back(
        grad_two * gain_two_ref[...][None], normed_two, inverse_two
    )
    grad_branch = grad_residual[...].astype(jnp.bfloat16)
    for chip in range(CHIPS):
        first = (chip + chip // 2) * 128
        grad_sent[chip] = dot_nt(grad_branch, proj_ref[first : first + PAD, :]).astype(
            jnp.bfloat16
        )
    pl.semaphore_wait(barrier, 13)
    owner_core = lax.rem(core + z, 2)
    grad_send, grad_recv = grad_sems.at[0], grad_sems.at[1]

    @pl.loop(0, CHIPS)
    def _(step):
        chip = lax.rem(z + step, CHIPS)
        mine_too = (chip == z) & (owner_core == core)

        @pl.when(jnp.logical_not(mine_too))
        def _():
            push(
                grad_sent.at[chip],
                grad_out.at[z],
                grad_send,
                grad_recv,
                chip,
                z,
                device(chip, owner_core),
            ).start()

        @pl.when(mine_too)
        def _():
            grad_out[z] = grad_sent[chip]

    for step in range(1, 8):
        place = lax.rem(mine + step, 8)
        copy = push(
            returned_hbm.at[:, slot_rows(place), :],
            returned.at[:, slot_rows(mine), :],
            returned_sems.at[0],
            returned_sems.at[1],
            0,
            0,
            (lax.axis_index("dp"), place),
        )
        copy.start()
    for load in loads[:4]:
        load.wait()
    big_sum = PlaneSum(big, big_first, big_direct, big_combined, big_sems.at[0], big_sems.at[1])
    big_sum.start_near()
    big_sum.second(waits=False)
    loads[5].wait()
    for chip in range(CHIPS):
        grads = dot_tn(attended_ref[chip], grad_branch).astype(jnp.bfloat16)
        first = (chip % 2) * HD
        for y in range(4):
            start = first + y * CAPACITY
            mid[chip, y, :, :WIDTH] = grads[start : start + CAPACITY]
    narrow = jnp.concatenate(
        [
            dot_nn(grad_logits, hidden_two_ref[...]),
            gain_two_grad,
            jnp.zeros((111, WIDTH), jnp.float32),
        ],
        axis=0,
    )
    mid[:, :, :, WIDTH : WIDTH + 128] = (
        jnp.transpose(narrow).astype(jnp.bfloat16).reshape(4, 4, CAPACITY, 128)
    )
    mid[:, :, :, WIDTH + 128 :] = jnp.zeros((4, 4, CAPACITY, 128), jnp.bfloat16)
    mid_sum = PlaneSum(mid, mid_first, mid_direct, mid_combined, mid_sems.at[0], mid_sems.at[1])
    mid_sum.start()
    out_sum = PlaneSpread(x_part, y_part, out_land, out_spread.at[0], out_spread.at[1])
    out_sum.start()

    grad_key[...] = jnp.zeros_like(grad_key)
    grad_value[...] = jnp.zeros_like(grad_value)
    projected[...] = jnp.zeros_like(projected)
    for load in loads[6:10]:
        load.wait()
    kind_bias = kind_ref[0].astype(jnp.float32) * NEGATIVE

    def attend(step):
        slot = lax.rem(z + step, CHIPS)
        block = slot * 2 + lax.rem(core + slot, 2)

        @pl.when(block != mine)
        def _():
            landed(grad_out.at[slot], grad_send, grad_recv, slot)

        queries = query_ref[block]
        grads = grad_out[slot]
        products = grads.astype(jnp.float32) * heads_ref[slot].astype(jnp.float32)
        selector = jnp.concatenate(
            [head_mask(z, head, 1.0, jnp.float32) for head in range(LOCAL_HEADS)]
            + [jnp.zeros((8 - LOCAL_HEADS, PAD), jnp.float32)],
            axis=0,
        )
        deltas = lax.dot_general(
            selector,
            products,
            (((1,), (1,)), ((), ())),
            preferred_element_type=jnp.float32,
            precision=lax.Precision.HIGHEST,
        )
        for head in range(LOCAL_HEADS):
            part = slice(head * BLOCK, (head + 1) * BLOCK)
            stacked[part, :] = queries * head_mask(z, head, HD ** (-0.5), jnp.bfloat16)
            grad_stacked[part, :] = grads * head_mask(z, head, 1.0, jnp.bfloat16)
        totals = total_ref[slot]
        delta_row = jnp.concatenate(
            [deltas[head : head + 1, :] for head in range(LOCAL_HEADS)], axis=1
        )
        total_row = jnp.concatenate(
            [totals[head : head + 1, :] for head in range(LOCAL_HEADS)], axis=1
        )

        def work(rows, bias, is_diagonal):
            keys, values = key_ref[rows, :], value_ref[rows, :]
            probs = jnp.exp(dot_nt(keys, stacked[...]) - (total_row - bias))
            if is_diagonal:
                row = lax.broadcasted_iota(jnp.int32, (BLOCK, STACK), 0)
                column = lax.broadcasted_iota(jnp.int32, (BLOCK, STACK), 1)
                probs = jnp.where(row <= lax.rem(column, BLOCK), probs, 0.0)
            grad_probs = dot_nt(values, grad_stacked[...])
            grad_scores = (probs * (grad_probs - delta_row)).astype(jnp.bfloat16)
            grad_value[rows, :] += dot_nn(probs.astype(jnp.bfloat16), grad_stacked[...])
            grad_key[rows, :] += dot_nn(grad_scores, stacked[...])
            return dot_tn(grad_scores, keys)

        grad_query[...] = work(block_rows(block), 0.0, True)

        @pl.when(block != 2 * slot)
        def _():
            grad_query[...] += work(block_rows(block - 1), 0.0, False)

        @pl.loop(0, slot)
        def _(chunk):
            bias = jnp.where((slot >= 2) & (chunk < 2), kind_bias, 0.0)
            grad_query[...] += work(chunk_rows(chunk), bias, False)

        combined = jnp.zeros((BLOCK, PAD), jnp.float32)
        for head in range(LOCAL_HEADS):
            part = slice(head * BLOCK, (head + 1) * BLOCK)
            combined += grad_query[part, :] * head_mask(z, head, HD ** (-0.5), jnp.float32)
        projected[block_rows(block), :PAD] = combined.astype(jnp.bfloat16)

    pl.loop(0, CHIPS)(attend)
    projected[:, PAD : 2 * PAD] = grad_key[...].astype(jnp.bfloat16)
    projected[:, 2 * PAD :] = grad_value[...].astype(jnp.bfloat16)
    for load in weight_loads:
        load.wait()

    def partial(chip, which):
        return dot_nt(projected[block_rows(chip * 2 + which), :], weight[...])

    sib_send, sib_recv = sib_sems.at[0], sib_sems.at[1]

    def sib_copy(index):
        return push(
            part_sib.at[index],
            land_sib.at[index],
            sib_send,
            sib_recv,
            index,
            index,
            device(z, 1 - core),
        )

    order = (far, up, down, z)
    for index, chip in enumerate(order):
        part_sib[index] = partial(chip, 1 - core).astype(jnp.bfloat16)
        sib_copy(index).start()

    loads[10].wait()
    for tile in range(3):
        lanes = slice(tile * PAD, (tile + 1) * PAD)
        weights = dot_tn(hidden_ref[...], projected[:, lanes]).astype(jnp.bfloat16)
        qkv[:, :, :, lanes] = weights.reshape(4, 4, CAPACITY, PAD)
    qkv_sum = PlaneSum(
        qkv, qkv_first, qkv_direct, qkv_combined, qkv_sems.at[0], qkv_sems.at[1]
    )
    qkv_sum.start()
    mid_sum.second()


    def own(index):
        value = partial(order[index], core)
        landed(land_sib.at[index], sib_send, sib_recv, index)
        return value + land_sib[index].astype(jnp.float32)

    first, second = pl.ds(0, HALF), pl.ds(HALF, HALF)
    ring_send, ring_recv = ring_sems.at[0], ring_sems.at[1]
    copies = []

    def ring(source, target, index, where):
        copy = push(source, target, ring_send, ring_recv, index, index, where)
        copy.start()
        copies.append(copy)

    above, below = device(up, core), device(down, core)
    part_own[0] = own(0).astype(jnp.bfloat16)
    ring(part_own.at[0, first], land_half.at[0], 0, above)
    ring(part_own.at[0, second], land_half.at[1], 1, below)
    part_own[1] = own(1).astype(jnp.bfloat16)
    ring(part_own.at[1, second], land_full.at[0, second], 2, above)
    part_own[2] = own(2).astype(jnp.bfloat16)
    ring(part_own.at[2, first], land_full.at[1, first], 3, below)
    grad_one = own(3)
    qkv_sum.second()
    landed(land_half.at[0], ring_send, ring_recv, 0)
    part_own[1, first, :] = added(part_own[1, first, :], land_half[0]).astype(jnp.bfloat16)
    ring(part_own.at[1, first], land_full.at[0, first], 4, above)
    landed(land_half.at[1], ring_send, ring_recv, 1)
    part_own[2, second, :] = added(part_own[2, second, :], land_half[1]).astype(jnp.bfloat16)
    ring(part_own.at[2, second], land_full.at[1, second], 5, below)
    mid_sum.third(mid_x, mid_y)
    mid_total = PlaneSpread(mid_x, mid_y, mid_land, mid_spread.at[0], mid_spread.at[1])
    mid_total.start()
    qkv_sum.third(qkv_x, qkv_y)
    qkv_total = PlaneSpread(qkv_x, qkv_y, qkv_land, qkv_spread.at[0], qkv_spread.at[1])
    qkv_total.start()
    big_sum.third(big_x, big_y)
    big_total = PlaneSpread(big_x, big_y, big_land, big_spread.at[0], big_spread.at[1])
    big_total.start()
    loads[4].wait()
    seven = returned.at[:, pl.ds(0, 7 * CAPACITY), :]
    pltpu.make_async_copy(seven, seven, returned_sems.at[1, 0]).wait()
    mixing = (
        jnp.where(at_zero, columns[:, 2:3], 0.0) + jnp.where(at_one, columns[:, 3:4], 0.0)
    ).astype(jnp.bfloat16)
    mixed_ref[...] = (
        residual_ref[...]
        + dot_nn(mixing[:, :EXPERT_ROWS], returned[0])
        + dot_nn(mixing[:, EXPERT_ROWS:], returned[1])
    ).astype(jnp.bfloat16)
    out_left, out_right = out_sum.total()
    out_sum_ref[:, : FF // 2] = out_left
    out_sum_ref[:, FF // 2 :] = out_right
    mid_left, mid_right = mid_total.total()
    qkv_left, qkv_right = qkv_total.total()
    share = CAPACITY // 8
    line = jnp.concatenate([mid_left, mid_right, qkv_left, qkv_right], axis=1)
    for piece in range(8):
        rows = slice(piece * share, (piece + 1) * share)
        dense_send[piece] = jnp.concatenate(
            [line[rows, :LINE], line[rows, LINE:], jnp.zeros((16 - 2 * share, LINE), jnp.float32)],
            axis=0,
        ).astype(jnp.bfloat16)
    dense_copies = []
    for step in range(1, 8):
        place = lax.rem(mine + step, 8)
        copy = push(
            dense_send.at[place],
            dense_land.at[mine],
            dense_sems.at[0],
            dense_sems.at[1],
            step - 1,
            step - 1,
            (lax.axis_index("dp"), place),
        )
        copy.start()
        dense_copies.append(copy)
    dense_land[mine] = dense_send[mine]
    landed(land_full.at[0, second], ring_send, ring_recv, 2)
    landed(land_full.at[1, first], ring_send, ring_recv, 3)
    landed(land_full.at[0, first], ring_send, ring_recv, 4)
    landed(land_full.at[1, second], ring_send, ring_recv, 5)
    grad_one += added(land_full[0], land_full[1])
    normed_one, inverse_one = norm_parts(tokens_ref[...].astype(jnp.float32))
    tokens_grad_ref[...] = grad_residual[...] + norm_back(
        grad_one * gain_ref[...][None], normed_one, inverse_one
    )
    left, right = big_total.total()
    in_sum_ref[:, : FF // 2] = left
    in_sum_ref[:, FF // 2 :] = right
    for step in range(1, 8):
        landed(
            dense_land.at[lax.rem(mine + 8 - step, 8)],
            dense_sems.at[0],
            dense_sems.at[1],
            step - 1,
        )
    lines = [dense_land[place].astype(jnp.float32) for place in range(8)]
    total = sum(lines[1:], lines[0])
    total = jnp.concatenate([total[:share], total[share : 2 * share]], axis=1)
    dense_sum_ref[...] = total[:, :DENSE]
    qkv_sum_ref[...] = jnp.zeros_like(qkv_sum_ref)
    for chip in range(CHIPS):
        line = lines[2 * chip] + lines[2 * chip + 1]
        line = jnp.concatenate([line[:share], line[share : 2 * share]], axis=1)[:, DENSE:]
        for part in range(3):
            start = part * WIDTH + (chip + chip // 2) * 128
            qkv_sum_ref[:, start : start + PAD] += line[:, part * PAD : (part + 1) * PAD]
    pltpu.make_async_copy(seven, seven, returned_sems.at[0, 0]).wait()
    for copy in dense_copies + copies:
        copy.wait_send()
    for user in (big_sum, out_sum, big_total, mid_sum, mid_total, qkv_sum, qkv_total):
        user.drain()
    for index in range(CHIPS):
        sib_copy(index).wait_send()

    @pl.loop(0, CHIPS)
    def _(chip):
        @pl.when((chip != z) | (owner_core != core))
        def _():
            push(
                grad_sent.at[chip],
                grad_out.at[chip],
                grad_send,
                grad_recv,
                chip,
                chip,
                device(z, 1 - core),
            ).wait_send()


def plane_scratch(lanes):
    return [
        pltpu.VMEM((4, 4, CAPACITY, lanes), HALF_TYPE),
        pltpu.VMEM((4, 2, CAPACITY, lanes // 2), HALF_TYPE),
        pltpu.VMEM((4, 2, CAPACITY, lanes // 2), HALF_TYPE),
        pltpu.VMEM((4, 2, CAPACITY, lanes // 2), HALF_TYPE),
        pltpu.VMEM((4, CAPACITY, lanes // 2), HALF_TYPE),
        pltpu.VMEM((4, CAPACITY, lanes // 2), HALF_TYPE),
        pltpu.VMEM((6, CAPACITY, lanes // 2), HALF_TYPE),
    ]


def back(*operands):
    def shape(*dims, dtype=FULL_TYPE):
        return jax.ShapeDtypeStruct(dims, dtype)

    def pair(count):
        return pltpu.SemaphoreType.DMA((2, count))

    return pl.pallas_call(
        back_kernel,
        out_shape=[
            shape(BLOCK, WIDTH, dtype=HALF_TYPE),
            shape(BLOCK, WIDTH),
            shape(CAPACITY, FF),
            shape(CAPACITY, FF),
            shape(CAPACITY // 8, DENSE),
            shape(CAPACITY // 8, 3 * WIDTH),
        ],
        in_specs=[smem()] + [vmem()] * 12 + [anywhere()] * 12,
        out_specs=[vmem()] * 6,
        scratch_shapes=[
            pltpu.VMEM((8, 16, LINE), HALF_TYPE),
            pltpu.VMEM((8, BLOCK, PAD), HALF_TYPE),
            pltpu.VMEM((LONG, PAD), HALF_TYPE),
            pltpu.VMEM((LONG, PAD), HALF_TYPE),
            pltpu.VMEM((CHIPS, BLOCK, PAD), HALF_TYPE),
            pltpu.VMEM((WIDTH, 3 * PAD), HALF_TYPE),
            pltpu.VMEM((LONG, WIDTH), HALF_TYPE),
            pltpu.VMEM((CHIPS, BLOCK, PAD), HALF_TYPE),
            pltpu.VMEM((4, CAPACITY, FF // 2), HALF_TYPE),
            pltpu.VMEM((4, CAPACITY, FF // 2), HALF_TYPE),
            pltpu.VMEM((6, CAPACITY, FF // 2), HALF_TYPE),
            pltpu.VMEM((2, EXPERT_ROWS, WIDTH), HALF_TYPE),
            pltpu.VMEM((BLOCK, WIDTH), FULL_TYPE),
            pltpu.VMEM((CHIPS, BLOCK, PAD), HALF_TYPE),
            pltpu.VMEM((CHIPS, BLOCK, PAD), HALF_TYPE),
            pltpu.VMEM((STACK, PAD), HALF_TYPE),
            pltpu.VMEM((STACK, PAD), HALF_TYPE),
            pltpu.VMEM((STACK, PAD), FULL_TYPE),
            pltpu.VMEM((LONG, PAD), FULL_TYPE),
            pltpu.VMEM((LONG, PAD), FULL_TYPE),
            pltpu.VMEM((LONG, 3 * PAD), HALF_TYPE),
            pltpu.VMEM((CHIPS, BLOCK, WIDTH), HALF_TYPE),
            pltpu.VMEM((CHIPS - 1, BLOCK, WIDTH), HALF_TYPE),
            pltpu.VMEM((CHIPS, BLOCK, WIDTH), HALF_TYPE),
            pltpu.VMEM((2, HALF, WIDTH), HALF_TYPE),
            pltpu.VMEM((2, BLOCK, WIDTH), HALF_TYPE),
            *plane_scratch(FF),
            *plane_scratch(DENSE),
            *plane_scratch(3 * PAD),
            pltpu.VMEM((8, 16, LINE), HALF_TYPE),
            pltpu.SemaphoreType.DMA((3,)),
            pltpu.SemaphoreType.DMA((11,)),
            pair(CHIPS),
            pair(CHIPS),
            pair(6),
            pair(12),
            pair(6),
            pair(6),
            pair(12),
            pair(6),
            pair(12),
            pair(6),
            pair(7),
            pair(1),
        ],
        compiler_params=pltpu.CompilerParams(
            collective_id=1, has_side_effects=True, vmem_limit_bytes=60 * 2**20
        ),
    )(*operands)


def as_row(column):
    size = column.shape[0]
    row = lax.broadcasted_iota(jnp.int32, (size, size), 0)
    lane = lax.broadcasted_iota(jnp.int32, (size, size), 1)
    return jnp.sum(jnp.where(row == lane, column, 0.0), axis=0, keepdims=True)


def finish_kernel(
    mixed_ref,
    tokens_grad_ref,
    in_sum_ref,
    out_sum_ref,
    dense_ref,
    qkv_ref,
    weight_ref,
    gain_ref,
    mixed_out,
    tokens_grad_out,
    gain_out,
    qkv_out,
    proj_out,
    gain_two_out,
    router_out,
    in_out,
    out_out,
    weight,
    mixed,
    tokens_grad,
    in_sum,
    out_sum,
    sem,
    load_sems,
    store_sems,
):
    loads = []
    for index, (source, target) in enumerate(
        (
            (tokens_grad_ref, tokens_grad),
            (in_sum_ref, in_sum),
            (out_sum_ref, out_sum),
            (mixed_ref, mixed),
        )
    ):
        copy = pltpu.make_async_copy(source, target, load_sems.at[index])
        copy.start()
        loads.append(copy)
    share = CAPACITY // 8
    first = (lax.axis_index("dp") * 8 + lax.axis_index("expert")) * share
    start = pl.multiple_of(jnp.minimum(first // 16, WIDTH // 16 - 2) * 16, 16)
    load = pltpu.make_async_copy(weight_ref.at[pl.ds(start, 32), :], weight, sem)
    load.start()
    pairs = [(0, tokens_grad, tokens_grad_out.at[0]), (1, in_sum, in_out.at[0])]
    for part in range(4):
        pairs.append(
            (
                2,
                out_sum.at[:, pl.ds(part * WIDTH, WIDTH)],
                out_out.at[0, pl.ds(part * CAPACITY, CAPACITY), :],
            )
        )
    pairs.append((3, mixed, mixed_out.at[0]))
    stores = []
    for index, (needs, source, target) in enumerate(pairs):
        if index < 3 or needs == 3:
            loads[needs].wait()
        copy = pltpu.make_async_copy(source, target, store_sems.at[index])
        copy.start()
        stores.append(copy)
    qkv_out[...] = qkv_ref[...]
    dense = dense_ref[...]
    proj_out[...] = dense[:, :WIDTH]
    router_out[...] = dense[:, WIDTH : WIDTH + EXPERTS]
    gain_two_out[...] = as_row(dense[:, WIDTH + EXPERTS : WIDTH + EXPERTS + 1])
    row = lax.broadcasted_iota(jnp.int32, (share, 32), 0)
    column = lax.broadcasted_iota(jnp.int32, (share, 32), 1)
    chosen = jnp.where(column == row + (first - start), 1.0, 0.0).astype(jnp.bfloat16)
    row = lax.broadcasted_iota(jnp.int32, (share, WIDTH), 0)
    column = lax.broadcasted_iota(jnp.int32, (share, WIDTH), 1)
    gain = jnp.sum(
        jnp.where(column == row + first, gain_ref[...][None], 0.0), axis=1, keepdims=True
    )
    load.wait()
    products = qkv_ref[...] * dot_nn(chosen, weight[...])
    gain_out[...] = as_row(jnp.sum(products, axis=1, keepdims=True) / gain)
    for copy in stores:
        copy.wait()


def finish(*operands):
    def shape(*dims, dtype=FULL_TYPE):
        return jax.ShapeDtypeStruct(dims, dtype)

    share = CAPACITY // 8
    shapes = [
        shape(1, BLOCK, WIDTH, dtype=HALF_TYPE),
        shape(1, BLOCK, WIDTH),
        shape(1, share),
        shape(share, 3 * WIDTH),
        shape(share, WIDTH),
        shape(1, share),
        shape(share, EXPERTS),
        shape(1, CAPACITY, FF),
        shape(1, 4 * CAPACITY, WIDTH),
    ]
    return pl.pallas_call(
        finish_kernel,
        out_shape=shapes,
        in_specs=[anywhere()] * 4 + [vmem()] * 2 + [anywhere(), vmem()],
        out_specs=[anywhere()] * 2 + [vmem()] * 5 + [anywhere()] * 2,
        scratch_shapes=[
            pltpu.VMEM((32, 3 * WIDTH), HALF_TYPE),
            pltpu.VMEM((BLOCK, WIDTH), HALF_TYPE),
            pltpu.VMEM((BLOCK, WIDTH), FULL_TYPE),
            pltpu.VMEM((CAPACITY, FF), FULL_TYPE),
            pltpu.VMEM((CAPACITY, FF), FULL_TYPE),
            pltpu.SemaphoreType.DMA,
            pltpu.SemaphoreType.DMA((4,)),
            pltpu.SemaphoreType.DMA((7,)),
        ],
        compiler_params=pltpu.CompilerParams(vmem_limit_bytes=62 * 2**20),
    )(*operands)


def on_device(
    tokens,
    group_kind,
    routes,
    norm1_gain,
    qkv_weight,
    proj_weight,
    norm2_gain,
    router_weight,
    frozen_in,
    frozen_out,
    new_in,
    new_out,
    out_grad,
):
    width = WIDTH
    router = router_weight.T
    (
        hidden,
        queries,
        keys,
        values,
        heads,
        attended,
        residual,
        hidden_two,
        totals,
        info,
        returned,
        in_grad,
        in_first,
        grad_back,
        match,
        x_part,
        y_part,
    ) = layer(
        group_kind,
        tokens[0],
        norm1_gain,
        qkv_weight,
        out_grad[0],
        routes[0].T,
        proj_weight,
        norm2_gain,
        router,
        frozen_in[0],
        frozen_out[0],
        new_in[0],
        new_out[0],
    )
    mixed, tokens_grad, in_sum, out_sum, dense_sum, qkv_sum = back(
        group_kind,
        tokens[0],
        norm1_gain,
        norm2_gain,
        out_grad[0],
        residual,
        info,
        match,
        grad_back,
        router,
        proj_weight,
        hidden_two,
        totals,
        queries,
        keys,
        values,
        heads,
        qkv_weight,
        hidden.reshape(LONG, width),
        attended,
        in_grad,
        in_first,
        returned,
        x_part,
        y_part,
    )
    outputs = finish(
        mixed, tokens_grad, in_sum, out_sum, dense_sum, qkv_sum, qkv_weight, norm1_gain
    )
    return tuple(
        value[0] if index in (2, 5) else value for index, value in enumerate(outputs)
    )


def solution(mesh):
    return jax.shard_map(
        on_device,
        mesh=mesh,
        in_specs=(
            P("dp", "expert", None),
            P("dp"),
            P("dp", "expert", None),
            P(),
            P(),
            P(),
            P(),
            P(),
            P("expert", None, None),
            P("expert", None, None),
            P("expert", None, None),
            P("expert", None, None),
            P("dp", "expert", None),
        ),
        out_specs=(
            P("dp", "expert", None),
            P("dp", "expert", None),
            P(("dp", "expert")),
            P(("dp", "expert"), None),
            P(("dp", "expert"), None),
            P(("dp", "expert")),
            P(("dp", "expert"), None),
            P("expert", "dp", None),
            P("expert", "dp", None),
        ),
        check_vma=False,
    )
```

```python
import jax
import jax.numpy as jnp
from jax import lax
from jax.experimental import pallas as pl
from jax.experimental.pallas import tpu as pltpu
from jax.sharding import PartitionSpec as P

HEADS = 12
HD = 64
LONG = 2048
MESH_ID = pl.DeviceIdType.MESH
CHIPS = 4
PAD = 256
BLOCK = 256
HALF = BLOCK // 2
CHUNK = 512
CHUNKS = LONG // CHUNK
LOCAL_HEADS = HEADS // CHIPS
STACK = LOCAL_HEADS * BLOCK
NEGATIVE = -1e30
WIDTH = 768
EXPERTS = 16
SLOTS = 768
EXPERT_ROWS = 384
CAPACITY = 48
FF = 3072
FF_TILE = 768
FF_TILES = 4
DENSE = 1024
LINE = (DENSE + 3 * PAD) // 2
HALF_TYPE = jnp.bfloat16
FULL_TYPE = jnp.float32

epsilon = 1e-05


def norm_parts(values):
    average = jnp.mean(values, axis=-1, keepdims=True)
    centred = values - average
    variance = jnp.mean(centred * centred, axis=-1, keepdims=True)
    inverse = lax.rsqrt(variance + epsilon)
    return (centred * inverse, inverse)


def norm_back(grad_normed, normed, inverse):
    first_mean = jnp.mean(grad_normed, axis=-1, keepdims=True)
    second_mean = jnp.mean(grad_normed * normed, axis=-1, keepdims=True)
    return inverse * (grad_normed - first_mean - normed * second_mean)


def here():
    position = lax.axis_index("expert")
    return position // 2, lax.rem(position, 2)


def device(z, core):
    return (lax.axis_index("dp"), z * 2 + core)


def greet(barrier):
    position = lax.axis_index("expert")
    for step in range(1, 8):
        pl.semaphore_signal(
            barrier,
            inc=1,
            device_id=(lax.axis_index("dp"), lax.rem(position + step, 8)),
            device_id_type=MESH_ID,
        )


def push(source, target, sends, receives, index_here, index_there, where):
    return pltpu.make_async_remote_copy(
        src_ref=source,
        dst_ref=target,
        send_sem=sends.at[index_here],
        recv_sem=receives.at[index_there],
        device_id=where,
        device_id_type=MESH_ID,
    )


def landed(region, sends, receives, index):
    z, core = here()
    push(region, region, sends, receives, index, index, device(z, 1 - core)).wait_recv()


def dot_nn(left, right):
    return jnp.dot(left, right, preferred_element_type=jnp.float32)


def dot_nt(left, right):
    return lax.dot_general(
        left, right, (((1,), (1,)), ((), ())), preferred_element_type=jnp.float32
    )


def dot_tn(left, right):
    return lax.dot_general(
        left, right, (((0,), (0,)), ((), ())), preferred_element_type=jnp.float32
    )


def window(chip):
    return (chip + chip // 2) * 128, lax.rem(chip, 2) * HD


def head_mask(chip, head, value, dtype):
    start = window(chip)[1] + head * HD
    lanes = lax.broadcasted_iota(jnp.int32, (1, PAD), 1)
    inside = (lanes >= start) & (lanes < start + HD)
    return jnp.where(inside, value, 0.0).astype(dtype)


def lane_tiles(values, combine):
    result = values[:, :128]
    for start in range(128, values.shape[1], 128):
        result = combine(result, values[:, start : start + 128])
    return result


def block_rows(block):
    return pl.ds(pl.multiple_of(block * BLOCK, BLOCK), BLOCK)


def chunk_rows(chunk):
    return pl.ds(pl.multiple_of(chunk * CHUNK, CHUNK), CHUNK)


def load_windows(weight_ref, target, sems, chip):
    copies = []
    for part in range(3):
        first = pl.multiple_of(part * WIDTH + window(chip)[0], 128)
        copies.append(
            pltpu.make_async_copy(
                weight_ref.at[:, pl.ds(first, PAD)],
                target.at[:, pl.ds(part * PAD, PAD)],
                sems.at[part],
            )
        )
    for copy in copies:
        copy.start()
    return copies


class RingGather:
    def __init__(self, ref, sends, receives):
        self.ref, self.sends, self.receives = ref, sends, receives
        self.z, self.core = here()
        self.up, self.down = lax.rem(self.z + 1, CHIPS), lax.rem(self.z + 3, CHIPS)
        self.far = lax.rem(self.z + 2, CHIPS)
        self.copies = []

    def region(self, chip, core, half):
        rows = slice(None) if half is None else pl.ds(half * HALF, HALF)
        return self.ref.at[chip * 2 + core, rows]

    def send(self, index, chip, half, where):
        region = self.region(chip, self.core, half)
        copy = push(region, region, self.sends, self.receives, index, index, where)
        copy.start()
        self.copies.append(copy)

    def wait(self, index, chip, core, half):
        landed(self.region(chip, core, half), self.sends, self.receives, index)

    def above(self):
        return device(self.up, self.core)

    def below(self):
        return device(self.down, self.core)

    def beside(self):
        return device(self.z, 1 - self.core)

    def start(self):
        self.send(0, self.z, 0, self.above())
        self.send(1, self.z, 1, self.below())
        self.send(2, self.z, 1, self.above())
        self.send(3, self.z, 0, self.below())
        self.send(4, self.z, None, self.beside())

    def relay(self):
        self.wait(0, self.down, self.core, 0)
        self.send(5, self.down, 0, self.above())
        self.send(7, self.down, 0, self.beside())
        self.wait(1, self.up, self.core, 1)
        self.send(6, self.up, 1, self.below())
        self.send(8, self.up, 1, self.beside())

    def share(self):
        self.wait(2, self.down, self.core, 1)
        self.send(9, self.down, 1, self.beside())
        self.wait(3, self.up, self.core, 0)
        self.send(10, self.up, 0, self.beside())

    def share_far(self):
        self.wait(5, self.far, self.core, 0)
        self.send(11, self.far, 0, self.beside())
        self.wait(6, self.far, self.core, 1)
        self.send(12, self.far, 1, self.beside())

    def other_own(self):
        self.wait(4, self.z, 1 - self.core, None)

    def other_down(self):
        self.wait(7, self.down, 1 - self.core, 0)
        self.wait(9, self.down, 1 - self.core, 1)

    def other_up(self):
        self.wait(8, self.up, 1 - self.core, 1)
        self.wait(10, self.up, 1 - self.core, 0)

    def other_far(self):
        self.wait(11, self.far, 1 - self.core, 0)
        self.wait(12, self.far, 1 - self.core, 1)

    def drain(self):
        for copy in self.copies:
            copy.wait_send()


def plane_device(x, y):
    return (x * 4 + y, lax.axis_index("expert"))


def plane_here():
    group = lax.axis_index("dp")
    return group // 4, lax.rem(group, 4)


def added(left, right):
    return left.astype(jnp.float32) + right.astype(jnp.float32)


class PlaneSum:
    def __init__(self, source, first, direct, combined, sends, receives):
        self.source, self.first = source, first
        self.direct, self.combined = direct, combined
        self.sends, self.receives = sends, receives
        self.x, self.y = plane_here()
        half = source.shape[-1] // 2
        self.left, self.right = pl.ds(0, half), pl.ds(half, half)
        self.low, self.high = pl.ds(0, 2), pl.ds(2, 2)
        self.copies = []

    def x_part(self, x, part):
        return self.source.at[x, part, :, self.left]

    def y_part(self, y, part):
        return self.source.at[part, y, :, self.right]

    def sides(self):
        return (
            (0, self.x, self.x_part, lambda p: plane_device(p, self.y)),
            (2, self.y, self.y_part, lambda p: plane_device(self.x, p)),
        )

    def send(self, source, target, index, where):
        copy = push(source, target, self.sends, self.receives, index, index, where)
        copy.start()
        self.copies.append(copy)

    def wait(self, region, index):
        landed(region, self.sends, self.receives, index)

    def neighbours(self, place):
        return lax.rem(place + 1, 4), lax.rem(place + 3, 4), lax.rem(place + 2, 4)

    def start_far(self):
        for base, place, part, where in self.sides():
            up, down, far = self.neighbours(place)
            self.send(part(far, self.low), self.first.at[base], base, where(up))
            self.send(part(far, self.high), self.first.at[base + 1], base + 1, where(down))

    def start_near(self):
        for base, place, part, where in self.sides():
            up, down, _ = self.neighbours(place)
            self.send(part(up, self.high), self.direct.at[base], base + 4, where(up))
            self.send(part(down, self.low), self.direct.at[base + 1], base + 5, where(down))

    def start(self):
        self.start_far()
        self.start_near()

    def settle_far(self):
        for index in range(4):
            self.wait(self.first.at[index], index)

    def second(self, waits=True):
        low, high = self.low, self.high
        for base, place, part, where in self.sides():
            up, down, _ = self.neighbours(place)
            for index, chosen, to in (
                (base, part(up, low), up),
                (base + 1, part(down, high), down),
            ):
                if waits:
                    self.wait(self.first.at[index], index)
                chosen[...] = added(chosen[...], self.first[index]).astype(jnp.bfloat16)
                self.send(chosen, self.combined.at[index], index + 8, where(to))

    def third(self, x_sum, y_sum):
        low, high = self.low, self.high
        for base, place, part, total in (
            (0, self.x, self.x_part, x_sum),
            (2, self.y, self.y_part, y_sum),
        ):
            self.wait(self.direct.at[base], base + 4)
            self.wait(self.direct.at[base + 1], base + 5)
            self.wait(self.combined.at[base], base + 8)
            self.wait(self.combined.at[base + 1], base + 9)
            total[low] = (
                added(part(place, low)[...], self.combined[base])
                + self.direct[base + 1].astype(jnp.float32)
            ).astype(jnp.bfloat16)
            total[high] = (
                added(part(place, high)[...], self.direct[base])
                + self.combined[base + 1].astype(jnp.float32)
            ).astype(jnp.bfloat16)

    def drain(self):
        for copy in self.copies:
            copy.wait_send()


class PlaneSpread:
    def __init__(self, x_sum, y_sum, land, sends, receives):
        self.x_sum, self.y_sum, self.land = x_sum, y_sum, land
        self.sends, self.receives = sends, receives
        self.x, self.y = plane_here()
        self.copies = []

    def start(self):
        for step in range(1, 4):
            y, x = lax.rem(self.y + step, 4), lax.rem(self.x + step, 4)
            for index, source, where in (
                (step - 1, self.x_sum.at[y], plane_device(self.x, y)),
                (step + 2, self.y_sum.at[x], plane_device(x, self.y)),
            ):
                copy = push(
                    source, self.land.at[index], self.sends, self.receives, index, index, where
                )
                copy.start()
                self.copies.append(copy)

    def total(self):
        sums = []
        for base, mine in ((0, self.x_sum[self.y]), (3, self.y_sum[self.x])):
            value = mine.astype(jnp.float32)
            for index in range(base, base + 3):
                landed(self.land.at[index], self.sends, self.receives, index)
                value += self.land[index].astype(jnp.float32)
            sums.append(value)
        return sums

    def drain(self):
        for copy in self.copies:
            copy.wait_send()


def greet_plane(barrier):
    x, y = plane_here()
    for step in range(1, 4):
        for where in (plane_device(lax.rem(x + step, 4), y), plane_device(x, lax.rem(y + step, 4))):
            pl.semaphore_signal(barrier, inc=1, device_id=where, device_id_type=MESH_ID)


def gelu_parts(u):
    scaled = jnp.abs(u) * 0.7071067811865476
    t = 1.0 / (1.0 + 0.3275911 * scaled)
    poly = t * (
        0.127414796
        + t * (-0.142248368 + t * (0.7107068705 + t * (-0.7265760135 + t * 0.5307027145)))
    )
    density = jnp.exp(-0.5 * u * u)
    tail = poly * density
    cumulative = jnp.where(u >= 0, 1.0 - tail, tail)
    return u * cumulative, cumulative + u * density * 0.3989422804014327


def vmem():
    return pl.BlockSpec(memory_space=pltpu.VMEM)


def smem():
    return pl.BlockSpec(memory_space=pltpu.SMEM)


def anywhere():
    return pl.BlockSpec(memory_space=pl.ANY)


def front_part(
    kind_ref,
    tokens_ref,
    gain_ref,
    weight_ref,
    grad_hbm,
    routes_ref,
    proj_hbm,
    gain_two_ref,
    router_ref,
    hidden_out,
    query_out,
    key_out,
    value_out,
    heads_out,
    attended_out,
    residual_out,
    hidden_two_out,
    total_ref,
    info_ref,
    hidden_ref,
    out_ref,
    attended_ref,
    residual_ref,
    hidden_two_ref,
    sent_ref,
    grad_rows_ref,
    grad_ref,
    proj_ref,
    gather_sems,
    out_sems,
    weight_sems,
    store_sems,
    begin_rows,
):
    z, core = here()
    mine = z * 2 + core
    up, down, far = lax.rem(z + 1, CHIPS), lax.rem(z + 3, CHIPS), lax.rem(z + 2, CHIPS)
    barrier = pltpu.get_barrier_semaphore()
    greet(barrier)
    greet_plane(barrier)
    late_loads = [
        pltpu.make_async_copy(grad_hbm, grad_ref, weight_sems.at[3]),
        pltpu.make_async_copy(proj_hbm, proj_ref, weight_sems.at[4]),
    ]
    for load in late_loads:
        load.start()
    tokens = tokens_ref[...].astype(jnp.float32)
    normed, _ = norm_parts(tokens)
    hidden_ref[mine] = (normed * gain_ref[...][None]).astype(jnp.bfloat16)
    pl.semaphore_wait(barrier, 13)
    gather = RingGather(hidden_ref, gather_sems.at[0], gather_sems.at[1])
    stores, store_count = [], [0]

    def store(source, target):
        copy = pltpu.make_async_copy(source, target, store_sems.at[store_count[0]])
        copy.start()
        store_count[0] += 1
        stores.append(copy)

    out_send, out_recv = out_sems.at[0], out_sems.at[1]
    gather.start()
    routes = routes_ref[...].astype(jnp.float32)
    names = lax.broadcasted_iota(jnp.int32, (EXPERTS, BLOCK), 0).astype(jnp.float32)
    pick_zero = jnp.where(names == routes[0:1, :], 1.0, 0.0)
    pick_one = jnp.where(names == routes[1:2, :], 1.0, 0.0)
    row = lax.broadcasted_iota(jnp.int32, (BLOCK, BLOCK), 0)
    column = lax.broadcasted_iota(jnp.int32, (BLOCK, BLOCK), 1)
    before = jnp.where(row < column, 1.0, 0.0).astype(jnp.bfloat16)
    earlier = dot_nn((pick_zero + pick_one).astype(jnp.bfloat16), before)
    places = []
    for index, pick in enumerate((pick_zero, pick_one)):
        slot = jnp.sum(earlier * pick, axis=0, keepdims=True)
        place = routes[index : index + 1, :] * CAPACITY + slot
        places.append(jnp.where(slot < CAPACITY, place, -1.0))

    def attention(
        query_ref,
        key_ref,
        value_ref,
        weight,
        stacked,
        diagonal,
        beside,
        scores,
        largest,
        sums,
        acc,
    ):
        loads = load_windows(weight_ref, weight, weight_sems, z)

        def project(block):
            projected = dot_nn(hidden_ref[block], weight[...]).astype(jnp.bfloat16)
            query_ref[block] = projected[:, :PAD]
            key_ref[block_rows(block), :] = projected[:, PAD : 2 * PAD]
            value_ref[block_rows(block), :] = projected[:, 2 * PAD :]

        for load in loads:
            load.wait()
        project(mine)
        gather.relay()
        gather.other_own()
        project(z * 2 + 1 - core)
        gather.share()
        project(down * 2 + core)
        project(up * 2 + core)
        gather.other_down()
        project(down * 2 + 1 - core)
        gather.other_up()
        project(up * 2 + 1 - core)
        gather.share_far()
        project(far * 2 + core)
        gather.other_far()
        project(far * 2 + 1 - core)
        store(hidden_ref, hidden_out)
        store(query_ref, query_out)
        store(key_ref, key_out)
        store(value_ref, value_out)

        kind_bias = kind_ref[0].astype(jnp.float32) * NEGATIVE

        def attend(step):
            slot = lax.rem(z + CHIPS - 1 - step, CHIPS)
            block = slot * 2 + lax.rem(core + slot, 2)
            queries = query_ref[block]
            for head in range(LOCAL_HEADS):
                stacked[head * BLOCK : (head + 1) * BLOCK, :] = queries * head_mask(
                    z, head, HD ** (-0.5), jnp.bfloat16
                )

            def bias_of(chunk):
                return jnp.where((slot >= 2) & (chunk < 2), kind_bias, 0.0)

            masked = dot_nt(stacked[...], key_ref[block_rows(block), :])
            row = lax.broadcasted_iota(jnp.int32, (BLOCK, BLOCK), 0)
            column = lax.broadcasted_iota(jnp.int32, (BLOCK, BLOCK), 1)
            for head in range(LOCAL_HEADS):
                part = slice(head * BLOCK, (head + 1) * BLOCK)
                values = jnp.where(column <= row, masked[part], NEGATIVE)
                diagonal[part, :] = values
                largest[part, :] = lane_tiles(values, jnp.maximum)
            is_odd = block != 2 * slot

            @pl.when(is_odd)
            def _():
                values = dot_nt(stacked[...], key_ref[block_rows(block - 1), :])
                beside[...] = values
                largest[...] = jnp.maximum(largest[...], lane_tiles(values, jnp.maximum))

            @pl.loop(0, slot)
            def _(chunk):
                values = dot_nt(stacked[...], key_ref[chunk_rows(chunk), :])
                scores[chunk] = values
                largest[...] = jnp.maximum(
                    largest[...], lane_tiles(values, jnp.maximum) + bias_of(chunk)
                )

            row_max = jnp.max(largest[...], axis=1, keepdims=True)
            largest[...] = jnp.broadcast_to(row_max, largest.shape)
            exponent = jnp.exp(diagonal[...] - row_max)
            sums[...] = lane_tiles(exponent, jnp.add)
            acc[...] = dot_nn(exponent.astype(jnp.bfloat16), value_ref[block_rows(block), :])

            @pl.when(is_odd)
            def _():
                exponent = jnp.exp(beside[...] - largest[:, :1])
                sums[...] += lane_tiles(exponent, jnp.add)
                acc[...] += dot_nn(exponent.astype(jnp.bfloat16), value_ref[block_rows(block - 1), :])

            @pl.loop(0, slot)
            def _(chunk):
                exponent = jnp.exp(scores[chunk] - (largest[:, :1] - bias_of(chunk)))
                sums[...] += lane_tiles(exponent, jnp.add)
                acc[...] += dot_nn(exponent.astype(jnp.bfloat16), value_ref[chunk_rows(chunk), :])

            total = jnp.sum(sums[...], axis=1, keepdims=True)
            inverse = 1.0 / total
            log_total = largest[...] + jnp.log(total)
            attended = jnp.zeros((BLOCK, PAD), jnp.float32)
            for head in range(LOCAL_HEADS):
                part = slice(head * BLOCK, (head + 1) * BLOCK)
                attended += acc[part, :] * inverse[part] * head_mask(z, head, 1.0, jnp.float32)
                total_ref[slot, head : head + 1, :] = jnp.transpose(log_total[part, :])[:1, :]
            out_ref[slot] = attended.astype(jnp.bfloat16)

            @pl.when(block != mine)
            def _():
                push(
                    out_ref.at[slot],
                    attended_ref.at[z],
                    out_send,
                    out_recv,
                    slot,
                    z,
                    device(slot, lax.rem(core + slot, 2)),
                ).start()

            @pl.when(block == mine)
            def _():
                attended_ref[z] = out_ref[slot]

        pl.loop(0, CHIPS)(attend)
        gather.drain()
        for copy in stores:
            copy.wait()

    pl.run_scoped(
        attention,
        pltpu.VMEM((8, BLOCK, PAD), HALF_TYPE),
        pltpu.VMEM((LONG, PAD), HALF_TYPE),
        pltpu.VMEM((LONG, PAD), HALF_TYPE),
        pltpu.VMEM((WIDTH, 3 * PAD), HALF_TYPE),
        pltpu.VMEM((STACK, PAD), HALF_TYPE),
        pltpu.VMEM((STACK, BLOCK), FULL_TYPE),
        pltpu.VMEM((STACK, BLOCK), FULL_TYPE),
        pltpu.VMEM((CHUNKS - 1, STACK, CHUNK), FULL_TYPE),
        pltpu.VMEM((STACK, 128), FULL_TYPE),
        pltpu.VMEM((STACK, 128), FULL_TYPE),
        pltpu.VMEM((STACK, PAD), FULL_TYPE),
    )
    stores.clear()
    store(out_ref, heads_out)

    @pl.loop(0, CHIPS)
    def _(slot):
        @pl.when((slot != z) | (lax.rem(core + z, 2) != core))
        def _():
            landed(attended_ref.at[slot], out_send, out_recv, slot)

    store(attended_ref, attended_out)
    for load in late_loads:
        load.wait()
    residual = tokens_ref[...].astype(jnp.float32)
    for chip in range(CHIPS):
        first = (chip + chip // 2) * 128
        residual += dot_nn(attended_ref[chip], proj_ref[first : first + PAD, :])
    residual_ref[...] = residual
    normed_two, _ = norm_parts(residual)
    hidden_two = (normed_two * gain_two_ref[...][None]).astype(jnp.bfloat16)
    hidden_two_ref[...] = hidden_two
    store(residual_ref, residual_out)
    store(hidden_two_ref, hidden_two_out)
    logits = dot_nt(router_ref[...], hidden_two)
    logit_zero = jnp.sum(logits * pick_zero, axis=0, keepdims=True)
    logit_one = jnp.sum(logits * pick_one, axis=0, keepdims=True)
    gate_zero = 1.0 / (1.0 + jnp.exp(logit_one - logit_zero))
    gate_one = 1.0 / (1.0 + jnp.exp(logit_zero - logit_one))
    for index, line in enumerate((*places, gate_zero, gate_one, routes[0:1], routes[1:2])):
        info_ref[index : index + 1, :] = line
    info_ref[6:8, :] = jnp.zeros((2, BLOCK), jnp.float32)
    ids = lax.broadcasted_iota(jnp.int32, (SLOTS, BLOCK), 0).astype(jnp.float32)
    chosen = jnp.where((ids == places[0]) | (ids == places[1]), 1.0, 0.0).astype(jnp.bfloat16)
    sent = dot_nn(chosen, hidden_two).astype(jnp.bfloat16)
    sent_ref[0] = sent[:EXPERT_ROWS]
    sent_ref[1] = sent[EXPERT_ROWS:]
    begin_rows(0)
    mixing = (
        jnp.where(ids == places[0], gate_zero, 0.0) + jnp.where(ids == places[1], gate_one, 0.0)
    ).astype(jnp.bfloat16)
    rows = dot_nn(mixing, grad_ref[...]).astype(jnp.bfloat16)
    grad_rows_ref[0] = rows[:EXPERT_ROWS]
    grad_rows_ref[1] = rows[EXPERT_ROWS:]
    begin_rows(1)

    def finish_front():

        @pl.loop(0, CHIPS)
        def _(slot):
            @pl.when(slot * 2 + lax.rem(core + slot, 2) != mine)
            def _():
                push(
                    out_ref.at[slot],
                    attended_ref.at[slot],
                    out_send,
                    out_recv,
                    slot,
                    slot,
                    device(z, 1 - core),
                ).wait_send()

        for copy in stores:
            copy.wait()

    return finish_front


def expert_part(
    sent_ref,
    grad_rows_ref,
    in_frozen,
    out_frozen,
    in_new,
    out_new,
    returned_ref,
    in_grad_ref,
    in_first_ref,
    grad_back_ref,
    match_ref,
    x_sum_ref,
    y_sum_ref,
    x_land,
    g_land,
    r_send,
    b_send,
    in_grad,
    out_grad,
    first,
    direct,
    combined,
    in_first,
    match_send,
    load_sems,
    x_sems,
    g_sems,
    b_sems,
    match_sems,
    plane_sems,
    in_sems,
    store_sems,
):
    mine = lax.axis_index("expert")

    def rows_of(place):
        return pl.ds(pl.multiple_of(place * CAPACITY, CAPACITY), CAPACITY)

    own_rows = rows_of(mine)

    def peer(step):
        return lax.rem(mine + step, 8)

    def exchange(source, target, sems, index, step):
        return push(
            source, target, sems.at[0], sems.at[1], index, index, (lax.axis_index("dp"), peer(step))
        )

    stores, used = [], []

    def store(source, target):
        copy = pltpu.make_async_copy(source, target, store_sems.at[len(stores)])
        copy.start()
        stores.append(copy)

    def seven(ref, sem):
        region = ref.at[0, pl.ds(0, 7 * CAPACITY), :]
        return pltpu.make_async_copy(region, region, sem)

    def spread_kind(kind, source, target, sems):
        for step in range(1, 8):
            exchange(
                source.at[kind, rows_of(peer(step)), :],
                target.at[kind, own_rows, :],
                sems,
                kind,
                step,
            ).start()
        used.append((target, sems.at[0, kind]))

    def collect_kind(kind, target, sems):
        seven(target, sems.at[1, kind]).wait()

    def begin_rows(which):
        source, target, sems = ((sent_ref, x_land, x_sems), (grad_rows_ref, g_land, g_sems))[which]
        if which == 1:
            spread_kind(1, source, target, sems)
            spread_kind(0, sent_ref, x_land, x_sems)
            spread_kind(0, source, target, sems)
        else:
            spread_kind(1, source, target, sems)
        target[:, own_rows, :] = source[:, own_rows, :]

    def work(w_in, w_out, activated, slope, acc):
        loads = []
        for index, (source, target) in enumerate(
            (
                (in_new, w_in.at[1]),
                (out_new, w_out.at[1]),
                (in_frozen, w_in.at[0]),
                (out_frozen, w_out.at[0]),
            )
        ):
            copy = pltpu.make_async_copy(source, target, load_sems.at[index])
            copy.start()
            loads.append(copy)

        def tile_of(index):
            return pl.ds(pl.multiple_of(index * FF_TILE, FF_TILE), FF_TILE)

        plane = PlaneSum(out_grad, first, direct, combined, plane_sems.at[0], plane_sems.at[1])
        in_plane = PlaneSum(in_grad, in_first, None, None, in_sems.at[0], in_sems.at[1])
        matches = [None, None]
        for kind in (1, 0):
            collect_kind(kind, x_land, x_sems)
            loads[0 if kind == 1 else 2].wait()
            loads[1 if kind == 1 else 3].wait()
            acc[...] = jnp.zeros_like(acc)

            @pl.loop(0, FF_TILES, unroll=True)
            def _(index):
                tile = tile_of(index)
                pre = dot_nn(x_land[kind], w_in[kind, :, tile])
                value, steep = gelu_parts(pre)
                value = value.astype(jnp.bfloat16)
                if kind == 1:
                    activated[:, tile] = value
                slope[:, tile] = steep.astype(jnp.bfloat16)
                acc[...] += dot_nn(value, w_out[kind, tile, :])

            collect_kind(kind, g_land, g_sems)
            result = acc[...].astype(jnp.bfloat16)
            r_send[kind] = result
            store(r_send.at[kind], returned_ref.at[kind])
            products = result.astype(jnp.float32) * g_land[kind].astype(jnp.float32)
            matches[kind] = jnp.sum(products, axis=1, keepdims=True)
            if kind == 1:

                @pl.loop(0, FF_TILES, unroll=True)
                def _(index):
                    weights = dot_tn(activated[:, tile_of(index)], g_land[1]).astype(jnp.bfloat16)
                    for y in range(4):
                        for part in range(4):
                            start = (y * 4 + part) * CAPACITY
                            out_grad[index, y, :, part * WIDTH : (part + 1) * WIDTH] = weights[
                                start : start + CAPACITY
                            ]

                plane.start()

            acc[...] = jnp.zeros_like(acc)

            @pl.loop(0, FF_TILES, unroll=True)
            def _(index):
                tile = tile_of(index)
                grad = dot_nt(g_land[kind], w_out[kind, tile, :])
                grad = (grad * slope[:, tile].astype(jnp.float32)).astype(jnp.bfloat16)
                acc[...] += dot_nt(grad, w_in[kind, :, tile])
                if kind == 1:
                    activated[:, tile] = grad

            b_send[kind] = acc[...].astype(jnp.bfloat16)
            grad_back_ref[kind, own_rows, :] = b_send[kind, own_rows, :]
            spread_kind(kind, b_send, grad_back_ref, b_sems)
            if kind == 1:

                @pl.loop(0, FF_TILES, unroll=True)
                def _(index):
                    tile = tile_of(index)
                    weights = dot_tn(x_land[1], activated[:, tile]).astype(jnp.bfloat16)
                    in_grad[:, :, :, tile] = weights.reshape(4, 4, CAPACITY, FF_TILE)

                in_plane.start_far()
                store(in_grad, in_grad_ref)
        lanes = lax.broadcasted_iota(jnp.int32, (EXPERT_ROWS, 128), 1)
        match_send[0] = jnp.where(lanes < 64, matches[0], matches[1])
        match_ref[0, own_rows, :] = match_send[0, own_rows, :]
        spread_kind(0, match_send, match_ref, match_sems)
        plane.second()
        plane.third(x_sum_ref, y_sum_ref)
        collect_kind(0, match_ref, match_sems)
        for kind in (1, 0):
            collect_kind(kind, grad_back_ref, b_sems)
        in_plane.settle_far()
        store(in_first, in_first_ref)
        for target, sem in used:
            seven(target, sem).wait()
        plane.drain()
        in_plane.drain()
        for copy in stores:
            copy.wait()

    def run():
        pl.run_scoped(
            work,
            pltpu.VMEM((2, WIDTH, FF), HALF_TYPE),
            pltpu.VMEM((2, FF, WIDTH), HALF_TYPE),
            pltpu.VMEM((EXPERT_ROWS, FF), HALF_TYPE),
            pltpu.VMEM((EXPERT_ROWS, FF), HALF_TYPE),
            pltpu.VMEM((EXPERT_ROWS, WIDTH), FULL_TYPE),
        )

    return begin_rows, run


def layer_kernel(*refs):
    front_in, rest = refs[:9], refs[9:]
    expert_in, rest = rest[:4], rest[4:]
    front_out, rest = rest[:10], rest[10:]
    expert_out, rest = rest[:7], rest[7:]
    front_scratch, expert_scratch = rest[:13], rest[13:]
    sent, grad_rows = front_scratch[5:7]
    begin_rows, run_experts = expert_part(sent, grad_rows, *expert_in, *expert_out, *expert_scratch)
    finish_front = front_part(*front_in, *front_out, *front_scratch, begin_rows)
    run_experts()
    finish_front()


def layer(*operands):
    def shape(*dims, dtype=HALF_TYPE):
        return jax.ShapeDtypeStruct(dims, dtype)

    def pair(count):
        return pltpu.SemaphoreType.DMA((2, count))

    shapes = [
        shape(8, BLOCK, WIDTH),
        shape(8, BLOCK, PAD),
        shape(LONG, PAD),
        shape(LONG, PAD),
        shape(CHIPS, BLOCK, PAD),
        shape(CHIPS, BLOCK, PAD),
        shape(BLOCK, WIDTH, dtype=FULL_TYPE),
        shape(BLOCK, WIDTH),
        shape(CHIPS, 8, BLOCK, dtype=FULL_TYPE),
        shape(8, BLOCK, dtype=FULL_TYPE),
        shape(2, EXPERT_ROWS, WIDTH),
        shape(4, 4, CAPACITY, FF),
        shape(4, 2, CAPACITY, FF // 2),
        shape(2, EXPERT_ROWS, WIDTH),
        shape(1, EXPERT_ROWS, 128, dtype=FULL_TYPE),
        shape(4, CAPACITY, FF // 2),
        shape(4, CAPACITY, FF // 2),
    ]
    return pl.pallas_call(
        layer_kernel,
        out_shape=shapes,
        in_specs=[
            smem(),
            vmem(),
            vmem(),
            anywhere(),
            anywhere(),
            vmem(),
            anywhere(),
            vmem(),
            vmem(),
        ]
        + [anywhere()] * 4,
        out_specs=[anywhere()] * 8 + [vmem()] * 2 + [anywhere()] * 3 + [vmem()] * 4,
        scratch_shapes=[
            pltpu.VMEM((8, BLOCK, WIDTH), HALF_TYPE),
            pltpu.VMEM((CHIPS, BLOCK, PAD), HALF_TYPE),
            pltpu.VMEM((CHIPS, BLOCK, PAD), HALF_TYPE),
            pltpu.VMEM((BLOCK, WIDTH), FULL_TYPE),
            pltpu.VMEM((BLOCK, WIDTH), HALF_TYPE),
            pltpu.VMEM((2, EXPERT_ROWS, WIDTH), HALF_TYPE),
            pltpu.VMEM((2, EXPERT_ROWS, WIDTH), HALF_TYPE),
            pltpu.VMEM((BLOCK, WIDTH), HALF_TYPE),
            pltpu.VMEM((WIDTH, WIDTH), HALF_TYPE),
            pair(13),
            pair(CHIPS),
            pltpu.SemaphoreType.DMA((5,)),
            pltpu.SemaphoreType.DMA((8,)),
            pltpu.VMEM((2, EXPERT_ROWS, WIDTH), HALF_TYPE),
            pltpu.VMEM((2, EXPERT_ROWS, WIDTH), HALF_TYPE),
            pltpu.VMEM((2, EXPERT_ROWS, WIDTH), HALF_TYPE),
            pltpu.VMEM((2, EXPERT_ROWS, WIDTH), HALF_TYPE),
            pltpu.VMEM((4, 4, CAPACITY, FF), HALF_TYPE),
            pltpu.VMEM((4, 4, CAPACITY, FF), HALF_TYPE),
            pltpu.VMEM((4, 2, CAPACITY, FF // 2), HALF_TYPE),
            pltpu.VMEM((4, 2, CAPACITY, FF // 2), HALF_TYPE),
            pltpu.VMEM((4, 2, CAPACITY, FF // 2), HALF_TYPE),
            pltpu.VMEM((4, 2, CAPACITY, FF // 2), HALF_TYPE),
            pltpu.VMEM((1, EXPERT_ROWS, 128), FULL_TYPE),
            pltpu.SemaphoreType.DMA((4,)),
            pair(2),
            pair(2),
            pair(2),
            pair(2),
            pair(12),
            pair(4),
            pltpu.SemaphoreType.DMA((4,)),
        ],
        compiler_params=pltpu.CompilerParams(
            collective_id=0, has_side_effects=True, vmem_limit_bytes=62 * 2**20
        ),
    )(*operands)


def slot_rows(place):
    return pl.ds(pl.multiple_of(place * CAPACITY, CAPACITY), CAPACITY)


def back_kernel(
    kind_ref,
    tokens_ref,
    gain_ref,
    gain_two_ref,
    grad_ref,
    residual_ref,
    info_ref,
    match_ref,
    grad_back_ref,
    router_ref,
    proj_ref,
    hidden_two_ref,
    total_ref,
    query_hbm,
    key_hbm,
    value_hbm,
    heads_hbm,
    weight_hbm,
    hidden_hbm,
    attended_hbm,
    in_grad_hbm,
    in_first_hbm,
    returned_hbm,
    x_part_hbm,
    y_part_hbm,
    mixed_ref,
    tokens_grad_ref,
    in_sum_ref,
    out_sum_ref,
    dense_sum_ref,
    qkv_sum_ref,
    dense_land,
    query_ref,
    key_ref,
    value_ref,
    heads_ref,
    weight,
    hidden_ref,
    attended_ref,
    x_part,
    y_part,
    out_land,
    returned,
    grad_residual,
    grad_sent,
    grad_out,
    stacked,
    grad_stacked,
    grad_query,
    grad_key,
    grad_value,
    projected,
    part_sib,
    part_own,
    land_sib,
    land_half,
    land_full,
    big,
    big_first,
    big_direct,
    big_combined,
    big_x,
    big_y,
    big_land,
    mid,
    mid_first,
    mid_direct,
    mid_combined,
    mid_x,
    mid_y,
    mid_land,
    qkv,
    qkv_first,
    qkv_direct,
    qkv_combined,
    qkv_x,
    qkv_y,
    qkv_land,
    dense_send,
    weight_sems,
    load_sems,
    grad_sems,
    sib_sems,
    ring_sems,
    big_sems,
    out_spread,
    big_spread,
    mid_sems,
    mid_spread,
    qkv_sems,
    qkv_spread,
    dense_sems,
    returned_sems,
):
    z, core = here()
    mine = z * 2 + core
    up, down, far = lax.rem(z + 1, CHIPS), lax.rem(z + 3, CHIPS), lax.rem(z + 2, CHIPS)
    barrier = pltpu.get_barrier_semaphore()
    greet(barrier)
    greet_plane(barrier)
    loads = []
    for index, (source, target) in enumerate(
        (
            (in_grad_hbm, big),
            (in_first_hbm, big_first),
            (x_part_hbm, x_part),
            (y_part_hbm, y_part),
            (
                returned_hbm.at[:, slot_rows(mine), :],
                returned.at[:, slot_rows(mine), :],
            ),
            (attended_hbm, attended_ref),
            (query_hbm, query_ref),
            (key_hbm, key_ref),
            (value_hbm, value_ref),
            (heads_hbm, heads_ref),
            (hidden_hbm, hidden_ref),
        )
    ):
        copy = pltpu.make_async_copy(source, target, load_sems.at[index])
        copy.start()
        loads.append(copy)
    weight_loads = load_windows(weight_hbm, weight, weight_sems, z)

    info = info_ref[...]
    columns = jnp.transpose(
        jnp.concatenate([info, jnp.zeros((120, BLOCK), jnp.float32)], axis=0)
    )
    lane_ids = lax.broadcasted_iota(jnp.int32, (BLOCK, SLOTS), 1).astype(jnp.float32)
    at_zero, at_one = lane_ids == columns[:, 0:1], lane_ids == columns[:, 1:2]
    ids = lax.broadcasted_iota(jnp.int32, (SLOTS, BLOCK), 0).astype(jnp.float32)
    lines = match_ref[0]
    match = jnp.concatenate(
        [jnp.broadcast_to(lines[:, lane : lane + 1], (EXPERT_ROWS, BLOCK)) for lane in (0, 64)],
        axis=0,
    )
    parts = []
    for place, gate in ((0, 2), (1, 3)):
        value = jnp.sum(
            jnp.where(ids == info[place : place + 1, :], match, 0.0), axis=0, keepdims=True
        )
        used = info[gate : gate + 1, :].astype(jnp.bfloat16).astype(jnp.float32)
        ratio = jnp.where(used > 0.0, info[gate : gate + 1, :] / jnp.where(used > 0.0, used, 1.0), 1.0)
        parts.append(value * ratio)
    gap = parts[0] * info[3:4, :] - parts[1] * info[2:3, :]
    names = lax.broadcasted_iota(jnp.int32, (EXPERTS, BLOCK), 0).astype(jnp.float32)
    pick_zero = jnp.where(names == info[4:5, :], 1.0, 0.0)
    pick_one = jnp.where(names == info[5:6, :], 1.0, 0.0)
    grad_logits = (gap * (pick_zero - pick_one)).astype(jnp.bfloat16)
    chosen = jnp.where(at_zero | at_one, 1.0, 0.0).astype(jnp.bfloat16)
    grad_two = (
        dot_tn(grad_logits, router_ref[...])
        + dot_nn(chosen[:, :EXPERT_ROWS], grad_back_ref[0])
        + dot_nn(chosen[:, EXPERT_ROWS:], grad_back_ref[1])
    )
    normed_two, inverse_two = norm_parts(residual_ref[...])
    gain_two_grad = jnp.sum(grad_two * normed_two, axis=0, keepdims=True)
    grad_residual[...] = grad_ref[...].astype(jnp.float32) + norm_back(
        grad_two * gain_two_ref[...][None], normed_two, inverse_two
    )
    grad_branch = grad_residual[...].astype(jnp.bfloat16)
    for chip in range(CHIPS):
        first = (chip + chip // 2) * 128
        grad_sent[chip] = dot_nt(grad_branch, proj_ref[first : first + PAD, :]).astype(
            jnp.bfloat16
        )
    pl.semaphore_wait(barrier, 13)
    owner_core = lax.rem(core + z, 2)
    grad_send, grad_recv = grad_sems.at[0], grad_sems.at[1]

    @pl.loop(0, CHIPS)
    def _(step):
        chip = lax.rem(z + step, CHIPS)
        mine_too = (chip == z) & (owner_core == core)

        @pl.when(jnp.logical_not(mine_too))
        def _():
            push(
                grad_sent.at[chip],
                grad_out.at[z],
                grad_send,
                grad_recv,
                chip,
                z,
                device(chip, owner_core),
            ).start()

        @pl.when(mine_too)
        def _():
            grad_out[z] = grad_sent[chip]

    for step in range(1, 8):
        place = lax.rem(mine + step, 8)
        copy = push(
            returned_hbm.at[:, slot_rows(place), :],
            returned.at[:, slot_rows(mine), :],
            returned_sems.at[0],
            returned_sems.at[1],
            0,
            0,
            (lax.axis_index("dp"), place),
        )
        copy.start()
    for load in loads[:4]:
        load.wait()
    big_sum = PlaneSum(big, big_first, big_direct, big_combined, big_sems.at[0], big_sems.at[1])
    big_sum.start_near()
    big_sum.second(waits=False)
    loads[5].wait()
    for chip in range(CHIPS):
        grads = dot_tn(attended_ref[chip], grad_branch).astype(jnp.bfloat16)
        first = (chip % 2) * HD
        for y in range(4):
            start = first + y * CAPACITY
            mid[chip, y, :, :WIDTH] = grads[start : start + CAPACITY]
    narrow = jnp.concatenate(
        [
            dot_nn(grad_logits, hidden_two_ref[...]),
            gain_two_grad,
            jnp.zeros((111, WIDTH), jnp.float32),
        ],
        axis=0,
    )
    mid[:, :, :, WIDTH : WIDTH + 128] = (
        jnp.transpose(narrow).astype(jnp.bfloat16).reshape(4, 4, CAPACITY, 128)
    )
    mid[:, :, :, WIDTH + 128 :] = jnp.zeros((4, 4, CAPACITY, 128), jnp.bfloat16)
    mid_sum = PlaneSum(mid, mid_first, mid_direct, mid_combined, mid_sems.at[0], mid_sems.at[1])
    mid_sum.start()
    out_sum = PlaneSpread(x_part, y_part, out_land, out_spread.at[0], out_spread.at[1])
    out_sum.start()

    grad_key[...] = jnp.zeros_like(grad_key)
    grad_value[...] = jnp.zeros_like(grad_value)
    projected[...] = jnp.zeros_like(projected)
    for load in loads[6:10]:
        load.wait()
    kind_bias = kind_ref[0].astype(jnp.float32) * NEGATIVE

    def attend(step):
        slot = lax.rem(z + step, CHIPS)
        block = slot * 2 + lax.rem(core + slot, 2)

        @pl.when(block != mine)
        def _():
            landed(grad_out.at[slot], grad_send, grad_recv, slot)

        queries = query_ref[block]
        grads = grad_out[slot]
        products = grads.astype(jnp.float32) * heads_ref[slot].astype(jnp.float32)
        selector = jnp.concatenate(
            [head_mask(z, head, 1.0, jnp.float32) for head in range(LOCAL_HEADS)]
            + [jnp.zeros((8 - LOCAL_HEADS, PAD), jnp.float32)],
            axis=0,
        )
        deltas = lax.dot_general(
            selector,
            products,
            (((1,), (1,)), ((), ())),
            preferred_element_type=jnp.float32,
            precision=lax.Precision.HIGHEST,
        )
        for head in range(LOCAL_HEADS):
            part = slice(head * BLOCK, (head + 1) * BLOCK)
            stacked[part, :] = queries * head_mask(z, head, HD ** (-0.5), jnp.bfloat16)
            grad_stacked[part, :] = grads * head_mask(z, head, 1.0, jnp.bfloat16)
        totals = total_ref[slot]
        delta_row = jnp.concatenate(
            [deltas[head : head + 1, :] for head in range(LOCAL_HEADS)], axis=1
        )
        total_row = jnp.concatenate(
            [totals[head : head + 1, :] for head in range(LOCAL_HEADS)], axis=1
        )

        def work(rows, bias, is_diagonal):
            keys, values = key_ref[rows, :], value_ref[rows, :]
            probs = jnp.exp(dot_nt(keys, stacked[...]) - (total_row - bias))
            if is_diagonal:
                row = lax.broadcasted_iota(jnp.int32, (BLOCK, STACK), 0)
                column = lax.broadcasted_iota(jnp.int32, (BLOCK, STACK), 1)
                probs = jnp.where(row <= lax.rem(column, BLOCK), probs, 0.0)
            grad_probs = dot_nt(values, grad_stacked[...])
            grad_scores = (probs * (grad_probs - delta_row)).astype(jnp.bfloat16)
            grad_value[rows, :] += dot_nn(probs.astype(jnp.bfloat16), grad_stacked[...])
            grad_key[rows, :] += dot_nn(grad_scores, stacked[...])
            return dot_tn(grad_scores, keys)

        grad_query[...] = work(block_rows(block), 0.0, True)

        @pl.when(block != 2 * slot)
        def _():
            grad_query[...] += work(block_rows(block - 1), 0.0, False)

        @pl.loop(0, slot)
        def _(chunk):
            bias = jnp.where((slot >= 2) & (chunk < 2), kind_bias, 0.0)
            grad_query[...] += work(chunk_rows(chunk), bias, False)

        combined = jnp.zeros((BLOCK, PAD), jnp.float32)
        for head in range(LOCAL_HEADS):
            part = slice(head * BLOCK, (head + 1) * BLOCK)
            combined += grad_query[part, :] * head_mask(z, head, HD ** (-0.5), jnp.float32)
        projected[block_rows(block), :PAD] = combined.astype(jnp.bfloat16)

    pl.loop(0, CHIPS)(attend)
    projected[:, PAD : 2 * PAD] = grad_key[...].astype(jnp.bfloat16)
    projected[:, 2 * PAD :] = grad_value[...].astype(jnp.bfloat16)
    for load in weight_loads:
        load.wait()

    def partial(chip, which):
        return dot_nt(projected[block_rows(chip * 2 + which), :], weight[...])

    sib_send, sib_recv = sib_sems.at[0], sib_sems.at[1]

    def sib_copy(index):
        return push(
            part_sib.at[index],
            land_sib.at[index],
            sib_send,
            sib_recv,
            index,
            index,
            device(z, 1 - core),
        )

    order = (far, up, down, z)
    for index, chip in enumerate(order):
        part_sib[index] = partial(chip, 1 - core).astype(jnp.bfloat16)
        sib_copy(index).start()

    loads[10].wait()
    for tile in range(3):
        lanes = slice(tile * PAD, (tile + 1) * PAD)
        weights = dot_tn(hidden_ref[...], projected[:, lanes]).astype(jnp.bfloat16)
        qkv[:, :, :, lanes] = weights.reshape(4, 4, CAPACITY, PAD)
    qkv_sum = PlaneSum(
        qkv, qkv_first, qkv_direct, qkv_combined, qkv_sems.at[0], qkv_sems.at[1]
    )
    qkv_sum.start()
    mid_sum.second()


    def own(index):
        value = partial(order[index], core)
        landed(land_sib.at[index], sib_send, sib_recv, index)
        return value + land_sib[index].astype(jnp.float32)

    first, second = pl.ds(0, HALF), pl.ds(HALF, HALF)
    ring_send, ring_recv = ring_sems.at[0], ring_sems.at[1]
    copies = []

    def ring(source, target, index, where):
        copy = push(source, target, ring_send, ring_recv, index, index, where)
        copy.start()
        copies.append(copy)

    above, below = device(up, core), device(down, core)
    part_own[0] = own(0).astype(jnp.bfloat16)
    ring(part_own.at[0, first], land_half.at[0], 0, above)
    ring(part_own.at[0, second], land_half.at[1], 1, below)
    part_own[1] = own(1).astype(jnp.bfloat16)
    ring(part_own.at[1, second], land_full.at[0, second], 2, above)
    part_own[2] = own(2).astype(jnp.bfloat16)
    ring(part_own.at[2, first], land_full.at[1, first], 3, below)
    grad_one = own(3)
    qkv_sum.second()
    landed(land_half.at[0], ring_send, ring_recv, 0)
    part_own[1, first, :] = added(part_own[1, first, :], land_half[0]).astype(jnp.bfloat16)
    ring(part_own.at[1, first], land_full.at[0, first], 4, above)
    landed(land_half.at[1], ring_send, ring_recv, 1)
    part_own[2, second, :] = added(part_own[2, second, :], land_half[1]).astype(jnp.bfloat16)
    ring(part_own.at[2, second], land_full.at[1, second], 5, below)
    mid_sum.third(mid_x, mid_y)
    mid_total = PlaneSpread(mid_x, mid_y, mid_land, mid_spread.at[0], mid_spread.at[1])
    mid_total.start()
    qkv_sum.third(qkv_x, qkv_y)
    qkv_total = PlaneSpread(qkv_x, qkv_y, qkv_land, qkv_spread.at[0], qkv_spread.at[1])
    qkv_total.start()
    big_sum.third(big_x, big_y)
    big_total = PlaneSpread(big_x, big_y, big_land, big_spread.at[0], big_spread.at[1])
    big_total.start()
    loads[4].wait()
    seven = returned.at[:, pl.ds(0, 7 * CAPACITY), :]
    pltpu.make_async_copy(seven, seven, returned_sems.at[1, 0]).wait()
    mixing = (
        jnp.where(at_zero, columns[:, 2:3], 0.0) + jnp.where(at_one, columns[:, 3:4], 0.0)
    ).astype(jnp.bfloat16)
    mixed_ref[...] = (
        residual_ref[...]
        + dot_nn(mixing[:, :EXPERT_ROWS], returned[0])
        + dot_nn(mixing[:, EXPERT_ROWS:], returned[1])
    ).astype(jnp.bfloat16)
    out_left, out_right = out_sum.total()
    out_sum_ref[:, : FF // 2] = out_left
    out_sum_ref[:, FF // 2 :] = out_right
    mid_left, mid_right = mid_total.total()
    qkv_left, qkv_right = qkv_total.total()
    share = CAPACITY // 8
    line = jnp.concatenate([mid_left, mid_right, qkv_left, qkv_right], axis=1)
    for piece in range(8):
        rows = slice(piece * share, (piece + 1) * share)
        dense_send[piece] = jnp.concatenate(
            [line[rows, :LINE], line[rows, LINE:], jnp.zeros((16 - 2 * share, LINE), jnp.float32)],
            axis=0,
        ).astype(jnp.bfloat16)
    dense_copies = []
    for step in range(1, 8):
        place = lax.rem(mine + step, 8)
        copy = push(
            dense_send.at[place],
            dense_land.at[mine],
            dense_sems.at[0],
            dense_sems.at[1],
            step - 1,
            step - 1,
            (lax.axis_index("dp"), place),
        )
        copy.start()
        dense_copies.append(copy)
    dense_land[mine] = dense_send[mine]
    landed(land_full.at[0, second], ring_send, ring_recv, 2)
    landed(land_full.at[1, first], ring_send, ring_recv, 3)
    landed(land_full.at[0, first], ring_send, ring_recv, 4)
    landed(land_full.at[1, second], ring_send, ring_recv, 5)
    grad_one += added(land_full[0], land_full[1])
    normed_one, inverse_one = norm_parts(tokens_ref[...].astype(jnp.float32))
    tokens_grad_ref[...] = grad_residual[...] + norm_back(
        grad_one * gain_ref[...][None], normed_one, inverse_one
    )
    left, right = big_total.total()
    in_sum_ref[:, : FF // 2] = left
    in_sum_ref[:, FF // 2 :] = right
    for step in range(1, 8):
        landed(
            dense_land.at[lax.rem(mine + 8 - step, 8)],
            dense_sems.at[0],
            dense_sems.at[1],
            step - 1,
        )
    lines = [dense_land[place].astype(jnp.float32) for place in range(8)]
    total = sum(lines[1:], lines[0])
    total = jnp.concatenate([total[:share], total[share : 2 * share]], axis=1)
    dense_sum_ref[...] = total[:, :DENSE]
    qkv_sum_ref[...] = jnp.zeros_like(qkv_sum_ref)
    for chip in range(CHIPS):
        line = lines[2 * chip] + lines[2 * chip + 1]
        line = jnp.concatenate([line[:share], line[share : 2 * share]], axis=1)[:, DENSE:]
        for part in range(3):
            start = part * WIDTH + (chip + chip // 2) * 128
            qkv_sum_ref[:, start : start + PAD] += line[:, part * PAD : (part + 1) * PAD]
    pltpu.make_async_copy(seven, seven, returned_sems.at[0, 0]).wait()
    for copy in dense_copies + copies:
        copy.wait_send()
    for user in (big_sum, out_sum, big_total, mid_sum, mid_total, qkv_sum, qkv_total):
        user.drain()
    for index in range(CHIPS):
        sib_copy(index).wait_send()

    @pl.loop(0, CHIPS)
    def _(chip):
        @pl.when((chip != z) | (owner_core != core))
        def _():
            push(
                grad_sent.at[chip],
                grad_out.at[chip],
                grad_send,
                grad_recv,
                chip,
                chip,
                device(z, 1 - core),
            ).wait_send()


def plane_scratch(lanes):
    return [
        pltpu.VMEM((4, 4, CAPACITY, lanes), HALF_TYPE),
        pltpu.VMEM((4, 2, CAPACITY, lanes // 2), HALF_TYPE),
        pltpu.VMEM((4, 2, CAPACITY, lanes // 2), HALF_TYPE),
        pltpu.VMEM((4, 2, CAPACITY, lanes // 2), HALF_TYPE),
        pltpu.VMEM((4, CAPACITY, lanes // 2), HALF_TYPE),
        pltpu.VMEM((4, CAPACITY, lanes // 2), HALF_TYPE),
        pltpu.VMEM((6, CAPACITY, lanes // 2), HALF_TYPE),
    ]


def back(*operands):
    def shape(*dims, dtype=FULL_TYPE):
        return jax.ShapeDtypeStruct(dims, dtype)

    def pair(count):
        return pltpu.SemaphoreType.DMA((2, count))

    return pl.pallas_call(
        back_kernel,
        out_shape=[
            shape(BLOCK, WIDTH, dtype=HALF_TYPE),
            shape(BLOCK, WIDTH),
            shape(CAPACITY, FF),
            shape(CAPACITY, FF),
            shape(CAPACITY // 8, DENSE),
            shape(CAPACITY // 8, 3 * WIDTH),
        ],
        in_specs=[smem()] + [vmem()] * 12 + [anywhere()] * 12,
        out_specs=[vmem()] * 6,
        scratch_shapes=[
            pltpu.VMEM((8, 16, LINE), HALF_TYPE),
            pltpu.VMEM((8, BLOCK, PAD), HALF_TYPE),
            pltpu.VMEM((LONG, PAD), HALF_TYPE),
            pltpu.VMEM((LONG, PAD), HALF_TYPE),
            pltpu.VMEM((CHIPS, BLOCK, PAD), HALF_TYPE),
            pltpu.VMEM((WIDTH, 3 * PAD), HALF_TYPE),
            pltpu.VMEM((LONG, WIDTH), HALF_TYPE),
            pltpu.VMEM((CHIPS, BLOCK, PAD), HALF_TYPE),
            pltpu.VMEM((4, CAPACITY, FF // 2), HALF_TYPE),
            pltpu.VMEM((4, CAPACITY, FF // 2), HALF_TYPE),
            pltpu.VMEM((6, CAPACITY, FF // 2), HALF_TYPE),
            pltpu.VMEM((2, EXPERT_ROWS, WIDTH), HALF_TYPE),
            pltpu.VMEM((BLOCK, WIDTH), FULL_TYPE),
            pltpu.VMEM((CHIPS, BLOCK, PAD), HALF_TYPE),
            pltpu.VMEM((CHIPS, BLOCK, PAD), HALF_TYPE),
            pltpu.VMEM((STACK, PAD), HALF_TYPE),
            pltpu.VMEM((STACK, PAD), HALF_TYPE),
            pltpu.VMEM((STACK, PAD), FULL_TYPE),
            pltpu.VMEM((LONG, PAD), FULL_TYPE),
            pltpu.VMEM((LONG, PAD), FULL_TYPE),
            pltpu.VMEM((LONG, 3 * PAD), HALF_TYPE),
            pltpu.VMEM((CHIPS, BLOCK, WIDTH), HALF_TYPE),
            pltpu.VMEM((CHIPS - 1, BLOCK, WIDTH), HALF_TYPE),
            pltpu.VMEM((CHIPS, BLOCK, WIDTH), HALF_TYPE),
            pltpu.VMEM((2, HALF, WIDTH), HALF_TYPE),
            pltpu.VMEM((2, BLOCK, WIDTH), HALF_TYPE),
            *plane_scratch(FF),
            *plane_scratch(DENSE),
            *plane_scratch(3 * PAD),
            pltpu.VMEM((8, 16, LINE), HALF_TYPE),
            pltpu.SemaphoreType.DMA((3,)),
            pltpu.SemaphoreType.DMA((11,)),
            pair(CHIPS),
            pair(CHIPS),
            pair(6),
            pair(12),
            pair(6),
            pair(6),
            pair(12),
            pair(6),
            pair(12),
            pair(6),
            pair(7),
            pair(1),
        ],
        compiler_params=pltpu.CompilerParams(
            collective_id=1, has_side_effects=True, vmem_limit_bytes=60 * 2**20
        ),
    )(*operands)


def as_row(column):
    size = column.shape[0]
    row = lax.broadcasted_iota(jnp.int32, (size, size), 0)
    lane = lax.broadcasted_iota(jnp.int32, (size, size), 1)
    return jnp.sum(jnp.where(row == lane, column, 0.0), axis=0, keepdims=True)


def finish_kernel(
    mixed_ref,
    tokens_grad_ref,
    in_sum_ref,
    out_sum_ref,
    dense_hbm,
    qkv_hbm,
    weight_ref,
    gain_hbm,
    mixed_out,
    tokens_grad_out,
    gain_hbm_out,
    qkv_hbm_out,
    proj_hbm_out,
    gain_two_hbm_out,
    router_hbm_out,
    in_out,
    out_out,
    weight,
    mixed,
    tokens_grad,
    in_sum,
    out_sum,
    dense_ref,
    qkv_ref,
    gain_ref,
    gain_out,
    proj_out,
    gain_two_out,
    router_out,
    sem,
    load_sems,
    store_sems,
):
    loads = []
    for index, (source, target) in enumerate(
        (
            (tokens_grad_ref, tokens_grad),
            (in_sum_ref, in_sum),
            (out_sum_ref, out_sum),
            (mixed_ref, mixed),
            (dense_hbm, dense_ref),
            (qkv_hbm, qkv_ref),
            (gain_hbm, gain_ref),
        )
    ):
        copy = pltpu.make_async_copy(source, target, load_sems.at[index])
        copy.start()
        loads.append(copy)
    share = CAPACITY // 8
    first = (lax.axis_index("dp") * 8 + lax.axis_index("expert")) * share
    start = pl.multiple_of(jnp.minimum(first // 16, WIDTH // 16 - 2) * 16, 16)
    load = pltpu.make_async_copy(weight_ref.at[pl.ds(start, 32), :], weight, sem)
    load.start()
    pairs = [(0, tokens_grad, tokens_grad_out.at[0]), (1, in_sum, in_out.at[0])]
    for part in range(4):
        pairs.append(
            (
                2,
                out_sum.at[:, pl.ds(part * WIDTH, WIDTH)],
                out_out.at[0, pl.ds(part * CAPACITY, CAPACITY), :],
            )
        )
    pairs.append((3, mixed, mixed_out.at[0]))
    stores = []
    for index, (needs, source, target) in enumerate(pairs):
        if index < 3 or needs == 3:
            loads[needs].wait()
        copy = pltpu.make_async_copy(source, target, store_sems.at[index])
        copy.start()
        stores.append(copy)
    for copy in loads[4:]:
        copy.wait()
    dense = dense_ref[...]
    proj_out[...] = dense[:, :WIDTH]
    router_out[...] = dense[:, WIDTH : WIDTH + EXPERTS]
    gain_two_out[...] = as_row(dense[:, WIDTH + EXPERTS : WIDTH + EXPERTS + 1])
    row = lax.broadcasted_iota(jnp.int32, (share, 32), 0)
    column = lax.broadcasted_iota(jnp.int32, (share, 32), 1)
    chosen = jnp.where(column == row + (first - start), 1.0, 0.0).astype(jnp.bfloat16)
    row = lax.broadcasted_iota(jnp.int32, (share, WIDTH), 0)
    column = lax.broadcasted_iota(jnp.int32, (share, WIDTH), 1)
    gain = jnp.sum(
        jnp.where(column == row + first, gain_ref[...][None], 0.0), axis=1, keepdims=True
    )
    load.wait()
    products = qkv_ref[...] * dot_nn(chosen, weight[...])
    gain_out[...] = as_row(jnp.sum(products, axis=1, keepdims=True) / gain)
    for index, (source, target) in enumerate(
        (
            (qkv_ref, qkv_hbm_out),
            (proj_out, proj_hbm_out),
            (router_out, router_hbm_out),
            (gain_two_out, gain_two_hbm_out),
            (gain_out, gain_hbm_out),
        )
    ):
        copy = pltpu.make_async_copy(source, target, store_sems.at[7 + index])
        copy.start()
        stores.append(copy)
    for copy in stores:
        copy.wait()


def finish(*operands):
    def shape(*dims, dtype=FULL_TYPE):
        return jax.ShapeDtypeStruct(dims, dtype)

    share = CAPACITY // 8
    shapes = [
        shape(1, BLOCK, WIDTH, dtype=HALF_TYPE),
        shape(1, BLOCK, WIDTH),
        shape(1, share),
        shape(share, 3 * WIDTH),
        shape(share, WIDTH),
        shape(1, share),
        shape(share, EXPERTS),
        shape(1, CAPACITY, FF),
        shape(1, 4 * CAPACITY, WIDTH),
    ]
    return pl.pallas_call(
        finish_kernel,
        out_shape=shapes,
        in_specs=[anywhere()] * 8,
        out_specs=[anywhere()] * 9,
        scratch_shapes=[
            pltpu.VMEM((32, 3 * WIDTH), HALF_TYPE),
            pltpu.VMEM((BLOCK, WIDTH), HALF_TYPE),
            pltpu.VMEM((BLOCK, WIDTH), FULL_TYPE),
            pltpu.VMEM((CAPACITY, FF), FULL_TYPE),
            pltpu.VMEM((CAPACITY, FF), FULL_TYPE),
            pltpu.VMEM((share, DENSE), FULL_TYPE),
            pltpu.VMEM((share, 3 * WIDTH), FULL_TYPE),
            pltpu.VMEM((WIDTH,), FULL_TYPE),
            pltpu.VMEM((1, share), FULL_TYPE),
            pltpu.VMEM((share, WIDTH), FULL_TYPE),
            pltpu.VMEM((1, share), FULL_TYPE),
            pltpu.VMEM((share, EXPERTS), FULL_TYPE),
            pltpu.SemaphoreType.DMA,
            pltpu.SemaphoreType.DMA((7,)),
            pltpu.SemaphoreType.DMA((12,)),
        ],
        compiler_params=pltpu.CompilerParams(vmem_limit_bytes=62 * 2**20),
    )(*operands)


def on_device(
    tokens,
    group_kind,
    routes,
    norm1_gain,
    qkv_weight,
    proj_weight,
    norm2_gain,
    router_weight,
    frozen_in,
    frozen_out,
    new_in,
    new_out,
    out_grad,
):
    width = WIDTH
    router = router_weight.T
    (
        hidden,
        queries,
        keys,
        values,
        heads,
        attended,
        residual,
        hidden_two,
        totals,
        info,
        returned,
        in_grad,
        in_first,
        grad_back,
        match,
        x_part,
        y_part,
    ) = layer(
        group_kind,
        tokens[0],
        norm1_gain,
        qkv_weight,
        out_grad[0],
        routes[0].T,
        proj_weight,
        norm2_gain,
        router,
        frozen_in[0],
        frozen_out[0],
        new_in[0],
        new_out[0],
    )
    mixed, tokens_grad, in_sum, out_sum, dense_sum, qkv_sum = back(
        group_kind,
        tokens[0],
        norm1_gain,
        norm2_gain,
        out_grad[0],
        residual,
        info,
        match,
        grad_back,
        router,
        proj_weight,
        hidden_two,
        totals,
        queries,
        keys,
        values,
        heads,
        qkv_weight,
        hidden.reshape(LONG, width),
        attended,
        in_grad,
        in_first,
        returned,
        x_part,
        y_part,
    )
    outputs = finish(
        mixed, tokens_grad, in_sum, out_sum, dense_sum, qkv_sum, qkv_weight, norm1_gain
    )
    return tuple(
        value[0] if index in (2, 5) else value for index, value in enumerate(outputs)
    )


def solution(mesh):
    return jax.shard_map(
        on_device,
        mesh=mesh,
        in_specs=(
            P("dp", "expert", None),
            P("dp"),
            P("dp", "expert", None),
            P(),
            P(),
            P(),
            P(),
            P(),
            P("expert", None, None),
            P("expert", None, None),
            P("expert", None, None),
            P("expert", None, None),
            P("dp", "expert", None),
        ),
        out_specs=(
            P("dp", "expert", None),
            P("dp", "expert", None),
            P(("dp", "expert")),
            P(("dp", "expert"), None),
            P(("dp", "expert"), None),
            P(("dp", "expert")),
            P(("dp", "expert"), None),
            P("expert", "dp", None),
            P("expert", "dp", None),
        ),
        check_vma=False,
    )
```
